32 devices in a mesh: dp: 4 (over z), axial: 8 (over y, x, core).
Axes of the slice: x: 2, y: 2, z: 4, core: 2. Of those that a mesh axis runs over, the one named last changes fastest.
Arguments:
- pair: bfloat16 [4, 256, 256, 128], P('dp', 'axial'), may hold values from -6 to 6
- cotangent: bfloat16 [4, 256, 256, 128], P('dp', 'axial'), may hold values from -6 to 6
- lengths: int32 [4], P('dp'), may hold values from 1 to 256, 640 in all
- outgo_norm: float32 [128], replicated, may hold values from 0.1 to 1.9
- outgo_proj: float32 [128, 640], replicated, may hold values from -0.5 to 0.5
- outgo_gain: float32 [128], replicated, may hold values from 0.1 to 1.9
- outgo_final: float32 [128, 128], replicated, may hold values from -0.5 to 0.5
- incom_norm: float32 [128], replicated, may hold values from 0.1 to 1.9
- incom_proj: float32 [128, 640], replicated, may hold values from -0.5 to 0.5
- incom_gain: float32 [128], replicated, may hold values from 0.1 to 1.9
- incom_final: float32 [128, 128], replicated, may hold values from -0.5 to 0.5
Outputs:
- grad_pair: float32 [4, 256, 256, 128], P('dp', 'axial')
- grad_outgo_norm: float32 [128], replicated
- grad_outgo_proj: float32 [128, 640], replicated
- grad_outgo_gain: float32 [128], replicated
- grad_outgo_final: float32 [128, 128], replicated
- grad_incom_norm: float32 [128], replicated
- grad_incom_proj: float32 [128, 640], replicated
- grad_incom_gain: float32 [128], replicated
- grad_incom_final: float32 [128, 128], replicated
The draws below stay inside these ranges and needn't reach their ends.
Inputs may be any that keep to these rules, and one draw needn't show every extreme that they name: lengths[c] is the crop length of complex c; some complex has exactly 256 tokens.
All inputs are finite; a program needn't handle non-finite values. No bound on the sum of `lengths` on one device may be relied on, other than what follows from the above.
Results may differ from the reference program's by a relative error of at most 0.03.
Values may be sent and summed in bfloat16 or wider, within the bound.
No kernel may reach another device: no remote copies, remote signals or barrier semaphores. Data moves between devices by JAX's collectives and lax.ppermute only.
A program may use at most 192 MiB of HBM per device.

```python
import math
import jax
import jax.numpy as jnp
import numpy as np
from jax import lax

C = 128
H = 128
TOK = 256
N_DP = 4


def steps_of(own_key, shape, split, low, top_value):
    def one(dim, blocks):
        heights = jax.random.uniform(jax.random.fold_in(jax.random.fold_in(own_key, 6), dim), (blocks,), jnp.float32, low / len(split), top_value / len(split))
        return jnp.repeat(jnp.exp(heights), shape[dim] // blocks).reshape((-1,) + (1,) * (len(shape) - dim - 1))

    factor_of = one(*split[0])
    for cut in split[1:]:
        factor_of = factor_of * one(*cut)
    return factor_of


def split_up(amount, total, bound, lean):
    loads = [(1 << 20) // math.isqrt(rank ** lean) + 1 for rank in range(2, amount + 1)]
    surplus, counts = total - bound - (amount - 1), [1] * (amount - 1)
    while surplus > 0:
        free = [i for i in range(amount - 1) if counts[i] < bound]
        mass, budget = sum([loads[i] for i in free]), surplus
        for i in free:
            extra = min(bound - counts[i], max(1, budget * loads[i] // mass), surplus)
            counts[i] = counts[i] + extra
            surplus = surplus - extra
    return np.array([bound] + counts)


def uneven(key, count, total, reach, skew):
    if count == 2:
        one = jax.random.randint(key, (), max(1, total - reach), min(reach, total - 1) + 1)
        return jnp.stack([one, total - one])
    sizes = jnp.asarray(split_up(count, total, reach, skew), jnp.int32)
    twos = (count - 1) // 2
    source_of, sink = sizes[1:1 + 2 * twos:2], sizes[2:2 + 2 * twos:2]
    slack = jnp.minimum(source_of - 1, reach - sink)
    passed = jax.random.randint(jax.random.fold_in(key, 1), (twos,), 0, 1 << 20) % (slack + 1)
    sizes = sizes.at[1:1 + 2 * twos:2].set(source_of - passed).at[2:2 + 2 * twos:2].set(sink + passed)
    return sizes[jax.random.permutation(jax.random.fold_in(key, 2), count)]


def noise(rng, dims, deviation, most, pieces=(), kind=jnp.bfloat16):
    entries = deviation * jax.random.normal(rng, dims, jnp.float32)
    if pieces:
        entries = entries * steps_of(rng, dims, pieces, -0.22, 0.18)
    return jnp.clip(entries, -most, most).astype(kind)


def setup_inputs(seed: int = 0) -> dict:
    arg_keys = jax.random.split(jax.random.key(seed), 12)
    return {
        "pair": noise(arg_keys[0], (N_DP, TOK, TOK, C), 1.0, 6.0, ((0, 4), (1, 8))),
        "cotangent": noise(arg_keys[1], (N_DP, TOK, TOK, C), 1.0, 6.0, ((0, 4), (1, 8))),
        "lengths": uneven(arg_keys[2], N_DP, N_DP * TOK * 5 // 8, TOK, 0).astype(jnp.int32),
        "outgo_norm": jnp.clip(1.0 + 0.18 * jax.random.normal(arg_keys[3], (C,), jnp.float32), 0.1, 1.9),
        "outgo_proj": noise(arg_keys[4], (C, 4 * H + C), C ** -0.5, 0.5, (), jnp.float32),
        "outgo_gain": jnp.clip(1.0 + 0.18 * jax.random.normal(arg_keys[5], (H,), jnp.float32), 0.1, 1.9),
        "outgo_final": noise(arg_keys[6], (H, C), H ** -0.5, 0.5, (), jnp.float32),
        "incom_norm": jnp.clip(1.0 + 0.18 * jax.random.normal(arg_keys[7], (C,), jnp.float32), 0.1, 1.9),
        "incom_proj": noise(arg_keys[8], (C, 4 * H + C), C ** -0.5, 0.5, (), jnp.float32),
        "incom_gain": jnp.clip(1.0 + 0.18 * jax.random.normal(arg_keys[9], (H,), jnp.float32), 0.1, 1.9),
        "incom_final": noise(arg_keys[10], (H, C), H ** -0.5, 0.5, (), jnp.float32),
    }


EPSILON = 1e-05

def rounded(inputs):
    return lax.optimization_barrier(inputs.astype(jnp.bfloat16)).astype(jnp.float32)

def layer_norm(inputs, factor):
    average = lax.optimization_barrier(jnp.mean(inputs, axis=-1, keepdims=True))
    centered = inputs - average
    spread = lax.optimization_barrier(jnp.mean(centered * centered, axis=-1, keepdims=True))
    return centered * lax.rsqrt(spread + EPSILON) * factor

def gating(mixture, pair_mask, hidden):
    left_part = mixture[:, :hidden] * jax.nn.sigmoid(mixture[:, 2 * hidden:3 * hidden]) * pair_mask
    right_part = mixture[:, hidden:2 * hidden] * jax.nn.sigmoid(mixture[:, 3 * hidden:4 * hidden]) * pair_mask
    gate_part = jax.nn.sigmoid(mixture[:, 4 * hidden:])
    return (left_part, right_part, gate_part)

def entry(flat_pair, norm_gain, projection, pair_mask, hidden):
    normed = layer_norm(flat_pair, norm_gain).astype(jnp.bfloat16)
    mixture = jnp.dot(normed, projection.astype(jnp.bfloat16), preferred_element_type=jnp.float32)
    left_part, right_part, gate_part = gating(mixture, pair_mask, hidden)
    return (normed, mixture, left_part, right_part, gate_part)

def entry_back(flat_pair, norm_gain, projection, pair_mask, hidden, normed, mixture, grad_left, grad_right, grad_gate):
    unused, pull_gate = jax.vjp(lambda inner_mix: gating(inner_mix, pair_mask, hidden), mixture)
    grad_mixture = pull_gate((grad_left, grad_right, grad_gate))[0].astype(jnp.bfloat16)
    grad_projection = jnp.dot(normed.T, grad_mixture, preferred_element_type=jnp.float32)
    grad_normed = jnp.dot(grad_mixture, projection.astype(jnp.bfloat16).T, preferred_element_type=jnp.float32)
    unused, pull_norm = jax.vjp(layer_norm, flat_pair, norm_gain)
    grad_flat, grad_gain = pull_norm(grad_normed)
    return (grad_flat, grad_gain, grad_projection)

def leave(inner_sum, gate_part, out_gain, final_weight):
    final_normed = layer_norm(inner_sum, out_gain).astype(jnp.bfloat16)
    product = jnp.dot(final_normed, final_weight.astype(jnp.bfloat16), preferred_element_type=jnp.float32)
    return (final_normed, product, product * gate_part)

def leave_back(inner_sum, gate_part, out_gain, final_weight, final_normed, product, grad_update):
    grad_product = (grad_update * gate_part).astype(jnp.bfloat16)
    grad_gate = grad_update * product
    grad_final = jnp.dot(final_normed.T, grad_product, preferred_element_type=jnp.float32)
    grad_normed = jnp.dot(grad_product, final_weight.astype(jnp.bfloat16).T, preferred_element_type=jnp.float32)
    unused, pull_norm = jax.vjp(layer_norm, inner_sum, out_gain)
    grad_inner, grad_gain = pull_norm(grad_normed)
    return (grad_inner, grad_gate, grad_gain, grad_final)

def one_complex(pair, cotangent, length, weights):
    outgo_norm, outgo_proj, outgo_gain, outgo_final, incom_norm, incom_proj, incom_gain, incom_final = weights
    tokens = pair.shape[0]
    channels = pair.shape[2]
    hidden = outgo_gain.shape[0]
    places = jnp.arange(tokens, dtype=jnp.int32)
    alive = (places < length).astype(jnp.float32)
    pair_mask = (alive[:, None] * alive[None, :]).reshape(-1, 1)
    flat_start = pair.reshape(-1, channels).astype(jnp.float32)
    normed_one, mixture_one, left_one, right_one, gate_one = entry(flat_start, outgo_norm, outgo_proj, pair_mask, hidden)
    left_first = rounded(left_one).reshape(tokens, tokens, hidden)
    right_first = rounded(right_one).reshape(tokens, tokens, hidden)
    inner_one = jnp.einsum('ikh,jkh->ijh', left_first, right_first).reshape(-1, hidden)
    final_one, product_one, update_one = leave(inner_one, gate_one, outgo_gain, outgo_final)
    flat_middle = rounded(flat_start + update_one)
    normed_two, mixture_two, left_two, right_two, gate_two = entry(flat_middle, incom_norm, incom_proj, pair_mask, hidden)
    left_second = rounded(left_two).reshape(tokens, tokens, hidden)
    right_second = rounded(right_two).reshape(tokens, tokens, hidden)
    inner_two = jnp.einsum('kih,kjh->ijh', left_second, right_second).reshape(-1, hidden)
    final_two, product_two, update_two = leave(inner_two, gate_two, incom_gain, incom_final)
    grad_end = cotangent.reshape(-1, channels).astype(jnp.float32)
    grad_inner_two, grad_gate_two, grad_gain_two, grad_final_two = leave_back(inner_two, gate_two, incom_gain, incom_final, final_two, product_two, grad_end)
    grad_cells_two = rounded(grad_inner_two).reshape(tokens, tokens, hidden)
    grad_left_two = jnp.einsum('ijh,kjh->kih', grad_cells_two, right_second).reshape(-1, hidden)
    grad_right_two = jnp.einsum('kih,ijh->kjh', left_second, grad_cells_two).reshape(-1, hidden)
    grad_flat_two, grad_norm_two, grad_proj_two = entry_back(flat_middle, incom_norm, incom_proj, pair_mask, hidden, normed_two, mixture_two, grad_left_two, grad_right_two, grad_gate_two)
    grad_middle = grad_end + grad_flat_two
    grad_inner_one, grad_gate_one, grad_gain_one, grad_final_one = leave_back(inner_one, gate_one, outgo_gain, outgo_final, final_one, product_one, grad_middle)
    grad_cells_one = rounded(grad_inner_one).reshape(tokens, tokens, hidden)
    grad_left_one = jnp.einsum('ijh,jkh->ikh', grad_cells_one, right_first).reshape(-1, hidden)
    grad_right_one = jnp.einsum('ijh,ikh->jkh', grad_cells_one, left_first).reshape(-1, hidden)
    grad_flat_one, grad_norm_one, grad_proj_one = entry_back(flat_start, outgo_norm, outgo_proj, pair_mask, hidden, normed_one, mixture_one, grad_left_one, grad_right_one, grad_gate_one)
    grad_begin = grad_middle + grad_flat_one
    grads = (grad_norm_one, grad_proj_one, grad_gain_one, grad_final_one, grad_norm_two, grad_proj_two, grad_gain_two, grad_final_two)
    return (grad_begin.reshape(tokens, tokens, channels), grads)

def reference(pair, cotangent, lengths, outgo_norm, outgo_proj, outgo_gain, outgo_final, incom_norm, incom_proj, incom_gain, incom_final):
    weights = (outgo_norm, outgo_proj, outgo_gain, outgo_final, incom_norm, incom_proj, incom_gain, incom_final)

    def advance(carry, items):
        grad_block, grads = one_complex(items[0], items[1], items[2], weights)
        return (jax.tree.map(lambda first, second: first + second, carry, grads), grad_block)
    zeros = tuple((jnp.zeros(weight.shape, jnp.float32) for weight in weights))
    totals, grad_pairs = lax.scan(advance, zeros, (pair, cotangent, lengths))
    scale = 1.0 / math.sqrt(N_DP * TOK * TOK)
    return (grad_pairs, totals[0] * scale, totals[1] * scale, totals[2] * scale, totals[3] * scale, totals[4] * scale, totals[5] * scale, totals[6] * scale, totals[7] * scale)
```

```python
import math

import jax
import jax.numpy as jnp
from jax import lax
from jax.experimental import pallas as pl
from jax.experimental.pallas import tpu as pltpu
from jax.sharding import PartitionSpec as P

EPSILON = 1e-05


def rounded(inputs):
    return lax.optimization_barrier(inputs.astype(jnp.bfloat16)).astype(jnp.float32)


def layer_norm(inputs, factor):
    average = jnp.mean(inputs, axis=-1, keepdims=True)
    centered = inputs - average
    spread = jnp.mean(centered * centered, axis=-1, keepdims=True)
    return centered * lax.rsqrt(spread + EPSILON) * factor


def gating(mixture, pair_mask, hidden):
    left_part = (
        mixture[:, :hidden] * jax.nn.sigmoid(mixture[:, 2 * hidden : 3 * hidden]) * pair_mask
    )
    right_part = (
        mixture[:, hidden : 2 * hidden]
        * jax.nn.sigmoid(mixture[:, 3 * hidden : 4 * hidden])
        * pair_mask
    )
    gate_part = jax.nn.sigmoid(mixture[:, 4 * hidden :])
    return (left_part, right_part, gate_part)


def entry(flat_pair, norm_gain, projection, pair_mask, hidden):
    normed = layer_norm(flat_pair, norm_gain).astype(jnp.bfloat16)
    mixture = jnp.dot(normed, projection.astype(jnp.bfloat16), preferred_element_type=jnp.float32)
    left_part, right_part, gate_part = gating(mixture, pair_mask, hidden)
    return (normed, mixture, left_part, right_part, gate_part)


def entry_back(
    flat_pair,
    norm_gain,
    projection,
    pair_mask,
    hidden,
    normed,
    mixture,
    grad_left,
    grad_right,
    grad_gate,
):
    unused, pull_gate = jax.vjp(lambda inner_mix: gating(inner_mix, pair_mask, hidden), mixture)
    grad_mixture = pull_gate((grad_left, grad_right, grad_gate))[0].astype(jnp.bfloat16)
    grad_projection = jnp.dot(normed.T, grad_mixture, preferred_element_type=jnp.float32)
    grad_normed = jnp.dot(
        grad_mixture, projection.astype(jnp.bfloat16).T, preferred_element_type=jnp.float32
    )
    unused, pull_norm = jax.vjp(layer_norm, flat_pair, norm_gain)
    grad_flat, grad_gain = pull_norm(grad_normed)
    return (grad_flat, grad_gain, grad_projection)


def leave(inner_sum, gate_part, out_gain, final_weight):
    final_normed = layer_norm(inner_sum, out_gain).astype(jnp.bfloat16)
    product = jnp.dot(
        final_normed, final_weight.astype(jnp.bfloat16), preferred_element_type=jnp.float32
    )
    return (final_normed, product, product * gate_part)


def leave_back(inner_sum, gate_part, out_gain, final_weight, final_normed, product, grad_update):
    grad_product = (grad_update * gate_part).astype(jnp.bfloat16)
    grad_gate = grad_update * product
    grad_final = jnp.dot(final_normed.T, grad_product, preferred_element_type=jnp.float32)
    grad_normed = jnp.dot(
        grad_product, final_weight.astype(jnp.bfloat16).T, preferred_element_type=jnp.float32
    )
    unused, pull_norm = jax.vjp(layer_norm, inner_sum, out_gain)
    grad_inner, grad_gain = pull_norm(grad_normed)
    return (grad_inner, grad_gate, grad_gain, grad_final)


def channel_major(field, row_count, tokens):
    hidden = field.shape[1]
    return jnp.transpose(field.reshape(row_count, tokens, hidden), (2, 0, 1))


def row_major(field):
    hidden = field.shape[0]
    return jnp.transpose(field, (1, 2, 0)).reshape(-1, hidden)


def plain_body(
    pair,
    cotangent,
    lengths,
    outgo_norm,
    outgo_proj,
    outgo_gain,
    outgo_final,
    incom_norm,
    incom_proj,
    incom_gain,
    incom_final,
):
    row_count = pair.shape[1]
    tokens = pair.shape[2]
    channels = pair.shape[3]
    hidden = outgo_gain.shape[0]
    length = lengths[0]
    first_row = lax.axis_index("axial") * row_count
    row_alive = (first_row + jnp.arange(row_count, dtype=jnp.int32) < length).astype(jnp.float32)
    column_alive = (jnp.arange(tokens, dtype=jnp.int32) < length).astype(jnp.float32)
    pair_mask = (row_alive[:, None] * column_alive[None, :]).reshape(-1, 1)
    flat_start = pair[0].reshape(-1, channels).astype(jnp.float32)
    normed_one, mixture_one, left_one, right_one, gate_one = entry(
        flat_start, outgo_norm, outgo_proj, pair_mask, hidden
    )
    left_first = channel_major(left_one.astype(jnp.bfloat16), row_count, tokens)
    right_first = channel_major(right_one.astype(jnp.bfloat16), row_count, tokens)
    left_owned, right_owned = (
        lax.all_to_all(left_first, "axial", split_axis=0, concat_axis=1, tiled=True),
        lax.all_to_all(right_first, "axial", split_axis=0, concat_axis=1, tiled=True),
    )
    inner_cols = jnp.einsum(
        "hik,hjk->hij", left_owned, right_owned, preferred_element_type=jnp.float32
    )
    inner_one = row_major(
        lax.all_to_all(
            inner_cols.astype(jnp.bfloat16), "axial", split_axis=1, concat_axis=0, tiled=True
        ).astype(inner_cols.dtype)
    )
    final_one, product_one, update_one = leave(inner_one, gate_one, outgo_gain, outgo_final)
    flat_middle = rounded(flat_start + update_one)
    normed_two, mixture_two, left_two, right_two, gate_two = entry(
        flat_middle, incom_norm, incom_proj, pair_mask, hidden
    )
    left_second = channel_major(left_two.astype(jnp.bfloat16), row_count, tokens)
    right_second = channel_major(right_two.astype(jnp.bfloat16), row_count, tokens)
    left_held, right_held = (
        lax.all_to_all(left_second, "axial", split_axis=0, concat_axis=1, tiled=True),
        lax.all_to_all(right_second, "axial", split_axis=0, concat_axis=1, tiled=True),
    )
    inner_held = jnp.einsum(
        "hki,hkj->hij", left_held, right_held, preferred_element_type=jnp.float32
    )
    inner_two = row_major(
        lax.all_to_all(
            inner_held.astype(jnp.bfloat16), "axial", split_axis=1, concat_axis=0, tiled=True
        ).astype(inner_held.dtype)
    )
    final_two, product_two, update_two = leave(inner_two, gate_two, incom_gain, incom_final)
    grad_end = cotangent[0].reshape(-1, channels).astype(jnp.float32)
    grad_inner_two, grad_gate_two, grad_gain_two, grad_final_two = leave_back(
        inner_two, gate_two, incom_gain, incom_final, final_two, product_two, grad_end
    )
    grad_cells_two = channel_major(grad_inner_two.astype(jnp.bfloat16), row_count, tokens)
    grad_held_two = lax.all_to_all(grad_cells_two, "axial", split_axis=0, concat_axis=1, tiled=True)
    left_back, right_back = (
        lax.all_to_all(left_second, "axial", split_axis=0, concat_axis=1, tiled=True),
        lax.all_to_all(right_second, "axial", split_axis=0, concat_axis=1, tiled=True),
    )
    grad_left_held = jnp.einsum(
        "hij,hkj->hki", grad_held_two, right_back, preferred_element_type=jnp.float32
    )
    grad_right_held = jnp.einsum(
        "hki,hij->hkj", left_back, grad_held_two, preferred_element_type=jnp.float32
    )
    grad_left_rows, grad_right_rows = (
        lax.all_to_all(
            grad_left_held.astype(jnp.bfloat16), "axial", split_axis=1, concat_axis=0, tiled=True
        ).astype(grad_left_held.dtype),
        lax.all_to_all(
            grad_right_held.astype(jnp.bfloat16), "axial", split_axis=1, concat_axis=0, tiled=True
        ).astype(grad_right_held.dtype),
    )
    grad_left_two = row_major(grad_left_rows)
    grad_right_two = row_major(grad_right_rows)
    grad_flat_two, grad_norm_two, grad_proj_two = entry_back(
        flat_middle,
        incom_norm,
        incom_proj,
        pair_mask,
        hidden,
        normed_two,
        mixture_two,
        grad_left_two,
        grad_right_two,
        grad_gate_two,
    )
    second_sums = lax.psum(
        (grad_norm_two, grad_proj_two, grad_gain_two, grad_final_two), ("dp", "axial")
    )
    grad_middle = grad_end + grad_flat_two
    grad_inner_one, grad_gate_one, grad_gain_one, grad_final_one = leave_back(
        inner_one, gate_one, outgo_gain, outgo_final, final_one, product_one, grad_middle
    )
    grad_cells_one = channel_major(grad_inner_one.astype(jnp.bfloat16), row_count, tokens)
    grad_owned_one = lax.all_to_all(
        grad_cells_one, "axial", split_axis=0, concat_axis=1, tiled=True
    )
    left_again, right_again = (
        lax.all_to_all(left_first, "axial", split_axis=0, concat_axis=1, tiled=True),
        lax.all_to_all(right_first, "axial", split_axis=0, concat_axis=1, tiled=True),
    )
    grad_left_owned = jnp.einsum(
        "hij,hjk->hik", grad_owned_one, right_again, preferred_element_type=jnp.float32
    )
    grad_right_owned = jnp.einsum(
        "hij,hik->hjk", grad_owned_one, left_again, preferred_element_type=jnp.float32
    )
    grad_left_back, grad_right_back = (
        lax.all_to_all(
            grad_left_owned.astype(jnp.bfloat16), "axial", split_axis=1, concat_axis=0, tiled=True
        ).astype(grad_left_owned.dtype),
        lax.all_to_all(
            grad_right_owned.astype(jnp.bfloat16), "axial", split_axis=1, concat_axis=0, tiled=True
        ).astype(grad_right_owned.dtype),
    )
    grad_left_one = row_major(grad_left_back)
    grad_right_one = row_major(grad_right_back)
    grad_flat_one, grad_norm_one, grad_proj_one = entry_back(
        flat_start,
        outgo_norm,
        outgo_proj,
        pair_mask,
        hidden,
        normed_one,
        mixture_one,
        grad_left_one,
        grad_right_one,
        grad_gate_one,
    )
    grad_begin = grad_middle + grad_flat_one
    first_sums = lax.psum(
        (grad_norm_one, grad_proj_one, grad_gain_one, grad_final_one), ("dp", "axial")
    )
    totals = tuple(first_sums) + tuple(second_sums)
    scale = 1.0 / math.sqrt(lax.axis_size("dp") * tokens * tokens)
    return (
        grad_begin.reshape(1, row_count, tokens, channels),
        totals[0] * scale,
        totals[1] * scale,
        totals[2] * scale,
        totals[3] * scale,
        totals[4] * scale,
        totals[5] * scale,
        totals[6] * scale,
        totals[7] * scale,
    )


BF16 = jnp.bfloat16
F32 = jnp.float32
BLOCK = 16
PAIRED = 2
LANES = 128
GROUP = 32
VMEM = 56 * 1024 * 1024


def dot_nn(a, b):
    return lax.dot_general(a, b, (((1,), (0,)), ((), ())), preferred_element_type=F32)


def dot_nt(a, b):
    return lax.dot_general(a, b, (((1,), (1,)), ((), ())), preferred_element_type=F32)


def dot_tn(a, b):
    return lax.dot_general(a, b, (((0,), (0,)), ((), ())), preferred_element_type=F32)


def sigmoid(v):
    return 0.5 * jnp.tanh(0.5 * v) + 0.5


def normalise(v):
    centered = v - jnp.mean(v, axis=0, keepdims=True)
    spread = lax.rsqrt(jnp.mean(centered * centered, axis=0, keepdims=True) + EPSILON)
    return centered * spread, spread


def normalise_back(grad, hat, spread):
    first = jnp.mean(grad, axis=0, keepdims=True)
    second = jnp.mean(grad * hat, axis=0, keepdims=True)
    return spread * (grad - first - hat * second)


def put_block(stage, half, channel, block):
    count = block.shape[0]
    hidden = stage.shape[0] // (2 * BLOCK)
    start = pl.multiple_of((half * hidden + channel) * BLOCK, BLOCK)
    stage[pl.ds(start, count * BLOCK), :] = block.astype(F32).reshape(count * BLOCK, LANES)


def get_block(stage, half, channel, count):
    hidden = stage.shape[0] // (2 * BLOCK)
    start = pl.multiple_of((half * hidden + channel) * BLOCK, BLOCK)
    return stage[pl.ds(start, count * BLOCK), :].reshape(count, BLOCK, LANES)


def put_row(stage, row, value):
    hidden = stage.shape[0] // (2 * BLOCK)
    for half in range(2):
        stage[pl.ds(half * hidden * BLOCK + row, hidden, stride=BLOCK), :] = value[
            :, half * LANES : (half + 1) * LANES
        ]


def get_row(stage, row):
    hidden = stage.shape[0] // (2 * BLOCK)
    return [
        stage[pl.ds(half * hidden * BLOCK + row, hidden, stride=BLOCK), :] for half in range(2)
    ]


def get_rows(stage, rows):
    return jnp.concatenate([half for row in rows for half in get_row(stage, row)], axis=1)


def put_rows(stage, rows, value):
    width = 2 * LANES
    for n, row in enumerate(rows):
        put_row(stage, row, value[:, n * width : (n + 1) * width])


def half_swap(first, second):
    low = lax.broadcasted_iota(jnp.int32, first.shape, first.ndim - 1) < LANES // 2
    axis = first.ndim - 1
    return (
        jnp.where(low, first, pltpu.roll(second, LANES // 2, axis)),
        jnp.where(low, pltpu.roll(first, LANES // 2, axis), second),
    )


def swap_blocks(first, second):
    shape = first.shape
    flat = (shape[0] * shape[1], shape[2])
    one, two = half_swap(first.reshape(flat), second.reshape(flat))
    return one.reshape(shape), two.reshape(shape)


def pick(flag, zero, one):
    return jnp.where(flag == 0, zero, one)


def mask_rows(info, step, rows):
    length = info[4]
    column = lax.broadcasted_iota(jnp.int32, (1, 2 * LANES), 1) < length
    masks = []
    for row in rows:
        live = (info[3] + step * BLOCK + row < length).astype(F32)
        masks.append(column.astype(F32) * live)
    return jnp.concatenate(masks, axis=1)


def each_rows(work):
    @pl.loop(0, BLOCK // PAIRED)
    def _(turn):
        work([turn * PAIRED + n for n in range(PAIRED)])


def turned(eye, ref, rows):
    return jnp.concatenate([dot_nt(eye, ref[row]) for row in rows], axis=1)


def unit(size):
    one = lax.broadcasted_iota(jnp.int32, (size, size), 0)
    two = lax.broadcasted_iota(jnp.int32, (size, size), 1)
    return jnp.where(one == two, 1.0, 0.0).astype(BF16)


def stacked(ref, rows):
    return jnp.concatenate([ref[row] for row in rows], axis=1)


def wide(gain):
    return jnp.concatenate([gain] * PAIRED, axis=1)


def entry_kernel(
    info, pair, norm_row, proj_w, a_same, a_other, b_same, b_other, left_st, right_st, norm, proj_t
):
    step = pl.program_id(0)
    channels = pair.shape[2]
    hidden = proj_w.shape[1] // 5
    eye = unit(channels)

    @pl.when(step == 0)
    def _():
        column = jnp.broadcast_to(norm_row[...], (channels, channels)).T
        norm[...] = jnp.concatenate([column, column], axis=1)
        proj_t[...] = proj_w[:, : 4 * hidden].T.astype(BF16)

    def work(rows):
        z = turned(eye, pair, rows)
        normed = (normalise(z)[0] * wide(norm[...])).astype(BF16)
        mixture = dot_nn(proj_t[...], normed)
        mask = mask_rows(info, step, rows)
        left = mixture[:hidden] * sigmoid(mixture[2 * hidden : 3 * hidden]) * mask
        right = mixture[hidden : 2 * hidden] * sigmoid(mixture[3 * hidden : 4 * hidden]) * mask
        put_rows(left_st, rows, left)
        put_rows(right_st, rows, right)

    each_rows(work)
    core = info[2]
    for owner, a_out, b_out in ((core, a_same, b_same), (1 - core, a_other, b_other)):
        base = owner * (2 * GROUP)
        for half in range(2):
            lanes = slice(half * LANES, (half + 1) * LANES)
            a_out[0, :, :, lanes] = get_block(left_st, half, base, GROUP).astype(BF16)
            b_out[0, :, :, lanes] = get_block(right_st, half, base, GROUP).astype(BF16)
            a_out[1, :, :, lanes] = get_block(right_st, half, base + GROUP, GROUP).astype(BF16)
            b_out[1, :, :, lanes] = get_block(left_st, half, base + GROUP, GROUP).astype(BF16)


def fill_split(info, stage, own, near, ypart, ycpart, xpart, xcpart, lanes):
    x, y, core = info[0], info[1], info[2]
    for owner, mine, yp, xp in ((core, own, ypart, xpart), (1 - core, near, ycpart, xcpart)):
        base = owner * (2 * GROUP)
        put_block(stage, y, base, mine[0, :, :, lanes])
        put_block(stage, 1 - y, base, yp[:, :, lanes])
        here = mine[1, :, :, lanes].astype(F32)
        there = xp[:, :, lanes].astype(F32)
        first, second = swap_blocks(pick(x, here, there), pick(x, there, here))
        put_block(stage, 0, base + GROUP, first)
        put_block(stage, 1, base + GROUP, second)


def split_out(info, stage):
    x, y, core = info[0], info[1], info[2]
    parts = []
    for owner in (core, 1 - core):
        base = owner * (2 * GROUP)
        keep = get_block(stage, y, base, GROUP)
        send = get_block(stage, 1 - y, base, GROUP)
        first, second = swap_blocks(
            get_block(stage, 0, base + GROUP, GROUP), get_block(stage, 1, base + GROUP, GROUP)
        )
        parts.append(
            (
                keep.astype(BF16),
                send.astype(BF16),
                pick(x, first, second).astype(BF16),
                pick(x, second, first).astype(BF16),
            )
        )
    return parts


def middle_kernel(
    info, pair, own, near, ypart, ycpart, xpart, xcpart,
    norm1, gate1_t, gain1, final1_t, norm2, proj2_t, eye,
    middle_out, inner_out, o_own, o_near, o_y, o_yc, o_x, o_xc,
    left_st, right_st,
):
    step = pl.program_id(0)
    hidden = norm1.shape[0]
    fill_split(info, left_st, own, near, ypart, ycpart, xpart, xcpart, slice(0, LANES))

    def work(rows):
        inner = get_rows(left_st, rows)
        z = turned(eye[...], pair, rows)
        normed = (normalise(z)[0] * wide(norm1[...])).astype(BF16)
        gate = sigmoid(dot_nn(gate1_t[...], normed))
        final = (normalise(inner)[0] * wide(gain1[...])).astype(BF16)
        middle = (z + dot_nn(final1_t[...], final) * gate).astype(BF16)
        width = 2 * LANES
        inner_b = inner.astype(BF16)
        for n, row in enumerate(rows):
            middle_out[row] = middle[:, n * width : (n + 1) * width]
            inner_out[row] = inner_b[:, n * width : (n + 1) * width]
        normed2 = (normalise(middle.astype(F32))[0] * wide(norm2[...])).astype(BF16)
        mixture = dot_nn(proj2_t[: 4 * hidden, :], normed2)
        mask = mask_rows(info, step, rows)
        left = mixture[:hidden] * sigmoid(mixture[2 * hidden : 3 * hidden]) * mask
        right = mixture[hidden : 2 * hidden] * sigmoid(mixture[3 * hidden : 4 * hidden]) * mask
        put_rows(left_st, rows, left)
        put_rows(right_st, rows, right)

    each_rows(work)
    core = info[2]
    parts = split_out(info, left_st)
    for owner, part, main, yo, xo in (
        (core, parts[0], o_own, o_y, o_x),
        (1 - core, parts[1], o_near, o_yc, o_xc),
    ):
        base = owner * (2 * GROUP)
        main[0, :, :, :LANES] = part[0]
        yo[:, :, :LANES] = part[1]
        main[1, :, :, :LANES] = part[2]
        xo[:, :, :LANES] = part[3]
        for half in range(2):
            lanes = slice((half + 1) * LANES, (half + 2) * LANES)
            first = get_block(right_st, half, base, GROUP).astype(BF16)
            second = get_block(right_st, half, base + GROUP, GROUP).astype(BF16)
            main[0, :, :, lanes] = first
            yo[:, :, lanes] = first
            main[1, :, :, lanes] = second
            xo[:, :, lanes] = second


def leave_back_rows(inner, gate, grad, gain, final_t, final_w, gfinal):
    hat, spread = normalise(inner)
    final = (hat * gain).astype(BF16)
    product = dot_nn(final_t, final)
    grad_product = (grad * gate).astype(BF16)
    grad_gate = (grad * product * gate * (1.0 - gate)).astype(BF16)
    gfinal[...] += dot_nt(final, grad_product)
    grad_final = dot_nn(final_w, grad_product)
    return normalise_back(grad_final * gain, hat, spread), grad_gate


def turn_kernel(
    info, middle, cot, own, near, xpart, xcpart, ypart, ycpart,
    norm2, gate2_t, gain2, final2_t, final2_w, eye,
    gate_out, same0, same1, other0, other1, gfinal,
    stage,
):
    core = info[2]

    @pl.when(pl.program_id(0) == 0)
    def _():
        gfinal[...] = jnp.zeros_like(gfinal)

    for owner, mine, xp, yp in ((core, own, xpart, ypart), (1 - core, near, xcpart, ycpart)):
        base = owner * (2 * GROUP)
        for half in range(2):
            lanes = slice(half * LANES, (half + 1) * LANES)
            put_block(stage, half, base, mine[0, :, :, lanes].astype(F32) + xp[:, :, lanes].astype(F32))
            put_block(
                stage, half, base + GROUP, mine[1, :, :, lanes].astype(F32) + yp[:, :, lanes].astype(F32)
            )

    def work(rows):
        inner = get_rows(stage, rows)
        normed = (normalise(stacked(middle, rows).astype(F32))[0] * wide(norm2[...])).astype(BF16)
        gate = sigmoid(dot_nn(gate2_t[...], normed))
        grad = turned(eye[...], cot, rows)
        grad_inner, grad_gate = leave_back_rows(
            inner, gate, grad, wide(gain2[...]), final2_t[...], final2_w[...], gfinal
        )
        width = 2 * LANES
        for n, row in enumerate(rows):
            gate_out[row] = grad_gate[:, n * width : (n + 1) * width]
        put_rows(stage, rows, grad_inner)

    each_rows(work)
    for owner, out0, out1 in ((core, same0, same1), (1 - core, other0, other1)):
        base = owner * (2 * GROUP)
        for half in range(2):
            lanes = slice(half * LANES, (half + 1) * LANES)
            out0[:, :, lanes] = get_block(stage, half, base, GROUP).astype(BF16)
            out1[:, :, lanes] = get_block(stage, half, base + GROUP, GROUP).astype(BF16)


def entry_back_rows(normed, hat, spread, norm, grad_left, grad_right, grad_gate, mask, proj_t, proj_w, gproj):
    hidden = norm.shape[0]
    mixture = dot_nn(proj_t[: 4 * hidden, :], normed)
    left_gate = sigmoid(mixture[2 * hidden : 3 * hidden])
    right_gate = sigmoid(mixture[3 * hidden : 4 * hidden])
    left_flow = grad_left * left_gate * mask
    right_flow = grad_right * right_gate * mask
    grad_mixture = jnp.concatenate(
        [
            left_flow.astype(BF16),
            right_flow.astype(BF16),
            (left_flow * mixture[:hidden] * (1.0 - left_gate)).astype(BF16),
            (right_flow * mixture[hidden : 2 * hidden] * (1.0 - right_gate)).astype(BF16),
            grad_gate,
        ],
        axis=0,
    )
    gproj[...] += dot_nt(normed, grad_mixture)
    grad_normed = dot_nn(proj_w, grad_mixture)
    return normalise_back(grad_normed * norm, hat, spread)


def inward_kernel(
    info, middle, pair, cot, inner_in, gate_in, own, near, ypart, ycpart, xpart, xcpart,
    norm2, proj2_t, proj2_w, norm1, gate1_t, gain1, final1_t, final1_w, eye,
    grad_out, gate_out, o_own, o_near, o_y, o_yc, o_x, o_xc, gproj, gfinal,
    left_st, right_st,
):
    step = pl.program_id(0)
    core = info[2]

    @pl.when(step == 0)
    def _():
        gproj[...] = jnp.zeros_like(gproj)
        gfinal[...] = jnp.zeros_like(gfinal)

    fill_split(info, left_st, own, near, ypart, ycpart, xpart, xcpart, slice(0, LANES))
    for owner, mine, yp, xp in ((core, own, ypart, xpart), (1 - core, near, ycpart, xcpart)):
        base = owner * (2 * GROUP)
        for half in range(2):
            lanes = slice((half + 1) * LANES, (half + 2) * LANES)
            put_block(
                right_st, half, base, mine[0, :, :, lanes].astype(F32) + yp[:, :, lanes].astype(F32)
            )
            put_block(
                right_st,
                half,
                base + GROUP,
                mine[1, :, :, lanes].astype(F32) + xp[:, :, lanes].astype(F32),
            )

    def work(rows):
        mask = mask_rows(info, step, rows)
        hat, spread = normalise(stacked(middle, rows).astype(F32))
        norm = wide(norm2[...])
        normed = (hat * norm).astype(BF16)
        grad_flat = entry_back_rows(
            normed, hat, spread, norm, get_rows(left_st, rows), get_rows(right_st, rows),
            stacked(gate_in, rows), mask, proj2_t, proj2_w[...], gproj,
        )
        grad = turned(eye[...], cot, rows) + grad_flat
        z = turned(eye[...], pair, rows)
        normed1 = (normalise(z)[0] * wide(norm1[...])).astype(BF16)
        gate = sigmoid(dot_nn(gate1_t[...], normed1))
        grad_inner, grad_gate = leave_back_rows(
            stacked(inner_in, rows).astype(F32), gate, grad, wide(gain1[...]),
            final1_t[...], final1_w[...], gfinal,
        )
        width = 2 * LANES
        for n, row in enumerate(rows):
            grad_out[row] = grad[:, n * width : (n + 1) * width]
            gate_out[row] = grad_gate[:, n * width : (n + 1) * width]
        put_rows(left_st, rows, grad_inner)

    each_rows(work)
    parts = split_out(info, left_st)
    for part, main, yo, xo in ((parts[0], o_own, o_y, o_x), (parts[1], o_near, o_yc, o_xc)):
        main[0] = part[0]
        yo[...] = part[1]
        main[1] = part[2]
        xo[...] = part[3]


def exit_kernel(
    info, pair, grad_in, gate_in, own, near, ypart, ycpart, xpart, xcpart,
    norm1, proj1_t, proj1_w, eye,
    out, gproj,
    left_st, right_st,
):
    step = pl.program_id(0)
    core = info[2]

    @pl.when(step == 0)
    def _():
        gproj[...] = jnp.zeros_like(gproj)

    for owner, mine, yp, xp in ((core, own, ypart, xpart), (1 - core, near, ycpart, xcpart)):
        base = owner * (2 * GROUP)
        for half in range(2):
            lanes = slice(half * LANES, (half + 1) * LANES)
            beyond = slice((half + 2) * LANES, (half + 3) * LANES)
            for group, stage_l, stage_r in ((0, yp, xp), (1, xp, yp)):
                put_block(
                    left_st,
                    half,
                    base + group * GROUP,
                    mine[group, :, :, lanes].astype(F32) + stage_l[group, :, :, lanes].astype(F32),
                )
                put_block(
                    right_st,
                    half,
                    base + group * GROUP,
                    mine[group, :, :, beyond].astype(F32) + stage_r[group, :, :, lanes].astype(F32),
                )

    def work(rows):
        mask = mask_rows(info, step, rows)
        hat, spread = normalise(turned(eye[...], pair, rows))
        norm = wide(norm1[...])
        normed = (hat * norm).astype(BF16)
        grad_flat = entry_back_rows(
            normed, hat, spread, norm, get_rows(left_st, rows), get_rows(right_st, rows),
            stacked(gate_in, rows), mask, proj1_t, proj1_w[...], gproj,
        )
        total = stacked(grad_in, rows) + grad_flat
        width = 2 * LANES
        for n, row in enumerate(rows):
            out[row] = total[:, n * width : (n + 1) * width].T

    each_rows(work)


CHANNELS = 8


def place(one, two):
    return pl.multiple_of((one * 2 + two) * 32, 32)


def outgoing_kernel(
    info, a_own, a_near, a_y, a_yc, b_own, b_near, b_x, b_xc,
    o_own, o_near, o_y, o_yc, o_x, o_xc, stage,
):
    x, y, core = info[0], info[1], info[2]
    rows = a_own.shape[2]
    for h in range(CHANNELS):
        for group in range(2):
            lefts = (a_own, a_near, a_y, a_yc) if group == 0 else (b_own, b_near, b_x, b_xc)
            rights = (b_own, b_near, b_x, b_xc) if group == 0 else (a_own, a_near, a_y, a_yc)
            at = x if group == 0 else y
            outs = (o_own, o_near) + ((o_y, o_yc) if group == 0 else (o_x, o_xc))
            slot = 2 * h + group
            for n, ref in enumerate(rights):
                where = place(at if n < 2 else 1 - at, core if n % 2 == 0 else 1 - core)
                stage[slot, pl.ds(where, rows), :] = ref[group, h]
            left = jnp.concatenate([ref[group, h] for ref in lefts], axis=0)
            inner = dot_nt(left, stage[slot]).astype(BF16)
            outs[0][group, h] = inner[:rows]
            outs[1][group, h] = inner[rows : 2 * rows]
            outs[2][h] = inner[2 * rows : 3 * rows]
            outs[3][h] = inner[3 * rows :]


def pieces(own, near, third, fourth, group, h, lanes):
    return jnp.concatenate(
        [own[group, h, :, lanes], near[group, h, :, lanes], third[h, :, lanes], fourth[h, :, lanes]],
        axis=0,
    )


def incoming_kernel(
    info, own, near, ypart, ycpart, xpart, xcpart, o_own, o_near, o_x, o_xc, o_y, o_yc, stage
):
    x, y, core = info[0], info[1], info[2]
    rows = own.shape[2]
    for h in range(CHANNELS):
        for group in range(2):
            far = (ypart, ycpart) if group == 0 else (xpart, xcpart)
            at = x if group == 0 else y
            outs = (o_own, o_near) + ((o_x, o_xc) if group == 0 else (o_y, o_yc))
            slot = 2 * h + group
            left = pieces(own, near, *far, group, h, slice(0, LANES))
            right = pieces(own, near, *far, group, h, slice(LANES, 3 * LANES))
            stage[slot] = dot_tn(left, right).astype(BF16)
            for n, out in enumerate(outs):
                where = place(at if n < 2 else 1 - at, core if n % 2 == 0 else 1 - core)
                part = stage[slot, pl.ds(where, rows), :]
                if n < 2:
                    out[group, h] = part
                else:
                    out[h] = part


def incoming_back_kernel(
    info, own, near, ypart, ycpart, xpart, xcpart, same0, same1, near0, near1, g_x, g_xc, g_y, g_yc,
    o_own, o_near, o_y, o_yc, o_x, o_xc, stage,
):
    x, y, core = info[0], info[1], info[2]
    rows = own.shape[2]
    for h in range(CHANNELS):
        for group in range(2):
            far = (ypart, ycpart) if group == 0 else (xpart, xcpart)
            at = x if group == 0 else y
            grads = (same0, near0, g_x, g_xc) if group == 0 else (same1, near1, g_y, g_yc)
            outs = (o_own, o_near) + ((o_y, o_yc) if group == 0 else (o_x, o_xc))
            slot = 2 * h + group
            for n, ref in enumerate(grads):
                where = place(at if n < 2 else 1 - at, core if n % 2 == 0 else 1 - core)
                stage[slot, pl.ds(where, rows), :] = ref[h]
            left = pieces(own, near, *far, group, h, slice(0, LANES))
            right = pieces(own, near, *far, group, h, slice(LANES, 3 * LANES))
            grad = stage[slot]
            grad_left = dot_nt(right, grad).astype(BF16)
            grad_right = dot_nn(left, grad).astype(BF16)
            for n, out in enumerate(outs):
                take = slice(n * rows, (n + 1) * rows)
                if n < 2:
                    out[group, h, :, :LANES] = grad_left[take]
                    out[group, h, :, LANES:] = grad_right[take]
                else:
                    out[h, :, :LANES] = grad_left[take]
                    out[h, :, LANES:] = grad_right[take]


def outgoing_back_kernel(
    info, a_own, a_near, a_y, a_yc, b_own, b_near, b_x, b_xc, g_own, g_near, g_y, g_yc, g_x, g_xc,
    o_own, o_near, o_y, o_yc, o_x, o_xc, stage, back,
):
    x, y, core = info[0], info[1], info[2]
    rows = a_own.shape[2]
    width = a_own.shape[3]
    for h in range(CHANNELS):
        for group in range(2):
            along_a, along_b = (a_own, a_near, a_y, a_yc), (b_own, b_near, b_x, b_xc)
            lefts, rights = (along_a, along_b) if group == 0 else (along_b, along_a)
            at = x if group == 0 else y
            far = (g_y, g_yc) if group == 0 else (g_x, g_xc)
            left_far, right_far = ((o_y, o_yc), (o_x, o_xc)) if group == 0 else ((o_x, o_xc), (o_y, o_yc))
            slot = 2 * h + group
            wheres = [
                place(at if n < 2 else 1 - at, core if n % 2 == 0 else 1 - core) for n in range(4)
            ]
            for where, ref in zip(wheres, rights):
                stage[slot, pl.ds(where, rows), :] = ref[group, h]
            left = jnp.concatenate([ref[group, h] for ref in lefts], axis=0)
            grad = jnp.concatenate([g_own[group, h], g_near[group, h], far[0][h], far[1][h]], axis=0)
            grad_left = dot_nn(grad, stage[slot]).astype(BF16)
            back[slot] = dot_tn(grad, left).astype(BF16)
            for n in range(4):
                left_part = grad_left[n * rows : (n + 1) * rows]
                right_part = back[slot, pl.ds(wheres[n], rows), :]
                if n < 2:
                    out = (o_own, o_near)[n]
                    out[group, h, :, :width] = left_part
                    out[group, h, :, width:] = right_part
                else:
                    left_far[n - 2][group, h] = left_part
                    right_far[n - 2][group, h] = right_part


def whole(shape):
    return pl.BlockSpec(shape, lambda step, info: (0,) * len(shape))


def cell_rows(shape):
    block = shape[:-2] + (BLOCK, shape[-1])
    return pl.BlockSpec(block, lambda step, info: (0,) * (len(shape) - 2) + (step, 0))


def row_first(shape):
    return pl.BlockSpec((BLOCK,) + shape[1:], lambda step, info: (step,) + (0,) * (len(shape) - 1))


def channel_rows(shape):
    if len(shape) == 4:
        return pl.BlockSpec((shape[0], CHANNELS) + shape[2:], lambda step, info: (0, step, 0, 0))
    return pl.BlockSpec((CHANNELS,) + shape[1:], lambda step, info: (step, 0, 0))


def call(kernel, info, steps, ins, outs, scratch):
    return pl.pallas_call(
        kernel,
        grid_spec=pltpu.PrefetchScalarGridSpec(
            num_scalar_prefetch=1,
            grid=(steps,),
            in_specs=[make(array.shape) for array, make in ins],
            out_specs=[make(shape) for shape, unused, make in outs],
            scratch_shapes=scratch,
        ),
        out_shape=[jax.ShapeDtypeStruct(shape, dtype) for shape, dtype, unused in outs],
        compiler_params=pltpu.CompilerParams(vmem_limit_bytes=VMEM),
    )(info, *[array for array, unused in ins])


def hop(array, offset):
    count = lax.axis_size("axial")
    return lax.ppermute(array, "axial", [(n, n ^ offset) for n in range(count)])


CORE, X, Y = 1, 2, 4


def add_up(share):
    count = lax.axis_size("axial")
    rows, width = share.shape
    parts = lax.all_to_all(
        share.reshape(count, rows // count, width), "axial", split_axis=0, concat_axis=0, tiled=True
    )
    mine = parts.sum(axis=0)
    depth = lax.axis_size("dp")
    terms = [mine] + [
        lax.ppermute(mine, "dp", [(n, n ^ offset) for n in range(depth)])
        for offset in range(1, depth)
    ]
    while len(terms) > 1:
        terms = [terms[n] + terms[n + 1] for n in range(0, len(terms), 2)]
    copies = jnp.broadcast_to(terms[0][None], (count,) + terms[0].shape)
    return lax.all_to_all(copies, "axial", split_axis=0, concat_axis=0, tiled=True).reshape(
        rows, width
    )


def gain_grad(weight_grad, weight, gain):
    return (weight.astype(F32) * weight_grad).sum(axis=1) / gain


def fast_body(
    pair,
    cotangent,
    lengths,
    outgo_norm,
    outgo_proj,
    outgo_gain,
    outgo_final,
    incom_norm,
    incom_proj,
    incom_gain,
    incom_final,
):
    rows, tokens, channels = pair.shape[1:]
    hidden = outgo_gain.shape[0]
    index = lax.axis_index("axial")
    info = jnp.stack(
        [(index // 2) % 2, index // 4, index % 2, index * rows, lengths[0]]
    ).astype(jnp.int32)
    pair = pair[0]
    cot = cotangent[0]
    eye = jnp.eye(channels, dtype=BF16)

    def spread(gain):
        return jnp.broadcast_to(gain[:, None], (gain.shape[0], tokens))

    norm1, gain1, norm2, gain2 = map(spread, (outgo_norm, outgo_gain, incom_norm, incom_gain))
    proj1, final1, proj2, final2 = (
        weight.astype(BF16) for weight in (outgo_proj, outgo_final, incom_proj, incom_final)
    )
    proj1_t, final1_t, proj2_t, final2_t = proj1.T, final1.T, proj2.T, final2.T
    gate1_t, gate2_t = proj1_t[4 * hidden :], proj2_t[4 * hidden :]
    steps = rows // BLOCK
    turns = GROUP // CHANNELS
    stage = pltpu.VMEM((2 * hidden * BLOCK, LANES), F32)

    def groups(width):
        return (2, GROUP, rows, width)

    def single(width):
        return (GROUP, rows, width)

    turned_shape = (rows, channels, tokens)

    a_same, a_other, b_same, b_other = call(
        entry_kernel,
        info,
        steps,
        [(pair, row_first), (outgo_norm[None], whole), (outgo_proj, whole)],
        [(groups(tokens), BF16, cell_rows)] * 4,
        [
            stage,
            stage,
            pltpu.VMEM((channels, tokens), F32),
            pltpu.VMEM((4 * hidden, channels), BF16),
        ],
    )
    a_y, b_x = hop(a_same, Y), hop(b_same, X)
    a_yc, b_xc = hop(a_other, Y | CORE), hop(b_other, X | CORE)
    a_near, b_near = hop(a_other, CORE), hop(b_other, CORE)
    held_one = [
        (array, channel_rows) for array in (a_same, a_near, a_y, a_yc, b_same, b_near, b_x, b_xc)
    ]
    own, near, to_y, to_yc, to_x, to_xc = call(
        outgoing_kernel,
        info,
        turns,
        held_one,
        [(groups(LANES), BF16, channel_rows)] * 2 + [(single(LANES), BF16, channel_rows)] * 4,
        [pltpu.VMEM((2 * CHANNELS, 4 * rows, tokens), BF16)],
    )
    back_one = [
        own,
        hop(near, CORE),
        hop(to_y, Y),
        hop(to_yc, Y | CORE),
        hop(to_x, X),
        hop(to_xc, X | CORE),
    ]

    middle, inner_one, own, near, to_y, to_yc, to_x, to_xc = call(
        middle_kernel,
        info,
        steps,
        [(pair, row_first)]
        + [(array, cell_rows) for array in back_one]
        + [
            (array, whole)
            for array in (norm1, gate1_t, gain1, final1_t, norm2, proj2_t, eye)
        ],
        [(turned_shape, BF16, row_first)] * 2
        + [(groups(3 * LANES), BF16, cell_rows)] * 2
        + [(single(3 * LANES), BF16, cell_rows)] * 4,
        [stage, stage],
    )
    held_two = [
        (array, channel_rows)
        for array in (
            own,
            hop(near, CORE),
            hop(to_y, Y),
            hop(to_yc, Y | CORE),
            hop(to_x, X),
            hop(to_xc, X | CORE),
        )
    ]
    own, near, to_x, to_xc, to_y, to_yc = call(
        incoming_kernel,
        info,
        turns,
        held_two,
        [(groups(tokens), BF16, channel_rows)] * 2 + [(single(tokens), BF16, channel_rows)] * 4,
        [pltpu.VMEM((2 * CHANNELS, 4 * rows, tokens), BF16)],
    )
    back_two = [
        own,
        hop(near, CORE),
        hop(to_x, X),
        hop(to_xc, X | CORE),
        hop(to_y, Y),
        hop(to_yc, Y | CORE),
    ]

    gate_grad_two, same0, same1, other0, other1, grad_final_two = call(
        turn_kernel,
        info,
        steps,
        [(middle, row_first), (cot, row_first)]
        + [(array, cell_rows) for array in back_two]
        + [(array, whole) for array in (norm2, gate2_t, gain2, final2_t, final2, eye)],
        [(turned_shape, BF16, row_first)]
        + [(single(tokens), BF16, cell_rows)] * 4
        + [((hidden, channels), F32, whole)],
        [stage],
    )
    grads_two = [
        same0,
        same1,
        hop(other0, CORE),
        hop(other1, CORE),
        hop(same0, X),
        hop(other0, X | CORE),
        hop(same1, Y),
        hop(other1, Y | CORE),
    ]
    own, near, to_y, to_yc, to_x, to_xc = call(
        incoming_back_kernel,
        info,
        turns,
        held_two + [(array, channel_rows) for array in grads_two],
        [(groups(3 * LANES), BF16, channel_rows)] * 2
        + [(single(3 * LANES), BF16, channel_rows)] * 4,
        [pltpu.VMEM((2 * CHANNELS, 4 * rows, tokens), BF16)],
    )
    rows_two = [
        own,
        hop(near, CORE),
        hop(to_y, Y),
        hop(to_yc, Y | CORE),
        hop(to_x, X),
        hop(to_xc, X | CORE),
    ]

    (
        grad_middle, gate_grad_one, own, near, to_y, to_yc, to_x, to_xc,
        grad_proj_two, grad_final_one,
    ) = call(
        inward_kernel,
        info,
        steps,
        [(array, row_first) for array in (middle, pair, cot, inner_one, gate_grad_two)]
        + [(array, cell_rows) for array in rows_two]
        + [
            (array, whole)
            for array in (norm2, proj2_t, proj2, norm1, gate1_t, gain1, final1_t, final1, eye)
        ],
        [(turned_shape, F32, row_first), (turned_shape, BF16, row_first)]
        + [(groups(LANES), BF16, cell_rows)] * 2
        + [(single(LANES), BF16, cell_rows)] * 4
        + [
            ((channels, 5 * hidden), F32, whole),
            ((hidden, channels), F32, whole),
        ],
        [stage, stage],
    )
    grads_one = [
        own,
        hop(near, CORE),
        hop(to_y, Y),
        hop(to_yc, Y | CORE),
        hop(to_x, X),
        hop(to_xc, X | CORE),
    ]
    own, near, to_y, to_yc, to_x, to_xc = call(
        outgoing_back_kernel,
        info,
        turns,
        held_one + [(array, channel_rows) for array in grads_one],
        [(groups(2 * tokens), BF16, channel_rows)] * 2
        + [(groups(tokens), BF16, channel_rows)] * 4,
        [pltpu.VMEM((2 * CHANNELS, 4 * rows, tokens), BF16)] * 2,
    )
    rows_one = [
        own,
        hop(near, CORE),
        hop(to_y, Y),
        hop(to_yc, Y | CORE),
        hop(to_x, X),
        hop(to_xc, X | CORE),
    ]
    early = add_up(jnp.concatenate([grad_proj_two, grad_final_two, grad_final_one], axis=1))
    grad_begin, grad_proj_one = call(
        exit_kernel,
        info,
        steps,
        [(array, row_first) for array in (pair, grad_middle, gate_grad_one)]
        + [(array, cell_rows) for array in rows_one]
        + [(array, whole) for array in (norm1, proj1_t, proj1, eye)],
        [
            ((rows, tokens, channels), F32, row_first),
            ((channels, 5 * hidden), F32, whole),
        ],
        [stage, stage],
    )
    late = add_up(grad_proj_one)
    scale = 1.0 / math.sqrt(lax.axis_size("dp") * tokens * tokens)
    early, late = early * scale, late * scale
    width = 5 * hidden
    totals_two, totals_final_two = early[:, :width], early[:, width : width + channels]
    totals_final_one = early[:, width + channels :]
    return (
        grad_begin[None],
        gain_grad(late, proj1, outgo_norm),
        late,
        gain_grad(totals_final_one, final1, outgo_gain),
        totals_final_one,
        gain_grad(totals_two, proj2, incom_norm),
        totals_two,
        gain_grad(totals_final_two, final2, incom_gain),
        totals_final_two,
    )


def solution(mesh):
    def body(pair, *rest):
        rows, tokens, channels = pair.shape[1:]
        hidden = rest[3].shape[0]
        plane = mesh.shape["axial"] == 8 and rows == 32 and tokens == 2 * LANES
        if plane and channels == LANES and hidden == 4 * GROUP:
            return fast_body(pair, *rest)
        return plain_body(pair, *rest)

    return jax.shard_map(
        body,
        mesh=mesh,
        in_specs=(P("dp", "axial", None, None), P("dp", "axial", None, None), P("dp")) + (P(),) * 8,
        out_specs=(P("dp", "axial", None, None),) + (P(),) * 8,
        check_vma=False,
    )
```

```python
import functools
import math

import jax
import jax.numpy as jnp
from jax import lax
from jax.experimental import pallas as pl
from jax.experimental.pallas import tpu as pltpu
from jax.sharding import PartitionSpec as P

EPSILON = 1e-05


def rounded(inputs):
    return lax.optimization_barrier(inputs.astype(jnp.bfloat16)).astype(jnp.float32)


def layer_norm(inputs, factor):
    average = jnp.mean(inputs, axis=-1, keepdims=True)
    centered = inputs - average
    spread = jnp.mean(centered * centered, axis=-1, keepdims=True)
    return centered * lax.rsqrt(spread + EPSILON) * factor


def gating(mixture, pair_mask, hidden):
    left_part = (
        mixture[:, :hidden] * jax.nn.sigmoid(mixture[:, 2 * hidden : 3 * hidden]) * pair_mask
    )
    right_part = (
        mixture[:, hidden : 2 * hidden]
        * jax.nn.sigmoid(mixture[:, 3 * hidden : 4 * hidden])
        * pair_mask
    )
    gate_part = jax.nn.sigmoid(mixture[:, 4 * hidden :])
    return (left_part, right_part, gate_part)


def entry(flat_pair, norm_gain, projection, pair_mask, hidden):
    normed = layer_norm(flat_pair, norm_gain).astype(jnp.bfloat16)
    mixture = jnp.dot(normed, projection.astype(jnp.bfloat16), preferred_element_type=jnp.float32)
    left_part, right_part, gate_part = gating(mixture, pair_mask, hidden)
    return (normed, mixture, left_part, right_part, gate_part)


def entry_back(
    flat_pair,
    norm_gain,
    projection,
    pair_mask,
    hidden,
    normed,
    mixture,
    grad_left,
    grad_right,
    grad_gate,
):
    unused, pull_gate = jax.vjp(lambda inner_mix: gating(inner_mix, pair_mask, hidden), mixture)
    grad_mixture = pull_gate((grad_left, grad_right, grad_gate))[0].astype(jnp.bfloat16)
    grad_projection = jnp.dot(normed.T, grad_mixture, preferred_element_type=jnp.float32)
    grad_normed = jnp.dot(
        grad_mixture, projection.astype(jnp.bfloat16).T, preferred_element_type=jnp.float32
    )
    unused, pull_norm = jax.vjp(layer_norm, flat_pair, norm_gain)
    grad_flat, grad_gain = pull_norm(grad_normed)
    return (grad_flat, grad_gain, grad_projection)


def leave(inner_sum, gate_part, out_gain, final_weight):
    final_normed = layer_norm(inner_sum, out_gain).astype(jnp.bfloat16)
    product = jnp.dot(
        final_normed, final_weight.astype(jnp.bfloat16), preferred_element_type=jnp.float32
    )
    return (final_normed, product, product * gate_part)


def leave_back(inner_sum, gate_part, out_gain, final_weight, final_normed, product, grad_update):
    grad_product = (grad_update * gate_part).astype(jnp.bfloat16)
    grad_gate = grad_update * product
    grad_final = jnp.dot(final_normed.T, grad_product, preferred_element_type=jnp.float32)
    grad_normed = jnp.dot(
        grad_product, final_weight.astype(jnp.bfloat16).T, preferred_element_type=jnp.float32
    )
    unused, pull_norm = jax.vjp(layer_norm, inner_sum, out_gain)
    grad_inner, grad_gain = pull_norm(grad_normed)
    return (grad_inner, grad_gate, grad_gain, grad_final)


def channel_major(field, row_count, tokens):
    hidden = field.shape[1]
    return jnp.transpose(field.reshape(row_count, tokens, hidden), (2, 0, 1))


def row_major(field):
    hidden = field.shape[0]
    return jnp.transpose(field, (1, 2, 0)).reshape(-1, hidden)


def plain_body(
    pair,
    cotangent,
    lengths,
    outgo_norm,
    outgo_proj,
    outgo_gain,
    outgo_final,
    incom_norm,
    incom_proj,
    incom_gain,
    incom_final,
):
    row_count = pair.shape[1]
    tokens = pair.shape[2]
    channels = pair.shape[3]
    hidden = outgo_gain.shape[0]
    length = lengths[0]
    first_row = lax.axis_index("axial") * row_count
    row_alive = (first_row + jnp.arange(row_count, dtype=jnp.int32) < length).astype(jnp.float32)
    column_alive = (jnp.arange(tokens, dtype=jnp.int32) < length).astype(jnp.float32)
    pair_mask = (row_alive[:, None] * column_alive[None, :]).reshape(-1, 1)
    flat_start = pair[0].reshape(-1, channels).astype(jnp.float32)
    normed_one, mixture_one, left_one, right_one, gate_one = entry(
        flat_start, outgo_norm, outgo_proj, pair_mask, hidden
    )
    left_first = channel_major(left_one.astype(jnp.bfloat16), row_count, tokens)
    right_first = channel_major(right_one.astype(jnp.bfloat16), row_count, tokens)
    left_owned, right_owned = (
        lax.all_to_all(left_first, "axial", split_axis=0, concat_axis=1, tiled=True),
        lax.all_to_all(right_first, "axial", split_axis=0, concat_axis=1, tiled=True),
    )
    inner_cols = jnp.einsum(
        "hik,hjk->hij", left_owned, right_owned, preferred_element_type=jnp.float32
    )
    inner_one = row_major(
        lax.all_to_all(
            inner_cols.astype(jnp.bfloat16), "axial", split_axis=1, concat_axis=0, tiled=True
        ).astype(inner_cols.dtype)
    )
    final_one, product_one, update_one = leave(inner_one, gate_one, outgo_gain, outgo_final)
    flat_middle = rounded(flat_start + update_one)
    normed_two, mixture_two, left_two, right_two, gate_two = entry(
        flat_middle, incom_norm, incom_proj, pair_mask, hidden
    )
    left_second = channel_major(left_two.astype(jnp.bfloat16), row_count, tokens)
    right_second = channel_major(right_two.astype(jnp.bfloat16), row_count, tokens)
    left_held, right_held = (
        lax.all_to_all(left_second, "axial", split_axis=0, concat_axis=1, tiled=True),
        lax.all_to_all(right_second, "axial", split_axis=0, concat_axis=1, tiled=True),
    )
    inner_held = jnp.einsum(
        "hki,hkj->hij", left_held, right_held, preferred_element_type=jnp.float32
    )
    inner_two = row_major(
        lax.all_to_all(
            inner_held.astype(jnp.bfloat16), "axial", split_axis=1, concat_axis=0, tiled=True
        ).astype(inner_held.dtype)
    )
    final_two, product_two, update_two = leave(inner_two, gate_two, incom_gain, incom_final)
    grad_end = cotangent[0].reshape(-1, channels).astype(jnp.float32)
    grad_inner_two, grad_gate_two, grad_gain_two, grad_final_two = leave_back(
        inner_two, gate_two, incom_gain, incom_final, final_two, product_two, grad_end
    )
    grad_cells_two = channel_major(grad_inner_two.astype(jnp.bfloat16), row_count, tokens)
    grad_held_two = lax.all_to_all(grad_cells_two, "axial", split_axis=0, concat_axis=1, tiled=True)
    left_back, right_back = (
        lax.all_to_all(left_second, "axial", split_axis=0, concat_axis=1, tiled=True),
        lax.all_to_all(right_second, "axial", split_axis=0, concat_axis=1, tiled=True),
    )
    grad_left_held = jnp.einsum(
        "hij,hkj->hki", grad_held_two, right_back, preferred_element_type=jnp.float32
    )
    grad_right_held = jnp.einsum(
        "hki,hij->hkj", left_back, grad_held_two, preferred_element_type=jnp.float32
    )
    grad_left_rows, grad_right_rows = (
        lax.all_to_all(
            grad_left_held.astype(jnp.bfloat16), "axial", split_axis=1, concat_axis=0, tiled=True
        ).astype(grad_left_held.dtype),
        lax.all_to_all(
            grad_right_held.astype(jnp.bfloat16), "axial", split_axis=1, concat_axis=0, tiled=True
        ).astype(grad_right_held.dtype),
    )
    grad_left_two = row_major(grad_left_rows)
    grad_right_two = row_major(grad_right_rows)
    grad_flat_two, grad_norm_two, grad_proj_two = entry_back(
        flat_middle,
        incom_norm,
        incom_proj,
        pair_mask,
        hidden,
        normed_two,
        mixture_two,
        grad_left_two,
        grad_right_two,
        grad_gate_two,
    )
    second_sums = lax.psum(
        (grad_norm_two, grad_proj_two, grad_gain_two, grad_final_two), ("dp", "axial")
    )
    grad_middle = grad_end + grad_flat_two
    grad_inner_one, grad_gate_one, grad_gain_one, grad_final_one = leave_back(
        inner_one, gate_one, outgo_gain, outgo_final, final_one, product_one, grad_middle
    )
    grad_cells_one = channel_major(grad_inner_one.astype(jnp.bfloat16), row_count, tokens)
    grad_owned_one = lax.all_to_all(
        grad_cells_one, "axial", split_axis=0, concat_axis=1, tiled=True
    )
    left_again, right_again = (
        lax.all_to_all(left_first, "axial", split_axis=0, concat_axis=1, tiled=True),
        lax.all_to_all(right_first, "axial", split_axis=0, concat_axis=1, tiled=True),
    )
    grad_left_owned = jnp.einsum(
        "hij,hjk->hik", grad_owned_one, right_again, preferred_element_type=jnp.float32
    )
    grad_right_owned = jnp.einsum(
        "hij,hik->hjk", grad_owned_one, left_again, preferred_element_type=jnp.float32
    )
    grad_left_back, grad_right_back = (
        lax.all_to_all(
            grad_left_owned.astype(jnp.bfloat16), "axial", split_axis=1, concat_axis=0, tiled=True
        ).astype(grad_left_owned.dtype),
        lax.all_to_all(
            grad_right_owned.astype(jnp.bfloat16), "axial", split_axis=1, concat_axis=0, tiled=True
        ).astype(grad_right_owned.dtype),
    )
    grad_left_one = row_major(grad_left_back)
    grad_right_one = row_major(grad_right_back)
    grad_flat_one, grad_norm_one, grad_proj_one = entry_back(
        flat_start,
        outgo_norm,
        outgo_proj,
        pair_mask,
        hidden,
        normed_one,
        mixture_one,
        grad_left_one,
        grad_right_one,
        grad_gate_one,
    )
    grad_begin = grad_middle + grad_flat_one
    first_sums = lax.psum(
        (grad_norm_one, grad_proj_one, grad_gain_one, grad_final_one), ("dp", "axial")
    )
    totals = tuple(first_sums) + tuple(second_sums)
    scale = 1.0 / math.sqrt(lax.axis_size("dp") * tokens * tokens)
    return (
        grad_begin.reshape(1, row_count, tokens, channels),
        totals[0] * scale,
        totals[1] * scale,
        totals[2] * scale,
        totals[3] * scale,
        totals[4] * scale,
        totals[5] * scale,
        totals[6] * scale,
        totals[7] * scale,
    )


BF16 = jnp.bfloat16
F32 = jnp.float32
BLOCK = 16
PAIRED = 2
LANES = 128
GROUP = 32
VMEM = 56 * 1024 * 1024


def dot_nn(a, b):
    return lax.dot_general(a, b, (((1,), (0,)), ((), ())), preferred_element_type=F32)


def dot_nt(a, b):
    return lax.dot_general(a, b, (((1,), (1,)), ((), ())), preferred_element_type=F32)


def dot_tn(a, b):
    return lax.dot_general(a, b, (((0,), (0,)), ((), ())), preferred_element_type=F32)


def sigmoid(v):
    return 0.5 * jnp.tanh(0.5 * v) + 0.5


def normalise(v):
    centered = v - jnp.mean(v, axis=0, keepdims=True)
    spread = lax.rsqrt(jnp.mean(centered * centered, axis=0, keepdims=True) + EPSILON)
    return centered * spread, spread


def normalise_back(grad, hat, spread):
    first = jnp.mean(grad, axis=0, keepdims=True)
    second = jnp.mean(grad * hat, axis=0, keepdims=True)
    return spread * (grad - first - hat * second)


def put_block(stage, half, channel, block):
    count = block.shape[0]
    hidden = stage.shape[0] // (2 * BLOCK)
    start = pl.multiple_of((half * hidden + channel) * BLOCK, BLOCK)
    stage[pl.ds(start, count * BLOCK), :] = block.astype(F32).reshape(count * BLOCK, LANES)


def get_block(stage, half, channel, count):
    hidden = stage.shape[0] // (2 * BLOCK)
    start = pl.multiple_of((half * hidden + channel) * BLOCK, BLOCK)
    return stage[pl.ds(start, count * BLOCK), :].reshape(count, BLOCK, LANES)


def put_row(stage, row, value):
    hidden = stage.shape[0] // (2 * BLOCK)
    for half in range(2):
        stage[pl.ds(half * hidden * BLOCK + row, hidden, stride=BLOCK), :] = value[
            :, half * LANES : (half + 1) * LANES
        ]


def get_row(stage, row):
    hidden = stage.shape[0] // (2 * BLOCK)
    return [
        stage[pl.ds(half * hidden * BLOCK + row, hidden, stride=BLOCK), :] for half in range(2)
    ]


def get_rows(stage, rows):
    return jnp.concatenate([half for row in rows for half in get_row(stage, row)], axis=1)


def put_rows(stage, rows, value):
    width = 2 * LANES
    for n, row in enumerate(rows):
        put_row(stage, row, value[:, n * width : (n + 1) * width])


def half_swap(first, second):
    low = lax.broadcasted_iota(jnp.int32, first.shape, first.ndim - 1) < LANES // 2
    axis = first.ndim - 1
    return (
        jnp.where(low, first, pltpu.roll(second, LANES // 2, axis)),
        jnp.where(low, pltpu.roll(first, LANES // 2, axis), second),
    )


def swap_blocks(first, second):
    shape = first.shape
    flat = (shape[0] * shape[1], shape[2])
    one, two = half_swap(first.reshape(flat), second.reshape(flat))
    return one.reshape(shape), two.reshape(shape)


def pick(flag, zero, one):
    return jnp.where(flag == 0, zero, one)


def mask_rows(info, part, rows):
    length = info[4]
    column = lax.broadcasted_iota(jnp.int32, (1, 2 * LANES), 1) < length
    masks = []
    for row in rows:
        live = (info[3] + part * BLOCK + row < length).astype(F32)
        masks.append(column.astype(F32) * live)
    return jnp.concatenate(masks, axis=1)


def each_rows(work):
    @pl.loop(0, BLOCK // PAIRED)
    def _(turn):
        work([turn * PAIRED + n for n in range(PAIRED)])


def turned(eye, ref, rows):
    return jnp.concatenate([dot_nt(eye, ref[row]) for row in rows], axis=1)


def unit(size):
    one = lax.broadcasted_iota(jnp.int32, (size, size), 0)
    two = lax.broadcasted_iota(jnp.int32, (size, size), 1)
    return jnp.where(one == two, 1.0, 0.0).astype(BF16)


def stacked(ref, rows):
    return jnp.concatenate([ref[row] for row in rows], axis=1)


def wide(gain):
    return jnp.concatenate([gain] * PAIRED, axis=1)


def entry_kernel(
    part, info, pair, norm_row, proj_w, a_same, a_other, b_same, b_other, left_st, right_st, norm, proj_t
):
    channels = pair.shape[2]
    hidden = proj_w.shape[1] // 5
    eye = unit(channels)
    column = jnp.broadcast_to(norm_row[...], (channels, channels)).T
    norm[...] = jnp.concatenate([column, column], axis=1)
    proj_t[...] = proj_w[:, : 4 * hidden].T.astype(BF16)

    def work(rows):
        z = turned(eye, pair, rows)
        normed = (normalise(z)[0] * wide(norm[...])).astype(BF16)
        mixture = dot_nn(proj_t[...], normed)
        mask = mask_rows(info, part, rows)
        left = mixture[:hidden] * sigmoid(mixture[2 * hidden : 3 * hidden]) * mask
        right = mixture[hidden : 2 * hidden] * sigmoid(mixture[3 * hidden : 4 * hidden]) * mask
        put_rows(left_st, rows, left)
        put_rows(right_st, rows, right)

    each_rows(work)
    core = info[2]
    for owner, a_out, b_out in ((core, a_same, b_same), (1 - core, a_other, b_other)):
        base = owner * (2 * GROUP)
        for half in range(2):
            lanes = slice(half * LANES, (half + 1) * LANES)
            a_out[0, :, :, lanes] = get_block(left_st, half, base, GROUP).astype(BF16)
            b_out[0, :, :, lanes] = get_block(right_st, half, base, GROUP).astype(BF16)
            a_out[1, :, :, lanes] = get_block(right_st, half, base + GROUP, GROUP).astype(BF16)
            b_out[1, :, :, lanes] = get_block(left_st, half, base + GROUP, GROUP).astype(BF16)


def fill_split(info, stage, own, near, ypart, ycpart, xpart, xcpart, lanes):
    x, y, core = info[0], info[1], info[2]
    for owner, mine, yp, xp in ((core, own, ypart, xpart), (1 - core, near, ycpart, xcpart)):
        base = owner * (2 * GROUP)
        put_block(stage, y, base, mine[0, :, :, lanes])
        put_block(stage, 1 - y, base, yp[:, :, lanes])
        here = mine[1, :, :, lanes].astype(F32)
        there = xp[:, :, lanes].astype(F32)
        first, second = swap_blocks(pick(x, here, there), pick(x, there, here))
        put_block(stage, 0, base + GROUP, first)
        put_block(stage, 1, base + GROUP, second)


def split_out(info, stage):
    x, y, core = info[0], info[1], info[2]
    parts = []
    for owner in (core, 1 - core):
        base = owner * (2 * GROUP)
        keep = get_block(stage, y, base, GROUP)
        send = get_block(stage, 1 - y, base, GROUP)
        first, second = swap_blocks(
            get_block(stage, 0, base + GROUP, GROUP), get_block(stage, 1, base + GROUP, GROUP)
        )
        parts.append(
            (
                keep.astype(BF16),
                send.astype(BF16),
                pick(x, first, second).astype(BF16),
                pick(x, second, first).astype(BF16),
            )
        )
    return parts


def middle_kernel(
    part, info, pair, own, near, ypart, ycpart, xpart, xcpart,
    norm1, gate1_t, gain1, final1_t, norm2, proj2_t, eye,
    middle_out, inner_out, o_own, o_near, o_y, o_yc, o_x, o_xc,
    left_st, right_st,
):
    hidden = norm1.shape[0]
    fill_split(info, left_st, own, near, ypart, ycpart, xpart, xcpart, slice(0, LANES))

    def work(rows):
        inner = get_rows(left_st, rows)
        z = turned(eye[...], pair, rows)
        normed = (normalise(z)[0] * wide(norm1[...])).astype(BF16)
        gate = sigmoid(dot_nn(gate1_t[...], normed))
        final = (normalise(inner)[0] * wide(gain1[...])).astype(BF16)
        middle = (z + dot_nn(final1_t[...], final) * gate).astype(BF16)
        width = 2 * LANES
        inner_b = inner.astype(BF16)
        for n, row in enumerate(rows):
            middle_out[row] = middle[:, n * width : (n + 1) * width]
            inner_out[row] = inner_b[:, n * width : (n + 1) * width]
        normed2 = (normalise(middle.astype(F32))[0] * wide(norm2[...])).astype(BF16)
        mixture = dot_nn(proj2_t[: 4 * hidden, :], normed2)
        mask = mask_rows(info, part, rows)
        left = mixture[:hidden] * sigmoid(mixture[2 * hidden : 3 * hidden]) * mask
        right = mixture[hidden : 2 * hidden] * sigmoid(mixture[3 * hidden : 4 * hidden]) * mask
        put_rows(left_st, rows, left)
        put_rows(right_st, rows, right)

    each_rows(work)
    core = info[2]
    parts = split_out(info, left_st)
    for owner, kept, main, yo, xo in (
        (core, parts[0], o_own, o_y, o_x),
        (1 - core, parts[1], o_near, o_yc, o_xc),
    ):
        base = owner * (2 * GROUP)
        main[0, :, :, :LANES] = kept[0]
        yo[:, :, :LANES] = kept[1]
        main[1, :, :, :LANES] = kept[2]
        xo[:, :, :LANES] = kept[3]
        for half in range(2):
            lanes = slice((half + 1) * LANES, (half + 2) * LANES)
            first = get_block(right_st, half, base, GROUP).astype(BF16)
            second = get_block(right_st, half, base + GROUP, GROUP).astype(BF16)
            main[0, :, :, lanes] = first
            yo[:, :, lanes] = first
            main[1, :, :, lanes] = second
            xo[:, :, lanes] = second


def leave_back_rows(inner, gate, grad, gain, final_t, final_w, gfinal):
    hat, spread = normalise(inner)
    final = (hat * gain).astype(BF16)
    product = dot_nn(final_t, final)
    grad_product = (grad * gate).astype(BF16)
    grad_gate = (grad * product * gate * (1.0 - gate)).astype(BF16)
    gfinal[...] += dot_nt(final, grad_product)
    grad_final = dot_nn(final_w, grad_product)
    return normalise_back(grad_final * gain, hat, spread), grad_gate


def turn_kernel(
    part, info, middle, cot, own, near, xpart, xcpart, ypart, ycpart,
    norm2, gate2_t, gain2, final2_t, final2_w, eye, gfinal_in,
    gate_out, same0, same1, other0, other1, gfinal,
    stage,
):
    core = info[2]

    gfinal[...] = gfinal_in[...]

    for owner, mine, xp, yp in ((core, own, xpart, ypart), (1 - core, near, xcpart, ycpart)):
        base = owner * (2 * GROUP)
        for half in range(2):
            lanes = slice(half * LANES, (half + 1) * LANES)
            put_block(stage, half, base, mine[0, :, :, lanes].astype(F32) + xp[:, :, lanes].astype(F32))
            put_block(
                stage, half, base + GROUP, mine[1, :, :, lanes].astype(F32) + yp[:, :, lanes].astype(F32)
            )

    def work(rows):
        inner = get_rows(stage, rows)
        normed = (normalise(stacked(middle, rows).astype(F32))[0] * wide(norm2[...])).astype(BF16)
        gate = sigmoid(dot_nn(gate2_t[...], normed))
        grad = turned(eye[...], cot, rows)
        grad_inner, grad_gate = leave_back_rows(
            inner, gate, grad, wide(gain2[...]), final2_t[...], final2_w[...], gfinal
        )
        width = 2 * LANES
        for n, row in enumerate(rows):
            gate_out[row] = grad_gate[:, n * width : (n + 1) * width]
        put_rows(stage, rows, grad_inner)

    each_rows(work)
    for owner, out0, out1 in ((core, same0, same1), (1 - core, other0, other1)):
        base = owner * (2 * GROUP)
        for half in range(2):
            lanes = slice(half * LANES, (half + 1) * LANES)
            out0[:, :, lanes] = get_block(stage, half, base, GROUP).astype(BF16)
            out1[:, :, lanes] = get_block(stage, half, base + GROUP, GROUP).astype(BF16)


def entry_back_rows(normed, hat, spread, norm, grad_left, grad_right, grad_gate, mask, proj_t, proj_w, gproj):
    hidden = norm.shape[0]
    mixture = dot_nn(proj_t[: 4 * hidden, :], normed)
    left_gate = sigmoid(mixture[2 * hidden : 3 * hidden])
    right_gate = sigmoid(mixture[3 * hidden : 4 * hidden])
    left_flow = grad_left * left_gate * mask
    right_flow = grad_right * right_gate * mask
    grad_mixture = jnp.concatenate(
        [
            left_flow.astype(BF16),
            right_flow.astype(BF16),
            (left_flow * mixture[:hidden] * (1.0 - left_gate)).astype(BF16),
            (right_flow * mixture[hidden : 2 * hidden] * (1.0 - right_gate)).astype(BF16),
            grad_gate,
        ],
        axis=0,
    )
    gproj[...] += dot_nt(normed, grad_mixture)
    grad_normed = dot_nn(proj_w, grad_mixture)
    return normalise_back(grad_normed * norm, hat, spread)


def inward_kernel(
    part, info, middle, pair, cot, inner_in, gate_in, own, near, ypart, ycpart, xpart, xcpart,
    norm2, proj2_t, proj2_w, norm1, gate1_t, gain1, final1_t, final1_w, eye, gproj_in, gfinal_in,
    grad_out, gate_out, o_own, o_near, o_y, o_yc, o_x, o_xc, gproj, gfinal,
    left_st, right_st,
):
    core = info[2]
    gproj[...] = gproj_in[...]
    gfinal[...] = gfinal_in[...]

    fill_split(info, left_st, own, near, ypart, ycpart, xpart, xcpart, slice(0, LANES))
    for owner, mine, yp, xp in ((core, own, ypart, xpart), (1 - core, near, ycpart, xcpart)):
        base = owner * (2 * GROUP)
        for half in range(2):
            lanes = slice((half + 1) * LANES, (half + 2) * LANES)
            put_block(
                right_st, half, base, mine[0, :, :, lanes].astype(F32) + yp[:, :, lanes].astype(F32)
            )
            put_block(
                right_st,
                half,
                base + GROUP,
                mine[1, :, :, lanes].astype(F32) + xp[:, :, lanes].astype(F32),
            )

    def work(rows):
        mask = mask_rows(info, part, rows)
        hat, spread = normalise(stacked(middle, rows).astype(F32))
        norm = wide(norm2[...])
        normed = (hat * norm).astype(BF16)
        grad_flat = entry_back_rows(
            normed, hat, spread, norm, get_rows(left_st, rows), get_rows(right_st, rows),
            stacked(gate_in, rows), mask, proj2_t, proj2_w[...], gproj,
        )
        grad = turned(eye[...], cot, rows) + grad_flat
        z = turned(eye[...], pair, rows)
        normed1 = (normalise(z)[0] * wide(norm1[...])).astype(BF16)
        gate = sigmoid(dot_nn(gate1_t[...], normed1))
        grad_inner, grad_gate = leave_back_rows(
            stacked(inner_in, rows).astype(F32), gate, grad, wide(gain1[...]),
            final1_t[...], final1_w[...], gfinal,
        )
        width = 2 * LANES
        for n, row in enumerate(rows):
            grad_out[row] = grad[:, n * width : (n + 1) * width]
            gate_out[row] = grad_gate[:, n * width : (n + 1) * width]
        put_rows(left_st, rows, grad_inner)

    each_rows(work)
    parts = split_out(info, left_st)
    for kept, main, yo, xo in ((parts[0], o_own, o_y, o_x), (parts[1], o_near, o_yc, o_xc)):
        main[0] = kept[0]
        yo[...] = kept[1]
        main[1] = kept[2]
        xo[...] = kept[3]


def exit_kernel(
    part, info, pair, grad_in, gate_in, own, near, ypart, ycpart, xpart, xcpart,
    norm1, proj1_t, proj1_w, eye, gproj_in, *rest,
):
    out, gproj, left_st, right_st = rest[-4:]
    core = info[2]
    gproj[...] = gproj_in[...]

    for owner, mine, yp, xp in ((core, own, ypart, xpart), (1 - core, near, ycpart, xcpart)):
        base = owner * (2 * GROUP)
        for half in range(2):
            lanes = slice(half * LANES, (half + 1) * LANES)
            beyond = slice((half + 2) * LANES, (half + 3) * LANES)
            for group, stage_l, stage_r in ((0, yp, xp), (1, xp, yp)):
                put_block(
                    left_st,
                    half,
                    base + group * GROUP,
                    mine[group, :, :, lanes].astype(F32) + stage_l[group, :, :, lanes].astype(F32),
                )
                put_block(
                    right_st,
                    half,
                    base + group * GROUP,
                    mine[group, :, :, beyond].astype(F32) + stage_r[group, :, :, lanes].astype(F32),
                )

    def work(rows):
        mask = mask_rows(info, part, rows)
        hat, spread = normalise(turned(eye[...], pair, rows))
        norm = wide(norm1[...])
        normed = (hat * norm).astype(BF16)
        grad_flat = entry_back_rows(
            normed, hat, spread, norm, get_rows(left_st, rows), get_rows(right_st, rows),
            stacked(gate_in, rows), mask, proj1_t, proj1_w[...], gproj,
        )
        total = stacked(grad_in, rows) + grad_flat
        width = 2 * LANES
        for n, row in enumerate(rows):
            out[row] = total[:, n * width : (n + 1) * width].T

    each_rows(work)


CHANNELS = 8
PARTS = 2


def paired(refs):
    return [refs[n : n + PARTS] for n in range(0, len(refs), PARTS)]


def place(one, two, part):
    return pl.multiple_of((one * 2 + two) * (PARTS * BLOCK) + part * BLOCK, BLOCK)


def places(info, group):
    at, core = info[group], info[2]
    return [
        place(at if n < 2 else 1 - at, core if n % 2 == 0 else 1 - core, part)
        for n in range(4)
        for part in range(PARTS)
    ]


def take(ref, group, h):
    return ref[group, h] if len(ref.shape) == 4 else ref[h]


def joined(quads, group, h):
    return jnp.concatenate([take(ref, group, h) for refs in quads for ref in refs], axis=0)


def gather(stage, slot, wheres, quads, group, h):
    for where, ref in zip(wheres, [ref for refs in quads for ref in refs]):
        stage[slot, pl.ds(where, BLOCK), :] = take(ref, group, h)
    return stage[slot]


def give(refs, group, h, lanes, value):
    if len(refs.shape) == 4:
        refs[group, h, :, lanes] = value
    else:
        refs[h, :, lanes] = value


def scatter(quads, group, h, lanes, value):
    for n, ref in enumerate([ref for refs in quads for ref in refs]):
        give(ref, group, h, lanes, value[n * BLOCK : (n + 1) * BLOCK])


def scatter_from(stage, slot, wheres, quads, group, h, lanes):
    for where, ref in zip(wheres, [ref for refs in quads for ref in refs]):
        give(ref, group, h, lanes, stage[slot, pl.ds(where, BLOCK), :])


def outgoing_kernel(info, *refs):
    *refs, stage = refs
    a_own, a_near, a_y, a_yc, b_own, b_near, b_x, b_xc, *outs = paired(refs)
    along_a, along_b = (a_own, a_near, a_y, a_yc), (b_own, b_near, b_x, b_xc)
    o_own, o_near, o_y, o_yc, o_x, o_xc = outs
    for h in range(CHANNELS):
        for group in range(2):
            lefts, rights = (along_a, along_b) if group == 0 else (along_b, along_a)
            far = (o_y, o_yc) if group == 0 else (o_x, o_xc)
            right = gather(stage, 2 * h + group, places(info, group), rights, group, h)
            inner = dot_nt(joined(lefts, group, h), right).astype(BF16)
            scatter((o_own, o_near) + far, group, h, slice(0, LANES), inner)


def halves(quads, group, h):
    both = joined(quads, group, h)
    return both[:, :LANES], both[:, LANES:]


def incoming_kernel(info, *refs):
    *refs, stage = refs
    own, near, ypart, ycpart, xpart, xcpart, o_own, o_near, o_x, o_xc, o_y, o_yc = paired(refs)
    for h in range(CHANNELS):
        for group in range(2):
            far = (ypart, ycpart) if group == 0 else (xpart, xcpart)
            outs = (o_own, o_near) + ((o_x, o_xc) if group == 0 else (o_y, o_yc))
            slot = 2 * h + group
            left, right = halves((own, near) + far, group, h)
            stage[slot] = dot_tn(left, right).astype(BF16)
            scatter_from(stage, slot, places(info, group), outs, group, h, slice(0, 2 * LANES))


def incoming_back_kernel(info, *refs):
    *refs, stage = refs
    own, near, ypart, ycpart, xpart, xcpart, *more = paired(refs)
    same0, same1, near0, near1, g_x, g_xc, g_y, g_yc, *more = more
    o_own, o_near, o_y, o_yc, o_x, o_xc = more
    for h in range(CHANNELS):
        for group in range(2):
            far = (ypart, ycpart) if group == 0 else (xpart, xcpart)
            grads = (same0, near0, g_x, g_xc) if group == 0 else (same1, near1, g_y, g_yc)
            outs = (o_own, o_near) + ((o_y, o_yc) if group == 0 else (o_x, o_xc))
            grad = gather(stage, 2 * h + group, places(info, group), grads, group, h)
            left, right = halves((own, near) + far, group, h)
            scatter(outs, group, h, slice(0, LANES), dot_nt(right, grad).astype(BF16))
            scatter(outs, group, h, slice(LANES, 3 * LANES), dot_nn(left, grad).astype(BF16))


def outgoing_back_kernel(info, *refs):
    *refs, stage, back = refs
    a_own, a_near, a_y, a_yc, b_own, b_near, b_x, b_xc, *more = paired(refs)
    g_own, g_near, g_y, g_yc, g_x, g_xc, o_own, o_near, o_y, o_yc, o_x, o_xc = more
    along_a, along_b = (a_own, a_near, a_y, a_yc), (b_own, b_near, b_x, b_xc)
    first, second = slice(0, 2 * LANES), slice(2 * LANES, 4 * LANES)
    for h in range(CHANNELS):
        for group in range(2):
            lefts, rights = (along_a, along_b) if group == 0 else (along_b, along_a)
            far = (g_y, g_yc) if group == 0 else (g_x, g_xc)
            left_far, right_far = ((o_y, o_yc), (o_x, o_xc)) if group == 0 else ((o_x, o_xc), (o_y, o_yc))
            slot = 2 * h + group
            wheres = places(info, group)
            right = gather(stage, slot, wheres, rights, group, h)
            grad = joined((g_own, g_near) + far, group, h)
            grad_left = dot_nn(grad, right).astype(BF16)
            back[slot] = dot_tn(grad, joined(lefts, group, h)).astype(BF16)
            core_rows = 2 * PARTS * BLOCK
            scatter((o_own, o_near), group, h, first, grad_left[:core_rows])
            scatter(left_far, group, h, first, grad_left[core_rows:])
            scatter_from(back, slot, wheres[: 2 * PARTS], (o_own, o_near), group, h, second)
            scatter_from(back, slot, wheres[2 * PARTS :], right_far, group, h, first)


def whole(shape):
    return pl.BlockSpec(shape, lambda step, info: (0,) * len(shape))


def rows_of(part):
    def make(shape):
        return pl.BlockSpec((BLOCK,) + shape[1:], lambda step, info: (part,) + (0,) * (len(shape) - 1))

    return make


def anywhere(shape):
    return pl.BlockSpec(memory_space=pl.ANY)


def channel_rows(shape):
    if len(shape) == 4:
        return pl.BlockSpec((shape[0], CHANNELS) + shape[2:], lambda step, info: (0, step, 0, 0))
    return pl.BlockSpec((CHANNELS,) + shape[1:], lambda step, info: (step, 0, 0))


def call(kernel, info, steps, ins, outs, scratch, aliases={}):
    return pl.pallas_call(
        kernel,
        grid_spec=pltpu.PrefetchScalarGridSpec(
            num_scalar_prefetch=1,
            grid=(steps,),
            in_specs=[make(array.shape) for array, make in ins],
            out_specs=[make(shape) for shape, unused, make in outs],
            scratch_shapes=scratch,
        ),
        out_shape=[jax.ShapeDtypeStruct(shape, dtype) for shape, dtype, unused in outs],
        compiler_params=pltpu.CompilerParams(vmem_limit_bytes=VMEM),
        input_output_aliases=aliases,
    )(info, *[array for array, unused in ins])


class Links:
    def __init__(self):
        self.last = {}

    def __call__(self, arrays, offset):
        count = lax.axis_size("axial")
        pairs = [(n, n ^ offset) for n in range(count)]
        results = []
        for array in arrays:
            if offset in self.last and offset != CORE:
                array, unused = lax.optimization_barrier((array, self.last[offset]))
            self.last[offset] = lax.ppermute(array, "axial", pairs)
            results.append(self.last[offset])
        return results


CORE, X, Y = 1, 2, 4


def add_up(share):
    count = lax.axis_size("axial")
    rows, width = share.shape
    shares = share.astype(BF16).reshape(count, rows // count, width)
    parts = lax.all_to_all(shares, "axial", split_axis=0, concat_axis=0, tiled=True)
    mine = parts.astype(F32).sum(axis=0).astype(BF16)
    depth = lax.axis_size("dp")
    terms = [mine] + [
        lax.ppermute(mine, "dp", [(n, n ^ offset) for n in range(depth)])
        for offset in range(1, depth)
    ]
    terms = [term.astype(F32) for term in terms]
    while len(terms) > 1:
        terms = [terms[n] + terms[n + 1] for n in range(0, len(terms), 2)]
    copies = jnp.broadcast_to(terms[0].astype(BF16)[None], shares.shape)
    return lax.all_to_all(copies, "axial", split_axis=0, concat_axis=0, tiled=True).reshape(
        rows, width
    )


def gain_grad(weight_grad, weight, gain_row):
    return jnp.sum((weight.astype(F32) * weight_grad).T, axis=0, keepdims=True) / gain_row


def finish_kernel(
    scale, info, sums, proj1, final1, proj2, final2, norm1, gain1, norm2, gain2,
    o_norm1, o_proj1, o_gain1, o_final1, o_norm2, o_proj2, o_gain2, o_final2,
):
    width, channels = proj1.shape[1], final1.shape[1]
    takes = (
        (0, proj1, norm1, o_proj1, o_norm1),
        (width, proj2, norm2, o_proj2, o_norm2),
        (2 * width, final2, gain2, o_final2, o_gain2),
        (2 * width + channels, final1, gain1, o_final1, o_gain1),
    )
    for start, weight, gain, out, gain_out in takes:
        total = sums[:, start : start + weight.shape[1]].astype(F32) * scale
        out[...] = total
        gain_out[...] = gain_grad(total, weight[...].astype(BF16), gain[...])


def fast_body(
    pair,
    cotangent,
    lengths,
    outgo_norm,
    outgo_proj,
    outgo_gain,
    outgo_final,
    incom_norm,
    incom_proj,
    incom_gain,
    incom_final,
):
    rows, tokens, channels = pair.shape[1:]
    hidden = outgo_gain.shape[0]
    index = lax.axis_index("axial")
    info = jnp.stack(
        [(index // 2) % 2, index // 4, index % 2, index * rows, lengths[0]]
    ).astype(jnp.int32)
    hop = Links()
    pair = pair[0]
    cot = cotangent[0]
    eye = jnp.eye(channels, dtype=BF16)

    def spread(gain):
        return jnp.broadcast_to(gain[:, None], (gain.shape[0], tokens))

    norm1, gain1, norm2, gain2 = map(spread, (outgo_norm, outgo_gain, incom_norm, incom_gain))
    proj1, final1, proj2, final2 = (
        weight.astype(BF16) for weight in (outgo_proj, outgo_final, incom_proj, incom_final)
    )
    proj1_t, final1_t, proj2_t, final2_t = proj1.T, final1.T, proj2.T, final2.T
    gate1_t, gate2_t = proj1_t[4 * hidden :], proj2_t[4 * hidden :]
    parts = range(PARTS)
    turns = GROUP // CHANNELS
    stage = pltpu.VMEM((2 * hidden * BLOCK, LANES), F32)
    square = pltpu.VMEM((2 * CHANNELS, 4 * rows, tokens), BF16)

    def two(width, height=BLOCK, make=whole):
        return ((2, GROUP, height, width), BF16, make)

    def one(width, height=BLOCK, make=whole):
        return ((GROUP, height, width), BF16, make)

    turned_block = ((BLOCK, channels, tokens), BF16, whole)

    def cells(kernel, ins, outs, scratch, aliases={}):
        results = []
        for part in parts:
            carried = ins(part, results)
            results.append(
                call(functools.partial(kernel, part), info, 1, carried, outs, scratch, aliases)
            )
        return [list(each) for each in zip(*results)]

    def wholes(arrays):
        return [(array, whole) for array in arrays]

    def triangle(kernel, operands, outs, scratch):
        ins = [(array, channel_rows) for arrays in operands for array in arrays]
        each = [out for out in outs for unused in parts]
        results = call(kernel, info, turns, ins, each, scratch)
        return [list(results[n : n + PARTS]) for n in range(0, len(results), PARTS)]

    a_same, a_other, b_same, b_other = cells(
        entry_kernel,
        lambda part, unused: [(pair, rows_of(part)), (outgo_norm[None], whole), (outgo_proj, whole)],
        [two(tokens)] * 4,
        [
            stage,
            stage,
            pltpu.VMEM((channels, tokens), F32),
            pltpu.VMEM((4 * hidden, channels), BF16),
        ],
    )
    a_y, b_x = hop(a_same, Y), hop(b_same, X)
    a_yc, b_xc = hop(a_other, Y | CORE), hop(b_other, X | CORE)
    near = hop([array for two_parts in zip(a_other, b_other) for array in two_parts], CORE)
    a_near, b_near = near[0::2], near[1::2]
    held_one = [a_same, a_near, a_y, a_yc, b_same, b_near, b_x, b_xc]
    own, near, to_y, to_yc, to_x, to_xc = triangle(
        outgoing_kernel,
        held_one,
        [two(LANES, make=channel_rows)] * 2 + [one(LANES, make=channel_rows)] * 4,
        [square],
    )
    back_one = [
        own,
        hop(near, CORE),
        hop(to_y, Y),
        hop(to_yc, Y | CORE),
        hop(to_x, X),
        hop(to_xc, X | CORE),
    ]

    middle, inner_one, own, near, to_y, to_yc, to_x, to_xc = cells(
        middle_kernel,
        lambda part, unused: [(pair, rows_of(part))]
        + wholes(arrays[part] for arrays in back_one)
        + wholes((norm1, gate1_t, gain1, final1_t, norm2, proj2_t, eye)),
        [turned_block] * 2 + [two(3 * LANES)] * 2 + [one(3 * LANES)] * 4,
        [stage, stage],
    )
    held_two = [
        own,
        hop(near, CORE),
        hop(to_y, Y),
        hop(to_yc, Y | CORE),
        hop(to_x, X),
        hop(to_xc, X | CORE),
    ]
    own, near, to_x, to_xc, to_y, to_yc = triangle(
        incoming_kernel,
        held_two,
        [two(tokens, make=channel_rows)] * 2 + [one(tokens, make=channel_rows)] * 4,
        [square],
    )
    back_two = [
        own,
        hop(near, CORE),
        hop(to_x, X),
        hop(to_xc, X | CORE),
        hop(to_y, Y),
        hop(to_yc, Y | CORE),
    ]

    square_zero = jnp.zeros((hidden, channels), F32)
    proj_zero = jnp.zeros((channels, 5 * hidden), F32)
    gate_grad_two, same0, same1, other0, other1, grad_final_two = cells(
        turn_kernel,
        lambda part, done: [(middle[part], whole), (cot, rows_of(part))]
        + wholes(arrays[part] for arrays in back_two)
        + wholes((norm2, gate2_t, gain2, final2_t, final2, eye))
        + wholes([done[-1][5] if done else square_zero]),
        [turned_block] + [one(tokens)] * 4 + [((hidden, channels), F32, whole)],
        [stage],
    )
    near = hop([array for two_parts in zip(other0, other1) for array in two_parts], CORE)
    grads_two = [
        same0,
        same1,
        near[0::2],
        near[1::2],
        hop(same0, X),
        hop(other0, X | CORE),
        hop(same1, Y),
        hop(other1, Y | CORE),
    ]
    own, near, to_y, to_yc, to_x, to_xc = triangle(
        incoming_back_kernel,
        held_two + grads_two,
        [two(3 * LANES, make=channel_rows)] * 2 + [one(3 * LANES, make=channel_rows)] * 4,
        [square],
    )
    rows_two = [
        own,
        hop(near, CORE),
        hop(to_y, Y),
        hop(to_yc, Y | CORE),
        hop(to_x, X),
        hop(to_xc, X | CORE),
    ]

    (
        grad_middle, gate_grad_one, own, near, to_y, to_yc, to_x, to_xc,
        grad_proj_two, grad_final_one,
    ) = cells(
        inward_kernel,
        lambda part, done: [
            (middle[part], whole),
            (pair, rows_of(part)),
            (cot, rows_of(part)),
            (inner_one[part], whole),
            (gate_grad_two[part], whole),
        ]
        + wholes(arrays[part] for arrays in rows_two)
        + wholes((norm2, proj2_t, proj2, norm1, gate1_t, gain1, final1_t, final1, eye))
        + wholes(done[-1][-2:] if done else (proj_zero, square_zero)),
        [((BLOCK, channels, tokens), F32, whole), turned_block]
        + [two(LANES)] * 2
        + [one(LANES)] * 4
        + [((channels, 5 * hidden), F32, whole), ((hidden, channels), F32, whole)],
        [stage, stage],
    )
    grads_one = [
        own,
        hop(near, CORE),
        hop(to_y, Y),
        hop(to_yc, Y | CORE),
        hop(to_x, X),
        hop(to_xc, X | CORE),
    ]
    own, near, to_y, to_yc, to_x, to_xc = triangle(
        outgoing_back_kernel,
        held_one + grads_one,
        [two(2 * tokens, make=channel_rows)] * 2 + [two(tokens, make=channel_rows)] * 4,
        [square, square],
    )
    rows_one = [
        own,
        hop(near, CORE),
        hop(to_y, Y),
        hop(to_yc, Y | CORE),
        hop(to_x, X),
        hop(to_xc, X | CORE),
    ]
    exit_ins = 10 + 4 + 1
    result = None
    for part in parts:
        result = call(
            functools.partial(exit_kernel, part),
            info,
            1,
            [(pair, rows_of(part))]
            + wholes((grad_middle[part], gate_grad_one[part]))
            + wholes(arrays[part] for arrays in rows_one)
            + wholes((norm1, proj1_t, proj1, eye))
            + wholes([result[1] if part else proj_zero])
            + ([(result[0], anywhere)] if part else []),
            [
                ((rows, tokens, channels), F32, rows_of(part)),
                ((channels, 5 * hidden), F32, whole),
            ],
            [stage, stage],
            {exit_ins: 0} if part else {},
        )
    grad_begin, grad_proj_one = result
    sums = add_up(
        jnp.concatenate(
            [grad_proj_one, grad_proj_two[-1], grad_final_two[-1], grad_final_one[-1]], axis=1
        )
    )
    scale = 1.0 / math.sqrt(lax.axis_size("dp") * tokens * tokens)
    weights = (outgo_proj, outgo_final, incom_proj, incom_final)
    gains = (outgo_norm, outgo_gain, incom_norm, incom_gain)
    order = (outgo_norm[None], outgo_proj, outgo_gain[None], outgo_final)
    order += (incom_norm[None], incom_proj, incom_gain[None], incom_final)
    totals = call(
        functools.partial(finish_kernel, scale),
        info,
        1,
        wholes((sums,) + weights + tuple(gain[None] for gain in gains)),
        [(array.shape, F32, whole) for array in order],
        [],
    )
    return (grad_begin[None],) + tuple(
        total.reshape(-1) if total.shape[0] == 1 else total for total in totals
    )


def solution(mesh):
    def body(pair, *rest):
        rows, tokens, channels = pair.shape[1:]
        hidden = rest[3].shape[0]
        plane = mesh.shape["axial"] == 8 and rows == 32 and tokens == 2 * LANES
        if plane and channels == LANES and hidden == 4 * GROUP:
            return fast_body(pair, *rest)
        return plain_body(pair, *rest)

    return jax.shard_map(
        body,
        mesh=mesh,
        in_specs=(P("dp", "axial", None, None), P("dp", "axial", None, None), P("dp")) + (P(),) * 8,
        out_specs=(P("dp", "axial", None, None),) + (P(),) * 8,
        check_vma=False,
    )
```

```python
import functools
import math

import jax
import jax.numpy as jnp
from jax import lax
from jax.experimental import pallas as pl
from jax.experimental.pallas import tpu as pltpu
from jax.sharding import PartitionSpec as P

EPSILON = 1e-05


def rounded(inputs):
    return lax.optimization_barrier(inputs.astype(jnp.bfloat16)).astype(jnp.float32)


def layer_norm(inputs, factor):
    average = jnp.mean(inputs, axis=-1, keepdims=True)
    centered = inputs - average
    spread = jnp.mean(centered * centered, axis=-1, keepdims=True)
    return centered * lax.rsqrt(spread + EPSILON) * factor


def gating(mixture, pair_mask, hidden):
    left_part = (
        mixture[:, :hidden] * jax.nn.sigmoid(mixture[:, 2 * hidden : 3 * hidden]) * pair_mask
    )
    right_part = (
        mixture[:, hidden : 2 * hidden]
        * jax.nn.sigmoid(mixture[:, 3 * hidden : 4 * hidden])
        * pair_mask
    )
    gate_part = jax.nn.sigmoid(mixture[:, 4 * hidden :])
    return (left_part, right_part, gate_part)


def entry(flat_pair, norm_gain, projection, pair_mask, hidden):
    normed = layer_norm(flat_pair, norm_gain).astype(jnp.bfloat16)
    mixture = jnp.dot(normed, projection.astype(jnp.bfloat16), preferred_element_type=jnp.float32)
    left_part, right_part, gate_part = gating(mixture, pair_mask, hidden)
    return (normed, mixture, left_part, right_part, gate_part)


def entry_back(
    flat_pair,
    norm_gain,
    projection,
    pair_mask,
    hidden,
    normed,
    mixture,
    grad_left,
    grad_right,
    grad_gate,
):
    unused, pull_gate = jax.vjp(lambda inner_mix: gating(inner_mix, pair_mask, hidden), mixture)
    grad_mixture = pull_gate((grad_left, grad_right, grad_gate))[0].astype(jnp.bfloat16)
    grad_projection = jnp.dot(normed.T, grad_mixture, preferred_element_type=jnp.float32)
    grad_normed = jnp.dot(
        grad_mixture, projection.astype(jnp.bfloat16).T, preferred_element_type=jnp.float32
    )
    unused, pull_norm = jax.vjp(layer_norm, flat_pair, norm_gain)
    grad_flat, grad_gain = pull_norm(grad_normed)
    return (grad_flat, grad_gain, grad_projection)


def leave(inner_sum, gate_part, out_gain, final_weight):
    final_normed = layer_norm(inner_sum, out_gain).astype(jnp.bfloat16)
    product = jnp.dot(
        final_normed, final_weight.astype(jnp.bfloat16), preferred_element_type=jnp.float32
    )
    return (final_normed, product, product * gate_part)


def leave_back(inner_sum, gate_part, out_gain, final_weight, final_normed, product, grad_update):
    grad_product = (grad_update * gate_part).astype(jnp.bfloat16)
    grad_gate = grad_update * product
    grad_final = jnp.dot(final_normed.T, grad_product, preferred_element_type=jnp.float32)
    grad_normed = jnp.dot(
        grad_product, final_weight.astype(jnp.bfloat16).T, preferred_element_type=jnp.float32
    )
    unused, pull_norm = jax.vjp(layer_norm, inner_sum, out_gain)
    grad_inner, grad_gain = pull_norm(grad_normed)
    return (grad_inner, grad_gate, grad_gain, grad_final)


def channel_major(field, row_count, tokens):
    hidden = field.shape[1]
    return jnp.transpose(field.reshape(row_count, tokens, hidden), (2, 0, 1))


def row_major(field):
    hidden = field.shape[0]
    return jnp.transpose(field, (1, 2, 0)).reshape(-1, hidden)


def plain_body(
    pair,
    cotangent,
    lengths,
    outgo_norm,
    outgo_proj,
    outgo_gain,
    outgo_final,
    incom_norm,
    incom_proj,
    incom_gain,
    incom_final,
):
    row_count = pair.shape[1]
    tokens = pair.shape[2]
    channels = pair.shape[3]
    hidden = outgo_gain.shape[0]
    length = lengths[0]
    first_row = lax.axis_index("axial") * row_count
    row_alive = (first_row + jnp.arange(row_count, dtype=jnp.int32) < length).astype(jnp.float32)
    column_alive = (jnp.arange(tokens, dtype=jnp.int32) < length).astype(jnp.float32)
    pair_mask = (row_alive[:, None] * column_alive[None, :]).reshape(-1, 1)
    flat_start = pair[0].reshape(-1, channels).astype(jnp.float32)
    normed_one, mixture_one, left_one, right_one, gate_one = entry(
        flat_start, outgo_norm, outgo_proj, pair_mask, hidden
    )
    left_first = channel_major(left_one.astype(jnp.bfloat16), row_count, tokens)
    right_first = channel_major(right_one.astype(jnp.bfloat16), row_count, tokens)
    left_owned, right_owned = (
        lax.all_to_all(left_first, "axial", split_axis=0, concat_axis=1, tiled=True),
        lax.all_to_all(right_first, "axial", split_axis=0, concat_axis=1, tiled=True),
    )
    inner_cols = jnp.einsum(
        "hik,hjk->hij", left_owned, right_owned, preferred_element_type=jnp.float32
    )
    inner_one = row_major(
        lax.all_to_all(
            inner_cols.astype(jnp.bfloat16), "axial", split_axis=1, concat_axis=0, tiled=True
        ).astype(inner_cols.dtype)
    )
    final_one, product_one, update_one = leave(inner_one, gate_one, outgo_gain, outgo_final)
    flat_middle = rounded(flat_start + update_one)
    normed_two, mixture_two, left_two, right_two, gate_two = entry(
        flat_middle, incom_norm, incom_proj, pair_mask, hidden
    )
    left_second = channel_major(left_two.astype(jnp.bfloat16), row_count, tokens)
    right_second = channel_major(right_two.astype(jnp.bfloat16), row_count, tokens)
    left_held, right_held = (
        lax.all_to_all(left_second, "axial", split_axis=0, concat_axis=1, tiled=True),
        lax.all_to_all(right_second, "axial", split_axis=0, concat_axis=1, tiled=True),
    )
    inner_held = jnp.einsum(
        "hki,hkj->hij", left_held, right_held, preferred_element_type=jnp.float32
    )
    inner_two = row_major(
        lax.all_to_all(
            inner_held.astype(jnp.bfloat16), "axial", split_axis=1, concat_axis=0, tiled=True
        ).astype(inner_held.dtype)
    )
    final_two, product_two, update_two = leave(inner_two, gate_two, incom_gain, incom_final)
    grad_end = cotangent[0].reshape(-1, channels).astype(jnp.float32)
    grad_inner_two, grad_gate_two, grad_gain_two, grad_final_two = leave_back(
        inner_two, gate_two, incom_gain, incom_final, final_two, product_two, grad_end
    )
    grad_cells_two = channel_major(grad_inner_two.astype(jnp.bfloat16), row_count, tokens)
    grad_held_two = lax.all_to_all(grad_cells_two, "axial", split_axis=0, concat_axis=1, tiled=True)
    left_back, right_back = (
        lax.all_to_all(left_second, "axial", split_axis=0, concat_axis=1, tiled=True),
        lax.all_to_all(right_second, "axial", split_axis=0, concat_axis=1, tiled=True),
    )
    grad_left_held = jnp.einsum(
        "hij,hkj->hki", grad_held_two, right_back, preferred_element_type=jnp.float32
    )
    grad_right_held = jnp.einsum(
        "hki,hij->hkj", left_back, grad_held_two, preferred_element_type=jnp.float32
    )
    grad_left_rows, grad_right_rows = (
        lax.all_to_all(
            grad_left_held.astype(jnp.bfloat16), "axial", split_axis=1, concat_axis=0, tiled=True
        ).astype(grad_left_held.dtype),
        lax.all_to_all(
            grad_right_held.astype(jnp.bfloat16), "axial", split_axis=1, concat_axis=0, tiled=True
        ).astype(grad_right_held.dtype),
    )
    grad_left_two = row_major(grad_left_rows)
    grad_right_two = row_major(grad_right_rows)
    grad_flat_two, grad_norm_two, grad_proj_two = entry_back(
        flat_middle,
        incom_norm,
        incom_proj,
        pair_mask,
        hidden,
        normed_two,
        mixture_two,
        grad_left_two,
        grad_right_two,
        grad_gate_two,
    )
    second_sums = lax.psum(
        (grad_norm_two, grad_proj_two, grad_gain_two, grad_final_two), ("dp", "axial")
    )
    grad_middle = grad_end + grad_flat_two
    grad_inner_one, grad_gate_one, grad_gain_one, grad_final_one = leave_back(
        inner_one, gate_one, outgo_gain, outgo_final, final_one, product_one, grad_middle
    )
    grad_cells_one = channel_major(grad_inner_one.astype(jnp.bfloat16), row_count, tokens)
    grad_owned_one = lax.all_to_all(
        grad_cells_one, "axial", split_axis=0, concat_axis=1, tiled=True
    )
    left_again, right_again = (
        lax.all_to_all(left_first, "axial", split_axis=0, concat_axis=1, tiled=True),
        lax.all_to_all(right_first, "axial", split_axis=0, concat_axis=1, tiled=True),
    )
    grad_left_owned = jnp.einsum(
        "hij,hjk->hik", grad_owned_one, right_again, preferred_element_type=jnp.float32
    )
    grad_right_owned = jnp.einsum(
        "hij,hik->hjk", grad_owned_one, left_again, preferred_element_type=jnp.float32
    )
    grad_left_back, grad_right_back = (
        lax.all_to_all(
            grad_left_owned.astype(jnp.bfloat16), "axial", split_axis=1, concat_axis=0, tiled=True
        ).astype(grad_left_owned.dtype),
        lax.all_to_all(
            grad_right_owned.astype(jnp.bfloat16), "axial", split_axis=1, concat_axis=0, tiled=True
        ).astype(grad_right_owned.dtype),
    )
    grad_left_one = row_major(grad_left_back)
    grad_right_one = row_major(grad_right_back)
    grad_flat_one, grad_norm_one, grad_proj_one = entry_back(
        flat_start,
        outgo_norm,
        outgo_proj,
        pair_mask,
        hidden,
        normed_one,
        mixture_one,
        grad_left_one,
        grad_right_one,
        grad_gate_one,
    )
    grad_begin = grad_middle + grad_flat_one
    first_sums = lax.psum(
        (grad_norm_one, grad_proj_one, grad_gain_one, grad_final_one), ("dp", "axial")
    )
    totals = tuple(first_sums) + tuple(second_sums)
    scale = 1.0 / math.sqrt(lax.axis_size("dp") * tokens * tokens)
    return (
        grad_begin.reshape(1, row_count, tokens, channels),
        totals[0] * scale,
        totals[1] * scale,
        totals[2] * scale,
        totals[3] * scale,
        totals[4] * scale,
        totals[5] * scale,
        totals[6] * scale,
        totals[7] * scale,
    )


BF16 = jnp.bfloat16
F32 = jnp.float32
BLOCK = 16
PAIRED = 2
STEPS = 2
SOME = BLOCK // STEPS
LANES = 128
GROUP = 32
VMEM = 56 * 1024 * 1024


def dot_nn(a, b):
    return lax.dot_general(a, b, (((1,), (0,)), ((), ())), preferred_element_type=F32)


def dot_nt(a, b):
    return lax.dot_general(a, b, (((1,), (1,)), ((), ())), preferred_element_type=F32)


def dot_tn(a, b):
    return lax.dot_general(a, b, (((0,), (0,)), ((), ())), preferred_element_type=F32)


def normalise(v):
    centered = v - jnp.mean(v, axis=0, keepdims=True)
    spread = lax.rsqrt(jnp.mean(centered * centered, axis=0, keepdims=True) + EPSILON)
    return centered * spread, spread


def normalise_back(grad, hat, spread):
    first = jnp.mean(grad, axis=0, keepdims=True)
    second = jnp.mean(grad * hat, axis=0, keepdims=True)
    return spread * (grad - first - hat * second)


def reorder():
    size = BLOCK * BLOCK
    one = lax.broadcasted_iota(jnp.int32, (size, size), 0)
    two = lax.broadcasted_iota(jnp.int32, (size, size), 1)
    return jnp.where((one % BLOCK) * BLOCK + one // BLOCK == two, 1.0, 0.0).astype(BF16)


def chunk(ref, group, at, lanes):
    if len(ref.shape) == 4:
        block = ref[group, at : at + BLOCK, :, lanes]
    else:
        block = ref[at : at + BLOCK, :, lanes]
    return block.reshape(BLOCK * BLOCK, block.shape[2])


def put_chunk(stage, half, channel, value):
    channel = pl.multiple_of(channel, BLOCK)
    for row in range(BLOCK):
        stage[half, row, pl.ds(channel, BLOCK), :] = value[row * BLOCK : (row + 1) * BLOCK]


def get_chunk(stage, halves, channel):
    channel = pl.multiple_of(channel, BLOCK)
    return jnp.concatenate(
        [
            jnp.concatenate(
                [stage[half, row, pl.ds(channel, BLOCK), :] for row in range(BLOCK)], axis=0
            )
            for half in halves
        ],
        axis=1,
    )


def give_chunk(ref, group, at, lanes, value):
    block = value.astype(BF16).reshape(BLOCK, BLOCK, value.shape[1])
    if len(ref.shape) == 4:
        ref[group, at : at + BLOCK, :, lanes] = block
    else:
        ref[at : at + BLOCK, :, lanes] = block


def put_rows(stage, rows, value):
    for n, row in enumerate(rows):
        for half in range(2):
            start = (2 * n + half) * LANES
            stage[half, row] = value[:, start : start + LANES].astype(stage.dtype)


def get_rows(stage, rows):
    return jnp.concatenate([stage[half, row] for row in rows for half in range(2)], axis=1)


def spread_out(ref, rows, value):
    width = 2 * LANES
    for n, row in enumerate(rows):
        ref[row] = value[:, n * width : (n + 1) * width].astype(ref.dtype)


LOW, HIGH, BOTH = slice(0, LANES), slice(LANES, 2 * LANES), slice(0, 2 * LANES)
CHUNKS = range(0, GROUP, BLOCK)


def half_swap(first, second):
    low = lax.broadcasted_iota(jnp.int32, first.shape, first.ndim - 1) < LANES // 2
    axis = first.ndim - 1
    return (
        jnp.where(low, first, pltpu.roll(second, LANES // 2, axis)),
        jnp.where(low, pltpu.roll(first, LANES // 2, axis), second),
    )


def pick(flag, zero, one):
    return jnp.where(flag == 0, zero, one)


def mask_rows(info, part, rows):
    length = info[4]
    column = (lax.broadcasted_iota(jnp.int32, (1, 2 * LANES), 1) < length).astype(F32)
    return jnp.concatenate(
        [column * (info[3] + part * BLOCK + row < length).astype(F32) for row in rows], axis=1
    )


def each_rows(work):
    step = pl.program_id(0)

    @pl.loop(0, SOME // PAIRED)
    def _(turn):
        here = [turn * PAIRED + n for n in range(PAIRED)]
        work(here, [step * SOME + row for row in here])


def first_step(work):
    pl.when(pl.program_id(0) == 0)(work)


def last_step(work):
    pl.when(pl.program_id(0) == STEPS - 1)(work)


def turned(ref, rows):
    return jnp.concatenate([ref[row].astype(F32).T for row in rows], axis=1)


def stacked(ref, rows):
    return jnp.concatenate([ref[row] for row in rows], axis=1)


def gated(mixture, hidden, mask):
    scale = 0.5 * mask
    left = mixture[:hidden] * (jnp.tanh(mixture[2 * hidden : 3 * hidden]) + 1.0) * scale
    right = mixture[hidden : 2 * hidden] * (jnp.tanh(mixture[3 * hidden : 4 * hidden]) + 1.0) * scale
    return left, right, opened(mixture[4 * hidden :])


def opened(gate):
    return 0.5 * jnp.tanh(gate) + 0.5


def column(row):
    size = row.shape[1]
    square = jnp.broadcast_to(row, (size, size)).T
    return jnp.concatenate([square] * (2 * PAIRED * LANES // size), axis=1)


def halved_turned(weight):
    values = 2 * weight.shape[0]
    return jnp.concatenate([weight[:, :values].T, weight[:, values:].T * 0.5], axis=0).astype(BF16)


def entry_kernel(part, info, pair, norm_row, proj_w, *rest):
    if part:
        raw, rest = rest[:6], rest[6:]
        gain1, final1, norm2, proj2, gain2, final2 = raw
        prepared, rest = rest[6:18], rest[:6] + rest[18:]
    a_same, a_other, b_same, b_other, to_core, gate_out, left_st, right_st, norm, proj_t, perm = rest
    hidden = proj_w.shape[1] // 5

    @first_step
    def _():
        norm[...] = column(norm_row[...])
        proj_t[...] = halved_turned(proj_w[...])
        perm[...] = reorder()
        if part:
            for row, out in zip((norm_row, gain1, norm2, gain2), prepared[:4]):
                out[...] = column(row[...])
            for weight, out in zip((proj_w, proj2), prepared[4:6]):
                out[...] = halved_turned(weight[...])
            for weight, out in zip((final1, final2), prepared[6:8]):
                out[...] = weight[...].T.astype(BF16)
            for weight, out in zip((proj_w, final1, proj2, final2), prepared[8:]):
                out[...] = weight[...].astype(BF16)

    def work(here, rows):
        normed = (normalise(turned(pair, here))[0] * norm[...]).astype(BF16)
        mixture = dot_nn(proj_t[...], normed)
        left, right, gate = gated(mixture, hidden, mask_rows(info, part, rows))
        put_rows(left_st, rows, left)
        put_rows(right_st, rows, right)
        spread_out(gate_out, here, gate)

    each_rows(work)

    @last_step
    def _():
        core = info[2]
        for owner, a_out, b_out in ((core, a_same, b_same), (1 - core, a_other, b_other)):
            for group in range(2):
                for at in CHUNKS:
                    channel = owner * (2 * GROUP) + group * GROUP + at
                    left = dot_nn(perm[...], get_chunk(left_st, (0, 1), channel)).astype(BF16)
                    right = dot_nn(perm[...], get_chunk(right_st, (0, 1), channel)).astype(BF16)
                    first, second = (left, right) if group == 0 else (right, left)
                    give_chunk(a_out, group, at, BOTH, first)
                    give_chunk(b_out, group, at, BOTH, second)
                    if a_out is a_other:
                        give_chunk(to_core, group, at, BOTH, first)
                        give_chunk(to_core, 2 + group, at, BOTH, second)


def fill_split(info, perm, stage, own, near, ypart, ycpart, xpart, xcpart):
    x, y, core = info[0], info[1], info[2]
    for owner, mine, yp, xp in ((core, own, ypart, xpart), (1 - core, near, ycpart, xcpart)):
        for at in CHUNKS:
            channel = owner * (2 * GROUP) + at
            both = jnp.concatenate([chunk(mine, 0, at, LOW), chunk(yp, 0, at, LOW)], axis=1)
            both = dot_nn(perm, both)
            put_chunk(stage, y, channel, both[:, LOW])
            put_chunk(stage, 1 - y, channel, both[:, HIGH])
            both = jnp.concatenate([chunk(mine, 1, at, LOW), chunk(xp, 0, at, LOW)], axis=1)
            both = dot_nn(perm, both)
            here, there = both[:, LOW], both[:, HIGH]
            first, second = half_swap(pick(x, here, there), pick(x, there, here))
            put_chunk(stage, 0, channel + GROUP, first)
            put_chunk(stage, 1, channel + GROUP, second)


def fill_sum(perm, stage, channel, first, second):
    both = (chunk(*first).astype(F32) + chunk(*second).astype(F32)).astype(BF16)
    total = dot_nn(perm, both)
    put_chunk(stage, 0, channel, total[:, LOW])
    put_chunk(stage, 1, channel, total[:, HIGH])


def split_out(info, perm, stage, owner, at):
    x, y = info[0], info[1]
    channel = owner * (2 * GROUP) + at
    both = dot_nn(perm, get_chunk(stage, (y, 1 - y), channel))
    swapped = dot_nn(perm, get_chunk(stage, (0, 1), channel + GROUP))
    first, second = half_swap(swapped[:, LOW], swapped[:, HIGH])
    return both[:, LOW], both[:, HIGH], pick(x, first, second), pick(x, second, first)


def middle_kernel(
    part, info, pair, own, ypart, xpart, ycpart, xcpart, near,
    gate1, gain1, final1_t, norm2, proj2_t,
    middle_out, inner_out, gate_out, o_own, o_near, o_y, o_yc, o_x, o_xc,
    stage, left_st, right_st, perm,
):
    @first_step
    def _():
        perm[...] = reorder()
        fill_split(info, perm[...], stage, own, near, ypart, ycpart, xpart, xcpart)

    def work(here, rows):
        inner = get_rows(stage, rows)
        final = (normalise(inner)[0] * gain1[...]).astype(BF16)
        update = dot_nn(final1_t[...], final) * stacked(gate1, here).astype(F32)
        middle = (turned(pair, here) + update).astype(BF16)
        spread_out(middle_out, here, middle)
        spread_out(inner_out, here, inner)
        normed = (normalise(middle.astype(F32))[0] * norm2[...]).astype(BF16)
        mixture = dot_nn(proj2_t[...], normed)
        left, right, gate = gated(mixture, norm2.shape[0], mask_rows(info, part, rows))
        put_rows(left_st, rows, left)
        put_rows(right_st, rows, right)
        spread_out(gate_out, here, gate)

    each_rows(work)

    @last_step
    def _():
        core = info[2]
        beyond = slice(LANES, 3 * LANES)
        for owner, main, yo, xo in ((core, o_own, o_y, o_x), (1 - core, o_near, o_yc, o_xc)):
            for at in CHUNKS:
                kept = split_out(info, perm[...], left_st, owner, at)
                give_chunk(main, 0, at, LOW, kept[0])
                give_chunk(yo, 0, at, LOW, kept[1])
                give_chunk(main, 1, at, LOW, kept[2])
                give_chunk(xo, 0, at, LOW, kept[3])
                for group, out in ((0, yo), (1, xo)):
                    channel = owner * (2 * GROUP) + group * GROUP + at
                    right = dot_nn(perm[...], get_chunk(right_st, (0, 1), channel)).astype(BF16)
                    give_chunk(main, group, at, beyond, right)
                    give_chunk(out, 0, at, beyond, right)


def start_sum(total, before):
    total[...] = before[0][...] if before else jnp.zeros_like(total)


def leave_rows_back(inner, gate, grad, gain, final_t, final_w, gfinal):
    hat, spread = normalise(inner)
    final = (hat * gain).astype(BF16)
    product = dot_nn(final_t, final)
    grad_product = (grad * gate).astype(BF16)
    grad_gate = (grad * product * gate * (1.0 - gate)).astype(BF16)
    gfinal[...] += dot_nt(final, grad_product)
    grad_final = dot_nn(final_w, grad_product)
    return normalise_back(grad_final * gain, hat, spread), grad_gate


def turn_kernel(
    part, info, gate2, cot, own, ypart, xpart, ycpart, xcpart, near,
    gain2, final2_t, final2_w, *rest,
):
    gate_out, same0, same1, other0, other1, to_core, gfinal, stage, out_st, perm = rest[-10:]
    core = info[2]

    @first_step
    def _():
        perm[...] = reorder()
        start_sum(gfinal, rest[:-10])
        for owner, mine, xp, yp in ((core, own, xpart, ypart), (1 - core, near, xcpart, ycpart)):
            for at in CHUNKS:
                channel = owner * (2 * GROUP) + at
                fill_sum(perm[...], stage, channel, (mine, 0, at, BOTH), (xp, 0, at, BOTH))
                fill_sum(perm[...], stage, channel + GROUP, (mine, 1, at, BOTH), (yp, 0, at, BOTH))

    def work(here, rows):
        grad_inner, grad_gate = leave_rows_back(
            get_rows(stage, rows), stacked(gate2, here).astype(F32), turned(cot, here), gain2[...],
            final2_t[...], final2_w[...], gfinal,
        )
        spread_out(gate_out, here, grad_gate)
        put_rows(out_st, rows, grad_inner)

    each_rows(work)

    @last_step
    def _():
        for owner, outs in ((core, (same0, same1)), (1 - core, (other0, other1))):
            for group, out in enumerate(outs):
                for at in CHUNKS:
                    channel = owner * (2 * GROUP) + group * GROUP + at
                    value = dot_nn(perm[...], get_chunk(out_st, (0, 1), channel)).astype(BF16)
                    give_chunk(out, 0, at, BOTH, value)
                    if out is other0 or out is other1:
                        give_chunk(to_core, group, at, BOTH, value)


def entry_rows_back(normed, hat, spread, norm, grads, grad_gate, mask, proj_t, proj_w, gproj):
    hidden = norm.shape[0]
    mixture = dot_nn(proj_t[: 4 * hidden, :], normed)
    flows, gates = [], []
    for block, grad in enumerate(grads):
        gate = opened(mixture[(2 + block) * hidden : (3 + block) * hidden])
        flow = grad * (gate * mask)
        flows.append(flow.astype(BF16))
        value = mixture[block * hidden : (block + 1) * hidden]
        gates.append((flow * value * (1.0 - gate)).astype(BF16))
    grad_mixture = jnp.concatenate(flows + gates + [grad_gate], axis=0)
    gproj[...] += dot_nt(grad_mixture, normed)
    grad_normed = dot_nn(proj_w, grad_mixture)
    return normalise_back(grad_normed * norm, hat, spread)


def inward_kernel(
    part, info, middle, gate1, cot, inner_in, gate_in, own, ypart, xpart, ycpart, xcpart, near,
    norm2, proj2_t, proj2_w, gain1, final1_t, final1_w, *rest,
):
    before, rest = rest[:-14], rest[-14:]
    grad_out, gate_out, o_own, o_near, o_y, o_yc, o_x, o_xc, gproj, gfinal, *rest = rest
    left_st, right_st, out_st, perm = rest
    core = info[2]

    @first_step
    def _():
        perm[...] = reorder()
        start_sum(gproj, before[:1])
        start_sum(gfinal, before[1:])
        fill_split(info, perm[...], left_st, own, near, ypart, ycpart, xpart, xcpart)
        beyond = slice(LANES, 3 * LANES)
        for owner, mine, yp, xp in ((core, own, ypart, xpart), (1 - core, near, ycpart, xcpart)):
            for at in CHUNKS:
                channel = owner * (2 * GROUP) + at
                fill_sum(perm[...], right_st, channel, (mine, 0, at, beyond), (yp, 0, at, beyond))
                fill_sum(
                    perm[...], right_st, channel + GROUP, (mine, 1, at, beyond), (xp, 0, at, beyond)
                )

    def work(here, rows):
        hat, spread = normalise(stacked(middle, here).astype(F32))
        norm = norm2[...]
        grad_flat = entry_rows_back(
            (hat * norm).astype(BF16), hat, spread, norm,
            (get_rows(left_st, rows), get_rows(right_st, rows)), stacked(gate_in, here),
            mask_rows(info, part, rows), proj2_t, proj2_w[...], gproj,
        )
        grad = turned(cot, here) + grad_flat
        spread_out(grad_out, here, grad)
        grad_inner, grad_gate = leave_rows_back(
            stacked(inner_in, here).astype(F32), stacked(gate1, here).astype(F32), grad, gain1[...],
            final1_t[...], final1_w[...], gfinal,
        )
        spread_out(gate_out, here, grad_gate)
        put_rows(out_st, rows, grad_inner)

    each_rows(work)

    @last_step
    def _():
        for owner, main, yo, xo in ((core, o_own, o_y, o_x), (1 - core, o_near, o_yc, o_xc)):
            for at in CHUNKS:
                kept = split_out(info, perm[...], out_st, owner, at)
                give_chunk(main, 0, at, LOW, kept[0])
                give_chunk(yo, 0, at, LOW, kept[1])
                give_chunk(main, 1, at, LOW, kept[2])
                give_chunk(xo, 0, at, LOW, kept[3])


def exit_kernel(
    part, info, pair, grad_in, gate_in, own, ypart, xpart, ycpart, xcpart, near,
    norm1, proj1_t, proj1_w, *rest,
):
    out, gproj, left_st, right_st, perm = rest[-5:]
    core = info[2]

    @first_step
    def _():
        perm[...] = reorder()
        start_sum(gproj, rest[:-5])
        beyond = slice(2 * LANES, 4 * LANES)
        for owner, mine, yp, xp in ((core, own, ypart, xpart), (1 - core, near, ycpart, xcpart)):
            for group, lefts, rights in ((0, yp, xp), (1, xp, yp)):
                for at in CHUNKS:
                    channel = owner * (2 * GROUP) + group * GROUP + at
                    fill_sum(
                        perm[...], left_st, channel, (mine, group, at, BOTH), (lefts, group, at, BOTH)
                    )
                    fill_sum(
                        perm[...],
                        right_st,
                        channel,
                        (mine, group, at, beyond),
                        (rights, group, at, BOTH),
                    )

    def work(here, rows):
        hat, spread = normalise(turned(pair, here))
        norm = norm1[...]
        grad_flat = entry_rows_back(
            (hat * norm).astype(BF16), hat, spread, norm,
            (get_rows(left_st, rows), get_rows(right_st, rows)), stacked(gate_in, here),
            mask_rows(info, part, rows), proj1_t, proj1_w[...], gproj,
        )
        total = stacked(grad_in, here) + grad_flat
        width = 2 * LANES
        for n, row in enumerate(here):
            out[row] = total[:, n * width : (n + 1) * width].T

    each_rows(work)


CHANNELS = 8
PARTS = 2


def paired(refs):
    return [refs[n : n + PARTS] for n in range(0, len(refs), PARTS)]


def place(one, two, part):
    return pl.multiple_of((one * 2 + two) * (PARTS * BLOCK) + part * BLOCK, BLOCK)


def places(info, group):
    at, core = info[group], info[2]
    return [
        place(at if n < 2 else 1 - at, core if n % 2 == 0 else 1 - core, part)
        for n in range(4)
        for part in range(PARTS)
    ]


def take(ref, group, h):
    return ref[group, h] if len(ref.shape) == 4 else ref[h]


def joined(quads, group, h):
    return jnp.concatenate([take(ref, group, h) for refs in quads for ref in refs], axis=0)


def gather(stage, slot, wheres, quads, group, h):
    for where, ref in zip(wheres, [ref for refs in quads for ref in refs]):
        stage[slot, pl.ds(where, BLOCK), :] = take(ref, group, h)
    return stage[slot]


def give(refs, group, h, lanes, value):
    if len(refs.shape) == 4:
        refs[group, h, :, lanes] = value
    else:
        refs[h, :, lanes] = value


def scatter(quads, group, h, lanes, value):
    for n, ref in enumerate([ref for refs in quads for ref in refs]):
        give(ref, group, h, lanes, value[n * BLOCK : (n + 1) * BLOCK])


def scatter_from(stage, slot, wheres, quads, group, h, lanes):
    for where, ref in zip(wheres, [ref for refs in quads for ref in refs]):
        give(ref, group, h, lanes, stage[slot, pl.ds(where, BLOCK), :])


def outgoing_kernel(info, *refs):
    *refs, stage = refs
    *refs, o_own, o_near, o_y, o_yc, o_x, o_xc = refs
    a_own, b_own, a_y, b_x, a_yc, b_xc, near = paired(refs)
    a_near, b_near = [ref.at[:2] for ref in near], [ref.at[2:] for ref in near]
    along_a, along_b = (a_own, a_near, a_y, a_yc), (b_own, b_near, b_x, b_xc)
    for h in range(CHANNELS):
        for group in range(2):
            lefts, rights = (along_a, along_b) if group == 0 else (along_b, along_a)
            far = (o_y, o_yc) if group == 0 else (o_x, o_xc)
            right = gather(stage, 2 * h + group, places(info, group), rights, group, h)
            inner = dot_nt(joined(lefts, group, h), right).astype(BF16)
            for n, out in enumerate((o_own, o_near) + far):
                rows = PARTS * BLOCK
                give(out, group, h, slice(0, LANES), inner[n * rows : (n + 1) * rows])


def halves(quads, group, h):
    both = joined(quads, group, h)
    return both[:, :LANES], both[:, LANES:]


def incoming_kernel(info, *refs):
    *refs, stage = refs
    own, ypart, xpart, ycpart, xcpart, near, o_own, o_near, o_x, o_xc, o_y, o_yc = paired(refs)
    for h in range(CHANNELS):
        for group in range(2):
            far = (ypart, ycpart) if group == 0 else (xpart, xcpart)
            outs = (o_own, o_near) + ((o_x, o_xc) if group == 0 else (o_y, o_yc))
            slot = 2 * h + group
            left, right = halves((own, near) + far, group, h)
            stage[slot] = dot_tn(left, right).astype(BF16)
            scatter_from(stage, slot, places(info, group), outs, group, h, slice(0, 2 * LANES))


def incoming_back_kernel(info, *refs):
    *refs, stage = refs
    own, ypart, xpart, ycpart, xcpart, near, *more = paired(refs)
    same0, same1, g_y, g_x, g_yc, g_xc, g_near, *more = more
    o_own, o_near, o_y, o_yc, o_x, o_xc = more
    for h in range(CHANNELS):
        for group in range(2):
            far = (ypart, ycpart) if group == 0 else (xpart, xcpart)
            grads = (same0, g_near, g_x, g_xc) if group == 0 else (same1, g_near, g_y, g_yc)
            outs = (o_own, o_near) + ((o_y, o_yc) if group == 0 else (o_x, o_xc))
            grad = gather(stage, 2 * h + group, places(info, group), grads, group, h)
            left, right = halves((own, near) + far, group, h)
            scatter(outs, group, h, slice(0, LANES), dot_nt(right, grad).astype(BF16))
            scatter(outs, group, h, slice(LANES, 3 * LANES), dot_nn(left, grad).astype(BF16))


def outgoing_back_kernel(info, *refs):
    *refs, stage, back = refs
    a_own, b_own, a_y, b_x, a_yc, b_xc, near, *more = paired(refs)
    a_near, b_near = [ref.at[:2] for ref in near], [ref.at[2:] for ref in near]
    g_own, g_y, g_x, g_yc, g_xc, g_near, o_own, o_near, o_y, o_yc, o_x, o_xc = more
    along_a, along_b = (a_own, a_near, a_y, a_yc), (b_own, b_near, b_x, b_xc)
    first, second = slice(0, 2 * LANES), slice(2 * LANES, 4 * LANES)
    for h in range(CHANNELS):
        for group in range(2):
            lefts, rights = (along_a, along_b) if group == 0 else (along_b, along_a)
            far = (g_y, g_yc) if group == 0 else (g_x, g_xc)
            left_far, right_far = ((o_y, o_yc), (o_x, o_xc)) if group == 0 else ((o_x, o_xc), (o_y, o_yc))
            slot = 2 * h + group
            wheres = places(info, group)
            right = gather(stage, slot, wheres, rights, group, h)
            grad = joined((g_own, g_near) + far, group, h)
            grad_left = dot_nn(grad, right).astype(BF16)
            back[slot] = dot_tn(grad, joined(lefts, group, h)).astype(BF16)
            core_rows = 2 * PARTS * BLOCK
            scatter((o_own, o_near), group, h, first, grad_left[:core_rows])
            scatter(left_far, group, h, first, grad_left[core_rows:])
            scatter_from(back, slot, wheres[: 2 * PARTS], (o_own, o_near), group, h, second)
            scatter_from(back, slot, wheres[2 * PARTS :], right_far, group, h, first)


def whole(shape):
    return pl.BlockSpec(shape, lambda step, info: (0,) * len(shape))


def rows_of(part):
    def make(shape):
        first = part * STEPS
        return pl.BlockSpec(
            (SOME,) + shape[1:], lambda step, info: (first + step,) + (0,) * (len(shape) - 1)
        )

    return make


def rows_block(part):
    def make(shape):
        return pl.BlockSpec(
            shape[:-2] + (BLOCK, shape[-1]),
            lambda step, info: (0,) * (len(shape) - 2) + (part, 0),
        )

    return make


def anywhere(shape):
    return pl.BlockSpec(memory_space=pl.ANY)


def channel_rows(shape):
    if len(shape) == 4:
        return pl.BlockSpec((shape[0], CHANNELS) + shape[2:], lambda step, info: (0, step, 0, 0))
    return pl.BlockSpec((CHANNELS,) + shape[1:], lambda step, info: (step, 0, 0))


def call(kernel, info, steps, ins, outs, scratch, aliases={}):
    return pl.pallas_call(
        kernel,
        grid_spec=pltpu.PrefetchScalarGridSpec(
            num_scalar_prefetch=1,
            grid=(steps,),
            in_specs=[make(array.shape) for array, make in ins],
            out_specs=[make(shape) for shape, unused, make in outs],
            scratch_shapes=scratch,
        ),
        out_shape=[jax.ShapeDtypeStruct(shape, dtype) for shape, dtype, unused in outs],
        compiler_params=pltpu.CompilerParams(vmem_limit_bytes=VMEM),
        input_output_aliases=aliases,
    )(info, *[array for array, unused in ins])


class Links:
    def __init__(self):
        self.last = {}

    def __call__(self, arrays, offset):
        count = lax.axis_size("axial")
        pairs = [(n, n ^ offset) for n in range(count)]
        results = []
        for array in arrays:
            if offset in self.last and offset != CORE:
                array, unused = lax.optimization_barrier((array, self.last[offset]))
            self.last[offset] = lax.ppermute(array, "axial", pairs)
            results.append(self.last[offset])
        return results


CORE, X, Y = 1, 2, 4


def add_up(share):
    count = lax.axis_size("axial")
    rows, width = share.shape
    shares = share.astype(BF16).reshape(count, rows // count, width)
    parts = lax.all_to_all(shares, "axial", split_axis=0, concat_axis=0, tiled=True)
    mine = parts.astype(F32).sum(axis=0).astype(BF16)
    depth = lax.axis_size("dp")
    terms = [mine] + [
        lax.ppermute(mine, "dp", [(n, n ^ offset) for n in range(depth)])
        for offset in range(1, depth)
    ]
    terms = [term.astype(F32) for term in terms]
    while len(terms) > 1:
        terms = [terms[n] + terms[n + 1] for n in range(0, len(terms), 2)]
    copies = jnp.broadcast_to(terms[0].astype(BF16)[None], shares.shape)
    return lax.all_to_all(copies, "axial", split_axis=0, concat_axis=0, tiled=True).reshape(
        rows, width
    )


def gain_grad(weight_grad, weight, gain_row):
    return jnp.sum((weight.astype(F32) * weight_grad).T, axis=0, keepdims=True) / gain_row


def finish_kernel(
    scale, info, sums, proj1, final1, proj2, final2, norm1, gain1, norm2, gain2,
    o_norm1, o_proj1, o_gain1, o_final1, o_norm2, o_proj2, o_gain2, o_final2,
):
    width, channels = proj1.shape[1], final1.shape[1]
    takes = (
        (0, True, proj1, norm1, o_proj1, o_norm1),
        (width, True, proj2, norm2, o_proj2, o_norm2),
        (2 * width, False, final2, gain2, o_final2, o_gain2),
        (2 * width + channels, False, final1, gain1, o_final1, o_gain1),
    )
    for start, flipped, weight, gain, out, gain_out in takes:
        total = sums[start : start + weight.shape[1], :].astype(F32) * scale
        total = total.T if flipped else total
        out[...] = total
        gain_out[...] = gain_grad(total, weight[...].astype(BF16), gain[...])


def fast_body(
    pair,
    cotangent,
    lengths,
    outgo_norm,
    outgo_proj,
    outgo_gain,
    outgo_final,
    incom_norm,
    incom_proj,
    incom_gain,
    incom_final,
):
    rows, tokens, channels = pair.shape[1:]
    hidden = outgo_gain.shape[0]
    index = lax.axis_index("axial")
    info = jnp.stack(
        [(index // 2) % 2, index // 4, index % 2, index * rows, lengths[0]]
    ).astype(jnp.int32)
    hop = Links()
    pair = pair[0]
    cot = cotangent[0]
    parts = range(PARTS)
    turns = GROUP // CHANNELS
    stage = pltpu.VMEM((2, BLOCK, hidden, LANES), F32)
    out_stage = pltpu.VMEM((2, BLOCK, hidden, LANES), BF16)
    perm = pltpu.VMEM((BLOCK * BLOCK, BLOCK * BLOCK), BF16)
    streamed = rows_of(0)
    square = pltpu.VMEM((2 * CHANNELS, 4 * rows, tokens), BF16)

    def two(width, height=BLOCK, make=whole, groups=2):
        return ((groups, GROUP, height, width), BF16, make)

    def one(width, height=BLOCK, make=whole):
        return ((GROUP, height, width), BF16, make)

    turned_block = ((BLOCK, channels, tokens), BF16, streamed)

    def cells(kernel, ins, outs, scratch, more=lambda part: []):
        results = []
        for part in parts:
            carried = ins(part, results)
            results.append(
                call(functools.partial(kernel, part), info, STEPS, carried, outs + more(part), scratch)
            )
        shared = results[-1][len(outs) :]
        return [list(each) for each in zip(*results)] + list(shared)

    def wholes(arrays):
        return [(array, whole) for array in arrays]

    def triangle(kernel, operands, outs, scratch, split=PARTS):
        ins = [(array, channel_rows) for arrays in operands for array in arrays]
        each = [out for out in outs for unused in range(split)]
        results = call(kernel, info, turns, ins, each, scratch)
        return [list(results[n : n + split]) for n in range(0, len(results), split)]

    raw = (outgo_gain[None], outgo_final, incom_norm[None], incom_proj, incom_gain[None], incom_final)
    gain_wide = ((channels, PAIRED * tokens), F32, whole)
    proj_turned = ((5 * hidden, channels), BF16, whole)
    proj_plain = ((channels, 5 * hidden), BF16, whole)
    final_plain = ((hidden, channels), BF16, whole)
    (
        a_same, a_other, b_same, b_other, to_core, gate_one,
        norm1, gain1, norm2, gain2, proj1_t, proj2_t, final1_t, final2_t,
        proj1, final1, proj2, final2,
    ) = cells(
        entry_kernel,
        lambda part, unused: [(pair, rows_of(part)), (outgo_norm[None], whole), (outgo_proj, whole)]
        + (wholes(raw) if part else []),
        [two(tokens)] * 4 + [two(tokens, groups=4), turned_block],
        [
            out_stage,
            out_stage,
            pltpu.VMEM((channels, PAIRED * tokens), F32),
            pltpu.VMEM((5 * hidden, channels), BF16),
            perm,
        ],
        lambda part: (
            [gain_wide] * 4
            + [proj_turned] * 2
            + [final_plain] * 2
            + [proj_plain, final_plain] * 2
            if part
            else []
        ),
    )
    a_y, b_x = hop(a_same, Y), hop(b_same, X)
    a_yc, b_xc = hop(a_other, Y | CORE), hop(b_other, X | CORE)
    held_one = [a_same, b_same, a_y, b_x, a_yc, b_xc, hop(to_core, CORE)]
    own, near, to_y, to_yc, to_x, to_xc = triangle(
        outgoing_kernel,
        held_one,
        [two(LANES, rows, channel_rows)] * 2 + [one(LANES, rows, channel_rows)] * 4,
        [square],
        split=1,
    )
    back_one = [
        own,
        hop(to_y, Y),
        hop(to_x, X),
        hop(to_yc, Y | CORE),
        hop(to_xc, X | CORE),
        hop(near, CORE),
    ]

    middle, inner_one, gate_two, own, near, to_y, to_yc, to_x, to_xc = cells(
        middle_kernel,
        lambda part, unused: [(pair, rows_of(part))]
        + [(array, rows_block(part)) for array, in back_one]
        + [(gate_one[part], streamed)]
        + wholes((gain1, final1_t, norm2, proj2_t)),
        [turned_block] * 3 + [two(3 * LANES)] * 2 + [one(3 * LANES)] * 4,
        [stage, out_stage, out_stage, perm],
    )
    held_two = [
        own,
        hop(to_y, Y),
        hop(to_x, X),
        hop(to_yc, Y | CORE),
        hop(to_xc, X | CORE),
        hop(near, CORE),
    ]
    own, near, to_x, to_xc, to_y, to_yc = triangle(
        incoming_kernel,
        held_two,
        [two(tokens, make=channel_rows)] * 2 + [one(tokens, make=channel_rows)] * 4,
        [square],
    )
    back_two = [
        own,
        hop(to_y, Y),
        hop(to_x, X),
        hop(to_yc, Y | CORE),
        hop(to_xc, X | CORE),
        hop(near, CORE),
    ]

    gate_grad_two, same0, same1, other0, other1, to_core, grad_final_two = cells(
        turn_kernel,
        lambda part, done: [(gate_two[part], streamed), (cot, rows_of(part))]
        + wholes(arrays[part] for arrays in back_two)
        + wholes((gain2, final2_t, final2))
        + wholes(done[-1][-1:] if done else ()),
        [turned_block]
        + [one(tokens)] * 4
        + [two(tokens), ((hidden, channels), F32, whole)],
        [stage, out_stage, perm],
    )
    grads_two = [
        same0,
        same1,
        hop(same1, Y),
        hop(same0, X),
        hop(other1, Y | CORE),
        hop(other0, X | CORE),
        hop(to_core, CORE),
    ]
    own, near, to_y, to_yc, to_x, to_xc = triangle(
        incoming_back_kernel,
        held_two + grads_two,
        [two(3 * LANES, make=channel_rows)] * 2 + [one(3 * LANES, make=channel_rows)] * 4,
        [square],
    )
    rows_two = [
        own,
        hop(to_y, Y),
        hop(to_x, X),
        hop(to_yc, Y | CORE),
        hop(to_xc, X | CORE),
        hop(near, CORE),
    ]

    (
        grad_middle, gate_grad_one, own, near, to_y, to_yc, to_x, to_xc,
        grad_proj_two, grad_final_one,
    ) = cells(
        inward_kernel,
        lambda part, done: [
            (middle[part], streamed),
            (gate_one[part], streamed),
            (cot, rows_of(part)),
            (inner_one[part], streamed),
            (gate_grad_two[part], streamed),
        ]
        + wholes(arrays[part] for arrays in rows_two)
        + wholes((norm2, proj2_t, proj2, gain1, final1_t, final1))
        + wholes(done[-1][-2:] if done else ()),
        [((BLOCK, channels, tokens), F32, streamed), turned_block]
        + [two(LANES)] * 2
        + [one(LANES)] * 4
        + [((5 * hidden, channels), F32, whole), ((hidden, channels), F32, whole)],
        [stage, stage, out_stage, perm],
    )
    grads_one = [
        own,
        hop(to_y, Y),
        hop(to_x, X),
        hop(to_yc, Y | CORE),
        hop(to_xc, X | CORE),
        hop(near, CORE),
    ]
    own, near, to_y, to_yc, to_x, to_xc = triangle(
        outgoing_back_kernel,
        held_one + grads_one,
        [two(2 * tokens, make=channel_rows)] * 2 + [two(tokens, make=channel_rows)] * 4,
        [square, square],
    )
    rows_one = [
        own,
        hop(to_y, Y),
        hop(to_x, X),
        hop(to_yc, Y | CORE),
        hop(to_xc, X | CORE),
        hop(near, CORE),
    ]
    exit_ins = 9 + 3 + 1 + 1
    result = None
    for part in parts:
        result = call(
            functools.partial(exit_kernel, part),
            info,
            STEPS,
            [(pair, rows_of(part)), (grad_middle[part], streamed), (gate_grad_one[part], streamed)]
            + wholes(arrays[part] for arrays in rows_one)
            + wholes((norm1, proj1_t, proj1))
            + ([(result[1], whole), (result[0], anywhere)] if part else []),
            [
                ((rows, tokens, channels), F32, rows_of(part)),
                ((5 * hidden, channels), F32, whole),
            ],
            [stage, stage, perm],
            {exit_ins: 0} if part else {},
        )
    grad_begin, grad_proj_one = result
    sums = add_up(
        jnp.concatenate(
            [grad_proj_one, grad_proj_two[-1], grad_final_two[-1], grad_final_one[-1]], axis=0
        )
    )
    scale = 1.0 / math.sqrt(lax.axis_size("dp") * tokens * tokens)
    weights = (outgo_proj, outgo_final, incom_proj, incom_final)
    gains = (outgo_norm, outgo_gain, incom_norm, incom_gain)
    order = (outgo_norm[None], outgo_proj, outgo_gain[None], outgo_final)
    order += (incom_norm[None], incom_proj, incom_gain[None], incom_final)
    totals = call(
        functools.partial(finish_kernel, scale),
        info,
        1,
        wholes((sums,) + weights + tuple(gain[None] for gain in gains)),
        [(array.shape, F32, whole) for array in order],
        [],
    )
    return (grad_begin[None],) + tuple(
        total.reshape(-1) if total.shape[0] == 1 else total for total in totals
    )


def solution(mesh):
    def body(pair, *rest):
        rows, tokens, channels = pair.shape[1:]
        hidden = rest[3].shape[0]
        plane = mesh.shape["axial"] == 8 and rows == 32 and tokens == 2 * LANES
        if plane and channels == LANES and hidden == 4 * GROUP:
            return fast_body(pair, *rest)
        return plain_body(pair, *rest)

    return jax.shard_map(
        body,
        mesh=mesh,
        in_specs=(P("dp", "axial", None, None), P("dp", "axial", None, None), P("dp")) + (P(),) * 8,
        out_specs=(P("dp", "axial", None, None),) + (P(),) * 8,
        check_vma=False,
    )
```

```python
import functools
import math

import jax
import jax.numpy as jnp
from jax import lax
from jax.experimental import pallas as pl
from jax.experimental.pallas import tpu as pltpu
from jax.sharding import PartitionSpec as P

EPSILON = 1e-05


def rounded(inputs):
    return lax.optimization_barrier(inputs.astype(jnp.bfloat16)).astype(jnp.float32)


def layer_norm(inputs, factor):
    average = jnp.mean(inputs, axis=-1, keepdims=True)
    centered = inputs - average
    spread = jnp.mean(centered * centered, axis=-1, keepdims=True)
    return centered * lax.rsqrt(spread + EPSILON) * factor


def gating(mixture, pair_mask, hidden):
    left_part = (
        mixture[:, :hidden] * jax.nn.sigmoid(mixture[:, 2 * hidden : 3 * hidden]) * pair_mask
    )
    right_part = (
        mixture[:, hidden : 2 * hidden]
        * jax.nn.sigmoid(mixture[:, 3 * hidden : 4 * hidden])
        * pair_mask
    )
    gate_part = jax.nn.sigmoid(mixture[:, 4 * hidden :])
    return (left_part, right_part, gate_part)


def entry(flat_pair, norm_gain, projection, pair_mask, hidden):
    normed = layer_norm(flat_pair, norm_gain).astype(jnp.bfloat16)
    mixture = jnp.dot(normed, projection.astype(jnp.bfloat16), preferred_element_type=jnp.float32)
    left_part, right_part, gate_part = gating(mixture, pair_mask, hidden)
    return (normed, mixture, left_part, right_part, gate_part)


def entry_back(
    flat_pair,
    norm_gain,
    projection,
    pair_mask,
    hidden,
    normed,
    mixture,
    grad_left,
    grad_right,
    grad_gate,
):
    unused, pull_gate = jax.vjp(lambda inner_mix: gating(inner_mix, pair_mask, hidden), mixture)
    grad_mixture = pull_gate((grad_left, grad_right, grad_gate))[0].astype(jnp.bfloat16)
    grad_projection = jnp.dot(normed.T, grad_mixture, preferred_element_type=jnp.float32)
    grad_normed = jnp.dot(
        grad_mixture, projection.astype(jnp.bfloat16).T, preferred_element_type=jnp.float32
    )
    unused, pull_norm = jax.vjp(layer_norm, flat_pair, norm_gain)
    grad_flat, grad_gain = pull_norm(grad_normed)
    return (grad_flat, grad_gain, grad_projection)


def leave(inner_sum, gate_part, out_gain, final_weight):
    final_normed = layer_norm(inner_sum, out_gain).astype(jnp.bfloat16)
    product = jnp.dot(
        final_normed, final_weight.astype(jnp.bfloat16), preferred_element_type=jnp.float32
    )
    return (final_normed, product, product * gate_part)


def leave_back(inner_sum, gate_part, out_gain, final_weight, final_normed, product, grad_update):
    grad_product = (grad_update * gate_part).astype(jnp.bfloat16)
    grad_gate = grad_update * product
    grad_final = jnp.dot(final_normed.T, grad_product, preferred_element_type=jnp.float32)
    grad_normed = jnp.dot(
        grad_product, final_weight.astype(jnp.bfloat16).T, preferred_element_type=jnp.float32
    )
    unused, pull_norm = jax.vjp(layer_norm, inner_sum, out_gain)
    grad_inner, grad_gain = pull_norm(grad_normed)
    return (grad_inner, grad_gate, grad_gain, grad_final)


def channel_major(field, row_count, tokens):
    hidden = field.shape[1]
    return jnp.transpose(field.reshape(row_count, tokens, hidden), (2, 0, 1))


def row_major(field):
    hidden = field.shape[0]
    return jnp.transpose(field, (1, 2, 0)).reshape(-1, hidden)


def plain_body(
    pair,
    cotangent,
    lengths,
    outgo_norm,
    outgo_proj,
    outgo_gain,
    outgo_final,
    incom_norm,
    incom_proj,
    incom_gain,
    incom_final,
):
    row_count = pair.shape[1]
    tokens = pair.shape[2]
    channels = pair.shape[3]
    hidden = outgo_gain.shape[0]
    length = lengths[0]
    first_row = lax.axis_index("axial") * row_count
    row_alive = (first_row + jnp.arange(row_count, dtype=jnp.int32) < length).astype(jnp.float32)
    column_alive = (jnp.arange(tokens, dtype=jnp.int32) < length).astype(jnp.float32)
    pair_mask = (row_alive[:, None] * column_alive[None, :]).reshape(-1, 1)
    flat_start = pair[0].reshape(-1, channels).astype(jnp.float32)
    normed_one, mixture_one, left_one, right_one, gate_one = entry(
        flat_start, outgo_norm, outgo_proj, pair_mask, hidden
    )
    left_first = channel_major(left_one.astype(jnp.bfloat16), row_count, tokens)
    right_first = channel_major(right_one.astype(jnp.bfloat16), row_count, tokens)
    left_owned, right_owned = (
        lax.all_to_all(left_first, "axial", split_axis=0, concat_axis=1, tiled=True),
        lax.all_to_all(right_first, "axial", split_axis=0, concat_axis=1, tiled=True),
    )
    inner_cols = jnp.einsum(
        "hik,hjk->hij", left_owned, right_owned, preferred_element_type=jnp.float32
    )
    inner_one = row_major(
        lax.all_to_all(
            inner_cols.astype(jnp.bfloat16), "axial", split_axis=1, concat_axis=0, tiled=True
        ).astype(inner_cols.dtype)
    )
    final_one, product_one, update_one = leave(inner_one, gate_one, outgo_gain, outgo_final)
    flat_middle = rounded(flat_start + update_one)
    normed_two, mixture_two, left_two, right_two, gate_two = entry(
        flat_middle, incom_norm, incom_proj, pair_mask, hidden
    )
    left_second = channel_major(left_two.astype(jnp.bfloat16), row_count, tokens)
    right_second = channel_major(right_two.astype(jnp.bfloat16), row_count, tokens)
    left_held, right_held = (
        lax.all_to_all(left_second, "axial", split_axis=0, concat_axis=1, tiled=True),
        lax.all_to_all(right_second, "axial", split_axis=0, concat_axis=1, tiled=True),
    )
    inner_held = jnp.einsum(
        "hki,hkj->hij", left_held, right_held, preferred_element_type=jnp.float32
    )
    inner_two = row_major(
        lax.all_to_all(
            inner_held.astype(jnp.bfloat16), "axial", split_axis=1, concat_axis=0, tiled=True
        ).astype(inner_held.dtype)
    )
    final_two, product_two, update_two = leave(inner_two, gate_two, incom_gain, incom_final)
    grad_end = cotangent[0].reshape(-1, channels).astype(jnp.float32)
    grad_inner_two, grad_gate_two, grad_gain_two, grad_final_two = leave_back(
        inner_two, gate_two, incom_gain, incom_final, final_two, product_two, grad_end
    )
    grad_cells_two = channel_major(grad_inner_two.astype(jnp.bfloat16), row_count, tokens)
    grad_held_two = lax.all_to_all(grad_cells_two, "axial", split_axis=0, concat_axis=1, tiled=True)
    left_back, right_back = (
        lax.all_to_all(left_second, "axial", split_axis=0, concat_axis=1, tiled=True),
        lax.all_to_all(right_second, "axial", split_axis=0, concat_axis=1, tiled=True),
    )
    grad_left_held = jnp.einsum(
        "hij,hkj->hki", grad_held_two, right_back, preferred_element_type=jnp.float32
    )
    grad_right_held = jnp.einsum(
        "hki,hij->hkj", left_back, grad_held_two, preferred_element_type=jnp.float32
    )
    grad_left_rows, grad_right_rows = (
        lax.all_to_all(
            grad_left_held.astype(jnp.bfloat16), "axial", split_axis=1, concat_axis=0, tiled=True
        ).astype(grad_left_held.dtype),
        lax.all_to_all(
            grad_right_held.astype(jnp.bfloat16), "axial", split_axis=1, concat_axis=0, tiled=True
        ).astype(grad_right_held.dtype),
    )
    grad_left_two = row_major(grad_left_rows)
    grad_right_two = row_major(grad_right_rows)
    grad_flat_two, grad_norm_two, grad_proj_two = entry_back(
        flat_middle,
        incom_norm,
        incom_proj,
        pair_mask,
        hidden,
        normed_two,
        mixture_two,
        grad_left_two,
        grad_right_two,
        grad_gate_two,
    )
    second_sums = lax.psum(
        (grad_norm_two, grad_proj_two, grad_gain_two, grad_final_two), ("dp", "axial")
    )
    grad_middle = grad_end + grad_flat_two
    grad_inner_one, grad_gate_one, grad_gain_one, grad_final_one = leave_back(
        inner_one, gate_one, outgo_gain, outgo_final, final_one, product_one, grad_middle
    )
    grad_cells_one = channel_major(grad_inner_one.astype(jnp.bfloat16), row_count, tokens)
    grad_owned_one = lax.all_to_all(
        grad_cells_one, "axial", split_axis=0, concat_axis=1, tiled=True
    )
    left_again, right_again = (
        lax.all_to_all(left_first, "axial", split_axis=0, concat_axis=1, tiled=True),
        lax.all_to_all(right_first, "axial", split_axis=0, concat_axis=1, tiled=True),
    )
    grad_left_owned = jnp.einsum(
        "hij,hjk->hik", grad_owned_one, right_again, preferred_element_type=jnp.float32
    )
    grad_right_owned = jnp.einsum(
        "hij,hik->hjk", grad_owned_one, left_again, preferred_element_type=jnp.float32
    )
    grad_left_back, grad_right_back = (
        lax.all_to_all(
            grad_left_owned.astype(jnp.bfloat16), "axial", split_axis=1, concat_axis=0, tiled=True
        ).astype(grad_left_owned.dtype),
        lax.all_to_all(
            grad_right_owned.astype(jnp.bfloat16), "axial", split_axis=1, concat_axis=0, tiled=True
        ).astype(grad_right_owned.dtype),
    )
    grad_left_one = row_major(grad_left_back)
    grad_right_one = row_major(grad_right_back)
    grad_flat_one, grad_norm_one, grad_proj_one = entry_back(
        flat_start,
        outgo_norm,
        outgo_proj,
        pair_mask,
        hidden,
        normed_one,
        mixture_one,
        grad_left_one,
        grad_right_one,
        grad_gate_one,
    )
    grad_begin = grad_middle + grad_flat_one
    first_sums = lax.psum(
        (grad_norm_one, grad_proj_one, grad_gain_one, grad_final_one), ("dp", "axial")
    )
    totals = tuple(first_sums) + tuple(second_sums)
    scale = 1.0 / math.sqrt(lax.axis_size("dp") * tokens * tokens)
    return (
        grad_begin.reshape(1, row_count, tokens, channels),
        totals[0] * scale,
        totals[1] * scale,
        totals[2] * scale,
        totals[3] * scale,
        totals[4] * scale,
        totals[5] * scale,
        totals[6] * scale,
        totals[7] * scale,
    )


BF16 = jnp.bfloat16
F32 = jnp.float32
BLOCK = 16
PAIRED = 2
STEPS = 2
SOME = BLOCK // STEPS
LANES = 128
GROUP = 32
VMEM = 56 * 1024 * 1024


def dot_nn(a, b):
    return lax.dot_general(a, b, (((1,), (0,)), ((), ())), preferred_element_type=F32)


def dot_nt(a, b):
    return lax.dot_general(a, b, (((1,), (1,)), ((), ())), preferred_element_type=F32)


def dot_tn(a, b):
    return lax.dot_general(a, b, (((0,), (0,)), ((), ())), preferred_element_type=F32)


def normalise(v):
    centered = v - jnp.mean(v, axis=0, keepdims=True)
    spread = lax.rsqrt(jnp.mean(centered * centered, axis=0, keepdims=True) + EPSILON)
    return centered * spread, spread


def normalise_back(grad, hat, spread):
    first = jnp.mean(grad, axis=0, keepdims=True)
    second = jnp.mean(grad * hat, axis=0, keepdims=True)
    return spread * (grad - first - hat * second)


def reorder():
    size = BLOCK * BLOCK
    one = lax.broadcasted_iota(jnp.int32, (size, size), 0)
    two = lax.broadcasted_iota(jnp.int32, (size, size), 1)
    return jnp.where((one % BLOCK) * BLOCK + one // BLOCK == two, 1.0, 0.0).astype(BF16)


def chunk(ref, group, at, lanes):
    if len(ref.shape) == 4:
        block = ref[group, at : at + BLOCK, :, lanes]
    else:
        block = ref[at : at + BLOCK, :, lanes]
    return block.reshape(BLOCK * BLOCK, block.shape[2])


def put_chunk(stage, half, channel, value):
    channel = pl.multiple_of(channel, BLOCK)
    for row in range(BLOCK):
        stage[half, row, pl.ds(channel, BLOCK), :] = value[row * BLOCK : (row + 1) * BLOCK]


def get_chunk(stage, halves, channel):
    channel = pl.multiple_of(channel, BLOCK)
    return jnp.concatenate(
        [
            jnp.concatenate(
                [stage[half, row, pl.ds(channel, BLOCK), :] for row in range(BLOCK)], axis=0
            )
            for half in halves
        ],
        axis=1,
    )


def give_chunk(ref, group, at, lanes, value):
    block = value.astype(BF16).reshape(BLOCK, BLOCK, value.shape[1])
    if len(ref.shape) == 4:
        ref[group, at : at + BLOCK, :, lanes] = block
    else:
        ref[at : at + BLOCK, :, lanes] = block


def put_rows(stage, rows, value):
    for n, row in enumerate(rows):
        for half in range(2):
            start = (2 * n + half) * LANES
            stage[half, row] = value[:, start : start + LANES].astype(stage.dtype)


def get_rows(stage, rows):
    return jnp.concatenate([stage[half, row] for row in rows for half in range(2)], axis=1)


def spread_out(ref, rows, value):
    width = 2 * LANES
    for n, row in enumerate(rows):
        ref[row] = value[:, n * width : (n + 1) * width].astype(ref.dtype)


LOW, HIGH, BOTH = slice(0, LANES), slice(LANES, 2 * LANES), slice(0, 2 * LANES)
CHUNKS = range(0, GROUP, BLOCK)


def half_swap(first, second):
    low = lax.broadcasted_iota(jnp.int32, first.shape, first.ndim - 1) < LANES // 2
    axis = first.ndim - 1
    return (
        jnp.where(low, first, pltpu.roll(second, LANES // 2, axis)),
        jnp.where(low, pltpu.roll(first, LANES // 2, axis), second),
    )


def pick(flag, zero, one):
    return jnp.where(flag == 0, zero, one)


def mask_rows(info, part, rows):
    length = info[4]
    column = (lax.broadcasted_iota(jnp.int32, (1, 2 * LANES), 1) < length).astype(F32)
    return jnp.concatenate(
        [column * (info[3] + part * BLOCK + row < length).astype(F32) for row in rows], axis=1
    )


def each_rows(work):
    step = pl.program_id(0)

    @pl.loop(0, SOME // PAIRED)
    def _(turn):
        here = [turn * PAIRED + n for n in range(PAIRED)]
        work(here, [step * SOME + row for row in here])


def first_step(work):
    pl.when(pl.program_id(0) == 0)(work)


def last_step(work):
    pl.when(pl.program_id(0) == STEPS - 1)(work)


def turned(ref, rows):
    return jnp.concatenate([ref[row].astype(F32).T for row in rows], axis=1)


def stacked(ref, rows):
    return jnp.concatenate([ref[row] for row in rows], axis=1)


def gated(mixture, hidden, mask):
    sides, opens, slopes = [], [], []
    for block in range(2):
        gate = opened(mixture[(2 + block) * hidden : (3 + block) * hidden])
        opening = gate * mask
        side = mixture[block * hidden : (block + 1) * hidden] * opening
        sides.append(side)
        opens.append(opening.astype(BF16))
        slopes.append((side * (1.0 - gate)).astype(BF16))
    factors = jnp.concatenate(opens + slopes, axis=0)
    return sides[0], sides[1], opened(mixture[4 * hidden :]), factors


def opened(gate):
    return 0.5 * jnp.tanh(gate) + 0.5


def column(row):
    size = row.shape[1]
    square = jnp.broadcast_to(row, (size, size)).T
    return jnp.concatenate([square] * (2 * PAIRED * LANES // size), axis=1)


def halved_turned(weight):
    values = 2 * weight.shape[0]
    return jnp.concatenate([weight[:, :values].T, weight[:, values:].T * 0.5], axis=0).astype(BF16)


def entry_kernel(part, info, pair, norm_row, proj_w, *rest):
    if part:
        raw, rest = rest[:6], rest[6:]
        gain1, final1, norm2, proj2, gain2, final2 = raw
        prepared, rest = rest[7:18], rest[:7] + rest[18:]
    a_same, a_other, b_same, b_other, to_core, gate_out, factor_out, *rest = rest
    left_st, right_st, norm, proj_t, perm = rest
    hidden = proj_w.shape[1] // 5

    @first_step
    def _():
        norm[...] = column(norm_row[...])
        proj_t[...] = halved_turned(proj_w[...])
        perm[...] = reorder()
        if part:
            for row, out in zip((norm_row, gain1, norm2, gain2), prepared[:4]):
                out[...] = column(row[...])
            prepared[4][...] = halved_turned(proj2[...])
            for weight, out in zip((final1, final2), prepared[5:7]):
                out[...] = weight[...].T.astype(BF16)
            for weight, out in zip((proj_w, final1, proj2, final2), prepared[7:]):
                out[...] = weight[...].astype(BF16)

    def work(here, rows):
        normed = (normalise(turned(pair, here))[0] * norm[...]).astype(BF16)
        mixture = dot_nn(proj_t[...], normed)
        left, right, gate, factors = gated(mixture, hidden, mask_rows(info, part, rows))
        put_rows(left_st, rows, left)
        put_rows(right_st, rows, right)
        spread_out(gate_out, here, gate)
        spread_out(factor_out, here, factors)

    each_rows(work)

    @last_step
    def _():
        core = info[2]
        for owner, a_out, b_out in ((core, a_same, b_same), (1 - core, a_other, b_other)):
            for group in range(2):
                for at in CHUNKS:
                    channel = owner * (2 * GROUP) + group * GROUP + at
                    left = dot_nn(perm[...], get_chunk(left_st, (0, 1), channel)).astype(BF16)
                    right = dot_nn(perm[...], get_chunk(right_st, (0, 1), channel)).astype(BF16)
                    first, second = (left, right) if group == 0 else (right, left)
                    give_chunk(a_out, group, at, BOTH, first)
                    give_chunk(b_out, group, at, BOTH, second)
                    if a_out is a_other:
                        give_chunk(to_core, group, at, BOTH, first)
                        give_chunk(to_core, 2 + group, at, BOTH, second)


def fill_split(info, perm, stage, own, near, ypart, ycpart, xpart, xcpart):
    x, y, core = info[0], info[1], info[2]
    for owner, mine, yp, xp in ((core, own, ypart, xpart), (1 - core, near, ycpart, xcpart)):
        for at in CHUNKS:
            channel = owner * (2 * GROUP) + at
            both = jnp.concatenate([chunk(mine, 0, at, LOW), chunk(yp, 0, at, LOW)], axis=1)
            both = dot_nn(perm, both)
            put_chunk(stage, y, channel, both[:, LOW])
            put_chunk(stage, 1 - y, channel, both[:, HIGH])
            both = jnp.concatenate([chunk(mine, 1, at, LOW), chunk(xp, 0, at, LOW)], axis=1)
            both = dot_nn(perm, both)
            here, there = both[:, LOW], both[:, HIGH]
            first, second = half_swap(pick(x, here, there), pick(x, there, here))
            put_chunk(stage, 0, channel + GROUP, first)
            put_chunk(stage, 1, channel + GROUP, second)


def fill_sum(perm, stage, channel, first, second):
    both = (chunk(*first).astype(F32) + chunk(*second).astype(F32)).astype(BF16)
    total = dot_nn(perm, both)
    put_chunk(stage, 0, channel, total[:, LOW])
    put_chunk(stage, 1, channel, total[:, HIGH])


def split_out(info, perm, stage, owner, at):
    x, y = info[0], info[1]
    channel = owner * (2 * GROUP) + at
    both = dot_nn(perm, get_chunk(stage, (y, 1 - y), channel))
    swapped = dot_nn(perm, get_chunk(stage, (0, 1), channel + GROUP))
    first, second = half_swap(swapped[:, LOW], swapped[:, HIGH])
    return both[:, LOW], both[:, HIGH], pick(x, first, second), pick(x, second, first)


def middle_kernel(
    part, info, pair, own, ypart, xpart, ycpart, xcpart, near,
    gate1, gain1, final1_t, norm2, proj2_t,
    middle_out, inner_out, gate_out, factor_out, normed_out, final_out, slope_out, o_own, o_near, o_y, o_yc, o_x, o_xc,
    stage, left_st, right_st, perm,
):
    @first_step
    def _():
        perm[...] = reorder()
        fill_split(info, perm[...], stage, own, near, ypart, ycpart, xpart, xcpart)

    def work(here, rows):
        inner = get_rows(stage, rows)
        final = (normalise(inner)[0] * gain1[...]).astype(BF16)
        spread_out(inner_out, here, inner)
        spread_out(final_out, here, final)
        gate = stacked(gate1, here).astype(F32)
        update = dot_nn(final1_t[...], final) * gate
        spread_out(slope_out, here, update * (1.0 - gate))
        middle = (turned(pair, here) + update).astype(BF16)
        spread_out(middle_out, here, middle)
        normed = (normalise(middle.astype(F32))[0] * norm2[...]).astype(BF16)
        spread_out(normed_out, here, normed)
        mixture = dot_nn(proj2_t[...], normed)
        left, right, gate, factors = gated(mixture, norm2.shape[0], mask_rows(info, part, rows))
        put_rows(left_st, rows, left)
        put_rows(right_st, rows, right)
        spread_out(gate_out, here, gate)
        spread_out(factor_out, here, factors)

    each_rows(work)

    @last_step
    def _():
        core = info[2]
        beyond = slice(LANES, 3 * LANES)
        for owner, main, yo, xo in ((core, o_own, o_y, o_x), (1 - core, o_near, o_yc, o_xc)):
            for at in CHUNKS:
                kept = split_out(info, perm[...], left_st, owner, at)
                give_chunk(main, 0, at, LOW, kept[0])
                give_chunk(yo, 0, at, LOW, kept[1])
                give_chunk(main, 1, at, LOW, kept[2])
                give_chunk(xo, 0, at, LOW, kept[3])
                for group, out in ((0, yo), (1, xo)):
                    channel = owner * (2 * GROUP) + group * GROUP + at
                    right = dot_nn(perm[...], get_chunk(right_st, (0, 1), channel)).astype(BF16)
                    give_chunk(main, group, at, beyond, right)
                    give_chunk(out, 0, at, beyond, right)


def leave_rows_back(hat, spread, gate, grad, gain, final_w):
    grad_product = (grad * gate).astype(BF16)
    grad_final = dot_nn(final_w, grad_product)
    return normalise_back(grad_final * gain, hat, spread), grad_product


def turn_kernel(
    part, info, gate2, cot, own, ypart, xpart, ycpart, xcpart, near,
    gain2, final2_t, final2_w,
    gate_out, final_out, product_out, same0, same1, other0, other1, to_core, stage, out_st, perm,
):
    core = info[2]

    @first_step
    def _():
        perm[...] = reorder()
        for owner, mine, xp, yp in ((core, own, xpart, ypart), (1 - core, near, xcpart, ycpart)):
            for at in CHUNKS:
                channel = owner * (2 * GROUP) + at
                fill_sum(perm[...], stage, channel, (mine, 0, at, BOTH), (xp, 0, at, BOTH))
                fill_sum(perm[...], stage, channel + GROUP, (mine, 1, at, BOTH), (yp, 0, at, BOTH))

    def work(here, rows):
        hat, spread = normalise(get_rows(stage, rows))
        gain, gate, grad = gain2[...], stacked(gate2, here).astype(F32), turned(cot, here)
        final = (hat * gain).astype(BF16)
        spread_out(final_out, here, final)
        product = dot_nn(final2_t[...], final)
        spread_out(gate_out, here, grad * product * gate * (1.0 - gate))
        grad_inner, grad_product = leave_rows_back(hat, spread, gate, grad, gain, final2_w[...])
        spread_out(product_out, here, grad_product)
        put_rows(out_st, rows, grad_inner)

    each_rows(work)

    @last_step
    def _():
        for owner, outs in ((core, (same0, same1)), (1 - core, (other0, other1))):
            for group, out in enumerate(outs):
                for at in CHUNKS:
                    channel = owner * (2 * GROUP) + group * GROUP + at
                    value = dot_nn(perm[...], get_chunk(out_st, (0, 1), channel)).astype(BF16)
                    give_chunk(out, 0, at, BOTH, value)
                    if out is other0 or out is other1:
                        give_chunk(to_core, group, at, BOTH, value)


def entry_rows_back(hat, spread, norm, grads, factors, grad_gate, proj_w):
    hidden = norm.shape[0]
    blocks = [
        (grads[n % 2] * factors[n * hidden : (n + 1) * hidden].astype(F32)).astype(BF16)
        for n in range(4)
    ]
    grad_mixture = jnp.concatenate(blocks + [grad_gate], axis=0)
    grad_normed = dot_nn(proj_w, grad_mixture)
    return normalise_back(grad_normed * norm, hat, spread), grad_mixture


def inward_kernel(
    part, info, middle, gate1, cot, inner_in, gate_in, factors, slopes, own, ypart, xpart, ycpart, xcpart, near,
    norm2, proj2_w, gain1, final1_w,
    grad_out, gate_out, mixture_out, product_out, o_own, o_near, o_y, o_yc, o_x, o_xc,
    left_st, right_st, out_st, perm,
):
    core = info[2]

    @first_step
    def _():
        perm[...] = reorder()
        fill_split(info, perm[...], left_st, own, near, ypart, ycpart, xpart, xcpart)
        beyond = slice(LANES, 3 * LANES)
        for owner, mine, yp, xp in ((core, own, ypart, xpart), (1 - core, near, ycpart, xcpart)):
            for at in CHUNKS:
                channel = owner * (2 * GROUP) + at
                fill_sum(perm[...], right_st, channel, (mine, 0, at, beyond), (yp, 0, at, beyond))
                fill_sum(
                    perm[...], right_st, channel + GROUP, (mine, 1, at, beyond), (xp, 0, at, beyond)
                )

    def work(here, rows):
        hat, spread = normalise(stacked(middle, here).astype(F32))
        grad_flat, grad_mixture = entry_rows_back(
            hat, spread, norm2[...], (get_rows(left_st, rows), get_rows(right_st, rows)),
            stacked(factors, here), stacked(gate_in, here), proj2_w[...],
        )
        spread_out(mixture_out, here, grad_mixture)
        grad = turned(cot, here) + grad_flat
        spread_out(grad_out, here, grad)
        spread_out(gate_out, here, grad * stacked(slopes, here).astype(F32))
        hat, spread = normalise(stacked(inner_in, here).astype(F32))
        grad_inner, grad_product = leave_rows_back(
            hat, spread, stacked(gate1, here).astype(F32), grad, gain1[...], final1_w[...]
        )
        spread_out(product_out, here, grad_product)
        put_rows(out_st, rows, grad_inner)

    each_rows(work)

    @last_step
    def _():
        for owner, main, yo, xo in ((core, o_own, o_y, o_x), (1 - core, o_near, o_yc, o_xc)):
            for at in CHUNKS:
                kept = split_out(info, perm[...], out_st, owner, at)
                give_chunk(main, 0, at, LOW, kept[0])
                give_chunk(yo, 0, at, LOW, kept[1])
                give_chunk(main, 1, at, LOW, kept[2])
                give_chunk(xo, 0, at, LOW, kept[3])


def weight_kernel(info, *refs):
    *refs, total = refs
    (mixtures, normeds, *pairs) = paired(refs)
    width, channels = mixtures[0].shape[1], normeds[0].shape[1]

    @pl.when(pl.program_id(0) == 0)
    def _():
        total[...] = jnp.zeros_like(total)

    for part in range(PARTS):
        for first in range(0, mixtures[part].shape[0], PAIRED):
            rows = [first + n for n in range(PAIRED)]
            mixture, normed = stacked(mixtures[part], rows), stacked(normeds[part], rows)
            total[:width, :] += dot_nt(mixture, normed)
            for n, (finals, products) in enumerate((pairs[:2], pairs[2:])):
                where = slice(width + n * channels, width + (n + 1) * channels)
                final, product = stacked(finals[part], rows), stacked(products[part], rows)
                total[where, :] += dot_nt(final, product)


def exit_kernel(
    part, info, pair, grad_in, gate_in, factors, own, ypart, xpart, ycpart, xcpart, near,
    norm1, proj1_w, early, *rest,
):
    out, gproj, *rest, left_st, right_st, perm = rest
    if part:
        before, unused, out, gproj, packed = (out, gproj, *rest)
    core = info[2]

    @first_step
    def _():
        perm[...] = reorder()
        gproj[...] = before[...] if part else jnp.zeros_like(gproj)
        beyond = slice(2 * LANES, 4 * LANES)
        for owner, mine, yp, xp in ((core, own, ypart, xpart), (1 - core, near, ycpart, xcpart)):
            for group, lefts, rights in ((0, yp, xp), (1, xp, yp)):
                for at in CHUNKS:
                    channel = owner * (2 * GROUP) + group * GROUP + at
                    fill_sum(
                        perm[...], left_st, channel, (mine, group, at, BOTH), (lefts, group, at, BOTH)
                    )
                    fill_sum(
                        perm[...],
                        right_st,
                        channel,
                        (mine, group, at, beyond),
                        (rights, group, at, BOTH),
                    )

    def work(here, rows):
        hat, spread = normalise(turned(pair, here))
        norm = norm1[...]
        grad_flat, grad_mixture = entry_rows_back(
            hat, spread, norm, (get_rows(left_st, rows), get_rows(right_st, rows)),
            stacked(factors, here), stacked(gate_in, here), proj1_w[...],
        )
        gproj[...] += dot_nt(grad_mixture, (hat * norm).astype(BF16))
        total = stacked(grad_in, here) + grad_flat
        width = 2 * LANES
        for n, row in enumerate(here):
            out[row] = total[:, n * width : (n + 1) * width].T

    each_rows(work)

    if part:

        @last_step
        def _():
            size = gproj.shape[0]
            packed[:size, :] = gproj[...].astype(BF16)
            packed[size:, :] = early[...].astype(BF16)


CHANNELS = 8
PARTS = 2


def paired(refs):
    return [refs[n : n + PARTS] for n in range(0, len(refs), PARTS)]


def place(one, two, part):
    return pl.multiple_of((one * 2 + two) * (PARTS * BLOCK) + part * BLOCK, BLOCK)


def places(info, group):
    at, core = info[group], info[2]
    return [
        place(at if n < 2 else 1 - at, core if n % 2 == 0 else 1 - core, part)
        for n in range(4)
        for part in range(PARTS)
    ]


def take(ref, group, h):
    return ref[group, h] if len(ref.shape) == 4 else ref[h]


def joined(quads, group, h):
    return jnp.concatenate([take(ref, group, h) for refs in quads for ref in refs], axis=0)


def gather(stage, slot, wheres, quads, group, h):
    for where, ref in zip(wheres, [ref for refs in quads for ref in refs]):
        stage[slot, pl.ds(where, BLOCK), :] = take(ref, group, h)
    return stage[slot]


def give(refs, group, h, lanes, value):
    if len(refs.shape) == 4:
        refs[group, h, :, lanes] = value
    else:
        refs[h, :, lanes] = value


def scatter(quads, group, h, lanes, value):
    for n, ref in enumerate([ref for refs in quads for ref in refs]):
        give(ref, group, h, lanes, value[n * BLOCK : (n + 1) * BLOCK])


def scatter_from(stage, slot, wheres, quads, group, h, lanes):
    for where, ref in zip(wheres, [ref for refs in quads for ref in refs]):
        give(ref, group, h, lanes, stage[slot, pl.ds(where, BLOCK), :])


def outgoing_kernel(info, *refs):
    *refs, stage = refs
    *refs, o_own, o_near, o_y, o_yc, o_x, o_xc = refs
    a_own, b_own, a_y, b_x, a_yc, b_xc, near = paired(refs)
    a_near, b_near = [ref.at[:2] for ref in near], [ref.at[2:] for ref in near]
    along_a, along_b = (a_own, a_near, a_y, a_yc), (b_own, b_near, b_x, b_xc)
    for h in range(CHANNELS):
        for group in range(2):
            lefts, rights = (along_a, along_b) if group == 0 else (along_b, along_a)
            far = (o_y, o_yc) if group == 0 else (o_x, o_xc)
            right = gather(stage, 2 * h + group, places(info, group), rights, group, h)
            inner = dot_nt(joined(lefts, group, h), right).astype(BF16)
            for n, out in enumerate((o_own, o_near) + far):
                rows = PARTS * BLOCK
                give(out, group, h, slice(0, LANES), inner[n * rows : (n + 1) * rows])


def halves(quads, group, h):
    both = joined(quads, group, h)
    return both[:, :LANES], both[:, LANES:]


def incoming_kernel(info, *refs):
    *refs, stage = refs
    own, ypart, xpart, ycpart, xcpart, near, o_own, o_near, o_x, o_xc, o_y, o_yc = paired(refs)
    for h in range(CHANNELS):
        for group in range(2):
            far = (ypart, ycpart) if group == 0 else (xpart, xcpart)
            outs = (o_own, o_near) + ((o_x, o_xc) if group == 0 else (o_y, o_yc))
            slot = 2 * h + group
            left, right = halves((own, near) + far, group, h)
            stage[slot] = dot_tn(left, right).astype(BF16)
            scatter_from(stage, slot, places(info, group), outs, group, h, slice(0, 2 * LANES))


def incoming_back_kernel(info, *refs):
    *refs, stage = refs
    own, ypart, xpart, ycpart, xcpart, near, *more = paired(refs)
    same0, same1, g_y, g_x, g_yc, g_xc, g_near, *more = more
    o_own, o_near, o_y, o_yc, o_x, o_xc = more
    for h in range(CHANNELS):
        for group in range(2):
            far = (ypart, ycpart) if group == 0 else (xpart, xcpart)
            grads = (same0, g_near, g_x, g_xc) if group == 0 else (same1, g_near, g_y, g_yc)
            outs = (o_own, o_near) + ((o_y, o_yc) if group == 0 else (o_x, o_xc))
            grad = gather(stage, 2 * h + group, places(info, group), grads, group, h)
            left, right = halves((own, near) + far, group, h)
            scatter(outs, group, h, slice(0, LANES), dot_nt(right, grad).astype(BF16))
            scatter(outs, group, h, slice(LANES, 3 * LANES), dot_nn(left, grad).astype(BF16))


def outgoing_back_kernel(info, *refs):
    *refs, stage, back = refs
    a_own, b_own, a_y, b_x, a_yc, b_xc, near, *more = paired(refs)
    a_near, b_near = [ref.at[:2] for ref in near], [ref.at[2:] for ref in near]
    g_own, g_y, g_x, g_yc, g_xc, g_near, o_own, o_near, o_y, o_yc, o_x, o_xc = more
    along_a, along_b = (a_own, a_near, a_y, a_yc), (b_own, b_near, b_x, b_xc)
    first, second = slice(0, 2 * LANES), slice(2 * LANES, 4 * LANES)
    for h in range(CHANNELS):
        for group in range(2):
            lefts, rights = (along_a, along_b) if group == 0 else (along_b, along_a)
            far = (g_y, g_yc) if group == 0 else (g_x, g_xc)
            left_far, right_far = ((o_y, o_yc), (o_x, o_xc)) if group == 0 else ((o_x, o_xc), (o_y, o_yc))
            slot = 2 * h + group
            wheres = places(info, group)
            right = gather(stage, slot, wheres, rights, group, h)
            grad = joined((g_own, g_near) + far, group, h)
            grad_left = dot_nn(grad, right).astype(BF16)
            back[slot] = dot_tn(grad, joined(lefts, group, h)).astype(BF16)
            core_rows = 2 * PARTS * BLOCK
            scatter((o_own, o_near), group, h, first, grad_left[:core_rows])
            scatter(left_far, group, h, first, grad_left[core_rows:])
            scatter_from(back, slot, wheres[: 2 * PARTS], (o_own, o_near), group, h, second)
            scatter_from(back, slot, wheres[2 * PARTS :], right_far, group, h, first)


def whole(shape):
    return pl.BlockSpec(shape, lambda step, info: (0,) * len(shape))


def rows_of(part, some=SOME):
    def make(shape):
        first = part * (BLOCK // some)
        return pl.BlockSpec(
            (some,) + shape[1:], lambda step, info: (first + step,) + (0,) * (len(shape) - 1)
        )

    return make


def rows_block(part):
    def make(shape):
        return pl.BlockSpec(
            shape[:-2] + (BLOCK, shape[-1]),
            lambda step, info: (0,) * (len(shape) - 2) + (part, 0),
        )

    return make


def anywhere(shape):
    return pl.BlockSpec(memory_space=pl.ANY)


def channel_rows(shape):
    if len(shape) == 4:
        return pl.BlockSpec((shape[0], CHANNELS) + shape[2:], lambda step, info: (0, step, 0, 0))
    return pl.BlockSpec((CHANNELS,) + shape[1:], lambda step, info: (step, 0, 0))


def call(kernel, info, steps, ins, outs, scratch, aliases={}):
    return pl.pallas_call(
        kernel,
        grid_spec=pltpu.PrefetchScalarGridSpec(
            num_scalar_prefetch=1,
            grid=(steps,),
            in_specs=[make(array.shape) for array, make in ins],
            out_specs=[make(shape) for shape, unused, make in outs],
            scratch_shapes=scratch,
        ),
        out_shape=[jax.ShapeDtypeStruct(shape, dtype) for shape, dtype, unused in outs],
        compiler_params=pltpu.CompilerParams(vmem_limit_bytes=VMEM),
        input_output_aliases=aliases,
    )(info, *[array for array, unused in ins])


class Links:
    def __init__(self):
        self.last = {}

    def send(self, array, offset):
        count = lax.axis_size("axial")
        if offset in self.last and offset in (X, Y):
            array, unused = lax.optimization_barrier((array, self.last[offset]))
        self.last[offset] = lax.ppermute(
            array, "axial", [(n, n ^ offset) for n in range(count)]
        )
        return self.last[offset]

    def __call__(self, *sends):
        results = [[] for unused in sends]
        for part in range(len(sends[0][0])):
            for result, (arrays, offset) in zip(results, sends):
                result.append(self.send(arrays[part], offset))
        return results


CORE, X, Y = 1, 2, 4


def add_up(share):
    count = lax.axis_size("axial")
    rows, width = share.shape
    shares = share.reshape(count, rows // count, width)
    parts = lax.all_to_all(shares, "axial", split_axis=0, concat_axis=0, tiled=True)
    mine = parts.astype(F32).sum(axis=0).astype(BF16)
    depth = lax.axis_size("dp")
    terms = [mine] + [
        lax.ppermute(mine, "dp", [(n, n ^ offset) for n in range(depth)])
        for offset in range(1, depth)
    ]
    terms = [term.astype(F32) for term in terms]
    while len(terms) > 1:
        terms = [terms[n] + terms[n + 1] for n in range(0, len(terms), 2)]
    copies = jnp.broadcast_to(terms[0].astype(BF16)[None], shares.shape)
    return lax.all_to_all(copies, "axial", split_axis=0, concat_axis=0, tiled=True).reshape(
        rows, width
    )


def gain_grad(weight_grad, weight, gain_row):
    return jnp.sum((weight.astype(F32) * weight_grad).T, axis=0, keepdims=True) / gain_row


def finish_kernel(
    scale, info, sums, proj1, final1, proj2, final2, norm1, gain1, norm2, gain2,
    o_norm1, o_proj1, o_gain1, o_final1, o_norm2, o_proj2, o_gain2, o_final2,
):
    width, channels = proj1.shape[1], final1.shape[1]
    takes = (
        (0, True, proj1, norm1, o_proj1, o_norm1),
        (width, True, proj2, norm2, o_proj2, o_norm2),
        (2 * width, False, final2, gain2, o_final2, o_gain2),
        (2 * width + channels, False, final1, gain1, o_final1, o_gain1),
    )
    for start, flipped, weight, gain, out, gain_out in takes:
        total = sums[start : start + weight.shape[1], :].astype(F32) * scale
        total = total.T if flipped else total
        out[...] = total
        gain_out[...] = gain_grad(total, weight[...].astype(BF16), gain[...])


def fast_body(
    pair,
    cotangent,
    lengths,
    outgo_norm,
    outgo_proj,
    outgo_gain,
    outgo_final,
    incom_norm,
    incom_proj,
    incom_gain,
    incom_final,
):
    rows, tokens, channels = pair.shape[1:]
    hidden = outgo_gain.shape[0]
    index = lax.axis_index("axial")
    info = jnp.stack(
        [(index // 2) % 2, index // 4, index % 2, index * rows, lengths[0]]
    ).astype(jnp.int32)
    hop = Links()
    pair = pair[0]
    cot = cotangent[0]
    parts = range(PARTS)
    turns = GROUP // CHANNELS
    stage = pltpu.VMEM((2, BLOCK, hidden, LANES), F32)
    out_stage = pltpu.VMEM((2, BLOCK, hidden, LANES), BF16)
    perm = pltpu.VMEM((BLOCK * BLOCK, BLOCK * BLOCK), BF16)
    streamed = rows_of(0)
    square = pltpu.VMEM((2 * CHANNELS, 4 * rows, tokens), BF16)

    def two(width, height=BLOCK, make=whole, groups=2):
        return ((groups, GROUP, height, width), BF16, make)

    def one(width, height=BLOCK, make=whole):
        return ((GROUP, height, width), BF16, make)

    turned_block = ((BLOCK, channels, tokens), BF16, streamed)
    factor_block = ((BLOCK, 4 * hidden, tokens), BF16, streamed)
    mixture_block = ((BLOCK, 5 * hidden, tokens), BF16, streamed)

    def cells(kernel, ins, outs, scratch, more=lambda part: []):
        results = []
        for part in parts:
            carried = ins(part, results)
            results.append(
                call(functools.partial(kernel, part), info, STEPS, carried, outs + more(part), scratch)
            )
        shared = results[-1][len(outs) :]
        return [list(each) for each in zip(*results)] + list(shared)

    def wholes(arrays):
        return [(array, whole) for array in arrays]

    def triangle(kernel, operands, outs, scratch, split=PARTS):
        ins = [(array, channel_rows) for arrays in operands for array in arrays]
        each = [out for out in outs for unused in range(split)]
        results = call(kernel, info, turns, ins, each, scratch)
        return [list(results[n : n + split]) for n in range(0, len(results), split)]

    raw = (outgo_gain[None], outgo_final, incom_norm[None], incom_proj, incom_gain[None], incom_final)
    gain_wide = ((channels, PAIRED * tokens), F32, whole)
    proj_turned = ((5 * hidden, channels), BF16, whole)
    proj_plain = ((channels, 5 * hidden), BF16, whole)
    final_plain = ((hidden, channels), BF16, whole)
    (
        a_same, a_other, b_same, b_other, to_core, gate_one, factors_one,
        norm1, gain1, norm2, gain2, proj2_t, final1_t, final2_t,
        proj1, final1, proj2, final2,
    ) = cells(
        entry_kernel,
        lambda part, unused: [(pair, rows_of(part)), (outgo_norm[None], whole), (outgo_proj, whole)]
        + (wholes(raw) if part else []),
        [two(tokens)] * 4 + [two(tokens, groups=4), turned_block, factor_block],
        [
            out_stage,
            out_stage,
            pltpu.VMEM((channels, PAIRED * tokens), F32),
            pltpu.VMEM((5 * hidden, channels), BF16),
            perm,
        ],
        lambda part: (
            [gain_wide] * 4
            + [proj_turned]
            + [final_plain] * 2
            + [proj_plain, final_plain] * 2
            if part
            else []
        ),
    )
    held_one = [a_same, b_same] + hop(
        (a_same, Y), (b_same, X), (a_other, Y | CORE), (b_other, X | CORE), (to_core, CORE)
    )
    own, near, to_y, to_yc, to_x, to_xc = triangle(
        outgoing_kernel,
        held_one,
        [two(LANES, rows, channel_rows)] * 2 + [one(LANES, rows, channel_rows)] * 4,
        [square],
        split=1,
    )
    back_one = [
        own,
        *hop(
            (to_y, Y), (to_x, X), (to_yc, Y | CORE), (to_xc, X | CORE), (near, CORE)
        ),
    ]

    (
        middle, inner_one, gate_two, factors_two, normed_two, finals_one, slopes_one,
        own, near, to_y, to_yc, to_x, to_xc,
    ) = cells(
        middle_kernel,
        lambda part, unused: [(pair, rows_of(part))]
        + [(array, rows_block(part)) for array, in back_one]
        + [(gate_one[part], streamed)]
        + wholes((gain1, final1_t, norm2, proj2_t)),
        [turned_block] * 3
        + [factor_block]
        + [turned_block] * 3
        + [two(3 * LANES)] * 2 + [one(3 * LANES)] * 4,
        [stage, out_stage, out_stage, perm],
    )
    held_two = [
        own,
        *hop(
            (to_y, Y), (to_x, X), (to_yc, Y | CORE), (to_xc, X | CORE), (near, CORE)
        ),
    ]
    own, near, to_x, to_xc, to_y, to_yc = triangle(
        incoming_kernel,
        held_two,
        [two(tokens, make=channel_rows)] * 2 + [one(tokens, make=channel_rows)] * 4,
        [square],
    )
    back_two = [
        own,
        *hop(
            (to_y, Y), (to_x, X), (to_yc, Y | CORE), (to_xc, X | CORE), (near, CORE)
        ),
    ]

    gate_grad_two, finals_two, products_two, same0, same1, other0, other1, to_core = cells(
        turn_kernel,
        lambda part, done: [(gate_two[part], streamed), (cot, rows_of(part))]
        + wholes(arrays[part] for arrays in back_two)
        + wholes((gain2, final2_t, final2)),
        [turned_block] * 3 + [one(tokens)] * 4 + [two(tokens)],
        [stage, out_stage, perm],
    )
    grads_two = [
        same0,
        same1,
        *hop(
            (same1, Y), (same0, X), (other1, Y | CORE), (other0, X | CORE), (to_core, CORE)
        ),
    ]
    own, near, to_y, to_yc, to_x, to_xc = triangle(
        incoming_back_kernel,
        held_two + grads_two,
        [two(3 * LANES, make=channel_rows)] * 2 + [one(3 * LANES, make=channel_rows)] * 4,
        [square],
    )
    rows_two = [
        own,
        *hop(
            (to_y, Y), (to_x, X), (to_yc, Y | CORE), (to_xc, X | CORE), (near, CORE)
        ),
    ]

    (
        grad_middle, gate_grad_one, mixtures_two, products_one,
        own, near, to_y, to_yc, to_x, to_xc,
    ) = cells(
        inward_kernel,
        lambda part, done: [
            (middle[part], streamed),
            (gate_one[part], streamed),
            (cot, rows_of(part)),
            (inner_one[part], streamed),
            (gate_grad_two[part], streamed),
            (factors_two[part], streamed),
            (slopes_one[part], streamed),
        ]
        + wholes(arrays[part] for arrays in rows_two)
        + wholes((norm2, proj2, gain1, final1)),
        [((BLOCK, channels, tokens), F32, streamed), turned_block, mixture_block, turned_block]
        + [two(LANES)] * 2
        + [one(LANES)] * 4,
        [stage, stage, out_stage, perm],
    )
    grads_one = [
        own,
        *hop(
            (to_y, Y), (to_x, X), (to_yc, Y | CORE), (to_xc, X | CORE), (near, CORE)
        ),
    ]
    own, near, to_y, to_yc, to_x, to_xc = triangle(
        outgoing_back_kernel,
        held_one + grads_one,
        [two(2 * tokens, make=channel_rows)] * 2 + [two(tokens, make=channel_rows)] * 4,
        [square, square],
    )
    rows_one = [
        own,
        *hop(
            (to_y, Y), (to_x, X), (to_yc, Y | CORE), (to_xc, X | CORE), (near, CORE)
        ),
    ]
    kept = (mixtures_two, normed_two, finals_two, products_two, finals_one, products_one)
    (early,) = call(
        weight_kernel,
        info,
        4,
        [
            (array, rows_of(0, BLOCK // 4))
            for arrays in kept
            for array in arrays
        ],
        [((5 * hidden + 2 * channels, channels), F32, whole)],
        [],
    )
    exit_ins = 10 + 3 + 1 + 1
    result = None
    for part in parts:
        result = call(
            functools.partial(exit_kernel, part),
            info,
            STEPS,
            [
                (pair, rows_of(part)),
                (grad_middle[part], streamed),
                (gate_grad_one[part], streamed),
                (factors_one[part], streamed),
            ]
            + wholes(arrays[part] for arrays in rows_one)
            + wholes((norm1, proj1, early))
            + ([(result[1], whole), (result[0], anywhere)] if part else []),
            [
                ((rows, tokens, channels), F32, rows_of(part)),
                ((5 * hidden, channels), F32, whole),
            ]
            + ([((10 * hidden + 2 * channels, channels), BF16, whole)] if part else []),
            [stage, stage, perm],
            {exit_ins: 0} if part else {},
        )
    grad_begin, unused, packed = result
    sums = add_up(packed)
    scale = 1.0 / math.sqrt(lax.axis_size("dp") * tokens * tokens)
    weights = (outgo_proj, outgo_final, incom_proj, incom_final)
    gains = (outgo_norm, outgo_gain, incom_norm, incom_gain)
    order = (outgo_norm[None], outgo_proj, outgo_gain[None], outgo_final)
    order += (incom_norm[None], incom_proj, incom_gain[None], incom_final)
    totals = call(
        functools.partial(finish_kernel, scale),
        info,
        1,
        wholes((sums,) + weights + tuple(gain[None] for gain in gains)),
        [(array.shape, F32, whole) for array in order],
        [],
    )
    return (grad_begin[None],) + tuple(
        total.reshape(-1) if total.shape[0] == 1 else total for total in totals
    )


def solution(mesh):
    def body(pair, *rest):
        rows, tokens, channels = pair.shape[1:]
        hidden = rest[3].shape[0]
        plane = mesh.shape["axial"] == 8 and rows == 32 and tokens == 2 * LANES
        if plane and channels == LANES and hidden == 4 * GROUP:
            return fast_body(pair, *rest)
        return plain_body(pair, *rest)

    return jax.shard_map(
        body,
        mesh=mesh,
        in_specs=(P("dp", "axial", None, None), P("dp", "axial", None, None), P("dp")) + (P(),) * 8,
        out_specs=(P("dp", "axial", None, None),) + (P(),) * 8,
        check_vma=False,
    )
```

```python
import functools
import math

import jax
import jax.numpy as jnp
from jax import lax
from jax.experimental import pallas as pl
from jax.experimental.pallas import tpu as pltpu
from jax.sharding import PartitionSpec as P

EPSILON = 1e-05


def rounded(inputs):
    return lax.optimization_barrier(inputs.astype(jnp.bfloat16)).astype(jnp.float32)


def layer_norm(inputs, factor):
    average = jnp.mean(inputs, axis=-1, keepdims=True)
    centered = inputs - average
    spread = jnp.mean(centered * centered, axis=-1, keepdims=True)
    return centered * lax.rsqrt(spread + EPSILON) * factor


def gating(mixture, pair_mask, hidden):
    left_part = (
        mixture[:, :hidden] * jax.nn.sigmoid(mixture[:, 2 * hidden : 3 * hidden]) * pair_mask
    )
    right_part = (
        mixture[:, hidden : 2 * hidden]
        * jax.nn.sigmoid(mixture[:, 3 * hidden : 4 * hidden])
        * pair_mask
    )
    gate_part = jax.nn.sigmoid(mixture[:, 4 * hidden :])
    return (left_part, right_part, gate_part)


def entry(flat_pair, norm_gain, projection, pair_mask, hidden):
    normed = layer_norm(flat_pair, norm_gain).astype(jnp.bfloat16)
    mixture = jnp.dot(normed, projection.astype(jnp.bfloat16), preferred_element_type=jnp.float32)
    left_part, right_part, gate_part = gating(mixture, pair_mask, hidden)
    return (normed, mixture, left_part, right_part, gate_part)


def entry_back(
    flat_pair,
    norm_gain,
    projection,
    pair_mask,
    hidden,
    normed,
    mixture,
    grad_left,
    grad_right,
    grad_gate,
):
    unused, pull_gate = jax.vjp(lambda inner_mix: gating(inner_mix, pair_mask, hidden), mixture)
    grad_mixture = pull_gate((grad_left, grad_right, grad_gate))[0].astype(jnp.bfloat16)
    grad_projection = jnp.dot(normed.T, grad_mixture, preferred_element_type=jnp.float32)
    grad_normed = jnp.dot(
        grad_mixture, projection.astype(jnp.bfloat16).T, preferred_element_type=jnp.float32
    )
    unused, pull_norm = jax.vjp(layer_norm, flat_pair, norm_gain)
    grad_flat, grad_gain = pull_norm(grad_normed)
    return (grad_flat, grad_gain, grad_projection)


def leave(inner_sum, gate_part, out_gain, final_weight):
    final_normed = layer_norm(inner_sum, out_gain).astype(jnp.bfloat16)
    product = jnp.dot(
        final_normed, final_weight.astype(jnp.bfloat16), preferred_element_type=jnp.float32
    )
    return (final_normed, product, product * gate_part)


def leave_back(inner_sum, gate_part, out_gain, final_weight, final_normed, product, grad_update):
    grad_product = (grad_update * gate_part).astype(jnp.bfloat16)
    grad_gate = grad_update * product
    grad_final = jnp.dot(final_normed.T, grad_product, preferred_element_type=jnp.float32)
    grad_normed = jnp.dot(
        grad_product, final_weight.astype(jnp.bfloat16).T, preferred_element_type=jnp.float32
    )
    unused, pull_norm = jax.vjp(layer_norm, inner_sum, out_gain)
    grad_inner, grad_gain = pull_norm(grad_normed)
    return (grad_inner, grad_gate, grad_gain, grad_final)


def channel_major(field, row_count, tokens):
    hidden = field.shape[1]
    return jnp.transpose(field.reshape(row_count, tokens, hidden), (2, 0, 1))


def row_major(field):
    hidden = field.shape[0]
    return jnp.transpose(field, (1, 2, 0)).reshape(-1, hidden)


def plain_body(
    pair,
    cotangent,
    lengths,
    outgo_norm,
    outgo_proj,
    outgo_gain,
    outgo_final,
    incom_norm,
    incom_proj,
    incom_gain,
    incom_final,
):
    row_count = pair.shape[1]
    tokens = pair.shape[2]
    channels = pair.shape[3]
    hidden = outgo_gain.shape[0]
    length = lengths[0]
    first_row = lax.axis_index("axial") * row_count
    row_alive = (first_row + jnp.arange(row_count, dtype=jnp.int32) < length).astype(jnp.float32)
    column_alive = (jnp.arange(tokens, dtype=jnp.int32) < length).astype(jnp.float32)
    pair_mask = (row_alive[:, None] * column_alive[None, :]).reshape(-1, 1)
    flat_start = pair[0].reshape(-1, channels).astype(jnp.float32)
    normed_one, mixture_one, left_one, right_one, gate_one = entry(
        flat_start, outgo_norm, outgo_proj, pair_mask, hidden
    )
    left_first = channel_major(left_one.astype(jnp.bfloat16), row_count, tokens)
    right_first = channel_major(right_one.astype(jnp.bfloat16), row_count, tokens)
    left_owned, right_owned = (
        lax.all_to_all(left_first, "axial", split_axis=0, concat_axis=1, tiled=True),
        lax.all_to_all(right_first, "axial", split_axis=0, concat_axis=1, tiled=True),
    )
    inner_cols = jnp.einsum(
        "hik,hjk->hij", left_owned, right_owned, preferred_element_type=jnp.float32
    )
    inner_one = row_major(
        lax.all_to_all(
            inner_cols.astype(jnp.bfloat16), "axial", split_axis=1, concat_axis=0, tiled=True
        ).astype(inner_cols.dtype)
    )
    final_one, product_one, update_one = leave(inner_one, gate_one, outgo_gain, outgo_final)
    flat_middle = rounded(flat_start + update_one)
    normed_two, mixture_two, left_two, right_two, gate_two = entry(
        flat_middle, incom_norm, incom_proj, pair_mask, hidden
    )
    left_second = channel_major(left_two.astype(jnp.bfloat16), row_count, tokens)
    right_second = channel_major(right_two.astype(jnp.bfloat16), row_count, tokens)
    left_held, right_held = (
        lax.all_to_all(left_second, "axial", split_axis=0, concat_axis=1, tiled=True),
        lax.all_to_all(right_second, "axial", split_axis=0, concat_axis=1, tiled=True),
    )
    inner_held = jnp.einsum(
        "hki,hkj->hij", left_held, right_held, preferred_element_type=jnp.float32
    )
    inner_two = row_major(
        lax.all_to_all(
            inner_held.astype(jnp.bfloat16), "axial", split_axis=1, concat_axis=0, tiled=True
        ).astype(inner_held.dtype)
    )
    final_two, product_two, update_two = leave(inner_two, gate_two, incom_gain, incom_final)
    grad_end = cotangent[0].reshape(-1, channels).astype(jnp.float32)
    grad_inner_two, grad_gate_two, grad_gain_two, grad_final_two = leave_back(
        inner_two, gate_two, incom_gain, incom_final, final_two, product_two, grad_end
    )
    grad_cells_two = channel_major(grad_inner_two.astype(jnp.bfloat16), row_count, tokens)
    grad_held_two = lax.all_to_all(grad_cells_two, "axial", split_axis=0, concat_axis=1, tiled=True)
    left_back, right_back = (
        lax.all_to_all(left_second, "axial", split_axis=0, concat_axis=1, tiled=True),
        lax.all_to_all(right_second, "axial", split_axis=0, concat_axis=1, tiled=True),
    )
    grad_left_held = jnp.einsum(
        "hij,hkj->hki", grad_held_two, right_back, preferred_element_type=jnp.float32
    )
    grad_right_held = jnp.einsum(
        "hki,hij->hkj", left_back, grad_held_two, preferred_element_type=jnp.float32
    )
    grad_left_rows, grad_right_rows = (
        lax.all_to_all(
            grad_left_held.astype(jnp.bfloat16), "axial", split_axis=1, concat_axis=0, tiled=True
        ).astype(grad_left_held.dtype),
        lax.all_to_all(
            grad_right_held.astype(jnp.bfloat16), "axial", split_axis=1, concat_axis=0, tiled=True
        ).astype(grad_right_held.dtype),
    )
    grad_left_two = row_major(grad_left_rows)
    grad_right_two = row_major(grad_right_rows)
    grad_flat_two, grad_norm_two, grad_proj_two = entry_back(
        flat_middle,
        incom_norm,
        incom_proj,
        pair_mask,
        hidden,
        normed_two,
        mixture_two,
        grad_left_two,
        grad_right_two,
        grad_gate_two,
    )
    second_sums = lax.psum(
        (grad_norm_two, grad_proj_two, grad_gain_two, grad_final_two), ("dp", "axial")
    )
    grad_middle = grad_end + grad_flat_two
    grad_inner_one, grad_gate_one, grad_gain_one, grad_final_one = leave_back(
        inner_one, gate_one, outgo_gain, outgo_final, final_one, product_one, grad_middle
    )
    grad_cells_one = channel_major(grad_inner_one.astype(jnp.bfloat16), row_count, tokens)
    grad_owned_one = lax.all_to_all(
        grad_cells_one, "axial", split_axis=0, concat_axis=1, tiled=True
    )
    left_again, right_again = (
        lax.all_to_all(left_first, "axial", split_axis=0, concat_axis=1, tiled=True),
        lax.all_to_all(right_first, "axial", split_axis=0, concat_axis=1, tiled=True),
    )
    grad_left_owned = jnp.einsum(
        "hij,hjk->hik", grad_owned_one, right_again, preferred_element_type=jnp.float32
    )
    grad_right_owned = jnp.einsum(
        "hij,hik->hjk", grad_owned_one, left_again, preferred_element_type=jnp.float32
    )
    grad_left_back, grad_right_back = (
        lax.all_to_all(
            grad_left_owned.astype(jnp.bfloat16), "axial", split_axis=1, concat_axis=0, tiled=True
        ).astype(grad_left_owned.dtype),
        lax.all_to_all(
            grad_right_owned.astype(jnp.bfloat16), "axial", split_axis=1, concat_axis=0, tiled=True
        ).astype(grad_right_owned.dtype),
    )
    grad_left_one = row_major(grad_left_back)
    grad_right_one = row_major(grad_right_back)
    grad_flat_one, grad_norm_one, grad_proj_one = entry_back(
        flat_start,
        outgo_norm,
        outgo_proj,
        pair_mask,
        hidden,
        normed_one,
        mixture_one,
        grad_left_one,
        grad_right_one,
        grad_gate_one,
    )
    grad_begin = grad_middle + grad_flat_one
    first_sums = lax.psum(
        (grad_norm_one, grad_proj_one, grad_gain_one, grad_final_one), ("dp", "axial")
    )
    totals = tuple(first_sums) + tuple(second_sums)
    scale = 1.0 / math.sqrt(lax.axis_size("dp") * tokens * tokens)
    return (
        grad_begin.reshape(1, row_count, tokens, channels),
        totals[0] * scale,
        totals[1] * scale,
        totals[2] * scale,
        totals[3] * scale,
        totals[4] * scale,
        totals[5] * scale,
        totals[6] * scale,
        totals[7] * scale,
    )


BF16 = jnp.bfloat16
F32 = jnp.float32
BLOCK = 16
PAIRED = 2
STEPS = 4
SOME = BLOCK // STEPS
LANES = 128
GROUP = 32
VMEM = 56 * 1024 * 1024


def dot_nn(a, b):
    return lax.dot_general(a, b, (((1,), (0,)), ((), ())), preferred_element_type=F32)


def dot_nt(a, b):
    return lax.dot_general(a, b, (((1,), (1,)), ((), ())), preferred_element_type=F32)


def dot_tn(a, b):
    return lax.dot_general(a, b, (((0,), (0,)), ((), ())), preferred_element_type=F32)


def normalise(v):
    centered = v - jnp.mean(v, axis=0, keepdims=True)
    spread = lax.rsqrt(jnp.mean(centered * centered, axis=0, keepdims=True) + EPSILON)
    return centered * spread, spread


def normalise_back(grad, hat, spread):
    first = jnp.mean(grad, axis=0, keepdims=True)
    second = jnp.mean(grad * hat, axis=0, keepdims=True)
    return spread * (grad - first - hat * second)


def reorder():
    size = BLOCK * BLOCK
    one = lax.broadcasted_iota(jnp.int32, (size, size), 0)
    two = lax.broadcasted_iota(jnp.int32, (size, size), 1)
    return jnp.where((one % BLOCK) * BLOCK + one // BLOCK == two, 1.0, 0.0).astype(BF16)


def chunk(ref, group, at, lanes):
    if len(ref.shape) == 4:
        block = ref[group, at : at + BLOCK, :, lanes]
    else:
        block = ref[at : at + BLOCK, :, lanes]
    return block.reshape(BLOCK * BLOCK, block.shape[2])


def put_chunk(stage, half, channel, value):
    channel = pl.multiple_of(channel, BLOCK)
    for row in range(BLOCK):
        stage[half, row, pl.ds(channel, BLOCK), :] = value[row * BLOCK : (row + 1) * BLOCK]


def get_chunk(stage, halves, channel):
    channel = pl.multiple_of(channel, BLOCK)
    return jnp.concatenate(
        [
            jnp.concatenate(
                [stage[half, row, pl.ds(channel, BLOCK), :] for row in range(BLOCK)], axis=0
            )
            for half in halves
        ],
        axis=1,
    )


def give_chunk(ref, group, at, lanes, value):
    block = value.astype(BF16).reshape(BLOCK, BLOCK, value.shape[1])
    if len(ref.shape) == 4:
        ref[group, at : at + BLOCK, :, lanes] = block
    else:
        ref[at : at + BLOCK, :, lanes] = block


LOW, HIGH, BOTH = slice(0, LANES), slice(LANES, 2 * LANES), slice(0, 2 * LANES)
CHUNKS = range(0, GROUP, BLOCK)


def half_swap(first, second):
    low = lax.broadcasted_iota(jnp.int32, first.shape, first.ndim - 1) < LANES // 2
    axis = first.ndim - 1
    return (
        jnp.where(low, first, pltpu.roll(second, LANES // 2, axis)),
        jnp.where(low, pltpu.roll(first, LANES // 2, axis), second),
    )


def pick(flag, zero, one):
    return jnp.where(flag == 0, zero, one)


def mask_chunk(info, part, row, half):
    token = lax.broadcasted_iota(jnp.int32, (1, LANES), 1) + half * LANES
    live = (info[3] + part * BLOCK + row < info[4]).astype(F32)
    return (token < info[4]).astype(F32) * live


def each_rows(work):
    step = pl.program_id(0)

    @pl.loop(0, SOME // PAIRED)
    def _(turn):
        here = [turn * PAIRED + n for n in range(PAIRED)]
        work(here, [step * SOME + row for row in here])


def first_step(work):
    pl.when(pl.program_id(0) == 0)(work)


def last_step(work):
    pl.when(pl.program_id(0) == STEPS - 1)(work)


def places_of(here, rows):
    for n, (spot, row) in enumerate(zip(here, rows)):
        for half in range(2):
            start = (2 * n + half) * LANES
            yield spot, row, half, (LOW, HIGH)[half], slice(start, start + LANES)


def turned(ref, spot, lanes):
    return ref[spot, lanes, :].astype(F32).T


def stacked(ref, rows):
    return jnp.concatenate([ref[row] for row in rows], axis=1)


def side_by_side(chunks):
    return jnp.concatenate(chunks, axis=1)


def put_gated(info, part, mixture, here, rows, left_st, right_st, gate_out, factor_out):
    size = left_st.shape[2]
    for spot, row, half, lanes, among in places_of(here, rows):
        mask = mask_chunk(info, part, row, half)
        for block, stage in enumerate((left_st, right_st)):
            gate = opened(mixture[(2 + block) * size : (3 + block) * size, among])
            opening = gate * mask
            side = mixture[block * size : (block + 1) * size, among] * opening
            stage[half, row] = side.astype(BF16)
            factor_out[spot, block * size : (block + 1) * size, lanes] = opening.astype(BF16)
            slope = (side * (1.0 - gate)).astype(BF16)
            factor_out[spot, (2 + block) * size : (3 + block) * size, lanes] = slope
        gate_out[spot, :, lanes] = opened(mixture[4 * size :, among]).astype(BF16)


def opened(gate):
    return 0.5 * jnp.tanh(gate) + 0.5


def column(row):
    return jnp.broadcast_to(row, (LANES, row.shape[1])).T


def halved_turned(weight):
    values = 2 * weight.shape[0]
    return jnp.concatenate([weight[:, :values].T, weight[:, values:].T * 0.5], axis=0).astype(BF16)


def entry_kernel(part, info, pair, norm_row, proj_w, *rest):
    if part:
        raw, rest = rest[:6], rest[6:]
        gain1, final1, norm2, proj2, gain2, final2 = raw
        prepared, rest = rest[7:18], rest[:7] + rest[18:]
    a_same, a_other, b_same, b_other, to_core, gate_out, factor_out, *rest = rest
    left_st, right_st, norm, proj_t, perm = rest
    hidden = proj_w.shape[1] // 5

    @first_step
    def _():
        norm[...] = column(norm_row[...])
        proj_t[...] = halved_turned(proj_w[...])
        perm[...] = reorder()
        if part:
            for row, out in zip((norm_row, gain1, norm2, gain2), prepared[:4]):
                out[...] = column(row[...])
            prepared[4][...] = halved_turned(proj2[...])
            for weight, out in zip((final1, final2), prepared[5:7]):
                out[...] = weight[...].T.astype(BF16)
            for weight, out in zip((proj_w, final1, proj2, final2), prepared[7:]):
                out[...] = weight[...].astype(BF16)

    def work(here, rows):
        normed = side_by_side(
            [
                (normalise(turned(pair, spot, lanes))[0] * norm[...]).astype(BF16)
                for spot, row, half, lanes, among in places_of(here, rows)
            ]
        )
        mixture = dot_nn(proj_t[...], normed)
        put_gated(info, part, mixture, here, rows, left_st, right_st, gate_out, factor_out)

    each_rows(work)

    @last_step
    def _():
        core = info[2]
        for owner, a_out, b_out in ((core, a_same, b_same), (1 - core, a_other, b_other)):
            for group in range(2):
                for at in CHUNKS:
                    channel = owner * (2 * GROUP) + group * GROUP + at
                    left = dot_nn(perm[...], get_chunk(left_st, (0, 1), channel)).astype(BF16)
                    right = dot_nn(perm[...], get_chunk(right_st, (0, 1), channel)).astype(BF16)
                    first, second = (left, right) if group == 0 else (right, left)
                    give_chunk(a_out, group, at, BOTH, first)
                    give_chunk(b_out, group, at, BOTH, second)
                    if a_out is a_other:
                        give_chunk(to_core, group, at, BOTH, first)
                        give_chunk(to_core, 2 + group, at, BOTH, second)


def fill_split(info, perm, stage, own, near, ypart, ycpart, xpart, xcpart):
    x, y, core = info[0], info[1], info[2]
    for owner, mine, yp, xp in ((core, own, ypart, xpart), (1 - core, near, ycpart, xcpart)):
        for at in CHUNKS:
            channel = owner * (2 * GROUP) + at
            both = jnp.concatenate([chunk(mine, 0, at, LOW), chunk(yp, 0, at, LOW)], axis=1)
            both = dot_nn(perm, both)
            put_chunk(stage, y, channel, both[:, LOW])
            put_chunk(stage, 1 - y, channel, both[:, HIGH])
            both = jnp.concatenate([chunk(mine, 1, at, LOW), chunk(xp, 0, at, LOW)], axis=1)
            both = dot_nn(perm, both)
            here, there = both[:, LOW], both[:, HIGH]
            first, second = half_swap(pick(x, here, there), pick(x, there, here))
            put_chunk(stage, 0, channel + GROUP, first)
            put_chunk(stage, 1, channel + GROUP, second)


def fill_sum(perm, stage, channel, first, second):
    both = (chunk(*first).astype(F32) + chunk(*second).astype(F32)).astype(BF16)
    total = dot_nn(perm, both)
    put_chunk(stage, 0, channel, total[:, LOW])
    put_chunk(stage, 1, channel, total[:, HIGH])


def split_out(info, perm, stage, owner, at):
    x, y = info[0], info[1]
    channel = owner * (2 * GROUP) + at
    both = dot_nn(perm, get_chunk(stage, (y, 1 - y), channel))
    swapped = dot_nn(perm, get_chunk(stage, (0, 1), channel + GROUP))
    first, second = half_swap(swapped[:, LOW], swapped[:, HIGH])
    return both[:, LOW], both[:, HIGH], pick(x, first, second), pick(x, second, first)


def middle_kernel(
    part, info, pair, own, ypart, xpart, ycpart, xcpart, near,
    gate1, gain1, final1_t, norm2, proj2_t,
    middle_out, inner_out, gate_out, factor_out, normed_out, final_out, slope_out, o_own, o_near, o_y, o_yc, o_x, o_xc,
    stage, left_st, right_st, perm,
):
    @first_step
    def _():
        perm[...] = reorder()
        fill_split(info, perm[...], stage, own, near, ypart, ycpart, xpart, xcpart)

    def work(here, rows):
        finals, normeds = [], []
        for spot, row, half, lanes, among in places_of(here, rows):
            inner = stage[half, row]
            final = (normalise(inner)[0] * gain1[...]).astype(BF16)
            inner_out[spot, :, lanes] = inner.astype(BF16)
            final_out[spot, :, lanes] = final
            finals.append(final)
        product = dot_nn(final1_t[...], side_by_side(finals))
        for spot, row, half, lanes, among in places_of(here, rows):
            gate = gate1[spot, :, lanes].astype(F32)
            update = product[:, among] * gate
            slope_out[spot, :, lanes] = (update * (1.0 - gate)).astype(BF16)
            middle = (turned(pair, spot, lanes) + update).astype(BF16)
            middle_out[spot, :, lanes] = middle
            normed = (normalise(middle.astype(F32))[0] * norm2[...]).astype(BF16)
            normed_out[spot, :, lanes] = normed
            normeds.append(normed)
        mixture = dot_nn(proj2_t[...], side_by_side(normeds))
        put_gated(info, part, mixture, here, rows, left_st, right_st, gate_out, factor_out)

    each_rows(work)

    @last_step
    def _():
        core = info[2]
        beyond = slice(LANES, 3 * LANES)
        for owner, main, yo, xo in ((core, o_own, o_y, o_x), (1 - core, o_near, o_yc, o_xc)):
            for at in CHUNKS:
                kept = split_out(info, perm[...], left_st, owner, at)
                give_chunk(main, 0, at, LOW, kept[0])
                give_chunk(yo, 0, at, LOW, kept[1])
                give_chunk(main, 1, at, LOW, kept[2])
                give_chunk(xo, 0, at, LOW, kept[3])
                for group, out in ((0, yo), (1, xo)):
                    channel = owner * (2 * GROUP) + group * GROUP + at
                    right = dot_nn(perm[...], get_chunk(right_st, (0, 1), channel)).astype(BF16)
                    give_chunk(main, group, at, beyond, right)
                    give_chunk(out, 0, at, beyond, right)


def turn_kernel(
    part, info, gate2, cot, own, ypart, xpart, ycpart, xcpart, near,
    gain2, final2_t, final2_w,
    gate_out, final_out, product_out, same0, same1, other0, other1, to_core, stage, out_st, perm,
):
    core = info[2]

    @first_step
    def _():
        perm[...] = reorder()
        for owner, mine, xp, yp in ((core, own, xpart, ypart), (1 - core, near, xcpart, ycpart)):
            for at in CHUNKS:
                channel = owner * (2 * GROUP) + at
                fill_sum(perm[...], stage, channel, (mine, 0, at, BOTH), (xp, 0, at, BOTH))
                fill_sum(perm[...], stage, channel + GROUP, (mine, 1, at, BOTH), (yp, 0, at, BOTH))

    def work(here, rows):
        finals, products = [], []
        for spot, row, half, lanes, among in places_of(here, rows):
            final = (normalise(stage[half, row])[0] * gain2[...]).astype(BF16)
            final_out[spot, :, lanes] = final
            finals.append(final)
            grad_product = turned(cot, spot, lanes) * gate2[spot, :, lanes].astype(F32)
            grad_product = grad_product.astype(BF16)
            product_out[spot, :, lanes] = grad_product
            products.append(grad_product)
        product = dot_nn(final2_t[...], side_by_side(finals))
        grad_final = dot_nn(final2_w[...], side_by_side(products))
        for spot, row, half, lanes, among in places_of(here, rows):
            gate = gate2[spot, :, lanes].astype(F32)
            grad_gate = turned(cot, spot, lanes) * product[:, among] * gate * (1.0 - gate)
            gate_out[spot, :, lanes] = grad_gate.astype(BF16)
            hat, spread = normalise(stage[half, row])
            grad_inner = normalise_back(grad_final[:, among] * gain2[...], hat, spread)
            out_st[half, row] = grad_inner.astype(BF16)

    each_rows(work)

    @last_step
    def _():
        for owner, outs in ((core, (same0, same1)), (1 - core, (other0, other1))):
            for group, out in enumerate(outs):
                for at in CHUNKS:
                    channel = owner * (2 * GROUP) + group * GROUP + at
                    value = dot_nn(perm[...], get_chunk(out_st, (0, 1), channel)).astype(BF16)
                    give_chunk(out, 0, at, BOTH, value)
                    if out is other0 or out is other1:
                        give_chunk(to_core, group, at, BOTH, value)


def mixture_chunk(left_st, right_st, factors, gate_in, spot, row, half, lanes):
    size = left_st.shape[2]
    grads = (left_st[half, row], right_st[half, row])
    blocks = [
        (grads[n % 2] * factors[spot, n * size : (n + 1) * size, lanes].astype(F32)).astype(BF16)
        for n in range(4)
    ]
    return jnp.concatenate(blocks + [gate_in[spot, :, lanes]], axis=0)


def inward_kernel(
    part, info, middle, gate1, cot, inner_in, gate_in, factors, slopes, own, ypart, xpart, ycpart, xcpart, near,
    norm2, proj2_w, gain1, final1_w,
    grad_out, gate_out, mixture_out, product_out, o_own, o_near, o_y, o_yc, o_x, o_xc,
    left_st, right_st, out_st, perm,
):
    core = info[2]

    @first_step
    def _():
        perm[...] = reorder()
        fill_split(info, perm[...], left_st, own, near, ypart, ycpart, xpart, xcpart)
        beyond = slice(LANES, 3 * LANES)
        for owner, mine, yp, xp in ((core, own, ypart, xpart), (1 - core, near, ycpart, xcpart)):
            for at in CHUNKS:
                channel = owner * (2 * GROUP) + at
                fill_sum(perm[...], right_st, channel, (mine, 0, at, beyond), (yp, 0, at, beyond))
                fill_sum(
                    perm[...], right_st, channel + GROUP, (mine, 1, at, beyond), (xp, 0, at, beyond)
                )

    def work(here, rows):
        mixtures, products = [], []
        for spot, row, half, lanes, among in places_of(here, rows):
            mixture = mixture_chunk(left_st, right_st, factors, gate_in, spot, row, half, lanes)
            mixture_out[spot, :, lanes] = mixture
            mixtures.append(mixture)
        grad_normed = dot_nn(proj2_w[...], side_by_side(mixtures))
        for spot, row, half, lanes, among in places_of(here, rows):
            hat, spread = normalise(middle[spot, :, lanes].astype(F32))
            grad = normalise_back(grad_normed[:, among] * norm2[...], hat, spread)
            grad = grad + turned(cot, spot, lanes)
            grad_out[spot, :, lanes] = grad
            gate_out[spot, :, lanes] = (grad * slopes[spot, :, lanes].astype(F32)).astype(BF16)
            grad_product = (grad * gate1[spot, :, lanes].astype(F32)).astype(BF16)
            product_out[spot, :, lanes] = grad_product
            products.append(grad_product)
        grad_final = dot_nn(final1_w[...], side_by_side(products))
        for spot, row, half, lanes, among in places_of(here, rows):
            hat, spread = normalise(inner_in[spot, :, lanes].astype(F32))
            grad_inner = normalise_back(grad_final[:, among] * gain1[...], hat, spread)
            out_st[half, row] = grad_inner.astype(BF16)

    each_rows(work)

    @last_step
    def _():
        for owner, main, yo, xo in ((core, o_own, o_y, o_x), (1 - core, o_near, o_yc, o_xc)):
            for at in CHUNKS:
                kept = split_out(info, perm[...], out_st, owner, at)
                give_chunk(main, 0, at, LOW, kept[0])
                give_chunk(yo, 0, at, LOW, kept[1])
                give_chunk(main, 1, at, LOW, kept[2])
                give_chunk(xo, 0, at, LOW, kept[3])


def weight_kernel(info, *refs):
    *refs, total = refs
    (mixtures, normeds, *pairs) = paired(refs)
    width, channels = mixtures[0].shape[1], normeds[0].shape[1]

    @pl.when(pl.program_id(0) == 0)
    def _():
        total[...] = jnp.zeros_like(total)

    for part in range(PARTS):
        for first in range(0, mixtures[part].shape[0], PAIRED):
            rows = [first + n for n in range(PAIRED)]
            mixture, normed = stacked(mixtures[part], rows), stacked(normeds[part], rows)
            total[:width, :] += dot_nt(mixture, normed)
            for n, (finals, products) in enumerate((pairs[:2], pairs[2:])):
                where = slice(width + n * channels, width + (n + 1) * channels)
                final, product = stacked(finals[part], rows), stacked(products[part], rows)
                total[where, :] += dot_nt(final, product)


def exit_kernel(
    part, info, pair, grad_in, gate_in, factors, own, ypart, xpart, ycpart, xcpart, near,
    norm1, proj1_w, early, *rest,
):
    out, gproj, *rest, left_st, right_st, perm = rest
    if part:
        before, unused, out, gproj, packed = (out, gproj, *rest)
    core = info[2]

    @first_step
    def _():
        perm[...] = reorder()
        gproj[...] = before[...] if part else jnp.zeros_like(gproj)
        beyond = slice(2 * LANES, 4 * LANES)
        for owner, mine, yp, xp in ((core, own, ypart, xpart), (1 - core, near, ycpart, xcpart)):
            for group, lefts, rights in ((0, yp, xp), (1, xp, yp)):
                for at in CHUNKS:
                    channel = owner * (2 * GROUP) + group * GROUP + at
                    fill_sum(
                        perm[...], left_st, channel, (mine, group, at, BOTH), (lefts, group, at, BOTH)
                    )
                    fill_sum(
                        perm[...],
                        right_st,
                        channel,
                        (mine, group, at, beyond),
                        (rights, group, at, BOTH),
                    )

    def work(here, rows):
        mixtures, normeds = [], []
        for spot, row, half, lanes, among in places_of(here, rows):
            normeds.append(
                (normalise(turned(pair, spot, lanes))[0] * norm1[...]).astype(BF16)
            )
            mixtures.append(
                mixture_chunk(left_st, right_st, factors, gate_in, spot, row, half, lanes)
            )
        mixture = side_by_side(mixtures)
        gproj[...] += dot_nt(mixture, side_by_side(normeds))
        grad_normed = dot_nn(proj1_w[...], mixture)
        for spot, row, half, lanes, among in places_of(here, rows):
            hat, spread = normalise(turned(pair, spot, lanes))
            grad = normalise_back(grad_normed[:, among] * norm1[...], hat, spread)
            out[spot, lanes, :] = (grad_in[spot, :, lanes] + grad).T

    each_rows(work)

    if part:

        @last_step
        def _():
            size = gproj.shape[0]
            packed[:size, :] = gproj[...].astype(BF16)
            packed[size:, :] = early[...].astype(BF16)


CHANNELS = 8
PARTS = 2


def paired(refs):
    return [refs[n : n + PARTS] for n in range(0, len(refs), PARTS)]


def place(one, two, part):
    return pl.multiple_of((one * 2 + two) * (PARTS * BLOCK) + part * BLOCK, BLOCK)


def places(info, group):
    at, core = info[group], info[2]
    return [
        place(at if n < 2 else 1 - at, core if n % 2 == 0 else 1 - core, part)
        for n in range(4)
        for part in range(PARTS)
    ]


def take(ref, group, h):
    return ref[group, h] if len(ref.shape) == 4 else ref[h]


def joined(quads, group, h):
    return jnp.concatenate([take(ref, group, h) for refs in quads for ref in refs], axis=0)


def gather(stage, slot, wheres, quads, group, h):
    for where, ref in zip(wheres, [ref for refs in quads for ref in refs]):
        stage[slot, pl.ds(where, BLOCK), :] = take(ref, group, h)
    return stage[slot]


def give(refs, group, h, lanes, value):
    if len(refs.shape) == 4:
        refs[group, h, :, lanes] = value
    else:
        refs[h, :, lanes] = value


def scatter(quads, group, h, lanes, value):
    for n, ref in enumerate([ref for refs in quads for ref in refs]):
        give(ref, group, h, lanes, value[n * BLOCK : (n + 1) * BLOCK])


def scatter_from(stage, slot, wheres, quads, group, h, lanes):
    for where, ref in zip(wheres, [ref for refs in quads for ref in refs]):
        give(ref, group, h, lanes, stage[slot, pl.ds(where, BLOCK), :])


def outgoing_kernel(info, *refs):
    *refs, stage = refs
    *refs, o_own, o_near, o_y, o_yc, o_x, o_xc = refs
    a_own, b_own, a_y, b_x, a_yc, b_xc, near = paired(refs)
    a_near, b_near = [ref.at[:2] for ref in near], [ref.at[2:] for ref in near]
    along_a, along_b = (a_own, a_near, a_y, a_yc), (b_own, b_near, b_x, b_xc)
    for h in range(CHANNELS):
        for group in range(2):
            lefts, rights = (along_a, along_b) if group == 0 else (along_b, along_a)
            far = (o_y, o_yc) if group == 0 else (o_x, o_xc)
            right = gather(stage, 2 * h + group, places(info, group), rights, group, h)
            inner = dot_nt(joined(lefts, group, h), right).astype(BF16)
            for n, out in enumerate((o_own, o_near) + far):
                rows = PARTS * BLOCK
                give(out, group, h, slice(0, LANES), inner[n * rows : (n + 1) * rows])


def halves(quads, group, h):
    both = joined(quads, group, h)
    return both[:, :LANES], both[:, LANES:]


def incoming_kernel(info, *refs):
    *refs, stage = refs
    own, ypart, xpart, ycpart, xcpart, near, o_own, o_near, o_x, o_xc, o_y, o_yc = paired(refs)
    for h in range(CHANNELS):
        for group in range(2):
            far = (ypart, ycpart) if group == 0 else (xpart, xcpart)
            outs = (o_own, o_near) + ((o_x, o_xc) if group == 0 else (o_y, o_yc))
            slot = 2 * h + group
            left, right = halves((own, near) + far, group, h)
            stage[slot] = dot_tn(left, right).astype(BF16)
            scatter_from(stage, slot, places(info, group), outs, group, h, slice(0, 2 * LANES))


def incoming_back_kernel(info, *refs):
    *refs, stage = refs
    own, ypart, xpart, ycpart, xcpart, near, *more = paired(refs)
    same0, same1, g_y, g_x, g_yc, g_xc, g_near, *more = more
    o_own, o_near, o_y, o_yc, o_x, o_xc = more
    for h in range(CHANNELS):
        for group in range(2):
            far = (ypart, ycpart) if group == 0 else (xpart, xcpart)
            grads = (same0, g_near, g_x, g_xc) if group == 0 else (same1, g_near, g_y, g_yc)
            outs = (o_own, o_near) + ((o_y, o_yc) if group == 0 else (o_x, o_xc))
            grad = gather(stage, 2 * h + group, places(info, group), grads, group, h)
            left, right = halves((own, near) + far, group, h)
            scatter(outs, group, h, slice(0, LANES), dot_nt(right, grad).astype(BF16))
            scatter(outs, group, h, slice(LANES, 3 * LANES), dot_nn(left, grad).astype(BF16))


def outgoing_back_kernel(info, *refs):
    *refs, stage, back = refs
    a_own, b_own, a_y, b_x, a_yc, b_xc, near, *more = paired(refs)
    a_near, b_near = [ref.at[:2] for ref in near], [ref.at[2:] for ref in near]
    g_own, g_y, g_x, g_yc, g_xc, g_near, o_own, o_near, o_y, o_yc, o_x, o_xc = more
    along_a, along_b = (a_own, a_near, a_y, a_yc), (b_own, b_near, b_x, b_xc)
    first, second = slice(0, 2 * LANES), slice(2 * LANES, 4 * LANES)
    for h in range(CHANNELS):
        for group in range(2):
            lefts, rights = (along_a, along_b) if group == 0 else (along_b, along_a)
            far = (g_y, g_yc) if group == 0 else (g_x, g_xc)
            left_far, right_far = ((o_y, o_yc), (o_x, o_xc)) if group == 0 else ((o_x, o_xc), (o_y, o_yc))
            slot = 2 * h + group
            wheres = places(info, group)
            right = gather(stage, slot, wheres, rights, group, h)
            grad = joined((g_own, g_near) + far, group, h)
            grad_left = dot_nn(grad, right).astype(BF16)
            back[slot] = dot_tn(grad, joined(lefts, group, h)).astype(BF16)
            core_rows = 2 * PARTS * BLOCK
            scatter((o_own, o_near), group, h, first, grad_left[:core_rows])
            scatter(left_far, group, h, first, grad_left[core_rows:])
            scatter_from(back, slot, wheres[: 2 * PARTS], (o_own, o_near), group, h, second)
            scatter_from(back, slot, wheres[2 * PARTS :], right_far, group, h, first)


def whole(shape):
    return pl.BlockSpec(shape, lambda step, info: (0,) * len(shape))


def rows_of(part, some=SOME):
    def make(shape):
        first = part * (BLOCK // some)
        return pl.BlockSpec(
            (some,) + shape[1:], lambda step, info: (first + step,) + (0,) * (len(shape) - 1)
        )

    return make


def rows_block(part):
    def make(shape):
        return pl.BlockSpec(
            shape[:-2] + (BLOCK, shape[-1]),
            lambda step, info: (0,) * (len(shape) - 2) + (part, 0),
        )

    return make


def anywhere(shape):
    return pl.BlockSpec(memory_space=pl.ANY)


def channel_rows(shape):
    if len(shape) == 4:
        return pl.BlockSpec((shape[0], CHANNELS) + shape[2:], lambda step, info: (0, step, 0, 0))
    return pl.BlockSpec((CHANNELS,) + shape[1:], lambda step, info: (step, 0, 0))


def call(kernel, info, steps, ins, outs, scratch, aliases={}):
    return pl.pallas_call(
        kernel,
        grid_spec=pltpu.PrefetchScalarGridSpec(
            num_scalar_prefetch=1,
            grid=(steps,),
            in_specs=[make(array.shape) for array, make in ins],
            out_specs=[make(shape) for shape, unused, make in outs],
            scratch_shapes=scratch,
        ),
        out_shape=[jax.ShapeDtypeStruct(shape, dtype) for shape, dtype, unused in outs],
        compiler_params=pltpu.CompilerParams(vmem_limit_bytes=VMEM),
        input_output_aliases=aliases,
    )(info, *[array for array, unused in ins])


class Links:
    def __init__(self):
        self.last = {}

    def send(self, array, offset, first=None):
        count = lax.axis_size("axial")
        if first is not None:
            array, unused = lax.optimization_barrier((array, first))
        if offset in self.last and offset in (X, Y):
            array, unused = lax.optimization_barrier((array, self.last[offset]))
        self.last[offset] = lax.ppermute(
            array, "axial", [(n, n ^ offset) for n in range(count)]
        )
        return self.last[offset]

    def __call__(self, *sends, between=None):
        results = [[] for unused in sends]
        for part in range(len(sends[0][0])):
            for result, (arrays, offset) in zip(results, sends):
                result.append(self.send(arrays[part], offset, between if part else None))
        return results


CORE, X, Y = 1, 2, 4


def add_up(share):
    count = lax.axis_size("axial")
    rows, width = share.shape
    shares = share.reshape(count, rows // count, width)
    parts = lax.all_to_all(shares, "axial", split_axis=0, concat_axis=0, tiled=True)
    mine = parts.astype(F32).sum(axis=0).astype(BF16)
    depth = lax.axis_size("dp")
    terms = [mine] + [
        lax.ppermute(mine, "dp", [(n, n ^ offset) for n in range(depth)])
        for offset in range(1, depth)
    ]
    terms = [term.astype(F32) for term in terms]
    while len(terms) > 1:
        terms = [terms[n] + terms[n + 1] for n in range(0, len(terms), 2)]
    copies = jnp.broadcast_to(terms[0].astype(BF16)[None], shares.shape)
    return lax.all_to_all(copies, "axial", split_axis=0, concat_axis=0, tiled=True).reshape(
        rows, width
    )


def gain_grad(weight_grad, weight, gain_row):
    return jnp.sum((weight.astype(F32) * weight_grad).T, axis=0, keepdims=True) / gain_row


def finish_kernel(
    scale, info, sums, proj1, final1, proj2, final2, norm1, gain1, norm2, gain2,
    o_norm1, o_proj1, o_gain1, o_final1, o_norm2, o_proj2, o_gain2, o_final2,
):
    width, channels = proj1.shape[1], final1.shape[1]
    takes = (
        (0, True, proj1, norm1, o_proj1, o_norm1),
        (width, True, proj2, norm2, o_proj2, o_norm2),
        (2 * width, False, final2, gain2, o_final2, o_gain2),
        (2 * width + channels, False, final1, gain1, o_final1, o_gain1),
    )
    for start, flipped, weight, gain, out, gain_out in takes:
        total = sums[start : start + weight.shape[1], :].astype(F32) * scale
        total = total.T if flipped else total
        out[...] = total
        gain_out[...] = gain_grad(total, weight[...].astype(BF16), gain[...])


def fast_body(
    pair,
    cotangent,
    lengths,
    outgo_norm,
    outgo_proj,
    outgo_gain,
    outgo_final,
    incom_norm,
    incom_proj,
    incom_gain,
    incom_final,
):
    rows, tokens, channels = pair.shape[1:]
    hidden = outgo_gain.shape[0]
    index = lax.axis_index("axial")
    info = jnp.stack(
        [(index // 2) % 2, index // 4, index % 2, index * rows, lengths[0]]
    ).astype(jnp.int32)
    hop = Links()
    pair = pair[0]
    cot = cotangent[0]
    parts = range(PARTS)
    turns = GROUP // CHANNELS
    stage = pltpu.VMEM((2, BLOCK, hidden, LANES), F32)
    out_stage = pltpu.VMEM((2, BLOCK, hidden, LANES), BF16)
    perm = pltpu.VMEM((BLOCK * BLOCK, BLOCK * BLOCK), BF16)
    streamed = rows_of(0)
    square = pltpu.VMEM((2 * CHANNELS, 4 * rows, tokens), BF16)

    def two(width, height=BLOCK, make=whole, groups=2):
        return ((groups, GROUP, height, width), BF16, make)

    def one(width, height=BLOCK, make=whole):
        return ((GROUP, height, width), BF16, make)

    turned_block = ((BLOCK, channels, tokens), BF16, streamed)
    factor_block = ((BLOCK, 4 * hidden, tokens), BF16, streamed)
    mixture_block = ((BLOCK, 5 * hidden, tokens), BF16, streamed)

    def cells(kernel, ins, outs, scratch, more=lambda part: []):
        results = []
        for part in parts:
            carried = ins(part, results)
            results.append(
                call(functools.partial(kernel, part), info, STEPS, carried, outs + more(part), scratch)
            )
        shared = results[-1][len(outs) :]
        return [list(each) for each in zip(*results)] + list(shared)

    def wholes(arrays):
        return [(array, whole) for array in arrays]

    def triangle(kernel, operands, outs, scratch, split=PARTS):
        ins = [(array, channel_rows) for arrays in operands for array in arrays]
        each = [out for out in outs for unused in range(split)]
        results = call(kernel, info, turns, ins, each, scratch)
        return [list(results[n : n + split]) for n in range(0, len(results), split)]

    raw = (outgo_gain[None], outgo_final, incom_norm[None], incom_proj, incom_gain[None], incom_final)
    gain_wide = ((channels, LANES), F32, whole)
    proj_turned = ((5 * hidden, channels), BF16, whole)
    proj_plain = ((channels, 5 * hidden), BF16, whole)
    final_plain = ((hidden, channels), BF16, whole)
    (
        a_same, a_other, b_same, b_other, to_core, gate_one, factors_one,
        norm1, gain1, norm2, gain2, proj2_t, final1_t, final2_t,
        proj1, final1, proj2, final2,
    ) = cells(
        entry_kernel,
        lambda part, unused: [(pair, rows_of(part)), (outgo_norm[None], whole), (outgo_proj, whole)]
        + (wholes(raw) if part else []),
        [two(tokens)] * 4 + [two(tokens, groups=4), turned_block, factor_block],
        [
            out_stage,
            out_stage,
            pltpu.VMEM((channels, LANES), F32),
            pltpu.VMEM((5 * hidden, channels), BF16),
            perm,
        ],
        lambda part: (
            [gain_wide] * 4
            + [proj_turned]
            + [final_plain] * 2
            + [proj_plain, final_plain] * 2
            if part
            else []
        ),
    )
    held_one = [a_same, b_same] + hop(
        (a_same, Y), (b_same, X), (a_other, Y | CORE), (b_other, X | CORE), (to_core, CORE)
    )
    own, near, to_y, to_yc, to_x, to_xc = triangle(
        outgoing_kernel,
        held_one,
        [two(LANES, rows, channel_rows)] * 2 + [one(LANES, rows, channel_rows)] * 4,
        [square],
        split=1,
    )
    back_one = [
        own,
        *hop(
            (to_y, Y), (to_x, X), (to_yc, Y | CORE), (to_xc, X | CORE), (near, CORE)
        ),
    ]

    (
        middle, inner_one, gate_two, factors_two, normed_two, finals_one, slopes_one,
        own, near, to_y, to_yc, to_x, to_xc,
    ) = cells(
        middle_kernel,
        lambda part, unused: [(pair, rows_of(part))]
        + [(array, rows_block(part)) for array, in back_one]
        + [(gate_one[part], streamed)]
        + wholes((gain1, final1_t, norm2, proj2_t)),
        [turned_block] * 3
        + [factor_block]
        + [turned_block] * 3
        + [two(3 * LANES)] * 2 + [one(3 * LANES)] * 4,
        [stage, out_stage, out_stage, perm],
    )
    held_two = [
        own,
        *hop(
            (to_y, Y), (to_x, X), (to_yc, Y | CORE), (to_xc, X | CORE), (near, CORE)
        ),
    ]
    own, near, to_x, to_xc, to_y, to_yc = triangle(
        incoming_kernel,
        held_two,
        [two(tokens, make=channel_rows)] * 2 + [one(tokens, make=channel_rows)] * 4,
        [square],
    )
    back_two = [
        own,
        *hop(
            (to_y, Y), (to_x, X), (to_yc, Y | CORE), (to_xc, X | CORE), (near, CORE)
        ),
    ]

    gate_grad_two, finals_two, products_two, same0, same1, other0, other1, to_core = cells(
        turn_kernel,
        lambda part, done: [(gate_two[part], streamed), (cot, rows_of(part))]
        + wholes(arrays[part] for arrays in back_two)
        + wholes((gain2, final2_t, final2)),
        [turned_block] * 3 + [one(tokens)] * 4 + [two(tokens)],
        [stage, out_stage, perm],
    )
    grads_two = [
        same0,
        same1,
        *hop(
            (same1, Y), (same0, X), (other1, Y | CORE), (other0, X | CORE), (to_core, CORE)
        ),
    ]
    own, near, to_y, to_yc, to_x, to_xc = triangle(
        incoming_back_kernel,
        held_two + grads_two,
        [two(3 * LANES, make=channel_rows)] * 2 + [one(3 * LANES, make=channel_rows)] * 4,
        [square],
    )
    rows_two = [
        own,
        *hop(
            (to_y, Y), (to_x, X), (to_yc, Y | CORE), (to_xc, X | CORE), (near, CORE)
        ),
    ]

    (
        grad_middle, gate_grad_one, mixtures_two, products_one,
        own, near, to_y, to_yc, to_x, to_xc,
    ) = cells(
        inward_kernel,
        lambda part, done: [
            (middle[part], streamed),
            (gate_one[part], streamed),
            (cot, rows_of(part)),
            (inner_one[part], streamed),
            (gate_grad_two[part], streamed),
            (factors_two[part], streamed),
            (slopes_one[part], streamed),
        ]
        + wholes(arrays[part] for arrays in rows_two)
        + wholes((norm2, proj2, gain1, final1)),
        [((BLOCK, channels, tokens), F32, streamed), turned_block, mixture_block, turned_block]
        + [two(LANES)] * 2
        + [one(LANES)] * 4,
        [stage, stage, out_stage, perm],
    )
    grads_one = [
        own,
        *hop(
            (to_y, Y), (to_x, X), (to_yc, Y | CORE), (to_xc, X | CORE), (near, CORE)
        ),
    ]
    own, near, to_y, to_yc, to_x, to_xc = triangle(
        outgoing_back_kernel,
        held_one + grads_one,
        [two(2 * tokens, make=channel_rows)] * 2 + [two(tokens, make=channel_rows)] * 4,
        [square, square],
    )
    kept = (mixtures_two, normed_two, finals_two, products_two, finals_one, products_one)
    (early,) = call(
        weight_kernel,
        info,
        4,
        [
            (array, rows_of(0, BLOCK // 4))
            for arrays in kept
            for array in arrays
        ],
        [((5 * hidden + 2 * channels, channels), F32, whole)],
        [],
    )
    rows_one = [own] + hop(
        (to_y, Y), (to_x, X), (to_yc, Y | CORE), (to_xc, X | CORE), (near, CORE), between=early
    )
    exit_ins = 10 + 3 + 1 + 1
    result = None
    for part in parts:
        result = call(
            functools.partial(exit_kernel, part),
            info,
            STEPS,
            [
                (pair, rows_of(part)),
                (grad_middle[part], streamed),
                (gate_grad_one[part], streamed),
                (factors_one[part], streamed),
            ]
            + wholes(arrays[part] for arrays in rows_one)
            + wholes((norm1, proj1, early))
            + ([(result[1], whole), (result[0], anywhere)] if part else []),
            [
                ((rows, tokens, channels), F32, rows_of(part)),
                ((5 * hidden, channels), F32, whole),
            ]
            + ([((10 * hidden + 2 * channels, channels), BF16, whole)] if part else []),
            [stage, stage, perm],
            {exit_ins: 0} if part else {},
        )
    grad_begin, unused, packed = result
    sums = add_up(packed)
    scale = 1.0 / math.sqrt(lax.axis_size("dp") * tokens * tokens)
    weights = (outgo_proj, outgo_final, incom_proj, incom_final)
    gains = (outgo_norm, outgo_gain, incom_norm, incom_gain)
    order = (outgo_norm[None], outgo_proj, outgo_gain[None], outgo_final)
    order += (incom_norm[None], incom_proj, incom_gain[None], incom_final)
    totals = call(
        functools.partial(finish_kernel, scale),
        info,
        1,
        wholes((sums,) + weights + tuple(gain[None] for gain in gains)),
        [(array.shape, F32, whole) for array in order],
        [],
    )
    return (grad_begin[None],) + tuple(
        total.reshape(-1) if total.shape[0] == 1 else total for total in totals
    )


def solution(mesh):
    def body(pair, *rest):
        rows, tokens, channels = pair.shape[1:]
        hidden = rest[3].shape[0]
        plane = mesh.shape["axial"] == 8 and rows == 32 and tokens == 2 * LANES
        if plane and channels == LANES and hidden == 4 * GROUP:
            return fast_body(pair, *rest)
        return plain_body(pair, *rest)

    return jax.shard_map(
        body,
        mesh=mesh,
        in_specs=(P("dp", "axial", None, None), P("dp", "axial", None, None), P("dp")) + (P(),) * 8,
        out_specs=(P("dp", "axial", None, None),) + (P(),) * 8,
        check_vma=False,
    )
```

```python
import functools
import math

import jax
import jax.numpy as jnp
from jax import lax
from jax.experimental import pallas as pl
from jax.experimental.pallas import tpu as pltpu
from jax.sharding import PartitionSpec as P

EPSILON = 1e-05


def rounded(inputs):
    return lax.optimization_barrier(inputs.astype(jnp.bfloat16)).astype(jnp.float32)


def layer_norm(inputs, factor):
    average = jnp.mean(inputs, axis=-1, keepdims=True)
    centered = inputs - average
    spread = jnp.mean(centered * centered, axis=-1, keepdims=True)
    return centered * lax.rsqrt(spread + EPSILON) * factor


def gating(mixture, pair_mask, hidden):
    left_part = (
        mixture[:, :hidden] * jax.nn.sigmoid(mixture[:, 2 * hidden : 3 * hidden]) * pair_mask
    )
    right_part = (
        mixture[:, hidden : 2 * hidden]
        * jax.nn.sigmoid(mixture[:, 3 * hidden : 4 * hidden])
        * pair_mask
    )
    gate_part = jax.nn.sigmoid(mixture[:, 4 * hidden :])
    return (left_part, right_part, gate_part)


def entry(flat_pair, norm_gain, projection, pair_mask, hidden):
    normed = layer_norm(flat_pair, norm_gain).astype(jnp.bfloat16)
    mixture = jnp.dot(normed, projection.astype(jnp.bfloat16), preferred_element_type=jnp.float32)
    left_part, right_part, gate_part = gating(mixture, pair_mask, hidden)
    return (normed, mixture, left_part, right_part, gate_part)


def entry_back(
    flat_pair,
    norm_gain,
    projection,
    pair_mask,
    hidden,
    normed,
    mixture,
    grad_left,
    grad_right,
    grad_gate,
):
    unused, pull_gate = jax.vjp(lambda inner_mix: gating(inner_mix, pair_mask, hidden), mixture)
    grad_mixture = pull_gate((grad_left, grad_right, grad_gate))[0].astype(jnp.bfloat16)
    grad_projection = jnp.dot(normed.T, grad_mixture, preferred_element_type=jnp.float32)
    grad_normed = jnp.dot(
        grad_mixture, projection.astype(jnp.bfloat16).T, preferred_element_type=jnp.float32
    )
    unused, pull_norm = jax.vjp(layer_norm, flat_pair, norm_gain)
    grad_flat, grad_gain = pull_norm(grad_normed)
    return (grad_flat, grad_gain, grad_projection)


def leave(inner_sum, gate_part, out_gain, final_weight):
    final_normed = layer_norm(inner_sum, out_gain).astype(jnp.bfloat16)
    product = jnp.dot(
        final_normed, final_weight.astype(jnp.bfloat16), preferred_element_type=jnp.float32
    )
    return (final_normed, product, product * gate_part)


def leave_back(inner_sum, gate_part, out_gain, final_weight, final_normed, product, grad_update):
    grad_product = (grad_update * gate_part).astype(jnp.bfloat16)
    grad_gate = grad_update * product
    grad_final = jnp.dot(final_normed.T, grad_product, preferred_element_type=jnp.float32)
    grad_normed = jnp.dot(
        grad_product, final_weight.astype(jnp.bfloat16).T, preferred_element_type=jnp.float32
    )
    unused, pull_norm = jax.vjp(layer_norm, inner_sum, out_gain)
    grad_inner, grad_gain = pull_norm(grad_normed)
    return (grad_inner, grad_gate, grad_gain, grad_final)


def channel_major(field, row_count, tokens):
    hidden = field.shape[1]
    return jnp.transpose(field.reshape(row_count, tokens, hidden), (2, 0, 1))


def row_major(field):
    hidden = field.shape[0]
    return jnp.transpose(field, (1, 2, 0)).reshape(-1, hidden)


def plain_body(
    pair,
    cotangent,
    lengths,
    outgo_norm,
    outgo_proj,
    outgo_gain,
    outgo_final,
    incom_norm,
    incom_proj,
    incom_gain,
    incom_final,
):
    row_count = pair.shape[1]
    tokens = pair.shape[2]
    channels = pair.shape[3]
    hidden = outgo_gain.shape[0]
    length = lengths[0]
    first_row = lax.axis_index("axial") * row_count
    row_alive = (first_row + jnp.arange(row_count, dtype=jnp.int32) < length).astype(jnp.float32)
    column_alive = (jnp.arange(tokens, dtype=jnp.int32) < length).astype(jnp.float32)
    pair_mask = (row_alive[:, None] * column_alive[None, :]).reshape(-1, 1)
    flat_start = pair[0].reshape(-1, channels).astype(jnp.float32)
    normed_one, mixture_one, left_one, right_one, gate_one = entry(
        flat_start, outgo_norm, outgo_proj, pair_mask, hidden
    )
    left_first = channel_major(left_one.astype(jnp.bfloat16), row_count, tokens)
    right_first = channel_major(right_one.astype(jnp.bfloat16), row_count, tokens)
    left_owned, right_owned = (
        lax.all_to_all(left_first, "axial", split_axis=0, concat_axis=1, tiled=True),
        lax.all_to_all(right_first, "axial", split_axis=0, concat_axis=1, tiled=True),
    )
    inner_cols = jnp.einsum(
        "hik,hjk->hij", left_owned, right_owned, preferred_element_type=jnp.float32
    )
    inner_one = row_major(
        lax.all_to_all(
            inner_cols.astype(jnp.bfloat16), "axial", split_axis=1, concat_axis=0, tiled=True
        ).astype(inner_cols.dtype)
    )
    final_one, product_one, update_one = leave(inner_one, gate_one, outgo_gain, outgo_final)
    flat_middle = rounded(flat_start + update_one)
    normed_two, mixture_two, left_two, right_two, gate_two = entry(
        flat_middle, incom_norm, incom_proj, pair_mask, hidden
    )
    left_second = channel_major(left_two.astype(jnp.bfloat16), row_count, tokens)
    right_second = channel_major(right_two.astype(jnp.bfloat16), row_count, tokens)
    left_held, right_held = (
        lax.all_to_all(left_second, "axial", split_axis=0, concat_axis=1, tiled=True),
        lax.all_to_all(right_second, "axial", split_axis=0, concat_axis=1, tiled=True),
    )
    inner_held = jnp.einsum(
        "hki,hkj->hij", left_held, right_held, preferred_element_type=jnp.float32
    )
    inner_two = row_major(
        lax.all_to_all(
            inner_held.astype(jnp.bfloat16), "axial", split_axis=1, concat_axis=0, tiled=True
        ).astype(inner_held.dtype)
    )
    final_two, product_two, update_two = leave(inner_two, gate_two, incom_gain, incom_final)
    grad_end = cotangent[0].reshape(-1, channels).astype(jnp.float32)
    grad_inner_two, grad_gate_two, grad_gain_two, grad_final_two = leave_back(
        inner_two, gate_two, incom_gain, incom_final, final_two, product_two, grad_end
    )
    grad_cells_two = channel_major(grad_inner_two.astype(jnp.bfloat16), row_count, tokens)
    grad_held_two = lax.all_to_all(grad_cells_two, "axial", split_axis=0, concat_axis=1, tiled=True)
    left_back, right_back = (
        lax.all_to_all(left_second, "axial", split_axis=0, concat_axis=1, tiled=True),
        lax.all_to_all(right_second, "axial", split_axis=0, concat_axis=1, tiled=True),
    )
    grad_left_held = jnp.einsum(
        "hij,hkj->hki", grad_held_two, right_back, preferred_element_type=jnp.float32
    )
    grad_right_held = jnp.einsum(
        "hki,hij->hkj", left_back, grad_held_two, preferred_element_type=jnp.float32
    )
    grad_left_rows, grad_right_rows = (
        lax.all_to_all(
            grad_left_held.astype(jnp.bfloat16), "axial", split_axis=1, concat_axis=0, tiled=True
        ).astype(grad_left_held.dtype),
        lax.all_to_all(
            grad_right_held.astype(jnp.bfloat16), "axial", split_axis=1, concat_axis=0, tiled=True
        ).astype(grad_right_held.dtype),
    )
    grad_left_two = row_major(grad_left_rows)
    grad_right_two = row_major(grad_right_rows)
    grad_flat_two, grad_norm_two, grad_proj_two = entry_back(
        flat_middle,
        incom_norm,
        incom_proj,
        pair_mask,
        hidden,
        normed_two,
        mixture_two,
        grad_left_two,
        grad_right_two,
        grad_gate_two,
    )
    second_sums = lax.psum(
        (grad_norm_two, grad_proj_two, grad_gain_two, grad_final_two), ("dp", "axial")
    )
    grad_middle = grad_end + grad_flat_two
    grad_inner_one, grad_gate_one, grad_gain_one, grad_final_one = leave_back(
        inner_one, gate_one, outgo_gain, outgo_final, final_one, product_one, grad_middle
    )
    grad_cells_one = channel_major(grad_inner_one.astype(jnp.bfloat16), row_count, tokens)
    grad_owned_one = lax.all_to_all(
        grad_cells_one, "axial", split_axis=0, concat_axis=1, tiled=True
    )
    left_again, right_again = (
        lax.all_to_all(left_first, "axial", split_axis=0, concat_axis=1, tiled=True),
        lax.all_to_all(right_first, "axial", split_axis=0, concat_axis=1, tiled=True),
    )
    grad_left_owned = jnp.einsum(
        "hij,hjk->hik", grad_owned_one, right_again, preferred_element_type=jnp.float32
    )
    grad_right_owned = jnp.einsum(
        "hij,hik->hjk", grad_owned_one, left_again, preferred_element_type=jnp.float32
    )
    grad_left_back, grad_right_back = (
        lax.all_to_all(
            grad_left_owned.astype(jnp.bfloat16), "axial", split_axis=1, concat_axis=0, tiled=True
        ).astype(grad_left_owned.dtype),
        lax.all_to_all(
            grad_right_owned.astype(jnp.bfloat16), "axial", split_axis=1, concat_axis=0, tiled=True
        ).astype(grad_right_owned.dtype),
    )
    grad_left_one = row_major(grad_left_back)
    grad_right_one = row_major(grad_right_back)
    grad_flat_one, grad_norm_one, grad_proj_one = entry_back(
        flat_start,
        outgo_norm,
        outgo_proj,
        pair_mask,
        hidden,
        normed_one,
        mixture_one,
        grad_left_one,
        grad_right_one,
        grad_gate_one,
    )
    grad_begin = grad_middle + grad_flat_one
    first_sums = lax.psum(
        (grad_norm_one, grad_proj_one, grad_gain_one, grad_final_one), ("dp", "axial")
    )
    totals = tuple(first_sums) + tuple(second_sums)
    scale = 1.0 / math.sqrt(lax.axis_size("dp") * tokens * tokens)
    return (
        grad_begin.reshape(1, row_count, tokens, channels),
        totals[0] * scale,
        totals[1] * scale,
        totals[2] * scale,
        totals[3] * scale,
        totals[4] * scale,
        totals[5] * scale,
        totals[6] * scale,
        totals[7] * scale,
    )


BF16 = jnp.bfloat16
F32 = jnp.float32
BLOCK = 16
PAIRED = 2
STEPS = 4
SOME = BLOCK // STEPS
LANES = 128
GROUP = 32
VMEM = 56 * 1024 * 1024


def dot_nn(a, b):
    return lax.dot_general(a, b, (((1,), (0,)), ((), ())), preferred_element_type=F32)


def dot_nt(a, b):
    return lax.dot_general(a, b, (((1,), (1,)), ((), ())), preferred_element_type=F32)


def dot_tn(a, b):
    return lax.dot_general(a, b, (((0,), (0,)), ((), ())), preferred_element_type=F32)


def normalise(v):
    centered = v - jnp.mean(v, axis=0, keepdims=True)
    spread = lax.rsqrt(jnp.mean(centered * centered, axis=0, keepdims=True) + EPSILON)
    return centered * spread, spread


def normalise_back(grad, hat, spread):
    first = jnp.mean(grad, axis=0, keepdims=True)
    second = jnp.mean(grad * hat, axis=0, keepdims=True)
    return spread * (grad - first - hat * second)


def reorder():
    size = BLOCK * BLOCK
    one = lax.broadcasted_iota(jnp.int32, (size, size), 0)
    two = lax.broadcasted_iota(jnp.int32, (size, size), 1)
    return jnp.where((one % BLOCK) * BLOCK + one // BLOCK == two, 1.0, 0.0).astype(BF16)


def chunk(ref, group, at, lanes):
    if len(ref.shape) == 4:
        block = ref[group, at : at + BLOCK, :, lanes]
    else:
        block = ref[at : at + BLOCK, :, lanes]
    return block.reshape(BLOCK * BLOCK, block.shape[2])


def put_chunk(stage, half, channel, value):
    channel = pl.multiple_of(channel, BLOCK)
    for row in range(BLOCK):
        stage[half, row, pl.ds(channel, BLOCK), :] = value[row * BLOCK : (row + 1) * BLOCK]


def get_chunk(stage, halves, channel):
    channel = pl.multiple_of(channel, BLOCK)
    return jnp.concatenate(
        [
            jnp.concatenate(
                [stage[half, row, pl.ds(channel, BLOCK), :] for row in range(BLOCK)], axis=0
            )
            for half in halves
        ],
        axis=1,
    )


def give_chunk(ref, group, at, lanes, value):
    block = value.astype(BF16).reshape(BLOCK, BLOCK, value.shape[1])
    if len(ref.shape) == 4:
        ref[group, at : at + BLOCK, :, lanes] = block
    else:
        ref[at : at + BLOCK, :, lanes] = block


LOW, HIGH, BOTH = slice(0, LANES), slice(LANES, 2 * LANES), slice(0, 2 * LANES)
CHUNKS = range(0, GROUP, BLOCK)


def half_swap(first, second):
    low = lax.broadcasted_iota(jnp.int32, first.shape, first.ndim - 1) < LANES // 2
    axis = first.ndim - 1
    return (
        jnp.where(low, first, pltpu.roll(second, LANES // 2, axis)),
        jnp.where(low, pltpu.roll(first, LANES // 2, axis), second),
    )


def pick(flag, zero, one):
    return jnp.where(flag == 0, zero, one)


def mask_chunk(info, part, row, half):
    token = lax.broadcasted_iota(jnp.int32, (1, LANES), 1) + half * LANES
    live = (info[3] + part * BLOCK + row < info[4]).astype(F32)
    return (token < info[4]).astype(F32) * live


def each_rows(work):
    step = pl.program_id(0)

    @pl.loop(0, SOME // PAIRED)
    def _(turn):
        here = [turn * PAIRED + n for n in range(PAIRED)]
        work(here, [step * SOME + row for row in here])


def first_step(work):
    pl.when(pl.program_id(0) == 0)(work)


def last_step(work):
    pl.when(pl.program_id(0) == STEPS - 1)(work)


def places_of(here, rows):
    for n, (spot, row) in enumerate(zip(here, rows)):
        for half in range(2):
            start = (2 * n + half) * LANES
            yield spot, row, half, (LOW, HIGH)[half], slice(start, start + LANES)


def turned(ref, spot, lanes):
    return ref[spot, lanes, :].astype(F32).T


def stacked(ref, rows):
    return jnp.concatenate([ref[row] for row in rows], axis=1)


def side_by_side(chunks):
    return jnp.concatenate(chunks, axis=1)


def put_gated(info, part, mixture, here, rows, left_st, right_st, gate_out, factor_out):
    size = left_st.shape[2]
    for spot, row, half, lanes, among in places_of(here, rows):
        mask = mask_chunk(info, part, row, half)
        for block, stage in enumerate((left_st, right_st)):
            gate = opened(mixture[(2 + block) * size : (3 + block) * size, among])
            opening = gate * mask
            side = mixture[block * size : (block + 1) * size, among] * opening
            stage[half, row] = side.astype(BF16)
            factor_out[spot, block * size : (block + 1) * size, lanes] = opening.astype(BF16)
            slope = (side * (1.0 - gate)).astype(BF16)
            factor_out[spot, (2 + block) * size : (3 + block) * size, lanes] = slope
        gate_out[spot, :, lanes] = opened(mixture[4 * size :, among]).astype(BF16)


def opened(gate):
    return 0.5 * jnp.tanh(gate) + 0.5


def column(row):
    return jnp.broadcast_to(row, (LANES, row.shape[1])).T


def halved_turned(weight):
    values = 2 * weight.shape[0]
    return jnp.concatenate([weight[:, :values].T, weight[:, values:].T * 0.5], axis=0).astype(BF16)


def entry_kernel(part, info, pair, norm_row, proj_w, *rest):
    if part:
        raw, rest = rest[:6], rest[6:]
        gain1, final1, norm2, proj2, gain2, final2 = raw
        prepared, rest = rest[7:18], rest[:7] + rest[18:]
    a_same, a_other, b_same, b_other, to_core, gate_out, factor_out, *rest = rest
    left_st, right_st, norm, proj_t, perm = rest
    hidden = proj_w.shape[1] // 5

    @first_step
    def _():
        norm[...] = column(norm_row[...])
        proj_t[...] = halved_turned(proj_w[...])
        perm[...] = reorder()
        if part:
            for row, out in zip((norm_row, gain1, norm2, gain2), prepared[:4]):
                out[...] = column(row[...])
            prepared[4][...] = halved_turned(proj2[...])
            for weight, out in zip((final1, final2), prepared[5:7]):
                out[...] = weight[...].T.astype(BF16)
            for weight, out in zip((proj_w, final1, proj2, final2), prepared[7:]):
                out[...] = weight[...].astype(BF16)

    def work(here, rows):
        normed = side_by_side(
            [
                (normalise(turned(pair, spot, lanes))[0] * norm[...]).astype(BF16)
                for spot, row, half, lanes, among in places_of(here, rows)
            ]
        )
        mixture = dot_nn(proj_t[...], normed)
        put_gated(info, part, mixture, here, rows, left_st, right_st, gate_out, factor_out)

    each_rows(work)

    @last_step
    def _():
        core = info[2]
        for owner, a_out, b_out in ((core, a_same, b_same), (1 - core, a_other, b_other)):
            for group in range(2):
                for at in CHUNKS:
                    channel = owner * (2 * GROUP) + group * GROUP + at
                    left = dot_nn(perm[...], get_chunk(left_st, (0, 1), channel)).astype(BF16)
                    right = dot_nn(perm[...], get_chunk(right_st, (0, 1), channel)).astype(BF16)
                    first, second = (left, right) if group == 0 else (right, left)
                    give_chunk(a_out, group, at, BOTH, first)
                    give_chunk(b_out, group, at, BOTH, second)
                    if a_out is a_other:
                        give_chunk(to_core, group, at, BOTH, first)
                        give_chunk(to_core, 2 + group, at, BOTH, second)


def fill_split(info, perm, stage, own, near, ypart, ycpart, xpart, xcpart):
    x, y, core = info[0], info[1], info[2]
    for owner, mine, yp, xp in ((core, own, ypart, xpart), (1 - core, near, ycpart, xcpart)):
        for at in CHUNKS:
            channel = owner * (2 * GROUP) + at
            both = jnp.concatenate([chunk(mine, 0, at, LOW), chunk(yp, 0, at, LOW)], axis=1)
            both = dot_nn(perm, both)
            put_chunk(stage, y, channel, both[:, LOW])
            put_chunk(stage, 1 - y, channel, both[:, HIGH])
            both = jnp.concatenate([chunk(mine, 1, at, LOW), chunk(xp, 0, at, LOW)], axis=1)
            both = dot_nn(perm, both)
            here, there = both[:, LOW], both[:, HIGH]
            first, second = half_swap(pick(x, here, there), pick(x, there, here))
            put_chunk(stage, 0, channel + GROUP, first)
            put_chunk(stage, 1, channel + GROUP, second)


def fill_sum(perm, stage, channel, first, second):
    both = (chunk(*first).astype(F32) + chunk(*second).astype(F32)).astype(BF16)
    total = dot_nn(perm, both)
    put_chunk(stage, 0, channel, total[:, LOW])
    put_chunk(stage, 1, channel, total[:, HIGH])


def split_out(info, perm, stage, owner, at):
    x, y = info[0], info[1]
    channel = owner * (2 * GROUP) + at
    both = dot_nn(perm, get_chunk(stage, (y, 1 - y), channel))
    swapped = dot_nn(perm, get_chunk(stage, (0, 1), channel + GROUP))
    first, second = half_swap(swapped[:, LOW], swapped[:, HIGH])
    return both[:, LOW], both[:, HIGH], pick(x, first, second), pick(x, second, first)


def middle_kernel(
    part, info, pair, own, ypart, xpart, ycpart, xcpart, near,
    gate1, gain1, final1_t, norm2, proj2_t,
    middle_out, inner_out, gate_out, factor_out, normed_out, final_out, slope_out, o_own, o_near, o_y, o_yc, o_x, o_xc,
    stage, left_st, right_st, perm,
):
    @first_step
    def _():
        perm[...] = reorder()
        fill_split(info, perm[...], stage, own, near, ypart, ycpart, xpart, xcpart)

    def work(here, rows):
        finals, normeds = [], []
        for spot, row, half, lanes, among in places_of(here, rows):
            inner = stage[half, row]
            final = (normalise(inner)[0] * gain1[...]).astype(BF16)
            inner_out[spot, :, lanes] = inner.astype(BF16)
            final_out[spot, :, lanes] = final
            finals.append(final)
        product = dot_nn(final1_t[...], side_by_side(finals))
        for spot, row, half, lanes, among in places_of(here, rows):
            gate = gate1[spot, :, lanes].astype(F32)
            update = product[:, among] * gate
            slope_out[spot, :, lanes] = (update * (1.0 - gate)).astype(BF16)
            middle = (turned(pair, spot, lanes) + update).astype(BF16)
            middle_out[spot, :, lanes] = middle
            normed = (normalise(middle.astype(F32))[0] * norm2[...]).astype(BF16)
            normed_out[spot, :, lanes] = normed
            normeds.append(normed)
        mixture = dot_nn(proj2_t[...], side_by_side(normeds))
        put_gated(info, part, mixture, here, rows, left_st, right_st, gate_out, factor_out)

    each_rows(work)

    @last_step
    def _():
        core = info[2]
        beyond = slice(LANES, 3 * LANES)
        for owner, main, yo, xo in ((core, o_own, o_y, o_x), (1 - core, o_near, o_yc, o_xc)):
            for at in CHUNKS:
                kept = split_out(info, perm[...], left_st, owner, at)
                give_chunk(main, 0, at, LOW, kept[0])
                give_chunk(yo, 0, at, LOW, kept[1])
                give_chunk(main, 1, at, LOW, kept[2])
                give_chunk(xo, 0, at, LOW, kept[3])
                for group, out in ((0, yo), (1, xo)):
                    channel = owner * (2 * GROUP) + group * GROUP + at
                    right = dot_nn(perm[...], get_chunk(right_st, (0, 1), channel)).astype(BF16)
                    give_chunk(main, group, at, beyond, right)
                    give_chunk(out, 0, at, beyond, right)


def turn_kernel(
    part, info, gate2, cot, own, ypart, xpart, ycpart, xcpart, near,
    gain2, final2_t, final2_w,
    gate_out, final_out, product_out, same0, same1, other0, other1, to_core, stage, out_st, perm,
):
    core = info[2]

    @first_step
    def _():
        perm[...] = reorder()
        for owner, mine, xp, yp in ((core, own, xpart, ypart), (1 - core, near, xcpart, ycpart)):
            for at in CHUNKS:
                channel = owner * (2 * GROUP) + at
                fill_sum(perm[...], stage, channel, (mine, 0, at, BOTH), (xp, 0, at, BOTH))
                fill_sum(perm[...], stage, channel + GROUP, (mine, 1, at, BOTH), (yp, 0, at, BOTH))

    def work(here, rows):
        finals, products = [], []
        for spot, row, half, lanes, among in places_of(here, rows):
            final = (normalise(stage[half, row])[0] * gain2[...]).astype(BF16)
            final_out[spot, :, lanes] = final
            finals.append(final)
            grad_product = turned(cot, spot, lanes) * gate2[spot, :, lanes].astype(F32)
            grad_product = grad_product.astype(BF16)
            product_out[spot, :, lanes] = grad_product
            products.append(grad_product)
        product = dot_nn(final2_t[...], side_by_side(finals))
        grad_final = dot_nn(final2_w[...], side_by_side(products))
        for spot, row, half, lanes, among in places_of(here, rows):
            gate = gate2[spot, :, lanes].astype(F32)
            grad_gate = turned(cot, spot, lanes) * product[:, among] * gate * (1.0 - gate)
            gate_out[spot, :, lanes] = grad_gate.astype(BF16)
            hat, spread = normalise(stage[half, row])
            grad_inner = normalise_back(grad_final[:, among] * gain2[...], hat, spread)
            out_st[half, row] = grad_inner.astype(BF16)

    each_rows(work)

    @last_step
    def _():
        for owner, outs in ((core, (same0, same1)), (1 - core, (other0, other1))):
            for group, out in enumerate(outs):
                for at in CHUNKS:
                    channel = owner * (2 * GROUP) + group * GROUP + at
                    value = dot_nn(perm[...], get_chunk(out_st, (0, 1), channel)).astype(BF16)
                    give_chunk(out, 0, at, BOTH, value)
                    if out is other0 or out is other1:
                        give_chunk(to_core, group, at, BOTH, value)


def mixture_chunk(left_st, right_st, factors, gate_in, spot, row, half, lanes):
    size = left_st.shape[2]
    grads = (left_st[half, row], right_st[half, row])
    blocks = [
        (grads[n % 2] * factors[spot, n * size : (n + 1) * size, lanes].astype(F32)).astype(BF16)
        for n in range(4)
    ]
    return jnp.concatenate(blocks + [gate_in[spot, :, lanes]], axis=0)


def inward_kernel(
    part, info, middle, gate1, cot, inner_in, gate_in, factors, slopes, own, ypart, xpart, ycpart, xcpart, near,
    norm2, proj2_w, gain1, final1_w,
    grad_out, gate_out, mixture_out, product_out, o_own, o_near, o_y, o_yc, o_x, o_xc,
    left_st, right_st, out_st, perm,
):
    core = info[2]

    @first_step
    def _():
        perm[...] = reorder()
        fill_split(info, perm[...], left_st, own, near, ypart, ycpart, xpart, xcpart)
        beyond = slice(LANES, 3 * LANES)
        for owner, mine, yp, xp in ((core, own, ypart, xpart), (1 - core, near, ycpart, xcpart)):
            for at in CHUNKS:
                channel = owner * (2 * GROUP) + at
                fill_sum(perm[...], right_st, channel, (mine, 0, at, beyond), (yp, 0, at, beyond))
                fill_sum(
                    perm[...], right_st, channel + GROUP, (mine, 1, at, beyond), (xp, 0, at, beyond)
                )

    def work(here, rows):
        mixtures, products = [], []
        for spot, row, half, lanes, among in places_of(here, rows):
            mixture = mixture_chunk(left_st, right_st, factors, gate_in, spot, row, half, lanes)
            mixture_out[spot, :, lanes] = mixture
            mixtures.append(mixture)
        grad_normed = dot_nn(proj2_w[...], side_by_side(mixtures))
        for spot, row, half, lanes, among in places_of(here, rows):
            hat, spread = normalise(middle[spot, :, lanes].astype(F32))
            grad = normalise_back(grad_normed[:, among] * norm2[...], hat, spread)
            grad = grad + turned(cot, spot, lanes)
            grad_out[spot, :, lanes] = grad
            gate_out[spot, :, lanes] = (grad * slopes[spot, :, lanes].astype(F32)).astype(BF16)
            grad_product = (grad * gate1[spot, :, lanes].astype(F32)).astype(BF16)
            product_out[spot, :, lanes] = grad_product
            products.append(grad_product)
        grad_final = dot_nn(final1_w[...], side_by_side(products))
        for spot, row, half, lanes, among in places_of(here, rows):
            hat, spread = normalise(inner_in[spot, :, lanes].astype(F32))
            grad_inner = normalise_back(grad_final[:, among] * gain1[...], hat, spread)
            out_st[half, row] = grad_inner.astype(BF16)

    each_rows(work)

    @last_step
    def _():
        for owner, main, yo, xo in ((core, o_own, o_y, o_x), (1 - core, o_near, o_yc, o_xc)):
            for at in CHUNKS:
                kept = split_out(info, perm[...], out_st, owner, at)
                give_chunk(main, 0, at, LOW, kept[0])
                give_chunk(yo, 0, at, LOW, kept[1])
                give_chunk(main, 1, at, LOW, kept[2])
                give_chunk(xo, 0, at, LOW, kept[3])


def weight_kernel(info, *refs):
    *refs, total = refs
    (mixtures, normeds, *pairs) = paired(refs)
    width, channels = mixtures[0].shape[1], normeds[0].shape[1]

    @pl.when(pl.program_id(0) == 0)
    def _():
        total[...] = jnp.zeros_like(total)

    for part in range(PARTS):
        for first in range(0, mixtures[part].shape[0], PAIRED):
            rows = [first + n for n in range(PAIRED)]
            mixture, normed = stacked(mixtures[part], rows), stacked(normeds[part], rows)
            total[:width, :] += dot_nt(mixture, normed)
            for n, (finals, products) in enumerate((pairs[:2], pairs[2:])):
                where = slice(width + n * channels, width + (n + 1) * channels)
                final, product = stacked(finals[part], rows), stacked(products[part], rows)
                total[where, :] += dot_nt(final, product)


def last_sum_kernel(
    part, info, pair, gate_in, factors, own, ypart, xpart, ycpart, xcpart, near, norm1, early, *rest,
):
    mixture_out, gproj, *packed, left_st, right_st, perm = rest
    if part:
        before, mixture_out, gproj, *packed = mixture_out, gproj, *packed
    core = info[2]

    @first_step
    def _():
        perm[...] = reorder()
        gproj[...] = before[...] if part else jnp.zeros_like(gproj)
        beyond = slice(2 * LANES, 4 * LANES)
        for owner, mine, yp, xp in ((core, own, ypart, xpart), (1 - core, near, ycpart, xcpart)):
            for group, lefts, rights in ((0, yp, xp), (1, xp, yp)):
                for at in CHUNKS:
                    channel = owner * (2 * GROUP) + group * GROUP + at
                    fill_sum(
                        perm[...], left_st, channel, (mine, group, at, BOTH), (lefts, group, at, BOTH)
                    )
                    fill_sum(
                        perm[...],
                        right_st,
                        channel,
                        (mine, group, at, beyond),
                        (rights, group, at, BOTH),
                    )

    def work(here, rows):
        mixtures, normeds = [], []
        for spot, row, half, lanes, among in places_of(here, rows):
            normeds.append(
                (normalise(turned(pair, spot, lanes))[0] * norm1[...]).astype(BF16)
            )
            mixture = mixture_chunk(left_st, right_st, factors, gate_in, spot, row, half, lanes)
            mixture_out[spot, :, lanes] = mixture
            mixtures.append(mixture)
        gproj[...] += dot_nt(side_by_side(mixtures), side_by_side(normeds))

    each_rows(work)

    if part:

        @last_step
        def _():
            size = gproj.shape[0]
            packed[0][:size, :] = gproj[...].astype(BF16)
            packed[0][size:, :] = early[...].astype(BF16)


def exit_kernel(info, pair, grad_in, mixture_in, norm1, proj1_w, *rest):
    out = rest[-1]

    def work(here, rows):
        grad_normed = dot_nn(proj1_w[...], stacked(mixture_in, here))
        for spot, row, half, lanes, among in places_of(here, rows):
            hat, spread = normalise(turned(pair, spot, lanes))
            grad = normalise_back(grad_normed[:, among] * norm1[...], hat, spread)
            out[spot, lanes, :] = (grad_in[spot, :, lanes] + grad).T

    each_rows(work)


CHANNELS = 8
PARTS = 2


def paired(refs):
    return [refs[n : n + PARTS] for n in range(0, len(refs), PARTS)]


def place(one, two, part):
    return pl.multiple_of((one * 2 + two) * (PARTS * BLOCK) + part * BLOCK, BLOCK)


def places(info, group):
    at, core = info[group], info[2]
    return [
        place(at if n < 2 else 1 - at, core if n % 2 == 0 else 1 - core, part)
        for n in range(4)
        for part in range(PARTS)
    ]


def take(ref, group, h):
    return ref[group, h] if len(ref.shape) == 4 else ref[h]


def joined(quads, group, h):
    return jnp.concatenate([take(ref, group, h) for refs in quads for ref in refs], axis=0)


def gather(stage, slot, wheres, quads, group, h):
    for where, ref in zip(wheres, [ref for refs in quads for ref in refs]):
        stage[slot, pl.ds(where, BLOCK), :] = take(ref, group, h)
    return stage[slot]


def give(refs, group, h, lanes, value):
    if len(refs.shape) == 4:
        refs[group, h, :, lanes] = value
    else:
        refs[h, :, lanes] = value


def scatter(quads, group, h, lanes, value):
    for n, ref in enumerate([ref for refs in quads for ref in refs]):
        give(ref, group, h, lanes, value[n * BLOCK : (n + 1) * BLOCK])


def scatter_from(stage, slot, wheres, quads, group, h, lanes):
    for where, ref in zip(wheres, [ref for refs in quads for ref in refs]):
        give(ref, group, h, lanes, stage[slot, pl.ds(where, BLOCK), :])


def outgoing_kernel(info, *refs):
    *refs, stage = refs
    *refs, o_own, o_near, o_y, o_yc, o_x, o_xc = refs
    a_own, b_own, a_y, b_x, a_yc, b_xc, near = paired(refs)
    a_near, b_near = [ref.at[:2] for ref in near], [ref.at[2:] for ref in near]
    along_a, along_b = (a_own, a_near, a_y, a_yc), (b_own, b_near, b_x, b_xc)
    for h in range(CHANNELS):
        for group in range(2):
            lefts, rights = (along_a, along_b) if group == 0 else (along_b, along_a)
            far = (o_y, o_yc) if group == 0 else (o_x, o_xc)
            right = gather(stage, 2 * h + group, places(info, group), rights, group, h)
            inner = dot_nt(joined(lefts, group, h), right).astype(BF16)
            for n, out in enumerate((o_own, o_near) + far):
                rows = PARTS * BLOCK
                give(out, group, h, slice(0, LANES), inner[n * rows : (n + 1) * rows])


def halves(quads, group, h):
    both = joined(quads, group, h)
    return both[:, :LANES], both[:, LANES:]


def incoming_kernel(info, *refs):
    *refs, stage = refs
    own, ypart, xpart, ycpart, xcpart, near, o_own, o_near, o_x, o_xc, o_y, o_yc = paired(refs)
    for h in range(CHANNELS):
        for group in range(2):
            far = (ypart, ycpart) if group == 0 else (xpart, xcpart)
            outs = (o_own, o_near) + ((o_x, o_xc) if group == 0 else (o_y, o_yc))
            slot = 2 * h + group
            left, right = halves((own, near) + far, group, h)
            stage[slot] = dot_tn(left, right).astype(BF16)
            scatter_from(stage, slot, places(info, group), outs, group, h, slice(0, 2 * LANES))


def incoming_back_kernel(info, *refs):
    *refs, stage = refs
    own, ypart, xpart, ycpart, xcpart, near, *more = paired(refs)
    same0, same1, g_y, g_x, g_yc, g_xc, g_near, *more = more
    o_own, o_near, o_y, o_yc, o_x, o_xc = more
    for h in range(CHANNELS):
        for group in range(2):
            far = (ypart, ycpart) if group == 0 else (xpart, xcpart)
            grads = (same0, g_near, g_x, g_xc) if group == 0 else (same1, g_near, g_y, g_yc)
            outs = (o_own, o_near) + ((o_y, o_yc) if group == 0 else (o_x, o_xc))
            grad = gather(stage, 2 * h + group, places(info, group), grads, group, h)
            left, right = halves((own, near) + far, group, h)
            scatter(outs, group, h, slice(0, LANES), dot_nt(right, grad).astype(BF16))
            scatter(outs, group, h, slice(LANES, 3 * LANES), dot_nn(left, grad).astype(BF16))


def outgoing_back_kernel(info, *refs):
    *refs, stage, back = refs
    a_own, b_own, a_y, b_x, a_yc, b_xc, near, *more = paired(refs)
    a_near, b_near = [ref.at[:2] for ref in near], [ref.at[2:] for ref in near]
    g_own, g_y, g_x, g_yc, g_xc, g_near, o_own, o_near, o_y, o_yc, o_x, o_xc = more
    along_a, along_b = (a_own, a_near, a_y, a_yc), (b_own, b_near, b_x, b_xc)
    first, second = slice(0, 2 * LANES), slice(2 * LANES, 4 * LANES)
    for h in range(CHANNELS):
        for group in range(2):
            lefts, rights = (along_a, along_b) if group == 0 else (along_b, along_a)
            far = (g_y, g_yc) if group == 0 else (g_x, g_xc)
            left_far, right_far = ((o_y, o_yc), (o_x, o_xc)) if group == 0 else ((o_x, o_xc), (o_y, o_yc))
            slot = 2 * h + group
            wheres = places(info, group)
            right = gather(stage, slot, wheres, rights, group, h)
            grad = joined((g_own, g_near) + far, group, h)
            grad_left = dot_nn(grad, right).astype(BF16)
            back[slot] = dot_tn(grad, joined(lefts, group, h)).astype(BF16)
            core_rows = 2 * PARTS * BLOCK
            scatter((o_own, o_near), group, h, first, grad_left[:core_rows])
            scatter(left_far, group, h, first, grad_left[core_rows:])
            scatter_from(back, slot, wheres[: 2 * PARTS], (o_own, o_near), group, h, second)
            scatter_from(back, slot, wheres[2 * PARTS :], right_far, group, h, first)


def whole(shape):
    return pl.BlockSpec(shape, lambda step, info: (0,) * len(shape))


def rows_of(part, some=SOME):
    def make(shape):
        first = part * (BLOCK // some)
        return pl.BlockSpec(
            (some,) + shape[1:], lambda step, info: (first + step,) + (0,) * (len(shape) - 1)
        )

    return make


def rows_block(part):
    def make(shape):
        return pl.BlockSpec(
            shape[:-2] + (BLOCK, shape[-1]),
            lambda step, info: (0,) * (len(shape) - 2) + (part, 0),
        )

    return make


def anywhere(shape):
    return pl.BlockSpec(memory_space=pl.ANY)


def channel_rows(shape):
    if len(shape) == 4:
        return pl.BlockSpec((shape[0], CHANNELS) + shape[2:], lambda step, info: (0, step, 0, 0))
    return pl.BlockSpec((CHANNELS,) + shape[1:], lambda step, info: (step, 0, 0))


def call(kernel, info, steps, ins, outs, scratch, aliases={}):
    return pl.pallas_call(
        kernel,
        grid_spec=pltpu.PrefetchScalarGridSpec(
            num_scalar_prefetch=1,
            grid=(steps,),
            in_specs=[make(array.shape) for array, make in ins],
            out_specs=[make(shape) for shape, unused, make in outs],
            scratch_shapes=scratch,
        ),
        out_shape=[jax.ShapeDtypeStruct(shape, dtype) for shape, dtype, unused in outs],
        compiler_params=pltpu.CompilerParams(vmem_limit_bytes=VMEM),
        input_output_aliases=aliases,
    )(info, *[array for array, unused in ins])


class Links:
    def __init__(self):
        self.last = {}

    def send(self, array, offset, first=None):
        count = lax.axis_size("axial")
        if first is not None:
            array, unused = lax.optimization_barrier((array, first))
        if offset in self.last and offset in (X, Y):
            array, unused = lax.optimization_barrier((array, self.last[offset]))
        self.last[offset] = lax.ppermute(
            array, "axial", [(n, n ^ offset) for n in range(count)]
        )
        return self.last[offset]

    def __call__(self, *sends, between=None):
        results = [[] for unused in sends]
        for part in range(len(sends[0][0])):
            for result, (arrays, offset) in zip(results, sends):
                result.append(self.send(arrays[part], offset, between if part else None))
        return results


CORE, X, Y = 1, 2, 4


def add_up(share):
    count = lax.axis_size("axial")
    rows, width = share.shape
    shares = share.reshape(count, rows // count, width)
    parts = lax.all_to_all(shares, "axial", split_axis=0, concat_axis=0, tiled=True)
    mine = parts.astype(F32).sum(axis=0).astype(BF16)
    depth = lax.axis_size("dp")
    terms = [mine] + [
        lax.ppermute(mine, "dp", [(n, n ^ offset) for n in range(depth)])
        for offset in range(1, depth)
    ]
    terms = [term.astype(F32) for term in terms]
    while len(terms) > 1:
        terms = [terms[n] + terms[n + 1] for n in range(0, len(terms), 2)]
    copies = jnp.broadcast_to(terms[0].astype(BF16)[None], shares.shape)
    return lax.all_to_all(copies, "axial", split_axis=0, concat_axis=0, tiled=True).reshape(
        rows, width
    )


def gain_grad(weight_grad, weight, gain_row):
    return jnp.sum((weight.astype(F32) * weight_grad).T, axis=0, keepdims=True) / gain_row


def finish_kernel(
    scale, info, sums, proj1, final1, proj2, final2, norm1, gain1, norm2, gain2,
    o_norm1, o_proj1, o_gain1, o_final1, o_norm2, o_proj2, o_gain2, o_final2,
):
    width, channels = proj1.shape[1], final1.shape[1]
    takes = (
        (0, True, proj1, norm1, o_proj1, o_norm1),
        (width, True, proj2, norm2, o_proj2, o_norm2),
        (2 * width, False, final2, gain2, o_final2, o_gain2),
        (2 * width + channels, False, final1, gain1, o_final1, o_gain1),
    )
    for start, flipped, weight, gain, out, gain_out in takes:
        total = sums[start : start + weight.shape[1], :].astype(F32) * scale
        total = total.T if flipped else total
        out[...] = total
        gain_out[...] = gain_grad(total, weight[...].astype(BF16), gain[...])


def fast_body(
    pair,
    cotangent,
    lengths,
    outgo_norm,
    outgo_proj,
    outgo_gain,
    outgo_final,
    incom_norm,
    incom_proj,
    incom_gain,
    incom_final,
):
    rows, tokens, channels = pair.shape[1:]
    hidden = outgo_gain.shape[0]
    index = lax.axis_index("axial")
    info = jnp.stack(
        [(index // 2) % 2, index // 4, index % 2, index * rows, lengths[0]]
    ).astype(jnp.int32)
    hop = Links()
    pair = pair[0]
    cot = cotangent[0]
    parts = range(PARTS)
    turns = GROUP // CHANNELS
    stage = pltpu.VMEM((2, BLOCK, hidden, LANES), F32)
    out_stage = pltpu.VMEM((2, BLOCK, hidden, LANES), BF16)
    perm = pltpu.VMEM((BLOCK * BLOCK, BLOCK * BLOCK), BF16)
    streamed = rows_of(0)
    square = pltpu.VMEM((2 * CHANNELS, 4 * rows, tokens), BF16)

    def two(width, height=BLOCK, make=whole, groups=2):
        return ((groups, GROUP, height, width), BF16, make)

    def one(width, height=BLOCK, make=whole):
        return ((GROUP, height, width), BF16, make)

    turned_block = ((BLOCK, channels, tokens), BF16, streamed)
    factor_block = ((BLOCK, 4 * hidden, tokens), BF16, streamed)
    mixture_block = ((BLOCK, 5 * hidden, tokens), BF16, streamed)

    def cells(kernel, ins, outs, scratch, more=lambda part: []):
        results = []
        for part in parts:
            carried = ins(part, results)
            results.append(
                call(functools.partial(kernel, part), info, STEPS, carried, outs + more(part), scratch)
            )
        shared = results[-1][len(outs) :]
        return [list(each) for each in zip(*results)] + list(shared)

    def wholes(arrays):
        return [(array, whole) for array in arrays]

    def triangle(kernel, operands, outs, scratch, split=PARTS):
        ins = [(array, channel_rows) for arrays in operands for array in arrays]
        each = [out for out in outs for unused in range(split)]
        results = call(kernel, info, turns, ins, each, scratch)
        return [list(results[n : n + split]) for n in range(0, len(results), split)]

    near_one = []

    def after_core(array, done):
        if done:
            near_one.append(hop.send(done[-1][4], CORE))
            array, unused = lax.optimization_barrier((array, near_one[-1]))
        return array

    raw = (outgo_gain[None], outgo_final, incom_norm[None], incom_proj, incom_gain[None], incom_final)
    gain_wide = ((channels, LANES), F32, whole)
    proj_turned = ((5 * hidden, channels), BF16, whole)
    proj_plain = ((channels, 5 * hidden), BF16, whole)
    final_plain = ((hidden, channels), BF16, whole)
    (
        a_same, a_other, b_same, b_other, to_core, gate_one, factors_one,
        norm1, gain1, norm2, gain2, proj2_t, final1_t, final2_t,
        proj1, final1, proj2, final2,
    ) = cells(
        entry_kernel,
        lambda part, done: [
            (after_core(pair, done), rows_of(part)),
            (outgo_norm[None], whole),
            (outgo_proj, whole),
        ]
        + (wholes(raw) if part else []),
        [two(tokens)] * 4 + [two(tokens, groups=4), turned_block, factor_block],
        [
            out_stage,
            out_stage,
            pltpu.VMEM((channels, LANES), F32),
            pltpu.VMEM((5 * hidden, channels), BF16),
            perm,
        ],
        lambda part: (
            [gain_wide] * 4
            + [proj_turned]
            + [final_plain] * 2
            + [proj_plain, final_plain] * 2
            if part
            else []
        ),
    )
    held_one = [a_same, b_same] + hop(
        (a_same, Y), (b_same, X), (a_other, Y | CORE), (b_other, X | CORE)
    )
    near_one.append(hop.send(to_core[-1], CORE))
    held_one.append(near_one)
    own, near, to_y, to_yc, to_x, to_xc = triangle(
        outgoing_kernel,
        held_one,
        [two(LANES, rows, channel_rows)] * 2 + [one(LANES, rows, channel_rows)] * 4,
        [square],
        split=1,
    )
    back_one = [
        own,
        *hop(
            (to_y, Y), (to_x, X), (to_yc, Y | CORE), (to_xc, X | CORE), (near, CORE)
        ),
    ]

    (
        middle, inner_one, gate_two, factors_two, normed_two, finals_one, slopes_one,
        own, near, to_y, to_yc, to_x, to_xc,
    ) = cells(
        middle_kernel,
        lambda part, unused: [(pair, rows_of(part))]
        + [(array, rows_block(part)) for array, in back_one]
        + [(gate_one[part], streamed)]
        + wholes((gain1, final1_t, norm2, proj2_t)),
        [turned_block] * 3
        + [factor_block]
        + [turned_block] * 3
        + [two(3 * LANES)] * 2 + [one(3 * LANES)] * 4,
        [stage, out_stage, out_stage, perm],
    )
    held_two = [
        own,
        *hop(
            (to_y, Y), (to_x, X), (to_yc, Y | CORE), (to_xc, X | CORE), (near, CORE)
        ),
    ]
    own, near, to_x, to_xc, to_y, to_yc = triangle(
        incoming_kernel,
        held_two,
        [two(tokens, make=channel_rows)] * 2 + [one(tokens, make=channel_rows)] * 4,
        [square],
    )
    back_two = [
        own,
        *hop(
            (to_y, Y), (to_x, X), (to_yc, Y | CORE), (to_xc, X | CORE), (near, CORE)
        ),
    ]

    gate_grad_two, finals_two, products_two, same0, same1, other0, other1, to_core = cells(
        turn_kernel,
        lambda part, done: [(gate_two[part], streamed), (cot, rows_of(part))]
        + wholes(arrays[part] for arrays in back_two)
        + wholes((gain2, final2_t, final2)),
        [turned_block] * 3 + [one(tokens)] * 4 + [two(tokens)],
        [stage, out_stage, perm],
    )
    grads_two = [
        same0,
        same1,
        *hop(
            (same1, Y), (same0, X), (other1, Y | CORE), (other0, X | CORE), (to_core, CORE)
        ),
    ]
    own, near, to_y, to_yc, to_x, to_xc = triangle(
        incoming_back_kernel,
        held_two + grads_two,
        [two(3 * LANES, make=channel_rows)] * 2 + [one(3 * LANES, make=channel_rows)] * 4,
        [square],
    )
    rows_two = [
        own,
        *hop(
            (to_y, Y), (to_x, X), (to_yc, Y | CORE), (to_xc, X | CORE), (near, CORE)
        ),
    ]

    (
        grad_middle, gate_grad_one, mixtures_two, products_one,
        own, near, to_y, to_yc, to_x, to_xc,
    ) = cells(
        inward_kernel,
        lambda part, done: [
            (middle[part], streamed),
            (gate_one[part], streamed),
            (cot, rows_of(part)),
            (inner_one[part], streamed),
            (gate_grad_two[part], streamed),
            (factors_two[part], streamed),
            (slopes_one[part], streamed),
        ]
        + wholes(arrays[part] for arrays in rows_two)
        + wholes((norm2, proj2, gain1, final1)),
        [((BLOCK, channels, tokens), F32, streamed), turned_block, mixture_block, turned_block]
        + [two(LANES)] * 2
        + [one(LANES)] * 4,
        [stage, stage, out_stage, perm],
    )
    grads_one = [
        own,
        *hop(
            (to_y, Y), (to_x, X), (to_yc, Y | CORE), (to_xc, X | CORE), (near, CORE)
        ),
    ]
    own, near, to_y, to_yc, to_x, to_xc = triangle(
        outgoing_back_kernel,
        held_one + grads_one,
        [two(2 * tokens, make=channel_rows)] * 2 + [two(tokens, make=channel_rows)] * 4,
        [square, square],
    )
    kept = (mixtures_two, normed_two, finals_two, products_two, finals_one, products_one)
    (early,) = call(
        weight_kernel,
        info,
        4,
        [
            (array, rows_of(0, BLOCK // 4))
            for arrays in kept
            for array in arrays
        ],
        [((5 * hidden + 2 * channels, channels), F32, whole)],
        [],
    )
    rows_one = [own] + hop(
        (to_y, Y), (to_x, X), (to_yc, Y | CORE), (to_xc, X | CORE), (near, CORE), between=early
    )
    mixtures_one, before = [], []
    for part in parts:
        mixture, *before = call(
            functools.partial(last_sum_kernel, part),
            info,
            STEPS,
            [
                (pair, rows_of(part)),
                (gate_grad_one[part], streamed),
                (factors_one[part], streamed),
            ]
            + wholes(arrays[part] for arrays in rows_one)
            + wholes((norm1, early, *before)),
            [mixture_block, ((5 * hidden, channels), F32, whole)]
            + ([((10 * hidden + 2 * channels, channels), BF16, whole)] if part else []),
            [stage, stage, perm],
        )
        mixtures_one.append(mixture)
    sums = add_up(before[-1])
    result = []
    for part in parts:
        result = call(
            exit_kernel,
            info,
            STEPS,
            [
                (pair, rows_of(part)),
                (grad_middle[part], streamed),
                (mixtures_one[part], streamed),
            ]
            + wholes((norm1, proj1))
            + [(array, anywhere) for array in result],
            [((rows, tokens, channels), F32, rows_of(part))],
            [],
            {6: 0} if part else {},
        )
    (grad_begin,) = result
    scale = 1.0 / math.sqrt(lax.axis_size("dp") * tokens * tokens)
    weights = (outgo_proj, outgo_final, incom_proj, incom_final)
    gains = (outgo_norm, outgo_gain, incom_norm, incom_gain)
    order = (outgo_norm[None], outgo_proj, outgo_gain[None], outgo_final)
    order += (incom_norm[None], incom_proj, incom_gain[None], incom_final)
    totals = call(
        functools.partial(finish_kernel, scale),
        info,
        1,
        wholes((sums,) + weights + tuple(gain[None] for gain in gains)),
        [(array.shape, F32, whole) for array in order],
        [],
    )
    return (grad_begin[None],) + tuple(
        total.reshape(-1) if total.shape[0] == 1 else total for total in totals
    )


def solution(mesh):
    def body(pair, *rest):
        rows, tokens, channels = pair.shape[1:]
        hidden = rest[3].shape[0]
        plane = mesh.shape["axial"] == 8 and rows == 32 and tokens == 2 * LANES
        if plane and channels == LANES and hidden == 4 * GROUP:
            return fast_body(pair, *rest)
        return plain_body(pair, *rest)

    return jax.shard_map(
        body,
        mesh=mesh,
        in_specs=(P("dp", "axial", None, None), P("dp", "axial", None, None), P("dp")) + (P(),) * 8,
        out_specs=(P("dp", "axial", None, None),) + (P(),) * 8,
        check_vma=False,
    )
```

```python
import functools
import math

import jax
import jax.numpy as jnp
from jax import lax
from jax.experimental import pallas as pl
from jax.experimental.pallas import tpu as pltpu
from jax.sharding import PartitionSpec as P

EPSILON = 1e-05


def rounded(inputs):
    return lax.optimization_barrier(inputs.astype(jnp.bfloat16)).astype(jnp.float32)


def layer_norm(inputs, factor):
    average = jnp.mean(inputs, axis=-1, keepdims=True)
    centered = inputs - average
    spread = jnp.mean(centered * centered, axis=-1, keepdims=True)
    return centered * lax.rsqrt(spread + EPSILON) * factor


def gating(mixture, pair_mask, hidden):
    left_part = (
        mixture[:, :hidden] * jax.nn.sigmoid(mixture[:, 2 * hidden : 3 * hidden]) * pair_mask
    )
    right_part = (
        mixture[:, hidden : 2 * hidden]
        * jax.nn.sigmoid(mixture[:, 3 * hidden : 4 * hidden])
        * pair_mask
    )
    gate_part = jax.nn.sigmoid(mixture[:, 4 * hidden :])
    return (left_part, right_part, gate_part)


def entry(flat_pair, norm_gain, projection, pair_mask, hidden):
    normed = layer_norm(flat_pair, norm_gain).astype(jnp.bfloat16)
    mixture = jnp.dot(normed, projection.astype(jnp.bfloat16), preferred_element_type=jnp.float32)
    left_part, right_part, gate_part = gating(mixture, pair_mask, hidden)
    return (normed, mixture, left_part, right_part, gate_part)


def entry_back(
    flat_pair,
    norm_gain,
    projection,
    pair_mask,
    hidden,
    normed,
    mixture,
    grad_left,
    grad_right,
    grad_gate,
):
    unused, pull_gate = jax.vjp(lambda inner_mix: gating(inner_mix, pair_mask, hidden), mixture)
    grad_mixture = pull_gate((grad_left, grad_right, grad_gate))[0].astype(jnp.bfloat16)
    grad_projection = jnp.dot(normed.T, grad_mixture, preferred_element_type=jnp.float32)
    grad_normed = jnp.dot(
        grad_mixture, projection.astype(jnp.bfloat16).T, preferred_element_type=jnp.float32
    )
    unused, pull_norm = jax.vjp(layer_norm, flat_pair, norm_gain)
    grad_flat, grad_gain = pull_norm(grad_normed)
    return (grad_flat, grad_gain, grad_projection)


def leave(inner_sum, gate_part, out_gain, final_weight):
    final_normed = layer_norm(inner_sum, out_gain).astype(jnp.bfloat16)
    product = jnp.dot(
        final_normed, final_weight.astype(jnp.bfloat16), preferred_element_type=jnp.float32
    )
    return (final_normed, product, product * gate_part)


def leave_back(inner_sum, gate_part, out_gain, final_weight, final_normed, product, grad_update):
    grad_product = (grad_update * gate_part).astype(jnp.bfloat16)
    grad_gate = grad_update * product
    grad_final = jnp.dot(final_normed.T, grad_product, preferred_element_type=jnp.float32)
    grad_normed = jnp.dot(
        grad_product, final_weight.astype(jnp.bfloat16).T, preferred_element_type=jnp.float32
    )
    unused, pull_norm = jax.vjp(layer_norm, inner_sum, out_gain)
    grad_inner, grad_gain = pull_norm(grad_normed)
    return (grad_inner, grad_gate, grad_gain, grad_final)


def channel_major(field, row_count, tokens):
    hidden = field.shape[1]
    return jnp.transpose(field.reshape(row_count, tokens, hidden), (2, 0, 1))


def row_major(field):
    hidden = field.shape[0]
    return jnp.transpose(field, (1, 2, 0)).reshape(-1, hidden)


def plain_body(
    pair,
    cotangent,
    lengths,
    outgo_norm,
    outgo_proj,
    outgo_gain,
    outgo_final,
    incom_norm,
    incom_proj,
    incom_gain,
    incom_final,
):
    row_count = pair.shape[1]
    tokens = pair.shape[2]
    channels = pair.shape[3]
    hidden = outgo_gain.shape[0]
    length = lengths[0]
    first_row = lax.axis_index("axial") * row_count
    row_alive = (first_row + jnp.arange(row_count, dtype=jnp.int32) < length).astype(jnp.float32)
    column_alive = (jnp.arange(tokens, dtype=jnp.int32) < length).astype(jnp.float32)
    pair_mask = (row_alive[:, None] * column_alive[None, :]).reshape(-1, 1)
    flat_start = pair[0].reshape(-1, channels).astype(jnp.float32)
    normed_one, mixture_one, left_one, right_one, gate_one = entry(
        flat_start, outgo_norm, outgo_proj, pair_mask, hidden
    )
    left_first = channel_major(left_one.astype(jnp.bfloat16), row_count, tokens)
    right_first = channel_major(right_one.astype(jnp.bfloat16), row_count, tokens)
    left_owned, right_owned = (
        lax.all_to_all(left_first, "axial", split_axis=0, concat_axis=1, tiled=True),
        lax.all_to_all(right_first, "axial", split_axis=0, concat_axis=1, tiled=True),
    )
    inner_cols = jnp.einsum(
        "hik,hjk->hij", left_owned, right_owned, preferred_element_type=jnp.float32
    )
    inner_one = row_major(
        lax.all_to_all(
            inner_cols.astype(jnp.bfloat16), "axial", split_axis=1, concat_axis=0, tiled=True
        ).astype(inner_cols.dtype)
    )
    final_one, product_one, update_one = leave(inner_one, gate_one, outgo_gain, outgo_final)
    flat_middle = rounded(flat_start + update_one)
    normed_two, mixture_two, left_two, right_two, gate_two = entry(
        flat_middle, incom_norm, incom_proj, pair_mask, hidden
    )
    left_second = channel_major(left_two.astype(jnp.bfloat16), row_count, tokens)
    right_second = channel_major(right_two.astype(jnp.bfloat16), row_count, tokens)
    left_held, right_held = (
        lax.all_to_all(left_second, "axial", split_axis=0, concat_axis=1, tiled=True),
        lax.all_to_all(right_second, "axial", split_axis=0, concat_axis=1, tiled=True),
    )
    inner_held = jnp.einsum(
        "hki,hkj->hij", left_held, right_held, preferred_element_type=jnp.float32
    )
    inner_two = row_major(
        lax.all_to_all(
            inner_held.astype(jnp.bfloat16), "axial", split_axis=1, concat_axis=0, tiled=True
        ).astype(inner_held.dtype)
    )
    final_two, product_two, update_two = leave(inner_two, gate_two, incom_gain, incom_final)
    grad_end = cotangent[0].reshape(-1, channels).astype(jnp.float32)
    grad_inner_two, grad_gate_two, grad_gain_two, grad_final_two = leave_back(
        inner_two, gate_two, incom_gain, incom_final, final_two, product_two, grad_end
    )
    grad_cells_two = channel_major(grad_inner_two.astype(jnp.bfloat16), row_count, tokens)
    grad_held_two = lax.all_to_all(grad_cells_two, "axial", split_axis=0, concat_axis=1, tiled=True)
    left_back, right_back = (
        lax.all_to_all(left_second, "axial", split_axis=0, concat_axis=1, tiled=True),
        lax.all_to_all(right_second, "axial", split_axis=0, concat_axis=1, tiled=True),
    )
    grad_left_held = jnp.einsum(
        "hij,hkj->hki", grad_held_two, right_back, preferred_element_type=jnp.float32
    )
    grad_right_held = jnp.einsum(
        "hki,hij->hkj", left_back, grad_held_two, preferred_element_type=jnp.float32
    )
    grad_left_rows, grad_right_rows = (
        lax.all_to_all(
            grad_left_held.astype(jnp.bfloat16), "axial", split_axis=1, concat_axis=0, tiled=True
        ).astype(grad_left_held.dtype),
        lax.all_to_all(
            grad_right_held.astype(jnp.bfloat16), "axial", split_axis=1, concat_axis=0, tiled=True
        ).astype(grad_right_held.dtype),
    )
    grad_left_two = row_major(grad_left_rows)
    grad_right_two = row_major(grad_right_rows)
    grad_flat_two, grad_norm_two, grad_proj_two = entry_back(
        flat_middle,
        incom_norm,
        incom_proj,
        pair_mask,
        hidden,
        normed_two,
        mixture_two,
        grad_left_two,
        grad_right_two,
        grad_gate_two,
    )
    second_sums = lax.psum(
        (grad_norm_two, grad_proj_two, grad_gain_two, grad_final_two), ("dp", "axial")
    )
    grad_middle = grad_end + grad_flat_two
    grad_inner_one, grad_gate_one, grad_gain_one, grad_final_one = leave_back(
        inner_one, gate_one, outgo_gain, outgo_final, final_one, product_one, grad_middle
    )
    grad_cells_one = channel_major(grad_inner_one.astype(jnp.bfloat16), row_count, tokens)
    grad_owned_one = lax.all_to_all(
        grad_cells_one, "axial", split_axis=0, concat_axis=1, tiled=True
    )
    left_again, right_again = (
        lax.all_to_all(left_first, "axial", split_axis=0, concat_axis=1, tiled=True),
        lax.all_to_all(right_first, "axial", split_axis=0, concat_axis=1, tiled=True),
    )
    grad_left_owned = jnp.einsum(
        "hij,hjk->hik", grad_owned_one, right_again, preferred_element_type=jnp.float32
    )
    grad_right_owned = jnp.einsum(
        "hij,hik->hjk", grad_owned_one, left_again, preferred_element_type=jnp.float32
    )
    grad_left_back, grad_right_back = (
        lax.all_to_all(
            grad_left_owned.astype(jnp.bfloat16), "axial", split_axis=1, concat_axis=0, tiled=True
        ).astype(grad_left_owned.dtype),
        lax.all_to_all(
            grad_right_owned.astype(jnp.bfloat16), "axial", split_axis=1, concat_axis=0, tiled=True
        ).astype(grad_right_owned.dtype),
    )
    grad_left_one = row_major(grad_left_back)
    grad_right_one = row_major(grad_right_back)
    grad_flat_one, grad_norm_one, grad_proj_one = entry_back(
        flat_start,
        outgo_norm,
        outgo_proj,
        pair_mask,
        hidden,
        normed_one,
        mixture_one,
        grad_left_one,
        grad_right_one,
        grad_gate_one,
    )
    grad_begin = grad_middle + grad_flat_one
    first_sums = lax.psum(
        (grad_norm_one, grad_proj_one, grad_gain_one, grad_final_one), ("dp", "axial")
    )
    totals = tuple(first_sums) + tuple(second_sums)
    scale = 1.0 / math.sqrt(lax.axis_size("dp") * tokens * tokens)
    return (
        grad_begin.reshape(1, row_count, tokens, channels),
        totals[0] * scale,
        totals[1] * scale,
        totals[2] * scale,
        totals[3] * scale,
        totals[4] * scale,
        totals[5] * scale,
        totals[6] * scale,
        totals[7] * scale,
    )


BF16 = jnp.bfloat16
F32 = jnp.float32
BLOCK = 16
PAIRED = 2
STEPS = 4
SOME = BLOCK // STEPS
LANES = 128
GROUP = 32
MIB = 1024 * 1024
CELL_VMEM = 30 * MIB
TRIANGLE_VMEM = 14 * MIB


def dot_nn(a, b):
    return lax.dot_general(a, b, (((1,), (0,)), ((), ())), preferred_element_type=F32)


def dot_nt(a, b):
    return lax.dot_general(a, b, (((1,), (1,)), ((), ())), preferred_element_type=F32)


def dot_tn(a, b):
    return lax.dot_general(a, b, (((0,), (0,)), ((), ())), preferred_element_type=F32)


def normalise(v):
    centered = v - jnp.mean(v, axis=0, keepdims=True)
    spread = lax.rsqrt(jnp.mean(centered * centered, axis=0, keepdims=True) + EPSILON)
    return centered * spread, spread


def normalise_back(grad, hat, spread):
    first = jnp.mean(grad, axis=0, keepdims=True)
    second = jnp.mean(grad * hat, axis=0, keepdims=True)
    return spread * (grad - first - hat * second)


def reorder():
    size = BLOCK * BLOCK
    one = lax.broadcasted_iota(jnp.int32, (size, size), 0)
    two = lax.broadcasted_iota(jnp.int32, (size, size), 1)
    return jnp.where((one % BLOCK) * BLOCK + one // BLOCK == two, 1.0, 0.0).astype(BF16)


def chunk(ref, group, at, lanes):
    if len(ref.shape) == 4:
        block = ref[group, at : at + BLOCK, :, lanes]
    else:
        block = ref[at : at + BLOCK, :, lanes]
    return block.reshape(BLOCK * BLOCK, block.shape[2])


def put_chunk(stage, half, channel, value):
    channel = pl.multiple_of(channel, BLOCK)
    for row in range(BLOCK):
        stage[half, row, pl.ds(channel, BLOCK), :] = value[row * BLOCK : (row + 1) * BLOCK]


def get_chunk(stage, halves, channel):
    channel = pl.multiple_of(channel, BLOCK)
    return jnp.concatenate(
        [
            jnp.concatenate(
                [stage[half, row, pl.ds(channel, BLOCK), :] for row in range(BLOCK)], axis=0
            )
            for half in halves
        ],
        axis=1,
    )


def give_chunk(ref, group, at, lanes, value):
    block = value.astype(BF16).reshape(BLOCK, BLOCK, value.shape[1])
    if len(ref.shape) == 4:
        ref[group, at : at + BLOCK, :, lanes] = block
    else:
        ref[at : at + BLOCK, :, lanes] = block


LOW, HIGH, BOTH = slice(0, LANES), slice(LANES, 2 * LANES), slice(0, 2 * LANES)
CHUNKS = range(0, GROUP, BLOCK)


def half_swap(first, second):
    low = lax.broadcasted_iota(jnp.int32, first.shape, first.ndim - 1) < LANES // 2
    axis = first.ndim - 1
    return (
        jnp.where(low, first, pltpu.roll(second, LANES // 2, axis)),
        jnp.where(low, pltpu.roll(first, LANES // 2, axis), second),
    )


def pick(flag, zero, one):
    return jnp.where(flag == 0, zero, one)


def mask_chunk(info, part, row, half):
    token = lax.broadcasted_iota(jnp.int32, (1, LANES), 1) + half * LANES
    live = (info[3] + part * BLOCK + row < info[4]).astype(F32)
    return (token < info[4]).astype(F32) * live


def each_rows(work):
    step = pl.program_id(0)

    @pl.loop(0, SOME // PAIRED)
    def _(turn):
        here = [turn * PAIRED + n for n in range(PAIRED)]
        work(here, [step * SOME + row for row in here])


def first_step(work):
    pl.when(pl.program_id(0) == 0)(work)


def last_step(work):
    pl.when(pl.program_id(0) == STEPS - 1)(work)


def places_of(here, rows):
    for n, (spot, row) in enumerate(zip(here, rows)):
        for half in range(2):
            start = (2 * n + half) * LANES
            yield spot, row, half, (LOW, HIGH)[half], slice(start, start + LANES)


def turned(ref, spot, lanes):
    return ref[spot, lanes, :].astype(F32).T


def stacked(ref, rows):
    return jnp.concatenate([ref[row] for row in rows], axis=1)


def side_by_side(chunks):
    return jnp.concatenate(chunks, axis=1)


def put_gated(info, part, mixture, here, rows, left_st, right_st, gate_out, factor_out):
    size = left_st.shape[2]
    for spot, row, half, lanes, among in places_of(here, rows):
        mask = mask_chunk(info, part, row, half)
        for block, stage in enumerate((left_st, right_st)):
            gate = opened(mixture[(2 + block) * size : (3 + block) * size, among])
            opening = gate * mask
            side = mixture[block * size : (block + 1) * size, among] * opening
            stage[half, row] = side.astype(BF16)
            factor_out[spot, block * size : (block + 1) * size, lanes] = opening.astype(BF16)
            slope = (side * (1.0 - gate)).astype(BF16)
            factor_out[spot, (2 + block) * size : (3 + block) * size, lanes] = slope
        gate_out[spot, :, lanes] = opened(mixture[4 * size :, among]).astype(BF16)


def opened(gate):
    return 0.5 * jnp.tanh(gate) + 0.5


def column(row):
    return jnp.broadcast_to(row, (LANES, row.shape[1])).T


def halved_turned(weight):
    values = 2 * weight.shape[0]
    return jnp.concatenate([weight[:, :values].T, weight[:, values:].T * 0.5], axis=0).astype(BF16)


def entry_kernel(part, info, pair, norm_row, proj_w, *rest):
    if part:
        raw, rest = rest[:6], rest[6:]
        gain1, final1, norm2, proj2, gain2, final2 = raw
        prepared, rest = rest[7:18], rest[:7] + rest[18:]
    a_same, a_other, b_same, b_other, to_core, gate_out, factor_out, *rest = rest
    left_st, right_st, norm, proj_t, perm = rest
    hidden = proj_w.shape[1] // 5

    @first_step
    def _():
        norm[...] = column(norm_row[...])
        proj_t[...] = halved_turned(proj_w[...])
        perm[...] = reorder()
        if part:
            for row, out in zip((norm_row, gain1, norm2, gain2), prepared[:4]):
                out[...] = column(row[...])
            prepared[4][...] = halved_turned(proj2[...])
            for weight, out in zip((final1, final2), prepared[5:7]):
                out[...] = weight[...].T.astype(BF16)
            for weight, out in zip((proj_w, final1, proj2, final2), prepared[7:]):
                out[...] = weight[...].astype(BF16)

    def work(here, rows):
        normed = side_by_side(
            [
                (normalise(turned(pair, spot, lanes))[0] * norm[...]).astype(BF16)
                for spot, row, half, lanes, among in places_of(here, rows)
            ]
        )
        mixture = dot_nn(proj_t[...], normed)
        put_gated(info, part, mixture, here, rows, left_st, right_st, gate_out, factor_out)

    each_rows(work)

    @last_step
    def _():
        core = info[2]
        for owner, a_out, b_out in ((core, a_same, b_same), (1 - core, a_other, b_other)):
            for group in range(2):
                for at in CHUNKS:
                    channel = owner * (2 * GROUP) + group * GROUP + at
                    left = dot_nn(perm[...], get_chunk(left_st, (0, 1), channel)).astype(BF16)
                    right = dot_nn(perm[...], get_chunk(right_st, (0, 1), channel)).astype(BF16)
                    first, second = (left, right) if group == 0 else (right, left)
                    give_chunk(a_out, group, at, BOTH, first)
                    give_chunk(b_out, group, at, BOTH, second)
                    if a_out is a_other:
                        give_chunk(to_core, group, at, BOTH, first)
                        give_chunk(to_core, 2 + group, at, BOTH, second)


def fill_split(info, perm, stage, own, near, ypart, ycpart, xpart, xcpart):
    x, y, core = info[0], info[1], info[2]
    for owner, mine, yp, xp in ((core, own, ypart, xpart), (1 - core, near, ycpart, xcpart)):
        for at in CHUNKS:
            channel = owner * (2 * GROUP) + at
            both = jnp.concatenate([chunk(mine, 0, at, LOW), chunk(yp, 0, at, LOW)], axis=1)
            both = dot_nn(perm, both)
            put_chunk(stage, y, channel, both[:, LOW])
            put_chunk(stage, 1 - y, channel, both[:, HIGH])
            both = jnp.concatenate([chunk(mine, 1, at, LOW), chunk(xp, 0, at, LOW)], axis=1)
            both = dot_nn(perm, both)
            here, there = both[:, LOW], both[:, HIGH]
            first, second = half_swap(pick(x, here, there), pick(x, there, here))
            put_chunk(stage, 0, channel + GROUP, first)
            put_chunk(stage, 1, channel + GROUP, second)


def fill_sum(perm, stage, channel, first, second):
    both = (chunk(*first).astype(F32) + chunk(*second).astype(F32)).astype(BF16)
    total = dot_nn(perm, both)
    put_chunk(stage, 0, channel, total[:, LOW])
    put_chunk(stage, 1, channel, total[:, HIGH])


def split_out(info, perm, stage, owner, at):
    x, y = info[0], info[1]
    channel = owner * (2 * GROUP) + at
    both = dot_nn(perm, get_chunk(stage, (y, 1 - y), channel))
    swapped = dot_nn(perm, get_chunk(stage, (0, 1), channel + GROUP))
    first, second = half_swap(swapped[:, LOW], swapped[:, HIGH])
    return both[:, LOW], both[:, HIGH], pick(x, first, second), pick(x, second, first)


def middle_kernel(
    part, info, pair, own, ypart, xpart, ycpart, xcpart, near,
    gate1, gain1, final1_t, norm2, proj2_t,
    middle_out, inner_out, gate_out, factor_out, normed_out, final_out, slope_out, o_own, o_near, o_y, o_yc, o_x, o_xc,
    stage, left_st, right_st, perm,
):
    @first_step
    def _():
        perm[...] = reorder()
        fill_split(info, perm[...], stage, own, near, ypart, ycpart, xpart, xcpart)

    def work(here, rows):
        finals, normeds = [], []
        for spot, row, half, lanes, among in places_of(here, rows):
            inner = stage[half, row]
            final = (normalise(inner)[0] * gain1[...]).astype(BF16)
            inner_out[spot, :, lanes] = inner.astype(BF16)
            final_out[spot, :, lanes] = final
            finals.append(final)
        product = dot_nn(final1_t[...], side_by_side(finals))
        for spot, row, half, lanes, among in places_of(here, rows):
            gate = gate1[spot, :, lanes].astype(F32)
            update = product[:, among] * gate
            slope_out[spot, :, lanes] = (update * (1.0 - gate)).astype(BF16)
            middle = (turned(pair, spot, lanes) + update).astype(BF16)
            middle_out[spot, :, lanes] = middle
            normed = (normalise(middle.astype(F32))[0] * norm2[...]).astype(BF16)
            normed_out[spot, :, lanes] = normed
            normeds.append(normed)
        mixture = dot_nn(proj2_t[...], side_by_side(normeds))
        put_gated(info, part, mixture, here, rows, left_st, right_st, gate_out, factor_out)

    each_rows(work)

    @last_step
    def _():
        core = info[2]
        beyond = slice(LANES, 3 * LANES)
        for owner, main, yo, xo in ((core, o_own, o_y, o_x), (1 - core, o_near, o_yc, o_xc)):
            for at in CHUNKS:
                kept = split_out(info, perm[...], left_st, owner, at)
                give_chunk(main, 0, at, LOW, kept[0])
                give_chunk(yo, 0, at, LOW, kept[1])
                give_chunk(main, 1, at, LOW, kept[2])
                give_chunk(xo, 0, at, LOW, kept[3])
                for group, out in ((0, yo), (1, xo)):
                    channel = owner * (2 * GROUP) + group * GROUP + at
                    right = dot_nn(perm[...], get_chunk(right_st, (0, 1), channel)).astype(BF16)
                    give_chunk(main, group, at, beyond, right)
                    give_chunk(out, 0, at, beyond, right)


def turn_kernel(
    part, info, gate2, cot, own, ypart, xpart, ycpart, xcpart, near,
    gain2, final2_t, final2_w,
    gate_out, final_out, product_out, same0, same1, other0, other1, to_core, stage, out_st, perm,
):
    core = info[2]

    @first_step
    def _():
        perm[...] = reorder()
        for owner, mine, xp, yp in ((core, own, xpart, ypart), (1 - core, near, xcpart, ycpart)):
            for at in CHUNKS:
                channel = owner * (2 * GROUP) + at
                fill_sum(perm[...], stage, channel, (mine, 0, at, BOTH), (xp, 0, at, BOTH))
                fill_sum(perm[...], stage, channel + GROUP, (mine, 1, at, BOTH), (yp, 0, at, BOTH))

    def work(here, rows):
        finals, products = [], []
        for spot, row, half, lanes, among in places_of(here, rows):
            final = (normalise(stage[half, row])[0] * gain2[...]).astype(BF16)
            final_out[spot, :, lanes] = final
            finals.append(final)
            grad_product = turned(cot, spot, lanes) * gate2[spot, :, lanes].astype(F32)
            grad_product = grad_product.astype(BF16)
            product_out[spot, :, lanes] = grad_product
            products.append(grad_product)
        product = dot_nn(final2_t[...], side_by_side(finals))
        grad_final = dot_nn(final2_w[...], side_by_side(products))
        for spot, row, half, lanes, among in places_of(here, rows):
            gate = gate2[spot, :, lanes].astype(F32)
            grad_gate = turned(cot, spot, lanes) * product[:, among] * gate * (1.0 - gate)
            gate_out[spot, :, lanes] = grad_gate.astype(BF16)
            hat, spread = normalise(stage[half, row])
            grad_inner = normalise_back(grad_final[:, among] * gain2[...], hat, spread)
            out_st[half, row] = grad_inner.astype(BF16)

    each_rows(work)

    @last_step
    def _():
        for owner, outs in ((core, (same0, same1)), (1 - core, (other0, other1))):
            for group, out in enumerate(outs):
                for at in CHUNKS:
                    channel = owner * (2 * GROUP) + group * GROUP + at
                    value = dot_nn(perm[...], get_chunk(out_st, (0, 1), channel)).astype(BF16)
                    give_chunk(out, 0, at, BOTH, value)
                    if out is other0 or out is other1:
                        give_chunk(to_core, group, at, BOTH, value)


def mixture_chunk(left_st, right_st, factors, gate_in, spot, row, half, lanes):
    size = left_st.shape[2]
    grads = (left_st[half, row], right_st[half, row])
    blocks = [
        (grads[n % 2] * factors[spot, n * size : (n + 1) * size, lanes].astype(F32)).astype(BF16)
        for n in range(4)
    ]
    return jnp.concatenate(blocks + [gate_in[spot, :, lanes]], axis=0)


def inward_kernel(
    part, info, middle, gate1, cot, inner_in, gate_in, factors, slopes, own, ypart, xpart, ycpart, xcpart, near,
    norm2, proj2_w, gain1, final1_w,
    grad_out, gate_out, mixture_out, product_out, o_own, o_near, o_y, o_yc, o_x, o_xc,
    left_st, right_st, out_st, perm,
):
    core = info[2]

    @first_step
    def _():
        perm[...] = reorder()
        fill_split(info, perm[...], left_st, own, near, ypart, ycpart, xpart, xcpart)
        beyond = slice(LANES, 3 * LANES)
        for owner, mine, yp, xp in ((core, own, ypart, xpart), (1 - core, near, ycpart, xcpart)):
            for at in CHUNKS:
                channel = owner * (2 * GROUP) + at
                fill_sum(perm[...], right_st, channel, (mine, 0, at, beyond), (yp, 0, at, beyond))
                fill_sum(
                    perm[...], right_st, channel + GROUP, (mine, 1, at, beyond), (xp, 0, at, beyond)
                )

    def work(here, rows):
        mixtures, products = [], []
        for spot, row, half, lanes, among in places_of(here, rows):
            mixture = mixture_chunk(left_st, right_st, factors, gate_in, spot, row, half, lanes)
            mixture_out[spot, :, lanes] = mixture
            mixtures.append(mixture)
        grad_normed = dot_nn(proj2_w[...], side_by_side(mixtures))
        for spot, row, half, lanes, among in places_of(here, rows):
            hat, spread = normalise(middle[spot, :, lanes].astype(F32))
            grad = normalise_back(grad_normed[:, among] * norm2[...], hat, spread)
            grad = grad + turned(cot, spot, lanes)
            grad_out[spot, :, lanes] = grad
            gate_out[spot, :, lanes] = (grad * slopes[spot, :, lanes].astype(F32)).astype(BF16)
            grad_product = (grad * gate1[spot, :, lanes].astype(F32)).astype(BF16)
            product_out[spot, :, lanes] = grad_product
            products.append(grad_product)
        grad_final = dot_nn(final1_w[...], side_by_side(products))
        for spot, row, half, lanes, among in places_of(here, rows):
            hat, spread = normalise(inner_in[spot, :, lanes].astype(F32))
            grad_inner = normalise_back(grad_final[:, among] * gain1[...], hat, spread)
            out_st[half, row] = grad_inner.astype(BF16)

    each_rows(work)

    @last_step
    def _():
        for owner, main, yo, xo in ((core, o_own, o_y, o_x), (1 - core, o_near, o_yc, o_xc)):
            for at in CHUNKS:
                kept = split_out(info, perm[...], out_st, owner, at)
                give_chunk(main, 0, at, LOW, kept[0])
                give_chunk(yo, 0, at, LOW, kept[1])
                give_chunk(main, 1, at, LOW, kept[2])
                give_chunk(xo, 0, at, LOW, kept[3])


def weight_kernel(info, *refs):
    *refs, total = refs
    (mixtures, normeds, *pairs) = paired(refs)
    width, channels = mixtures[0].shape[1], normeds[0].shape[1]

    @pl.when(pl.program_id(0) == 0)
    def _():
        total[...] = jnp.zeros_like(total)

    for part in range(PARTS):
        for first in range(0, mixtures[part].shape[0], PAIRED):
            rows = [first + n for n in range(PAIRED)]
            mixture, normed = stacked(mixtures[part], rows), stacked(normeds[part], rows)
            total[:width, :] += dot_nt(mixture, normed)
            for n, (finals, products) in enumerate((pairs[:2], pairs[2:])):
                where = slice(width + n * channels, width + (n + 1) * channels)
                final, product = stacked(finals[part], rows), stacked(products[part], rows)
                total[where, :] += dot_nt(final, product)


def exit_kernel(
    part, info, pair, grad_in, gate_in, factors, own, ypart, xpart, ycpart, xcpart, near,
    norm1, proj1_w, early, *rest,
):
    out, gproj, *rest, left_st, right_st, perm = rest
    if part:
        before, unused, out, gproj, packed = (out, gproj, *rest)
    core = info[2]

    @first_step
    def _():
        perm[...] = reorder()
        gproj[...] = before[...] if part else jnp.zeros_like(gproj)
        beyond = slice(2 * LANES, 4 * LANES)
        for owner, mine, yp, xp in ((core, own, ypart, xpart), (1 - core, near, ycpart, xcpart)):
            for group, lefts, rights in ((0, yp, xp), (1, xp, yp)):
                for at in CHUNKS:
                    channel = owner * (2 * GROUP) + group * GROUP + at
                    fill_sum(
                        perm[...], left_st, channel, (mine, group, at, BOTH), (lefts, group, at, BOTH)
                    )
                    fill_sum(
                        perm[...],
                        right_st,
                        channel,
                        (mine, group, at, beyond),
                        (rights, group, at, BOTH),
                    )

    def work(here, rows):
        mixtures, normeds = [], []
        for spot, row, half, lanes, among in places_of(here, rows):
            normeds.append(
                (normalise(turned(pair, spot, lanes))[0] * norm1[...]).astype(BF16)
            )
            mixtures.append(
                mixture_chunk(left_st, right_st, factors, gate_in, spot, row, half, lanes)
            )
        mixture = side_by_side(mixtures)
        gproj[...] += dot_nt(mixture, side_by_side(normeds))
        grad_normed = dot_nn(proj1_w[...], mixture)
        for spot, row, half, lanes, among in places_of(here, rows):
            hat, spread = normalise(turned(pair, spot, lanes))
            grad = normalise_back(grad_normed[:, among] * norm1[...], hat, spread)
            out[spot, lanes, :] = (grad_in[spot, :, lanes] + grad).T

    each_rows(work)

    if part:

        @last_step
        def _():
            size = gproj.shape[0]
            packed[:size, :] = gproj[...].astype(BF16)
            packed[size:, :] = early[...].astype(BF16)


CHANNELS = 8
PARTS = 2


def paired(refs):
    return [refs[n : n + PARTS] for n in range(0, len(refs), PARTS)]


def place(one, two, part):
    return pl.multiple_of((one * 2 + two) * (PARTS * BLOCK) + part * BLOCK, BLOCK)


def places(info, group):
    at, core = info[group], info[2]
    return [
        place(at if n < 2 else 1 - at, core if n % 2 == 0 else 1 - core, part)
        for n in range(4)
        for part in range(PARTS)
    ]


def take(ref, group, h):
    return ref[group, h] if len(ref.shape) == 4 else ref[h]


def joined(quads, group, h):
    return jnp.concatenate([take(ref, group, h) for refs in quads for ref in refs], axis=0)


def gather(stage, slot, wheres, quads, group, h):
    for where, ref in zip(wheres, [ref for refs in quads for ref in refs]):
        stage[slot, pl.ds(where, BLOCK), :] = take(ref, group, h)
    return stage[slot]


def give(refs, group, h, lanes, value):
    if len(refs.shape) == 4:
        refs[group, h, :, lanes] = value
    else:
        refs[h, :, lanes] = value


def scatter(quads, group, h, lanes, value):
    for n, ref in enumerate([ref for refs in quads for ref in refs]):
        give(ref, group, h, lanes, value[n * BLOCK : (n + 1) * BLOCK])


def scatter_from(stage, slot, wheres, quads, group, h, lanes):
    for where, ref in zip(wheres, [ref for refs in quads for ref in refs]):
        give(ref, group, h, lanes, stage[slot, pl.ds(where, BLOCK), :])


def outgoing_kernel(info, *refs):
    *refs, stage = refs
    *refs, o_own, o_near, o_y, o_yc, o_x, o_xc = refs
    a_own, b_own, a_y, b_x, a_yc, b_xc, near = paired(refs)
    a_near, b_near = [ref.at[:2] for ref in near], [ref.at[2:] for ref in near]
    along_a, along_b = (a_own, a_near, a_y, a_yc), (b_own, b_near, b_x, b_xc)
    for h in range(CHANNELS):
        for group in range(2):
            lefts, rights = (along_a, along_b) if group == 0 else (along_b, along_a)
            far = (o_y, o_yc) if group == 0 else (o_x, o_xc)
            right = gather(stage, 2 * h + group, places(info, group), rights, group, h)
            inner = dot_nt(joined(lefts, group, h), right).astype(BF16)
            for n, out in enumerate((o_own, o_near) + far):
                rows = PARTS * BLOCK
                give(out, group, h, slice(0, LANES), inner[n * rows : (n + 1) * rows])


def halves(quads, group, h):
    both = joined(quads, group, h)
    return both[:, :LANES], both[:, LANES:]


def incoming_kernel(info, *refs):
    *refs, stage = refs
    own, ypart, xpart, ycpart, xcpart, near, o_own, o_near, o_x, o_xc, o_y, o_yc = paired(refs)
    for h in range(CHANNELS):
        for group in range(2):
            far = (ypart, ycpart) if group == 0 else (xpart, xcpart)
            outs = (o_own, o_near) + ((o_x, o_xc) if group == 0 else (o_y, o_yc))
            slot = 2 * h + group
            left, right = halves((own, near) + far, group, h)
            stage[slot] = dot_tn(left, right).astype(BF16)
            scatter_from(stage, slot, places(info, group), outs, group, h, slice(0, 2 * LANES))


def incoming_back_kernel(info, *refs):
    *refs, stage = refs
    own, ypart, xpart, ycpart, xcpart, near, *more = paired(refs)
    same0, same1, g_y, g_x, g_yc, g_xc, g_near, *more = more
    o_own, o_near, o_y, o_yc, o_x, o_xc = more
    for h in range(CHANNELS):
        for group in range(2):
            far = (ypart, ycpart) if group == 0 else (xpart, xcpart)
            grads = (same0, g_near, g_x, g_xc) if group == 0 else (same1, g_near, g_y, g_yc)
            outs = (o_own, o_near) + ((o_y, o_yc) if group == 0 else (o_x, o_xc))
            grad = gather(stage, 2 * h + group, places(info, group), grads, group, h)
            left, right = halves((own, near) + far, group, h)
            scatter(outs, group, h, slice(0, LANES), dot_nt(right, grad).astype(BF16))
            scatter(outs, group, h, slice(LANES, 3 * LANES), dot_nn(left, grad).astype(BF16))


def outgoing_back_kernel(info, *refs):
    *refs, stage, back = refs
    a_own, b_own, a_y, b_x, a_yc, b_xc, near, *more = paired(refs)
    a_near, b_near = [ref.at[:2] for ref in near], [ref.at[2:] for ref in near]
    g_own, g_y, g_x, g_yc, g_xc, g_near, o_own, o_near, o_y, o_yc, o_x, o_xc = more
    along_a, along_b = (a_own, a_near, a_y, a_yc), (b_own, b_near, b_x, b_xc)
    first, second = slice(0, 2 * LANES), slice(2 * LANES, 4 * LANES)
    for h in range(CHANNELS):
        for group in range(2):
            lefts, rights = (along_a, along_b) if group == 0 else (along_b, along_a)
            far = (g_y, g_yc) if group == 0 else (g_x, g_xc)
            left_far, right_far = ((o_y, o_yc), (o_x, o_xc)) if group == 0 else ((o_x, o_xc), (o_y, o_yc))
            slot = 2 * h + group
            wheres = places(info, group)
            right = gather(stage, slot, wheres, rights, group, h)
            grad = joined((g_own, g_near) + far, group, h)
            grad_left = dot_nn(grad, right).astype(BF16)
            back[slot] = dot_tn(grad, joined(lefts, group, h)).astype(BF16)
            core_rows = 2 * PARTS * BLOCK
            scatter((o_own, o_near), group, h, first, grad_left[:core_rows])
            scatter(left_far, group, h, first, grad_left[core_rows:])
            scatter_from(back, slot, wheres[: 2 * PARTS], (o_own, o_near), group, h, second)
            scatter_from(back, slot, wheres[2 * PARTS :], right_far, group, h, first)


def whole(shape):
    return pl.BlockSpec(shape, lambda step, info: (0,) * len(shape))


def rows_of(part, some=SOME):
    def make(shape):
        first = part * (BLOCK // some)
        return pl.BlockSpec(
            (some,) + shape[1:], lambda step, info: (first + step,) + (0,) * (len(shape) - 1)
        )

    return make


def rows_block(part):
    def make(shape):
        return pl.BlockSpec(
            shape[:-2] + (BLOCK, shape[-1]),
            lambda step, info: (0,) * (len(shape) - 2) + (part, 0),
        )

    return make


def anywhere(shape):
    return pl.BlockSpec(memory_space=pl.ANY)


def channel_rows(shape):
    if len(shape) == 4:
        return pl.BlockSpec((shape[0], CHANNELS) + shape[2:], lambda step, info: (0, step, 0, 0))
    return pl.BlockSpec((CHANNELS,) + shape[1:], lambda step, info: (step, 0, 0))


def call(kernel, info, steps, ins, outs, scratch, aliases={}, vmem=CELL_VMEM):
    return pl.pallas_call(
        kernel,
        grid_spec=pltpu.PrefetchScalarGridSpec(
            num_scalar_prefetch=1,
            grid=(steps,),
            in_specs=[make(array.shape) for array, make in ins],
            out_specs=[make(shape) for shape, unused, make in outs],
            scratch_shapes=scratch,
        ),
        out_shape=[jax.ShapeDtypeStruct(shape, dtype) for shape, dtype, unused in outs],
        compiler_params=pltpu.CompilerParams(vmem_limit_bytes=vmem),
        input_output_aliases=aliases,
    )(info, *[array for array, unused in ins])


class Links:
    def __init__(self):
        self.last = {}

    def send(self, array, offset, first=None):
        count = lax.axis_size("axial")
        if first is not None:
            array, unused = lax.optimization_barrier((array, first))
        if offset in self.last and offset in (X, Y):
            array, unused = lax.optimization_barrier((array, self.last[offset]))
        self.last[offset] = lax.ppermute(
            array, "axial", [(n, n ^ offset) for n in range(count)]
        )
        return self.last[offset]

    def __call__(self, *sends, between=None):
        results = [[] for unused in sends]
        for part in range(len(sends[0][0])):
            for result, (arrays, offset) in zip(results, sends):
                result.append(self.send(arrays[part], offset, between if part else None))
        return results


CORE, X, Y = 1, 2, 4


def add_up(share):
    count = lax.axis_size("axial")
    rows, width = share.shape
    shares = share.reshape(count, rows // count, width)
    parts = lax.all_to_all(shares, "axial", split_axis=0, concat_axis=0, tiled=True)
    mine = parts.astype(F32).sum(axis=0).astype(BF16)
    depth = lax.axis_size("dp")
    terms = [mine] + [
        lax.ppermute(mine, "dp", [(n, n ^ offset) for n in range(depth)])
        for offset in range(1, depth)
    ]
    terms = [term.astype(F32) for term in terms]
    while len(terms) > 1:
        terms = [terms[n] + terms[n + 1] for n in range(0, len(terms), 2)]
    copies = jnp.broadcast_to(terms[0].astype(BF16)[None], shares.shape)
    return lax.all_to_all(copies, "axial", split_axis=0, concat_axis=0, tiled=True).reshape(
        rows, width
    )


def gain_grad(weight_grad, weight, gain_row):
    return jnp.sum((weight.astype(F32) * weight_grad).T, axis=0, keepdims=True) / gain_row


def finish_kernel(
    scale, info, sums, proj1, final1, proj2, final2, norm1, gain1, norm2, gain2,
    o_norm1, o_proj1, o_gain1, o_final1, o_norm2, o_proj2, o_gain2, o_final2,
):
    width, channels = proj1.shape[1], final1.shape[1]
    takes = (
        (0, True, proj1, norm1, o_proj1, o_norm1),
        (width, True, proj2, norm2, o_proj2, o_norm2),
        (2 * width, False, final2, gain2, o_final2, o_gain2),
        (2 * width + channels, False, final1, gain1, o_final1, o_gain1),
    )
    for start, flipped, weight, gain, out, gain_out in takes:
        total = sums[start : start + weight.shape[1], :].astype(F32) * scale
        total = total.T if flipped else total
        out[...] = total
        gain_out[...] = gain_grad(total, weight[...].astype(BF16), gain[...])


def fast_body(
    pair,
    cotangent,
    lengths,
    outgo_norm,
    outgo_proj,
    outgo_gain,
    outgo_final,
    incom_norm,
    incom_proj,
    incom_gain,
    incom_final,
):
    rows, tokens, channels = pair.shape[1:]
    hidden = outgo_gain.shape[0]
    index = lax.axis_index("axial")
    info = jnp.stack(
        [(index // 2) % 2, index // 4, index % 2, index * rows, lengths[0]]
    ).astype(jnp.int32)
    hop = Links()
    pair = pair[0]
    cot = cotangent[0]
    parts = range(PARTS)
    turns = GROUP // CHANNELS
    stage = pltpu.VMEM((2, BLOCK, hidden, LANES), F32)
    out_stage = pltpu.VMEM((2, BLOCK, hidden, LANES), BF16)
    perm = pltpu.VMEM((BLOCK * BLOCK, BLOCK * BLOCK), BF16)
    streamed = rows_of(0)
    square = pltpu.VMEM((2 * CHANNELS, 4 * rows, tokens), BF16)

    def two(width, height=BLOCK, make=whole, groups=2):
        return ((groups, GROUP, height, width), BF16, make)

    def one(width, height=BLOCK, make=whole):
        return ((GROUP, height, width), BF16, make)

    turned_block = ((BLOCK, channels, tokens), BF16, streamed)
    factor_block = ((BLOCK, 4 * hidden, tokens), BF16, streamed)
    mixture_block = ((BLOCK, 5 * hidden, tokens), BF16, streamed)

    def cells(kernel, ins, outs, scratch, more=lambda part: []):
        results = []
        for part in parts:
            carried = ins(part, results)
            results.append(
                call(functools.partial(kernel, part), info, STEPS, carried, outs + more(part), scratch)
            )
        shared = results[-1][len(outs) :]
        return [list(each) for each in zip(*results)] + list(shared)

    def wholes(arrays):
        return [(array, whole) for array in arrays]

    def triangle(kernel, operands, outs, scratch, split=PARTS):
        ins = [(array, channel_rows) for arrays in operands for array in arrays]
        each = [out for out in outs for unused in range(split)]
        results = call(kernel, info, turns, ins, each, scratch, vmem=TRIANGLE_VMEM)
        return [list(results[n : n + split]) for n in range(0, len(results), split)]

    raw = (outgo_gain[None], outgo_final, incom_norm[None], incom_proj, incom_gain[None], incom_final)
    gain_wide = ((channels, LANES), F32, whole)
    proj_turned = ((5 * hidden, channels), BF16, whole)
    proj_plain = ((channels, 5 * hidden), BF16, whole)
    final_plain = ((hidden, channels), BF16, whole)
    (
        a_same, a_other, b_same, b_other, to_core, gate_one, factors_one,
        norm1, gain1, norm2, gain2, proj2_t, final1_t, final2_t,
        proj1, final1, proj2, final2,
    ) = cells(
        entry_kernel,
        lambda part, unused: [(pair, rows_of(part)), (outgo_norm[None], whole), (outgo_proj, whole)]
        + (wholes(raw) if part else []),
        [two(tokens)] * 4 + [two(tokens, groups=4), turned_block, factor_block],
        [
            out_stage,
            out_stage,
            pltpu.VMEM((channels, LANES), F32),
            pltpu.VMEM((5 * hidden, channels), BF16),
            perm,
        ],
        lambda part: (
            [gain_wide] * 4
            + [proj_turned]
            + [final_plain] * 2
            + [proj_plain, final_plain] * 2
            if part
            else []
        ),
    )
    held_one = [a_same, b_same] + hop(
        (a_same, Y), (b_same, X), (a_other, Y | CORE), (b_other, X | CORE), (to_core, CORE)
    )
    own, near, to_y, to_yc, to_x, to_xc = triangle(
        outgoing_kernel,
        held_one,
        [two(LANES, rows, channel_rows)] * 2 + [one(LANES, rows, channel_rows)] * 4,
        [square],
        split=1,
    )
    back_one = [
        own,
        *hop(
            (to_y, Y), (to_x, X), (to_yc, Y | CORE), (to_xc, X | CORE), (near, CORE)
        ),
    ]

    (
        middle, inner_one, gate_two, factors_two, normed_two, finals_one, slopes_one,
        own, near, to_y, to_yc, to_x, to_xc,
    ) = cells(
        middle_kernel,
        lambda part, unused: [(pair, rows_of(part))]
        + [(array, rows_block(part)) for array, in back_one]
        + [(gate_one[part], streamed)]
        + wholes((gain1, final1_t, norm2, proj2_t)),
        [turned_block] * 3
        + [factor_block]
        + [turned_block] * 3
        + [two(3 * LANES)] * 2 + [one(3 * LANES)] * 4,
        [stage, out_stage, out_stage, perm],
    )
    held_two = [
        own,
        *hop(
            (to_y, Y), (to_x, X), (to_yc, Y | CORE), (to_xc, X | CORE), (near, CORE)
        ),
    ]
    own, near, to_x, to_xc, to_y, to_yc = triangle(
        incoming_kernel,
        held_two,
        [two(tokens, make=channel_rows)] * 2 + [one(tokens, make=channel_rows)] * 4,
        [square],
    )
    back_two = [
        own,
        *hop(
            (to_y, Y), (to_x, X), (to_yc, Y | CORE), (to_xc, X | CORE), (near, CORE)
        ),
    ]

    gate_grad_two, finals_two, products_two, same0, same1, other0, other1, to_core = cells(
        turn_kernel,
        lambda part, done: [(gate_two[part], streamed), (cot, rows_of(part))]
        + wholes(arrays[part] for arrays in back_two)
        + wholes((gain2, final2_t, final2)),
        [turned_block] * 3 + [one(tokens)] * 4 + [two(tokens)],
        [stage, out_stage, perm],
    )
    grads_two = [
        same0,
        same1,
        *hop(
            (same1, Y), (same0, X), (other1, Y | CORE), (other0, X | CORE), (to_core, CORE)
        ),
    ]
    own, near, to_y, to_yc, to_x, to_xc = triangle(
        incoming_back_kernel,
        held_two + grads_two,
        [two(3 * LANES, make=channel_rows)] * 2 + [one(3 * LANES, make=channel_rows)] * 4,
        [square],
    )
    rows_two = [
        own,
        *hop(
            (to_y, Y), (to_x, X), (to_yc, Y | CORE), (to_xc, X | CORE), (near, CORE)
        ),
    ]

    (
        grad_middle, gate_grad_one, mixtures_two, products_one,
        own, near, to_y, to_yc, to_x, to_xc,
    ) = cells(
        inward_kernel,
        lambda part, done: [
            (middle[part], streamed),
            (gate_one[part], streamed),
            (cot, rows_of(part)),
            (inner_one[part], streamed),
            (gate_grad_two[part], streamed),
            (factors_two[part], streamed),
            (slopes_one[part], streamed),
        ]
        + wholes(arrays[part] for arrays in rows_two)
        + wholes((norm2, proj2, gain1, final1)),
        [((BLOCK, channels, tokens), F32, streamed), turned_block, mixture_block, turned_block]
        + [two(LANES)] * 2
        + [one(LANES)] * 4,
        [stage, stage, out_stage, perm],
    )
    grads_one = [
        own,
        *hop(
            (to_y, Y), (to_x, X), (to_yc, Y | CORE), (to_xc, X | CORE), (near, CORE)
        ),
    ]
    own, near, to_y, to_yc, to_x, to_xc = triangle(
        outgoing_back_kernel,
        held_one + grads_one,
        [two(2 * tokens, make=channel_rows)] * 2 + [two(tokens, make=channel_rows)] * 4,
        [square, square],
    )
    kept = (mixtures_two, normed_two, finals_two, products_two, finals_one, products_one)
    (early,) = call(
        weight_kernel,
        info,
        4,
        [
            (array, rows_of(0, BLOCK // 4))
            for arrays in kept
            for array in arrays
        ],
        [((5 * hidden + 2 * channels, channels), F32, whole)],
        [],
    )
    rows_one = [own] + hop(
        (to_y, Y), (to_x, X), (to_yc, Y | CORE), (to_xc, X | CORE), (near, CORE), between=early
    )
    exit_ins = 10 + 3 + 1 + 1
    result = None
    for part in parts:
        result = call(
            functools.partial(exit_kernel, part),
            info,
            STEPS,
            [
                (pair, rows_of(part)),
                (grad_middle[part], streamed),
                (gate_grad_one[part], streamed),
                (factors_one[part], streamed),
            ]
            + wholes(arrays[part] for arrays in rows_one)
            + wholes((norm1, proj1, early))
            + ([(result[1], whole), (result[0], anywhere)] if part else []),
            [
                ((rows, tokens, channels), F32, rows_of(part)),
                ((5 * hidden, channels), F32, whole),
            ]
            + ([((10 * hidden + 2 * channels, channels), BF16, whole)] if part else []),
            [stage, stage, perm],
            {exit_ins: 0} if part else {},
        )
    grad_begin, unused, packed = result
    sums = add_up(packed)
    scale = 1.0 / math.sqrt(lax.axis_size("dp") * tokens * tokens)
    weights = (outgo_proj, outgo_final, incom_proj, incom_final)
    gains = (outgo_norm, outgo_gain, incom_norm, incom_gain)
    order = (outgo_norm[None], outgo_proj, outgo_gain[None], outgo_final)
    order += (incom_norm[None], incom_proj, incom_gain[None], incom_final)
    totals = call(
        functools.partial(finish_kernel, scale),
        info,
        1,
        wholes((sums,) + weights + tuple(gain[None] for gain in gains)),
        [(array.shape, F32, whole) for array in order],
        [],
    )
    return (grad_begin[None],) + tuple(
        total.reshape(-1) if total.shape[0] == 1 else total for total in totals
    )


def solution(mesh):
    def body(pair, *rest):
        rows, tokens, channels = pair.shape[1:]
        hidden = rest[3].shape[0]
        plane = mesh.shape["axial"] == 8 and rows == 32 and tokens == 2 * LANES
        if plane and channels == LANES and hidden == 4 * GROUP:
            return fast_body(pair, *rest)
        return plain_body(pair, *rest)

    return jax.shard_map(
        body,
        mesh=mesh,
        in_specs=(P("dp", "axial", None, None), P("dp", "axial", None, None), P("dp")) + (P(),) * 8,
        out_specs=(P("dp", "axial", None, None),) + (P(),) * 8,
        check_vma=False,
    )
```

```python
import functools
import math

import jax
import jax.numpy as jnp
from jax import lax
from jax.experimental import pallas as pl
from jax.experimental.pallas import tpu as pltpu
from jax.sharding import PartitionSpec as P

EPSILON = 1e-05


def rounded(inputs):
    return lax.optimization_barrier(inputs.astype(jnp.bfloat16)).astype(jnp.float32)


def layer_norm(inputs, factor):
    average = jnp.mean(inputs, axis=-1, keepdims=True)
    centered = inputs - average
    spread = jnp.mean(centered * centered, axis=-1, keepdims=True)
    return centered * lax.rsqrt(spread + EPSILON) * factor


def gating(mixture, pair_mask, hidden):
    left_part = (
        mixture[:, :hidden] * jax.nn.sigmoid(mixture[:, 2 * hidden : 3 * hidden]) * pair_mask
    )
    right_part = (
        mixture[:, hidden : 2 * hidden]
        * jax.nn.sigmoid(mixture[:, 3 * hidden : 4 * hidden])
        * pair_mask
    )
    gate_part = jax.nn.sigmoid(mixture[:, 4 * hidden :])
    return (left_part, right_part, gate_part)


def entry(flat_pair, norm_gain, projection, pair_mask, hidden):
    normed = layer_norm(flat_pair, norm_gain).astype(jnp.bfloat16)
    mixture = jnp.dot(normed, projection.astype(jnp.bfloat16), preferred_element_type=jnp.float32)
    left_part, right_part, gate_part = gating(mixture, pair_mask, hidden)
    return (normed, mixture, left_part, right_part, gate_part)


def entry_back(
    flat_pair,
    norm_gain,
    projection,
    pair_mask,
    hidden,
    normed,
    mixture,
    grad_left,
    grad_right,
    grad_gate,
):
    unused, pull_gate = jax.vjp(lambda inner_mix: gating(inner_mix, pair_mask, hidden), mixture)
    grad_mixture = pull_gate((grad_left, grad_right, grad_gate))[0].astype(jnp.bfloat16)
    grad_projection = jnp.dot(normed.T, grad_mixture, preferred_element_type=jnp.float32)
    grad_normed = jnp.dot(
        grad_mixture, projection.astype(jnp.bfloat16).T, preferred_element_type=jnp.float32
    )
    unused, pull_norm = jax.vjp(layer_norm, flat_pair, norm_gain)
    grad_flat, grad_gain = pull_norm(grad_normed)
    return (grad_flat, grad_gain, grad_projection)


def leave(inner_sum, gate_part, out_gain, final_weight):
    final_normed = layer_norm(inner_sum, out_gain).astype(jnp.bfloat16)
    product = jnp.dot(
        final_normed, final_weight.astype(jnp.bfloat16), preferred_element_type=jnp.float32
    )
    return (final_normed, product, product * gate_part)


def leave_back(inner_sum, gate_part, out_gain, final_weight, final_normed, product, grad_update):
    grad_product = (grad_update * gate_part).astype(jnp.bfloat16)
    grad_gate = grad_update * product
    grad_final = jnp.dot(final_normed.T, grad_product, preferred_element_type=jnp.float32)
    grad_normed = jnp.dot(
        grad_product, final_weight.astype(jnp.bfloat16).T, preferred_element_type=jnp.float32
    )
    unused, pull_norm = jax.vjp(layer_norm, inner_sum, out_gain)
    grad_inner, grad_gain = pull_norm(grad_normed)
    return (grad_inner, grad_gate, grad_gain, grad_final)


def channel_major(field, row_count, tokens):
    hidden = field.shape[1]
    return jnp.transpose(field.reshape(row_count, tokens, hidden), (2, 0, 1))


def row_major(field):
    hidden = field.shape[0]
    return jnp.transpose(field, (1, 2, 0)).reshape(-1, hidden)


def plain_body(
    pair,
    cotangent,
    lengths,
    outgo_norm,
    outgo_proj,
    outgo_gain,
    outgo_final,
    incom_norm,
    incom_proj,
    incom_gain,
    incom_final,
):
    row_count = pair.shape[1]
    tokens = pair.shape[2]
    channels = pair.shape[3]
    hidden = outgo_gain.shape[0]
    length = lengths[0]
    first_row = lax.axis_index("axial") * row_count
    row_alive = (first_row + jnp.arange(row_count, dtype=jnp.int32) < length).astype(jnp.float32)
    column_alive = (jnp.arange(tokens, dtype=jnp.int32) < length).astype(jnp.float32)
    pair_mask = (row_alive[:, None] * column_alive[None, :]).reshape(-1, 1)
    flat_start = pair[0].reshape(-1, channels).astype(jnp.float32)
    normed_one, mixture_one, left_one, right_one, gate_one = entry(
        flat_start, outgo_norm, outgo_proj, pair_mask, hidden
    )
    left_first = channel_major(left_one.astype(jnp.bfloat16), row_count, tokens)
    right_first = channel_major(right_one.astype(jnp.bfloat16), row_count, tokens)
    left_owned, right_owned = (
        lax.all_to_all(left_first, "axial", split_axis=0, concat_axis=1, tiled=True),
        lax.all_to_all(right_first, "axial", split_axis=0, concat_axis=1, tiled=True),
    )
    inner_cols = jnp.einsum(
        "hik,hjk->hij", left_owned, right_owned, preferred_element_type=jnp.float32
    )
    inner_one = row_major(
        lax.all_to_all(
            inner_cols.astype(jnp.bfloat16), "axial", split_axis=1, concat_axis=0, tiled=True
        ).astype(inner_cols.dtype)
    )
    final_one, product_one, update_one = leave(inner_one, gate_one, outgo_gain, outgo_final)
    flat_middle = rounded(flat_start + update_one)
    normed_two, mixture_two, left_two, right_two, gate_two = entry(
        flat_middle, incom_norm, incom_proj, pair_mask, hidden
    )
    left_second = channel_major(left_two.astype(jnp.bfloat16), row_count, tokens)
    right_second = channel_major(right_two.astype(jnp.bfloat16), row_count, tokens)
    left_held, right_held = (
        lax.all_to_all(left_second, "axial", split_axis=0, concat_axis=1, tiled=True),
        lax.all_to_all(right_second, "axial", split_axis=0, concat_axis=1, tiled=True),
    )
    inner_held = jnp.einsum(
        "hki,hkj->hij", left_held, right_held, preferred_element_type=jnp.float32
    )
    inner_two = row_major(
        lax.all_to_all(
            inner_held.astype(jnp.bfloat16), "axial", split_axis=1, concat_axis=0, tiled=True
        ).astype(inner_held.dtype)
    )
    final_two, product_two, update_two = leave(inner_two, gate_two, incom_gain, incom_final)
    grad_end = cotangent[0].reshape(-1, channels).astype(jnp.float32)
    grad_inner_two, grad_gate_two, grad_gain_two, grad_final_two = leave_back(
        inner_two, gate_two, incom_gain, incom_final, final_two, product_two, grad_end
    )
    grad_cells_two = channel_major(grad_inner_two.astype(jnp.bfloat16), row_count, tokens)
    grad_held_two = lax.all_to_all(grad_cells_two, "axial", split_axis=0, concat_axis=1, tiled=True)
    left_back, right_back = (
        lax.all_to_all(left_second, "axial", split_axis=0, concat_axis=1, tiled=True),
        lax.all_to_all(right_second, "axial", split_axis=0, concat_axis=1, tiled=True),
    )
    grad_left_held = jnp.einsum(
        "hij,hkj->hki", grad_held_two, right_back, preferred_element_type=jnp.float32
    )
    grad_right_held = jnp.einsum(
        "hki,hij->hkj", left_back, grad_held_two, preferred_element_type=jnp.float32
    )
    grad_left_rows, grad_right_rows = (
        lax.all_to_all(
            grad_left_held.astype(jnp.bfloat16), "axial", split_axis=1, concat_axis=0, tiled=True
        ).astype(grad_left_held.dtype),
        lax.all_to_all(
            grad_right_held.astype(jnp.bfloat16), "axial", split_axis=1, concat_axis=0, tiled=True
        ).astype(grad_right_held.dtype),
    )
    grad_left_two = row_major(grad_left_rows)
    grad_right_two = row_major(grad_right_rows)
    grad_flat_two, grad_norm_two, grad_proj_two = entry_back(
        flat_middle,
        incom_norm,
        incom_proj,
        pair_mask,
        hidden,
        normed_two,
        mixture_two,
        grad_left_two,
        grad_right_two,
        grad_gate_two,
    )
    second_sums = lax.psum(
        (grad_norm_two, grad_proj_two, grad_gain_two, grad_final_two), ("dp", "axial")
    )
    grad_middle = grad_end + grad_flat_two
    grad_inner_one, grad_gate_one, grad_gain_one, grad_final_one = leave_back(
        inner_one, gate_one, outgo_gain, outgo_final, final_one, product_one, grad_middle
    )
    grad_cells_one = channel_major(grad_inner_one.astype(jnp.bfloat16), row_count, tokens)
    grad_owned_one = lax.all_to_all(
        grad_cells_one, "axial", split_axis=0, concat_axis=1, tiled=True
    )
    left_again, right_again = (
        lax.all_to_all(left_first, "axial", split_axis=0, concat_axis=1, tiled=True),
        lax.all_to_all(right_first, "axial", split_axis=0, concat_axis=1, tiled=True),
    )
    grad_left_owned = jnp.einsum(
        "hij,hjk->hik", grad_owned_one, right_again, preferred_element_type=jnp.float32
    )
    grad_right_owned = jnp.einsum(
        "hij,hik->hjk", grad_owned_one, left_again, preferred_element_type=jnp.float32
    )
    grad_left_back, grad_right_back = (
        lax.all_to_all(
            grad_left_owned.astype(jnp.bfloat16), "axial", split_axis=1, concat_axis=0, tiled=True
        ).astype(grad_left_owned.dtype),
        lax.all_to_all(
            grad_right_owned.astype(jnp.bfloat16), "axial", split_axis=1, concat_axis=0, tiled=True
        ).astype(grad_right_owned.dtype),
    )
    grad_left_one = row_major(grad_left_back)
    grad_right_one = row_major(grad_right_back)
    grad_flat_one, grad_norm_one, grad_proj_one = entry_back(
        flat_start,
        outgo_norm,
        outgo_proj,
        pair_mask,
        hidden,
        normed_one,
        mixture_one,
        grad_left_one,
        grad_right_one,
        grad_gate_one,
    )
    grad_begin = grad_middle + grad_flat_one
    first_sums = lax.psum(
        (grad_norm_one, grad_proj_one, grad_gain_one, grad_final_one), ("dp", "axial")
    )
    totals = tuple(first_sums) + tuple(second_sums)
    scale = 1.0 / math.sqrt(lax.axis_size("dp") * tokens * tokens)
    return (
        grad_begin.reshape(1, row_count, tokens, channels),
        totals[0] * scale,
        totals[1] * scale,
        totals[2] * scale,
        totals[3] * scale,
        totals[4] * scale,
        totals[5] * scale,
        totals[6] * scale,
        totals[7] * scale,
    )


BF16 = jnp.bfloat16
F32 = jnp.float32
BLOCK = 16
PAIRED = 2
STEPS = 4
SOME = BLOCK // STEPS
LANES = 128
GROUP = 32
MIB = 1024 * 1024
CELL_VMEM = 30 * MIB
TRIANGLE_VMEM = 14 * MIB


def dot_nn(a, b):
    return lax.dot_general(a, b, (((1,), (0,)), ((), ())), preferred_element_type=F32)


def dot_nt(a, b):
    return lax.dot_general(a, b, (((1,), (1,)), ((), ())), preferred_element_type=F32)


def dot_tn(a, b):
    return lax.dot_general(a, b, (((0,), (0,)), ((), ())), preferred_element_type=F32)


def normalise(v):
    centered = v - jnp.mean(v, axis=0, keepdims=True)
    spread = lax.rsqrt(jnp.mean(centered * centered, axis=0, keepdims=True) + EPSILON)
    return centered * spread, spread


def normalise_back(grad, hat, spread):
    first = jnp.mean(grad, axis=0, keepdims=True)
    second = jnp.mean(grad * hat, axis=0, keepdims=True)
    return spread * (grad - first - hat * second)


def reorder():
    size = BLOCK * BLOCK
    one = lax.broadcasted_iota(jnp.int32, (size, size), 0)
    two = lax.broadcasted_iota(jnp.int32, (size, size), 1)
    return jnp.where((one % BLOCK) * BLOCK + one // BLOCK == two, 1.0, 0.0).astype(BF16)


def chunk(ref, group, at, lanes):
    if len(ref.shape) == 4:
        block = ref[group, at : at + BLOCK, :, lanes]
    else:
        block = ref[at : at + BLOCK, :, lanes]
    return block.reshape(BLOCK * BLOCK, block.shape[2])


def put_chunk(stage, half, channel, value):
    channel = pl.multiple_of(channel, BLOCK)
    for row in range(BLOCK):
        stage[half, row, pl.ds(channel, BLOCK), :] = value[row * BLOCK : (row + 1) * BLOCK]


def get_chunk(stage, halves, channel):
    channel = pl.multiple_of(channel, BLOCK)
    return jnp.concatenate(
        [
            jnp.concatenate(
                [stage[half, row, pl.ds(channel, BLOCK), :] for row in range(BLOCK)], axis=0
            )
            for half in halves
        ],
        axis=1,
    )


def give_chunk(ref, group, at, lanes, value):
    block = value.astype(BF16).reshape(BLOCK, BLOCK, value.shape[1])
    if len(ref.shape) == 4:
        ref[group, at : at + BLOCK, :, lanes] = block
    else:
        ref[at : at + BLOCK, :, lanes] = block


LOW, HIGH, BOTH = slice(0, LANES), slice(LANES, 2 * LANES), slice(0, 2 * LANES)
CHUNKS = range(0, GROUP, BLOCK)


def half_swap(first, second):
    low = lax.broadcasted_iota(jnp.int32, first.shape, first.ndim - 1) < LANES // 2
    axis = first.ndim - 1
    return (
        jnp.where(low, first, pltpu.roll(second, LANES // 2, axis)),
        jnp.where(low, pltpu.roll(first, LANES // 2, axis), second),
    )


def pick(flag, zero, one):
    return jnp.where(flag == 0, zero, one)


def mask_chunk(info, part, row, half):
    token = lax.broadcasted_iota(jnp.int32, (1, LANES), 1) + half * LANES
    live = (info[3] + part * BLOCK + row < info[4]).astype(F32)
    return (token < info[4]).astype(F32) * live


def each_rows(work):
    step = pl.program_id(0)

    @pl.loop(0, SOME // PAIRED)
    def _(turn):
        here = [turn * PAIRED + n for n in range(PAIRED)]
        work(here, [step * SOME + row for row in here])


def first_step(work):
    pl.when(pl.program_id(0) == 0)(work)


def last_step(work):
    pl.when(pl.program_id(0) == STEPS - 1)(work)


def places_of(here, rows):
    for n, (spot, row) in enumerate(zip(here, rows)):
        for half in range(2):
            start = (2 * n + half) * LANES
            yield spot, row, half, (LOW, HIGH)[half], slice(start, start + LANES)


def turned(ref, spot, lanes):
    return ref[spot, lanes, :].astype(F32).T


def stacked(ref, rows):
    return jnp.concatenate([ref[row] for row in rows], axis=1)


def side_by_side(chunks):
    return jnp.concatenate(chunks, axis=1)


def put_gated(info, part, mixture, here, rows, left_st, right_st, gate_out, factor_out):
    size = left_st.shape[2]
    for spot, row, half, lanes, among in places_of(here, rows):
        mask = mask_chunk(info, part, row, half)
        for block, stage in enumerate((left_st, right_st)):
            gate = opened(mixture[(2 + block) * size : (3 + block) * size, among])
            opening = gate * mask
            side = mixture[block * size : (block + 1) * size, among] * opening
            stage[half, row] = side.astype(BF16)
            factor_out[spot, block * size : (block + 1) * size, lanes] = opening.astype(BF16)
            slope = (side * (1.0 - gate)).astype(BF16)
            factor_out[spot, (2 + block) * size : (3 + block) * size, lanes] = slope
        gate_out[spot, :, lanes] = opened(mixture[4 * size :, among]).astype(BF16)


def opened(gate):
    return 0.5 * jnp.tanh(gate) + 0.5


def column(row):
    return jnp.broadcast_to(row, (LANES, row.shape[1])).T


def halved_turned(weight):
    values = 2 * weight.shape[0]
    return jnp.concatenate([weight[:, :values].T, weight[:, values:].T * 0.5], axis=0).astype(BF16)


def entry_kernel(part, info, pair, norm_row, proj_w, *rest):
    if part:
        raw, rest = rest[:6], rest[6:]
        gain1, final1, norm2, proj2, gain2, final2 = raw
        prepared, rest = rest[7:18], rest[:7] + rest[18:]
    a_same, a_other, b_same, b_other, to_core, gate_out, factor_out, *rest = rest
    left_st, right_st, norm, proj_t, perm = rest
    hidden = proj_w.shape[1] // 5

    @first_step
    def _():
        norm[...] = column(norm_row[...])
        proj_t[...] = halved_turned(proj_w[...])
        perm[...] = reorder()
        if part:
            for row, out in zip((norm_row, gain1, norm2, gain2), prepared[:4]):
                out[...] = column(row[...])
            prepared[4][...] = halved_turned(proj2[...])
            for weight, out in zip((final1, final2), prepared[5:7]):
                out[...] = weight[...].T.astype(BF16)
            for weight, out in zip((proj_w, final1, proj2, final2), prepared[7:]):
                out[...] = weight[...].astype(BF16)

    def work(here, rows):
        normed = side_by_side(
            [
                (normalise(turned(pair, spot, lanes))[0] * norm[...]).astype(BF16)
                for spot, row, half, lanes, among in places_of(here, rows)
            ]
        )
        mixture = dot_nn(proj_t[...], normed)
        put_gated(info, part, mixture, here, rows, left_st, right_st, gate_out, factor_out)

    each_rows(work)

    @last_step
    def _():
        core = info[2]
        for owner, a_out, b_out in ((core, a_same, b_same), (1 - core, a_other, b_other)):
            for group in range(2):
                for at in CHUNKS:
                    channel = owner * (2 * GROUP) + group * GROUP + at
                    left = dot_nn(perm[...], get_chunk(left_st, (0, 1), channel)).astype(BF16)
                    right = dot_nn(perm[...], get_chunk(right_st, (0, 1), channel)).astype(BF16)
                    first, second = (left, right) if group == 0 else (right, left)
                    give_chunk(a_out, group, at, BOTH, first)
                    give_chunk(b_out, group, at, BOTH, second)
                    if a_out is a_other:
                        give_chunk(to_core, group, at, BOTH, first)
                        give_chunk(to_core, 2 + group, at, BOTH, second)


def fill_split(info, perm, stage, own, near, ypart, ycpart, xpart, xcpart):
    x, y, core = info[0], info[1], info[2]
    for owner, mine, yp, xp in ((core, own, ypart, xpart), (1 - core, near, ycpart, xcpart)):
        for at in CHUNKS:
            channel = owner * (2 * GROUP) + at
            both = jnp.concatenate([chunk(mine, 0, at, LOW), chunk(yp, 0, at, LOW)], axis=1)
            both = dot_nn(perm, both)
            put_chunk(stage, y, channel, both[:, LOW])
            put_chunk(stage, 1 - y, channel, both[:, HIGH])
            both = jnp.concatenate([chunk(mine, 1, at, LOW), chunk(xp, 0, at, LOW)], axis=1)
            both = dot_nn(perm, both)
            here, there = both[:, LOW], both[:, HIGH]
            first, second = half_swap(pick(x, here, there), pick(x, there, here))
            put_chunk(stage, 0, channel + GROUP, first)
            put_chunk(stage, 1, channel + GROUP, second)


def fill_sum(perm, stage, channel, first, second):
    both = (chunk(*first).astype(F32) + chunk(*second).astype(F32)).astype(BF16)
    total = dot_nn(perm, both)
    put_chunk(stage, 0, channel, total[:, LOW])
    put_chunk(stage, 1, channel, total[:, HIGH])


def split_out(info, perm, stage, owner, at):
    x, y = info[0], info[1]
    channel = owner * (2 * GROUP) + at
    both = dot_nn(perm, get_chunk(stage, (y, 1 - y), channel))
    swapped = dot_nn(perm, get_chunk(stage, (0, 1), channel + GROUP))
    first, second = half_swap(swapped[:, LOW], swapped[:, HIGH])
    return both[:, LOW], both[:, HIGH], pick(x, first, second), pick(x, second, first)


def middle_kernel(
    part, info, pair, own, ypart, xpart, ycpart, xcpart, near,
    gate1, gain1, final1_t, norm2, proj2_t,
    middle_out, inner_out, gate_out, factor_out, normed_out, final_out, slope_out, o_own, o_near, o_y, o_yc, o_x, o_xc,
    stage, left_st, right_st, perm,
):
    @first_step
    def _():
        perm[...] = reorder()
        fill_split(info, perm[...], stage, own, near, ypart, ycpart, xpart, xcpart)

    def work(here, rows):
        finals, normeds = [], []
        for spot, row, half, lanes, among in places_of(here, rows):
            inner = stage[half, row]
            final = (normalise(inner)[0] * gain1[...]).astype(BF16)
            inner_out[spot, :, lanes] = inner.astype(BF16)
            final_out[spot, :, lanes] = final
            finals.append(final)
        product = dot_nn(final1_t[...], side_by_side(finals))
        for spot, row, half, lanes, among in places_of(here, rows):
            gate = gate1[spot, :, lanes].astype(F32)
            update = product[:, among] * gate
            slope_out[spot, :, lanes] = (update * (1.0 - gate)).astype(BF16)
            middle = (turned(pair, spot, lanes) + update).astype(BF16)
            middle_out[spot, :, lanes] = middle
            normed = (normalise(middle.astype(F32))[0] * norm2[...]).astype(BF16)
            normed_out[spot, :, lanes] = normed
            normeds.append(normed)
        mixture = dot_nn(proj2_t[...], side_by_side(normeds))
        put_gated(info, part, mixture, here, rows, left_st, right_st, gate_out, factor_out)

    each_rows(work)

    @last_step
    def _():
        core = info[2]
        beyond = slice(LANES, 3 * LANES)
        for owner, main, yo, xo in ((core, o_own, o_y, o_x), (1 - core, o_near, o_yc, o_xc)):
            for at in CHUNKS:
                kept = split_out(info, perm[...], left_st, owner, at)
                give_chunk(main, 0, at, LOW, kept[0])
                give_chunk(yo, 0, at, LOW, kept[1])
                give_chunk(main, 1, at, LOW, kept[2])
                give_chunk(xo, 0, at, LOW, kept[3])
                for group, out in ((0, yo), (1, xo)):
                    channel = owner * (2 * GROUP) + group * GROUP + at
                    right = dot_nn(perm[...], get_chunk(right_st, (0, 1), channel)).astype(BF16)
                    give_chunk(main, group, at, beyond, right)
                    give_chunk(out, 0, at, beyond, right)


def turn_kernel(
    part, info, gate2, cot, own, ypart, xpart, ycpart, xcpart, near,
    gain2, final2_t, final2_w,
    gate_out, final_out, product_out, same0, same1, other0, other1, to_core, stage, out_st, perm,
):
    core = info[2]

    @first_step
    def _():
        perm[...] = reorder()
        for owner, mine, xp, yp in ((core, own, xpart, ypart), (1 - core, near, xcpart, ycpart)):
            for at in CHUNKS:
                channel = owner * (2 * GROUP) + at
                fill_sum(perm[...], stage, channel, (mine, 0, at, BOTH), (xp, 0, at, BOTH))
                fill_sum(perm[...], stage, channel + GROUP, (mine, 1, at, BOTH), (yp, 0, at, BOTH))

    def work(here, rows):
        finals, products = [], []
        for spot, row, half, lanes, among in places_of(here, rows):
            final = (normalise(stage[half, row])[0] * gain2[...]).astype(BF16)
            final_out[spot, :, lanes] = final
            finals.append(final)
            grad_product = turned(cot, spot, lanes) * gate2[spot, :, lanes].astype(F32)
            grad_product = grad_product.astype(BF16)
            product_out[spot, :, lanes] = grad_product
            products.append(grad_product)
        product = dot_nn(final2_t[...], side_by_side(finals))
        grad_final = dot_nn(final2_w[...], side_by_side(products))
        for spot, row, half, lanes, among in places_of(here, rows):
            gate = gate2[spot, :, lanes].astype(F32)
            grad_gate = turned(cot, spot, lanes) * product[:, among] * gate * (1.0 - gate)
            gate_out[spot, :, lanes] = grad_gate.astype(BF16)
            hat, spread = normalise(stage[half, row])
            grad_inner = normalise_back(grad_final[:, among] * gain2[...], hat, spread)
            out_st[half, row] = grad_inner.astype(BF16)

    each_rows(work)

    @last_step
    def _():
        for owner, outs in ((core, (same0, same1)), (1 - core, (other0, other1))):
            for group, out in enumerate(outs):
                for at in CHUNKS:
                    channel = owner * (2 * GROUP) + group * GROUP + at
                    value = dot_nn(perm[...], get_chunk(out_st, (0, 1), channel)).astype(BF16)
                    give_chunk(out, 0, at, BOTH, value)
                    if out is other0 or out is other1:
                        give_chunk(to_core, group, at, BOTH, value)


def mixture_chunk(left_st, right_st, factors, gate_in, spot, row, half, lanes):
    size = left_st.shape[2]
    grads = (left_st[half, row], right_st[half, row])
    blocks = [
        (grads[n % 2] * factors[spot, n * size : (n + 1) * size, lanes].astype(F32)).astype(BF16)
        for n in range(4)
    ]
    return jnp.concatenate(blocks + [gate_in[spot, :, lanes]], axis=0)


def inward_kernel(
    part, info, middle, gate1, cot, inner_in, gate_in, factors, slopes, own, ypart, xpart, ycpart, xcpart, near,
    norm2, proj2_w, gain1, final1_w,
    grad_out, gate_out, mixture_out, product_out, o_own, o_near, o_y, o_yc, o_x, o_xc,
    left_st, right_st, out_st, perm,
):
    core = info[2]

    @first_step
    def _():
        perm[...] = reorder()
        fill_split(info, perm[...], left_st, own, near, ypart, ycpart, xpart, xcpart)
        beyond = slice(LANES, 3 * LANES)
        for owner, mine, yp, xp in ((core, own, ypart, xpart), (1 - core, near, ycpart, xcpart)):
            for at in CHUNKS:
                channel = owner * (2 * GROUP) + at
                fill_sum(perm[...], right_st, channel, (mine, 0, at, beyond), (yp, 0, at, beyond))
                fill_sum(
                    perm[...], right_st, channel + GROUP, (mine, 1, at, beyond), (xp, 0, at, beyond)
                )

    def work(here, rows):
        mixtures, products = [], []
        for spot, row, half, lanes, among in places_of(here, rows):
            mixture = mixture_chunk(left_st, right_st, factors, gate_in, spot, row, half, lanes)
            mixture_out[spot, :, lanes] = mixture
            mixtures.append(mixture)
        grad_normed = dot_nn(proj2_w[...], side_by_side(mixtures))
        for spot, row, half, lanes, among in places_of(here, rows):
            hat, spread = normalise(middle[spot, :, lanes].astype(F32))
            grad = normalise_back(grad_normed[:, among] * norm2[...], hat, spread)
            grad = grad + turned(cot, spot, lanes)
            grad_out[spot, :, lanes] = grad
            gate_out[spot, :, lanes] = (grad * slopes[spot, :, lanes].astype(F32)).astype(BF16)
            grad_product = (grad * gate1[spot, :, lanes].astype(F32)).astype(BF16)
            product_out[spot, :, lanes] = grad_product
            products.append(grad_product)
        grad_final = dot_nn(final1_w[...], side_by_side(products))
        for spot, row, half, lanes, among in places_of(here, rows):
            hat, spread = normalise(inner_in[spot, :, lanes].astype(F32))
            grad_inner = normalise_back(grad_final[:, among] * gain1[...], hat, spread)
            out_st[half, row] = grad_inner.astype(BF16)

    each_rows(work)

    @last_step
    def _():
        for owner, main, yo, xo in ((core, o_own, o_y, o_x), (1 - core, o_near, o_yc, o_xc)):
            for at in CHUNKS:
                kept = split_out(info, perm[...], out_st, owner, at)
                give_chunk(main, 0, at, LOW, kept[0])
                give_chunk(yo, 0, at, LOW, kept[1])
                give_chunk(main, 1, at, LOW, kept[2])
                give_chunk(xo, 0, at, LOW, kept[3])


def weight_kernel(info, *refs):
    *refs, total = refs
    (mixtures, normeds, *pairs) = paired(refs)
    width, channels = mixtures[0].shape[1], normeds[0].shape[1]

    @pl.when(pl.program_id(0) == 0)
    def _():
        total[...] = jnp.zeros_like(total)

    for part in range(PARTS):
        for first in range(0, mixtures[part].shape[0], PAIRED):
            rows = [first + n for n in range(PAIRED)]
            mixture, normed = stacked(mixtures[part], rows), stacked(normeds[part], rows)
            total[:width, :] += dot_nt(mixture, normed)
            for n, (finals, products) in enumerate((pairs[:2], pairs[2:])):
                where = slice(width + n * channels, width + (n + 1) * channels)
                final, product = stacked(finals[part], rows), stacked(products[part], rows)
                total[where, :] += dot_nt(final, product)


def exit_kernel(
    part, info, pair, grad_in, gate_in, factors, own, ypart, xpart, ycpart, xcpart, near,
    norm1, proj1_w, early, *rest,
):
    out, gproj, *rest, left_st, right_st, perm = rest
    if part:
        before, unused, out, gproj, packed = (out, gproj, *rest)
    core = info[2]

    @first_step
    def _():
        perm[...] = reorder()
        gproj[...] = before[...] if part else jnp.zeros_like(gproj)
        beyond = slice(2 * LANES, 4 * LANES)
        for owner, mine, yp, xp in ((core, own, ypart, xpart), (1 - core, near, ycpart, xcpart)):
            for group, lefts, rights in ((0, yp, xp), (1, xp, yp)):
                for at in CHUNKS:
                    channel = owner * (2 * GROUP) + group * GROUP + at
                    fill_sum(
                        perm[...], left_st, channel, (mine, group, at, BOTH), (lefts, group, at, BOTH)
                    )
                    fill_sum(
                        perm[...],
                        right_st,
                        channel,
                        (mine, group, at, beyond),
                        (rights, group, at, BOTH),
                    )

    def work(here, rows):
        mixtures, normeds = [], []
        for spot, row, half, lanes, among in places_of(here, rows):
            normeds.append(
                (normalise(turned(pair, spot, lanes))[0] * norm1[...]).astype(BF16)
            )
            mixtures.append(
                mixture_chunk(left_st, right_st, factors, gate_in, spot, row, half, lanes)
            )
        mixture = side_by_side(mixtures)
        gproj[...] += dot_nt(mixture, side_by_side(normeds))
        grad_normed = dot_nn(proj1_w[...], mixture)
        for spot, row, half, lanes, among in places_of(here, rows):
            hat, spread = normalise(turned(pair, spot, lanes))
            grad = normalise_back(grad_normed[:, among] * norm1[...], hat, spread)
            out[spot, lanes, :] = (grad_in[spot, :, lanes] + grad).T

    each_rows(work)

    if part:

        @last_step
        def _():
            size = gproj.shape[0]
            packed[:size, :] = gproj[...].astype(BF16)
            packed[size:, :] = early[...].astype(BF16)


CHANNELS = 8
PARTS = 2


def paired(refs):
    return [refs[n : n + PARTS] for n in range(0, len(refs), PARTS)]


def place(one, two, part):
    return pl.multiple_of((one * 2 + two) * (PARTS * BLOCK) + part * BLOCK, BLOCK)


def places(info, group):
    at, core = info[group], info[2]
    return [
        place(at if n < 2 else 1 - at, core if n % 2 == 0 else 1 - core, part)
        for n in range(4)
        for part in range(PARTS)
    ]


def take(ref, group, h):
    return ref[group, h] if len(ref.shape) == 4 else ref[h]


def joined(quads, group, h):
    return jnp.concatenate([take(ref, group, h) for refs in quads for ref in refs], axis=0)


def gather(stage, slot, wheres, quads, group, h):
    for where, ref in zip(wheres, [ref for refs in quads for ref in refs]):
        stage[slot, pl.ds(where, BLOCK), :] = take(ref, group, h)
    return stage[slot]


def give(refs, group, h, lanes, value):
    if len(refs.shape) == 4:
        refs[group, h, :, lanes] = value
    else:
        refs[h, :, lanes] = value


def scatter(quads, group, h, lanes, value):
    for n, ref in enumerate([ref for refs in quads for ref in refs]):
        give(ref, group, h, lanes, value[n * BLOCK : (n + 1) * BLOCK])


def scatter_from(stage, slot, wheres, quads, group, h, lanes):
    for where, ref in zip(wheres, [ref for refs in quads for ref in refs]):
        give(ref, group, h, lanes, stage[slot, pl.ds(where, BLOCK), :])


def outgoing_kernel(info, *refs):
    *refs, stage = refs
    *refs, o_own, o_near, o_y, o_yc, o_x, o_xc = refs
    a_own, b_own, a_y, b_x, a_yc, b_xc, near = paired(refs)
    a_near, b_near = [ref.at[:2] for ref in near], [ref.at[2:] for ref in near]
    along_a, along_b = (a_own, a_near, a_y, a_yc), (b_own, b_near, b_x, b_xc)
    for h in range(CHANNELS):
        for group in range(2):
            lefts, rights = (along_a, along_b) if group == 0 else (along_b, along_a)
            far = (o_y, o_yc) if group == 0 else (o_x, o_xc)
            right = gather(stage, 2 * h + group, places(info, group), rights, group, h)
            inner = dot_nt(joined(lefts, group, h), right).astype(BF16)
            for n, out in enumerate((o_own, o_near) + far):
                rows = PARTS * BLOCK
                give(out, group, h, slice(0, LANES), inner[n * rows : (n + 1) * rows])


def halves(quads, group, h):
    both = joined(quads, group, h)
    return both[:, :LANES], both[:, LANES:]


def incoming_kernel(info, *refs):
    *refs, stage = refs
    own, ypart, xpart, ycpart, xcpart, near, o_own, o_near, o_x, o_xc, o_y, o_yc = paired(refs)
    for h in range(CHANNELS):
        for group in range(2):
            far = (ypart, ycpart) if group == 0 else (xpart, xcpart)
            outs = (o_own, o_near) + ((o_x, o_xc) if group == 0 else (o_y, o_yc))
            slot = 2 * h + group
            left, right = halves((own, near) + far, group, h)
            stage[slot] = dot_tn(left, right).astype(BF16)
            scatter_from(stage, slot, places(info, group), outs, group, h, slice(0, 2 * LANES))


def incoming_back_kernel(info, *refs):
    *refs, stage = refs
    own, ypart, xpart, ycpart, xcpart, near, *more = paired(refs)
    same0, same1, g_y, g_x, g_yc, g_xc, g_near, *more = more
    o_own, o_near, o_y, o_yc, o_x, o_xc = more
    for h in range(CHANNELS):
        for group in range(2):
            far = (ypart, ycpart) if group == 0 else (xpart, xcpart)
            grads = (same0, g_near, g_x, g_xc) if group == 0 else (same1, g_near, g_y, g_yc)
            outs = (o_own, o_near) + ((o_y, o_yc) if group == 0 else (o_x, o_xc))
            grad = gather(stage, 2 * h + group, places(info, group), grads, group, h)
            left, right = halves((own, near) + far, group, h)
            scatter(outs, group, h, slice(0, LANES), dot_nt(right, grad).astype(BF16))
            scatter(outs, group, h, slice(LANES, 3 * LANES), dot_nn(left, grad).astype(BF16))


def outgoing_back_kernel(info, *refs):
    *refs, stage, back = refs
    a_own, b_own, a_y, b_x, a_yc, b_xc, near, *more = paired(refs)
    a_near, b_near = [ref.at[:2] for ref in near], [ref.at[2:] for ref in near]
    g_own, g_y, g_x, g_yc, g_xc, g_near, o_own, o_near, o_y, o_yc, o_x, o_xc = more
    along_a, along_b = (a_own, a_near, a_y, a_yc), (b_own, b_near, b_x, b_xc)
    first, second = slice(0, 2 * LANES), slice(2 * LANES, 4 * LANES)
    for h in range(CHANNELS):
        for group in range(2):
            lefts, rights = (along_a, along_b) if group == 0 else (along_b, along_a)
            far = (g_y, g_yc) if group == 0 else (g_x, g_xc)
            left_far, right_far = ((o_y, o_yc), (o_x, o_xc)) if group == 0 else ((o_x, o_xc), (o_y, o_yc))
            slot = 2 * h + group
            wheres = places(info, group)
            right = gather(stage, slot, wheres, rights, group, h)
            grad = joined((g_own, g_near) + far, group, h)
            grad_left = dot_nn(grad, right).astype(BF16)
            back[slot] = dot_tn(grad, joined(lefts, group, h)).astype(BF16)
            core_rows = 2 * PARTS * BLOCK
            scatter((o_own, o_near), group, h, first, grad_left[:core_rows])
            scatter(left_far, group, h, first, grad_left[core_rows:])
            scatter_from(back, slot, wheres[: 2 * PARTS], (o_own, o_near), group, h, second)
            scatter_from(back, slot, wheres[2 * PARTS :], right_far, group, h, first)


def whole(shape):
    return pl.BlockSpec(shape, lambda step, info: (0,) * len(shape))


def rows_of(part, some=SOME):
    def make(shape):
        first = part * (BLOCK // some)
        return pl.BlockSpec(
            (some,) + shape[1:], lambda step, info: (first + step,) + (0,) * (len(shape) - 1)
        )

    make.kept = True
    return make


def rows_block(part):
    def make(shape):
        return pl.BlockSpec(
            shape[:-2] + (BLOCK, shape[-1]),
            lambda step, info: (0,) * (len(shape) - 2) + (part, 0),
        )

    return make


def anywhere(shape):
    return pl.BlockSpec(memory_space=pl.ANY)


def channel_rows(shape):
    if len(shape) == 4:
        return pl.BlockSpec((shape[0], CHANNELS) + shape[2:], lambda step, info: (0, step, 0, 0))
    return pl.BlockSpec((CHANNELS,) + shape[1:], lambda step, info: (step, 0, 0))


def call(kernel, info, steps, ins, outs, scratch, aliases={}, vmem=CELL_VMEM):
    return pl.pallas_call(
        kernel,
        grid_spec=pltpu.PrefetchScalarGridSpec(
            num_scalar_prefetch=1,
            grid=(steps,),
            in_specs=[make(array.shape) for array, make in ins],
            out_specs=[make(shape) for shape, unused, make in outs],
            scratch_shapes=scratch,
        ),
        out_shape=[
            (pltpu.HBM if getattr(make, "kept", False) else jax.ShapeDtypeStruct)(shape, dtype)
            for shape, dtype, make in outs
        ],
        compiler_params=pltpu.CompilerParams(vmem_limit_bytes=vmem),
        input_output_aliases=aliases,
    )(info, *[array for array, unused in ins])


class Links:
    def __init__(self):
        self.last = {}

    def send(self, array, offset, first=None):
        count = lax.axis_size("axial")
        if first is not None:
            array, unused = lax.optimization_barrier((array, first))
        if offset in self.last and offset in (X, Y):
            array, unused = lax.optimization_barrier((array, self.last[offset]))
        self.last[offset] = lax.ppermute(
            array, "axial", [(n, n ^ offset) for n in range(count)]
        )
        return self.last[offset]

    def __call__(self, *sends, between=None):
        results = [[] for unused in sends]
        for part in range(len(sends[0][0])):
            for result, (arrays, offset) in zip(results, sends):
                result.append(self.send(arrays[part], offset, between if part else None))
        return results


CORE, X, Y = 1, 2, 4


def add_up(share):
    count = lax.axis_size("axial")
    rows, width = share.shape
    shares = share.reshape(count, rows // count, width)
    parts = lax.all_to_all(shares, "axial", split_axis=0, concat_axis=0, tiled=True)
    mine = parts.astype(F32).sum(axis=0).astype(BF16)
    depth = lax.axis_size("dp")
    terms = [mine] + [
        lax.ppermute(mine, "dp", [(n, n ^ offset) for n in range(depth)])
        for offset in range(1, depth)
    ]
    terms = [term.astype(F32) for term in terms]
    while len(terms) > 1:
        terms = [terms[n] + terms[n + 1] for n in range(0, len(terms), 2)]
    copies = jnp.broadcast_to(terms[0].astype(BF16)[None], shares.shape)
    return lax.all_to_all(copies, "axial", split_axis=0, concat_axis=0, tiled=True).reshape(
        rows, width
    )


def gain_grad(weight_grad, weight, gain_row):
    return jnp.sum((weight.astype(F32) * weight_grad).T, axis=0, keepdims=True) / gain_row


def finish_kernel(
    scale, info, sums, proj1, final1, proj2, final2, norm1, gain1, norm2, gain2,
    o_norm1, o_proj1, o_gain1, o_final1, o_norm2, o_proj2, o_gain2, o_final2,
):
    width, channels = proj1.shape[1], final1.shape[1]
    takes = (
        (0, True, proj1, norm1, o_proj1, o_norm1),
        (width, True, proj2, norm2, o_proj2, o_norm2),
        (2 * width, False, final2, gain2, o_final2, o_gain2),
        (2 * width + channels, False, final1, gain1, o_final1, o_gain1),
    )
    for start, flipped, weight, gain, out, gain_out in takes:
        total = sums[start : start + weight.shape[1], :].astype(F32) * scale
        total = total.T if flipped else total
        out[...] = total
        gain_out[...] = gain_grad(total, weight[...].astype(BF16), gain[...])


def fast_body(
    pair,
    cotangent,
    lengths,
    outgo_norm,
    outgo_proj,
    outgo_gain,
    outgo_final,
    incom_norm,
    incom_proj,
    incom_gain,
    incom_final,
):
    rows, tokens, channels = pair.shape[1:]
    hidden = outgo_gain.shape[0]
    index = lax.axis_index("axial")
    info = jnp.stack(
        [(index // 2) % 2, index // 4, index % 2, index * rows, lengths[0]]
    ).astype(jnp.int32)
    hop = Links()
    pair = pair[0]
    cot = cotangent[0]
    parts = range(PARTS)
    turns = GROUP // CHANNELS
    stage = pltpu.VMEM((2, BLOCK, hidden, LANES), F32)
    out_stage = pltpu.VMEM((2, BLOCK, hidden, LANES), BF16)
    perm = pltpu.VMEM((BLOCK * BLOCK, BLOCK * BLOCK), BF16)
    streamed = rows_of(0)
    square = pltpu.VMEM((2 * CHANNELS, 4 * rows, tokens), BF16)

    def two(width, height=BLOCK, make=whole, groups=2):
        return ((groups, GROUP, height, width), BF16, make)

    def one(width, height=BLOCK, make=whole):
        return ((GROUP, height, width), BF16, make)

    turned_block = ((BLOCK, channels, tokens), BF16, streamed)
    factor_block = ((BLOCK, 4 * hidden, tokens), BF16, streamed)
    mixture_block = ((BLOCK, 5 * hidden, tokens), BF16, streamed)

    def cells(kernel, ins, outs, scratch, more=lambda part: []):
        results = []
        for part in parts:
            carried = ins(part, results)
            results.append(
                call(functools.partial(kernel, part), info, STEPS, carried, outs + more(part), scratch)
            )
        shared = results[-1][len(outs) :]
        return [list(each) for each in zip(*results)] + list(shared)

    def wholes(arrays):
        return [(array, whole) for array in arrays]

    def triangle(kernel, operands, outs, scratch, split=PARTS):
        ins = [(array, channel_rows) for arrays in operands for array in arrays]
        each = [out for out in outs for unused in range(split)]
        results = call(kernel, info, turns, ins, each, scratch, vmem=TRIANGLE_VMEM)
        return [list(results[n : n + split]) for n in range(0, len(results), split)]

    raw = (outgo_gain[None], outgo_final, incom_norm[None], incom_proj, incom_gain[None], incom_final)
    gain_wide = ((channels, LANES), F32, whole)
    proj_turned = ((5 * hidden, channels), BF16, whole)
    proj_plain = ((channels, 5 * hidden), BF16, whole)
    final_plain = ((hidden, channels), BF16, whole)
    (
        a_same, a_other, b_same, b_other, to_core, gate_one, factors_one,
        norm1, gain1, norm2, gain2, proj2_t, final1_t, final2_t,
        proj1, final1, proj2, final2,
    ) = cells(
        entry_kernel,
        lambda part, unused: [(pair, rows_of(part)), (outgo_norm[None], whole), (outgo_proj, whole)]
        + (wholes(raw) if part else []),
        [two(tokens)] * 4 + [two(tokens, groups=4), turned_block, factor_block],
        [
            out_stage,
            out_stage,
            pltpu.VMEM((channels, LANES), F32),
            pltpu.VMEM((5 * hidden, channels), BF16),
            perm,
        ],
        lambda part: (
            [gain_wide] * 4
            + [proj_turned]
            + [final_plain] * 2
            + [proj_plain, final_plain] * 2
            if part
            else []
        ),
    )
    held_one = [a_same, b_same] + hop(
        (a_same, Y), (b_same, X), (a_other, Y | CORE), (b_other, X | CORE), (to_core, CORE)
    )
    own, near, to_y, to_yc, to_x, to_xc = triangle(
        outgoing_kernel,
        held_one,
        [two(LANES, rows, channel_rows)] * 2 + [one(LANES, rows, channel_rows)] * 4,
        [square],
        split=1,
    )
    back_one = [
        own,
        *hop(
            (to_y, Y), (to_x, X), (to_yc, Y | CORE), (to_xc, X | CORE), (near, CORE)
        ),
    ]

    (
        middle, inner_one, gate_two, factors_two, normed_two, finals_one, slopes_one,
        own, near, to_y, to_yc, to_x, to_xc,
    ) = cells(
        middle_kernel,
        lambda part, unused: [(pair, rows_of(part))]
        + [(array, rows_block(part)) for array, in back_one]
        + [(gate_one[part], streamed)]
        + wholes((gain1, final1_t, norm2, proj2_t)),
        [turned_block] * 3
        + [factor_block]
        + [turned_block] * 3
        + [two(3 * LANES)] * 2 + [one(3 * LANES)] * 4,
        [stage, out_stage, out_stage, perm],
    )
    held_two = [
        own,
        *hop(
            (to_y, Y), (to_x, X), (to_yc, Y | CORE), (to_xc, X | CORE), (near, CORE)
        ),
    ]
    own, near, to_x, to_xc, to_y, to_yc = triangle(
        incoming_kernel,
        held_two,
        [two(tokens, make=channel_rows)] * 2 + [one(tokens, make=channel_rows)] * 4,
        [square],
    )
    back_two = [
        own,
        *hop(
            (to_y, Y), (to_x, X), (to_yc, Y | CORE), (to_xc, X | CORE), (near, CORE)
        ),
    ]

    gate_grad_two, finals_two, products_two, same0, same1, other0, other1, to_core = cells(
        turn_kernel,
        lambda part, done: [(gate_two[part], streamed), (cot, rows_of(part))]
        + wholes(arrays[part] for arrays in back_two)
        + wholes((gain2, final2_t, final2)),
        [turned_block] * 3 + [one(tokens)] * 4 + [two(tokens)],
        [stage, out_stage, perm],
    )
    grads_two = [
        same0,
        same1,
        *hop(
            (same1, Y), (same0, X), (other1, Y | CORE), (other0, X | CORE), (to_core, CORE)
        ),
    ]
    own, near, to_y, to_yc, to_x, to_xc = triangle(
        incoming_back_kernel,
        held_two + grads_two,
        [two(3 * LANES, make=channel_rows)] * 2 + [one(3 * LANES, make=channel_rows)] * 4,
        [square],
    )
    rows_two = [
        own,
        *hop(
            (to_y, Y), (to_x, X), (to_yc, Y | CORE), (to_xc, X | CORE), (near, CORE)
        ),
    ]

    (
        grad_middle, gate_grad_one, mixtures_two, products_one,
        own, near, to_y, to_yc, to_x, to_xc,
    ) = cells(
        inward_kernel,
        lambda part, done: [
            (middle[part], streamed),
            (gate_one[part], streamed),
            (cot, rows_of(part)),
            (inner_one[part], streamed),
            (gate_grad_two[part], streamed),
            (factors_two[part], streamed),
            (slopes_one[part], streamed),
        ]
        + wholes(arrays[part] for arrays in rows_two)
        + wholes((norm2, proj2, gain1, final1)),
        [((BLOCK, channels, tokens), F32, streamed), turned_block, mixture_block, turned_block]
        + [two(LANES)] * 2
        + [one(LANES)] * 4,
        [stage, stage, out_stage, perm],
    )
    grads_one = [
        own,
        *hop(
            (to_y, Y), (to_x, X), (to_yc, Y | CORE), (to_xc, X | CORE), (near, CORE)
        ),
    ]
    own, near, to_y, to_yc, to_x, to_xc = triangle(
        outgoing_back_kernel,
        held_one + grads_one,
        [two(2 * tokens, make=channel_rows)] * 2 + [two(tokens, make=channel_rows)] * 4,
        [square, square],
    )
    kept = (mixtures_two, normed_two, finals_two, products_two, finals_one, products_one)
    (early,) = call(
        weight_kernel,
        info,
        4,
        [
            (array, rows_of(0, BLOCK // 4))
            for arrays in kept
            for array in arrays
        ],
        [((5 * hidden + 2 * channels, channels), F32, whole)],
        [],
    )
    rows_one = [own] + hop(
        (to_y, Y), (to_x, X), (to_yc, Y | CORE), (to_xc, X | CORE), (near, CORE), between=early
    )
    exit_ins = 10 + 3 + 1 + 1
    result = None
    for part in parts:
        result = call(
            functools.partial(exit_kernel, part),
            info,
            STEPS,
            [
                (pair, rows_of(part)),
                (grad_middle[part], streamed),
                (gate_grad_one[part], streamed),
                (factors_one[part], streamed),
            ]
            + wholes(arrays[part] for arrays in rows_one)
            + wholes((norm1, proj1, early))
            + ([(result[1], whole), (result[0], anywhere)] if part else []),
            [
                ((rows, tokens, channels), F32, rows_of(part)),
                ((5 * hidden, channels), F32, whole),
            ]
            + ([((10 * hidden + 2 * channels, channels), BF16, whole)] if part else []),
            [stage, stage, perm],
            {exit_ins: 0} if part else {},
        )
    grad_begin, unused, packed = result
    sums = add_up(packed)
    scale = 1.0 / math.sqrt(lax.axis_size("dp") * tokens * tokens)
    weights = (outgo_proj, outgo_final, incom_proj, incom_final)
    gains = (outgo_norm, outgo_gain, incom_norm, incom_gain)
    order = (outgo_norm[None], outgo_proj, outgo_gain[None], outgo_final)
    order += (incom_norm[None], incom_proj, incom_gain[None], incom_final)
    totals = call(
        functools.partial(finish_kernel, scale),
        info,
        1,
        wholes((sums,) + weights + tuple(gain[None] for gain in gains)),
        [(array.shape, F32, whole) for array in order],
        [],
    )
    return (grad_begin[None],) + tuple(
        total.reshape(-1) if total.shape[0] == 1 else total for total in totals
    )


def solution(mesh):
    def body(pair, *rest):
        rows, tokens, channels = pair.shape[1:]
        hidden = rest[3].shape[0]
        plane = mesh.shape["axial"] == 8 and rows == 32 and tokens == 2 * LANES
        if plane and channels == LANES and hidden == 4 * GROUP:
            return fast_body(pair, *rest)
        return plain_body(pair, *rest)

    return jax.shard_map(
        body,
        mesh=mesh,
        in_specs=(P("dp", "axial", None, None), P("dp", "axial", None, None), P("dp")) + (P(),) * 8,
        out_specs=(P("dp", "axial", None, None),) + (P(),) * 8,
        check_vma=False,
    )
```

```python
import functools
import math

import jax
import jax.numpy as jnp
from jax import lax
from jax.experimental import pallas as pl
from jax.experimental.pallas import tpu as pltpu
from jax.sharding import PartitionSpec as P

EPSILON = 1e-05


def rounded(inputs):
    return lax.optimization_barrier(inputs.astype(jnp.bfloat16)).astype(jnp.float32)


def layer_norm(inputs, factor):
    average = jnp.mean(inputs, axis=-1, keepdims=True)
    centered = inputs - average
    spread = jnp.mean(centered * centered, axis=-1, keepdims=True)
    return centered * lax.rsqrt(spread + EPSILON) * factor


def gating(mixture, pair_mask, hidden):
    left_part = (
        mixture[:, :hidden] * jax.nn.sigmoid(mixture[:, 2 * hidden : 3 * hidden]) * pair_mask
    )
    right_part = (
        mixture[:, hidden : 2 * hidden]
        * jax.nn.sigmoid(mixture[:, 3 * hidden : 4 * hidden])
        * pair_mask
    )
    gate_part = jax.nn.sigmoid(mixture[:, 4 * hidden :])
    return (left_part, right_part, gate_part)


def entry(flat_pair, norm_gain, projection, pair_mask, hidden):
    normed = layer_norm(flat_pair, norm_gain).astype(jnp.bfloat16)
    mixture = jnp.dot(normed, projection.astype(jnp.bfloat16), preferred_element_type=jnp.float32)
    left_part, right_part, gate_part = gating(mixture, pair_mask, hidden)
    return (normed, mixture, left_part, right_part, gate_part)


def entry_back(
    flat_pair,
    norm_gain,
    projection,
    pair_mask,
    hidden,
    normed,
    mixture,
    grad_left,
    grad_right,
    grad_gate,
):
    unused, pull_gate = jax.vjp(lambda inner_mix: gating(inner_mix, pair_mask, hidden), mixture)
    grad_mixture = pull_gate((grad_left, grad_right, grad_gate))[0].astype(jnp.bfloat16)
    grad_projection = jnp.dot(normed.T, grad_mixture, preferred_element_type=jnp.float32)
    grad_normed = jnp.dot(
        grad_mixture, projection.astype(jnp.bfloat16).T, preferred_element_type=jnp.float32
    )
    unused, pull_norm = jax.vjp(layer_norm, flat_pair, norm_gain)
    grad_flat, grad_gain = pull_norm(grad_normed)
    return (grad_flat, grad_gain, grad_projection)


def leave(inner_sum, gate_part, out_gain, final_weight):
    final_normed = layer_norm(inner_sum, out_gain).astype(jnp.bfloat16)
    product = jnp.dot(
        final_normed, final_weight.astype(jnp.bfloat16), preferred_element_type=jnp.float32
    )
    return (final_normed, product, product * gate_part)


def leave_back(inner_sum, gate_part, out_gain, final_weight, final_normed, product, grad_update):
    grad_product = (grad_update * gate_part).astype(jnp.bfloat16)
    grad_gate = grad_update * product
    grad_final = jnp.dot(final_normed.T, grad_product, preferred_element_type=jnp.float32)
    grad_normed = jnp.dot(
        grad_product, final_weight.astype(jnp.bfloat16).T, preferred_element_type=jnp.float32
    )
    unused, pull_norm = jax.vjp(layer_norm, inner_sum, out_gain)
    grad_inner, grad_gain = pull_norm(grad_normed)
    return (grad_inner, grad_gate, grad_gain, grad_final)


def channel_major(field, row_count, tokens):
    hidden = field.shape[1]
    return jnp.transpose(field.reshape(row_count, tokens, hidden), (2, 0, 1))


def row_major(field):
    hidden = field.shape[0]
    return jnp.transpose(field, (1, 2, 0)).reshape(-1, hidden)


def plain_body(
    pair,
    cotangent,
    lengths,
    outgo_norm,
    outgo_proj,
    outgo_gain,
    outgo_final,
    incom_norm,
    incom_proj,
    incom_gain,
    incom_final,
):
    row_count = pair.shape[1]
    tokens = pair.shape[2]
    channels = pair.shape[3]
    hidden = outgo_gain.shape[0]
    length = lengths[0]
    first_row = lax.axis_index("axial") * row_count
    row_alive = (first_row + jnp.arange(row_count, dtype=jnp.int32) < length).astype(jnp.float32)
    column_alive = (jnp.arange(tokens, dtype=jnp.int32) < length).astype(jnp.float32)
    pair_mask = (row_alive[:, None] * column_alive[None, :]).reshape(-1, 1)
    flat_start = pair[0].reshape(-1, channels).astype(jnp.float32)
    normed_one, mixture_one, left_one, right_one, gate_one = entry(
        flat_start, outgo_norm, outgo_proj, pair_mask, hidden
    )
    left_first = channel_major(left_one.astype(jnp.bfloat16), row_count, tokens)
    right_first = channel_major(right_one.astype(jnp.bfloat16), row_count, tokens)
    left_owned, right_owned = (
        lax.all_to_all(left_first, "axial", split_axis=0, concat_axis=1, tiled=True),
        lax.all_to_all(right_first, "axial", split_axis=0, concat_axis=1, tiled=True),
    )
    inner_cols = jnp.einsum(
        "hik,hjk->hij", left_owned, right_owned, preferred_element_type=jnp.float32
    )
    inner_one = row_major(
        lax.all_to_all(
            inner_cols.astype(jnp.bfloat16), "axial", split_axis=1, concat_axis=0, tiled=True
        ).astype(inner_cols.dtype)
    )
    final_one, product_one, update_one = leave(inner_one, gate_one, outgo_gain, outgo_final)
    flat_middle = rounded(flat_start + update_one)
    normed_two, mixture_two, left_two, right_two, gate_two = entry(
        flat_middle, incom_norm, incom_proj, pair_mask, hidden
    )
    left_second = channel_major(left_two.astype(jnp.bfloat16), row_count, tokens)
    right_second = channel_major(right_two.astype(jnp.bfloat16), row_count, tokens)
    left_held, right_held = (
        lax.all_to_all(left_second, "axial", split_axis=0, concat_axis=1, tiled=True),
        lax.all_to_all(right_second, "axial", split_axis=0, concat_axis=1, tiled=True),
    )
    inner_held = jnp.einsum(
        "hki,hkj->hij", left_held, right_held, preferred_element_type=jnp.float32
    )
    inner_two = row_major(
        lax.all_to_all(
            inner_held.astype(jnp.bfloat16), "axial", split_axis=1, concat_axis=0, tiled=True
        ).astype(inner_held.dtype)
    )
    final_two, product_two, update_two = leave(inner_two, gate_two, incom_gain, incom_final)
    grad_end = cotangent[0].reshape(-1, channels).astype(jnp.float32)
    grad_inner_two, grad_gate_two, grad_gain_two, grad_final_two = leave_back(
        inner_two, gate_two, incom_gain, incom_final, final_two, product_two, grad_end
    )
    grad_cells_two = channel_major(grad_inner_two.astype(jnp.bfloat16), row_count, tokens)
    grad_held_two = lax.all_to_all(grad_cells_two, "axial", split_axis=0, concat_axis=1, tiled=True)
    left_back, right_back = (
        lax.all_to_all(left_second, "axial", split_axis=0, concat_axis=1, tiled=True),
        lax.all_to_all(right_second, "axial", split_axis=0, concat_axis=1, tiled=True),
    )
    grad_left_held = jnp.einsum(
        "hij,hkj->hki", grad_held_two, right_back, preferred_element_type=jnp.float32
    )
    grad_right_held = jnp.einsum(
        "hki,hij->hkj", left_back, grad_held_two, preferred_element_type=jnp.float32
    )
    grad_left_rows, grad_right_rows = (
        lax.all_to_all(
            grad_left_held.astype(jnp.bfloat16), "axial", split_axis=1, concat_axis=0, tiled=True
        ).astype(grad_left_held.dtype),
        lax.all_to_all(
            grad_right_held.astype(jnp.bfloat16), "axial", split_axis=1, concat_axis=0, tiled=True
        ).astype(grad_right_held.dtype),
    )
    grad_left_two = row_major(grad_left_rows)
    grad_right_two = row_major(grad_right_rows)
    grad_flat_two, grad_norm_two, grad_proj_two = entry_back(
        flat_middle,
        incom_norm,
        incom_proj,
        pair_mask,
        hidden,
        normed_two,
        mixture_two,
        grad_left_two,
        grad_right_two,
        grad_gate_two,
    )
    second_sums = lax.psum(
        (grad_norm_two, grad_proj_two, grad_gain_two, grad_final_two), ("dp", "axial")
    )
    grad_middle = grad_end + grad_flat_two
    grad_inner_one, grad_gate_one, grad_gain_one, grad_final_one = leave_back(
        inner_one, gate_one, outgo_gain, outgo_final, final_one, product_one, grad_middle
    )
    grad_cells_one = channel_major(grad_inner_one.astype(jnp.bfloat16), row_count, tokens)
    grad_owned_one = lax.all_to_all(
        grad_cells_one, "axial", split_axis=0, concat_axis=1, tiled=True
    )
    left_again, right_again = (
        lax.all_to_all(left_first, "axial", split_axis=0, concat_axis=1, tiled=True),
        lax.all_to_all(right_first, "axial", split_axis=0, concat_axis=1, tiled=True),
    )
    grad_left_owned = jnp.einsum(
        "hij,hjk->hik", grad_owned_one, right_again, preferred_element_type=jnp.float32
    )
    grad_right_owned = jnp.einsum(
        "hij,hik->hjk", grad_owned_one, left_again, preferred_element_type=jnp.float32
    )
    grad_left_back, grad_right_back = (
        lax.all_to_all(
            grad_left_owned.astype(jnp.bfloat16), "axial", split_axis=1, concat_axis=0, tiled=True
        ).astype(grad_left_owned.dtype),
        lax.all_to_all(
            grad_right_owned.astype(jnp.bfloat16), "axial", split_axis=1, concat_axis=0, tiled=True
        ).astype(grad_right_owned.dtype),
    )
    grad_left_one = row_major(grad_left_back)
    grad_right_one = row_major(grad_right_back)
    grad_flat_one, grad_norm_one, grad_proj_one = entry_back(
        flat_start,
        outgo_norm,
        outgo_proj,
        pair_mask,
        hidden,
        normed_one,
        mixture_one,
        grad_left_one,
        grad_right_one,
        grad_gate_one,
    )
    grad_begin = grad_middle + grad_flat_one
    first_sums = lax.psum(
        (grad_norm_one, grad_proj_one, grad_gain_one, grad_final_one), ("dp", "axial")
    )
    totals = tuple(first_sums) + tuple(second_sums)
    scale = 1.0 / math.sqrt(lax.axis_size("dp") * tokens * tokens)
    return (
        grad_begin.reshape(1, row_count, tokens, channels),
        totals[0] * scale,
        totals[1] * scale,
        totals[2] * scale,
        totals[3] * scale,
        totals[4] * scale,
        totals[5] * scale,
        totals[6] * scale,
        totals[7] * scale,
    )


BF16 = jnp.bfloat16
F32 = jnp.float32
BLOCK = 16
PAIRED = 2
STEPS = 4
SOME = BLOCK // STEPS
LANES = 128
GROUP = 32
MIB = 1024 * 1024
CELL_VMEM = 30 * MIB
TRIANGLE_VMEM = 14 * MIB


def dot_nn(a, b):
    return lax.dot_general(a, b, (((1,), (0,)), ((), ())), preferred_element_type=F32)


def dot_nt(a, b):
    return lax.dot_general(a, b, (((1,), (1,)), ((), ())), preferred_element_type=F32)


def dot_tn(a, b):
    return lax.dot_general(a, b, (((0,), (0,)), ((), ())), preferred_element_type=F32)


def normalise(v):
    centered = v - jnp.mean(v, axis=0, keepdims=True)
    spread = lax.rsqrt(jnp.mean(centered * centered, axis=0, keepdims=True) + EPSILON)
    return centered * spread, spread


def normalise_back(grad, hat, spread):
    first = jnp.mean(grad, axis=0, keepdims=True)
    second = jnp.mean(grad * hat, axis=0, keepdims=True)
    return spread * (grad - first - hat * second)


def reorder():
    size = BLOCK * BLOCK
    one = lax.broadcasted_iota(jnp.int32, (size, size), 0)
    two = lax.broadcasted_iota(jnp.int32, (size, size), 1)
    return jnp.where((one % BLOCK) * BLOCK + one // BLOCK == two, 1.0, 0.0).astype(BF16)


def chunk(ref, group, at, lanes):
    if len(ref.shape) == 4:
        block = ref[group, at : at + BLOCK, :, lanes]
    else:
        block = ref[at : at + BLOCK, :, lanes]
    return block.reshape(BLOCK * BLOCK, block.shape[2])


def put_chunk(stage, half, channel, value):
    channel = pl.multiple_of(channel, BLOCK)
    for row in range(BLOCK):
        stage[half, row, pl.ds(channel, BLOCK), :] = value[row * BLOCK : (row + 1) * BLOCK]


def get_chunk(stage, halves, channel):
    channel = pl.multiple_of(channel, BLOCK)
    return jnp.concatenate(
        [
            jnp.concatenate(
                [stage[half, row, pl.ds(channel, BLOCK), :] for row in range(BLOCK)], axis=0
            )
            for half in halves
        ],
        axis=1,
    )


def give_chunk(ref, group, at, lanes, value):
    block = value.astype(BF16).reshape(BLOCK, BLOCK, value.shape[1])
    if len(ref.shape) == 4:
        ref[group, at : at + BLOCK, :, lanes] = block
    else:
        ref[at : at + BLOCK, :, lanes] = block


LOW, HIGH, BOTH = slice(0, LANES), slice(LANES, 2 * LANES), slice(0, 2 * LANES)
CHUNKS = range(0, GROUP, BLOCK)


def half_swap(first, second):
    low = lax.broadcasted_iota(jnp.int32, first.shape, first.ndim - 1) < LANES // 2
    axis = first.ndim - 1
    return (
        jnp.where(low, first, pltpu.roll(second, LANES // 2, axis)),
        jnp.where(low, pltpu.roll(first, LANES // 2, axis), second),
    )


def pick(flag, zero, one):
    return jnp.where(flag == 0, zero, one)


def mask_chunk(info, part, row, half):
    token = lax.broadcasted_iota(jnp.int32, (1, LANES), 1) + half * LANES
    live = (info[3] + part * BLOCK + row < info[4]).astype(F32)
    return (token < info[4]).astype(F32) * live


def each_rows(work):
    step = pl.program_id(0)

    @pl.loop(0, SOME // PAIRED)
    def _(turn):
        here = [turn * PAIRED + n for n in range(PAIRED)]
        work(here, [step * SOME + row for row in here])


def first_step(work):
    pl.when(pl.program_id(0) == 0)(work)


def last_step(work):
    pl.when(pl.program_id(0) == STEPS - 1)(work)


def places_of(here, rows):
    for n, (spot, row) in enumerate(zip(here, rows)):
        for half in range(2):
            start = (2 * n + half) * LANES
            yield spot, row, half, (LOW, HIGH)[half], slice(start, start + LANES)


def turned(ref, spot, lanes):
    return ref[spot, lanes, :].astype(F32).T


def stacked(ref, rows):
    return jnp.concatenate([ref[row] for row in rows], axis=1)


def side_by_side(chunks):
    return jnp.concatenate(chunks, axis=1)


def put_gated(info, part, mixture, here, rows, left_st, right_st, gate_out, factor_out):
    size = left_st.shape[2]
    for spot, row, half, lanes, among in places_of(here, rows):
        mask = mask_chunk(info, part, row, half)
        for block, stage in enumerate((left_st, right_st)):
            gate = opened(mixture[(2 + block) * size : (3 + block) * size, among])
            opening = gate * mask
            side = mixture[block * size : (block + 1) * size, among] * opening
            stage[half, row] = side.astype(BF16)
            factor_out[spot, block * size : (block + 1) * size, lanes] = opening.astype(BF16)
            slope = (side * (1.0 - gate)).astype(BF16)
            factor_out[spot, (2 + block) * size : (3 + block) * size, lanes] = slope
        gate_out[spot, :, lanes] = opened(mixture[4 * size :, among]).astype(BF16)


def opened(gate):
    return 0.5 * jnp.tanh(gate) + 0.5


def column(row):
    return jnp.broadcast_to(row, (LANES, row.shape[1])).T


def halved_turned(weight):
    values = 2 * weight.shape[0]
    return jnp.concatenate([weight[:, :values].T, weight[:, values:].T * 0.5], axis=0).astype(BF16)


def entry_kernel(part, info, pair, norm_row, proj_w, *rest):
    if part:
        raw, rest = rest[:6], rest[6:]
        gain1, final1, norm2, proj2, gain2, final2 = raw
        prepared, rest = rest[7:18], rest[:7] + rest[18:]
    a_same, a_other, b_same, b_other, to_core, gate_out, factor_out, *rest = rest
    left_st, right_st, norm, proj_t, perm = rest
    hidden = proj_w.shape[1] // 5

    @first_step
    def _():
        norm[...] = column(norm_row[...])
        proj_t[...] = halved_turned(proj_w[...])
        perm[...] = reorder()
        if part:
            for row, out in zip((norm_row, gain1, norm2, gain2), prepared[:4]):
                out[...] = column(row[...])
            prepared[4][...] = halved_turned(proj2[...])
            for weight, out in zip((final1, final2), prepared[5:7]):
                out[...] = weight[...].T.astype(BF16)
            for weight, out in zip((proj_w, final1, proj2, final2), prepared[7:]):
                out[...] = weight[...].astype(BF16)

    def work(here, rows):
        normed = side_by_side(
            [
                (normalise(turned(pair, spot, lanes))[0] * norm[...]).astype(BF16)
                for spot, row, half, lanes, among in places_of(here, rows)
            ]
        )
        mixture = dot_nn(proj_t[...], normed)
        put_gated(info, part, mixture, here, rows, left_st, right_st, gate_out, factor_out)

    each_rows(work)

    @last_step
    def _():
        core = info[2]
        for owner, a_out, b_out in ((core, a_same, b_same), (1 - core, a_other, b_other)):
            for group in range(2):
                for at in CHUNKS:
                    channel = owner * (2 * GROUP) + group * GROUP + at
                    left = dot_nn(perm[...], get_chunk(left_st, (0, 1), channel)).astype(BF16)
                    right = dot_nn(perm[...], get_chunk(right_st, (0, 1), channel)).astype(BF16)
                    first, second = (left, right) if group == 0 else (right, left)
                    give_chunk(a_out, group, at, BOTH, first)
                    give_chunk(b_out, group, at, BOTH, second)
                    if a_out is a_other:
                        give_chunk(to_core, group, at, BOTH, first)
                        give_chunk(to_core, 2 + group, at, BOTH, second)


def fill_split(info, perm, stage, own, near, ypart, ycpart, xpart, xcpart):
    x, y, core = info[0], info[1], info[2]
    for owner, mine, yp, xp in ((core, own, ypart, xpart), (1 - core, near, ycpart, xcpart)):
        for at in CHUNKS:
            channel = owner * (2 * GROUP) + at
            both = jnp.concatenate([chunk(mine, 0, at, LOW), chunk(yp, 0, at, LOW)], axis=1)
            both = dot_nn(perm, both)
            put_chunk(stage, y, channel, both[:, LOW])
            put_chunk(stage, 1 - y, channel, both[:, HIGH])
            both = jnp.concatenate([chunk(mine, 1, at, LOW), chunk(xp, 0, at, LOW)], axis=1)
            both = dot_nn(perm, both)
            here, there = both[:, LOW], both[:, HIGH]
            first, second = half_swap(pick(x, here, there), pick(x, there, here))
            put_chunk(stage, 0, channel + GROUP, first)
            put_chunk(stage, 1, channel + GROUP, second)


def fill_sum(perm, stage, channel, first, second):
    both = (chunk(*first).astype(F32) + chunk(*second).astype(F32)).astype(BF16)
    total = dot_nn(perm, both)
    put_chunk(stage, 0, channel, total[:, LOW])
    put_chunk(stage, 1, channel, total[:, HIGH])


def split_out(info, perm, stage, owner, at):
    x, y = info[0], info[1]
    channel = owner * (2 * GROUP) + at
    both = dot_nn(perm, get_chunk(stage, (y, 1 - y), channel))
    swapped = dot_nn(perm, get_chunk(stage, (0, 1), channel + GROUP))
    first, second = half_swap(swapped[:, LOW], swapped[:, HIGH])
    return both[:, LOW], both[:, HIGH], pick(x, first, second), pick(x, second, first)


def middle_kernel(
    part, info, pair, own, ypart, xpart, ycpart, xcpart, near,
    gate1, gain1, final1_t, norm2, proj2_t,
    middle_out, inner_out, gate_out, factor_out, normed_out, final_out, slope_out, o_own, o_near, o_y, o_yc, o_x, o_xc,
    stage, left_st, right_st, perm,
):
    @first_step
    def _():
        perm[...] = reorder()
        fill_split(info, perm[...], stage, own, near, ypart, ycpart, xpart, xcpart)

    def work(here, rows):
        finals, normeds = [], []
        for spot, row, half, lanes, among in places_of(here, rows):
            inner = stage[half, row]
            final = (normalise(inner)[0] * gain1[...]).astype(BF16)
            inner_out[spot, :, lanes] = inner.astype(BF16)
            final_out[spot, :, lanes] = final
            finals.append(final)
        product = dot_nn(final1_t[...], side_by_side(finals))
        for spot, row, half, lanes, among in places_of(here, rows):
            gate = gate1[spot, :, lanes].astype(F32)
            update = product[:, among] * gate
            slope_out[spot, :, lanes] = (update * (1.0 - gate)).astype(BF16)
            middle = (turned(pair, spot, lanes) + update).astype(BF16)
            middle_out[spot, :, lanes] = middle
            normed = (normalise(middle.astype(F32))[0] * norm2[...]).astype(BF16)
            normed_out[spot, :, lanes] = normed
            normeds.append(normed)
        mixture = dot_nn(proj2_t[...], side_by_side(normeds))
        put_gated(info, part, mixture, here, rows, left_st, right_st, gate_out, factor_out)

    each_rows(work)

    @last_step
    def _():
        core = info[2]
        beyond = slice(LANES, 3 * LANES)
        for owner, main, yo, xo in ((core, o_own, o_y, o_x), (1 - core, o_near, o_yc, o_xc)):
            for at in CHUNKS:
                kept = split_out(info, perm[...], left_st, owner, at)
                give_chunk(main, 0, at, LOW, kept[0])
                give_chunk(yo, 0, at, LOW, kept[1])
                give_chunk(main, 1, at, LOW, kept[2])
                give_chunk(xo, 0, at, LOW, kept[3])
                for group, out in ((0, yo), (1, xo)):
                    channel = owner * (2 * GROUP) + group * GROUP + at
                    right = dot_nn(perm[...], get_chunk(right_st, (0, 1), channel)).astype(BF16)
                    give_chunk(main, group, at, beyond, right)
                    give_chunk(out, 0, at, beyond, right)


def turn_kernel(
    part, info, gate2, cot, own, ypart, xpart, ycpart, xcpart, near,
    gain2, final2_t, final2_w,
    gate_out, final_out, product_out, same0, same1, other0, other1, to_core, stage, out_st, perm,
):
    core = info[2]

    @first_step
    def _():
        perm[...] = reorder()
        for owner, mine, xp, yp in ((core, own, xpart, ypart), (1 - core, near, xcpart, ycpart)):
            for at in CHUNKS:
                channel = owner * (2 * GROUP) + at
                fill_sum(perm[...], stage, channel, (mine, 0, at, BOTH), (xp, 0, at, BOTH))
                fill_sum(perm[...], stage, channel + GROUP, (mine, 1, at, BOTH), (yp, 0, at, BOTH))

    def work(here, rows):
        finals, products = [], []
        for spot, row, half, lanes, among in places_of(here, rows):
            final = (normalise(stage[half, row])[0] * gain2[...]).astype(BF16)
            final_out[spot, :, lanes] = final
            finals.append(final)
            grad_product = turned(cot, spot, lanes) * gate2[spot, :, lanes].astype(F32)
            grad_product = grad_product.astype(BF16)
            product_out[spot, :, lanes] = grad_product
            products.append(grad_product)
        product = dot_nn(final2_t[...], side_by_side(finals))
        grad_final = dot_nn(final2_w[...], side_by_side(products))
        for spot, row, half, lanes, among in places_of(here, rows):
            gate = gate2[spot, :, lanes].astype(F32)
            grad_gate = turned(cot, spot, lanes) * product[:, among] * gate * (1.0 - gate)
            gate_out[spot, :, lanes] = grad_gate.astype(BF16)
            hat, spread = normalise(stage[half, row])
            grad_inner = normalise_back(grad_final[:, among] * gain2[...], hat, spread)
            out_st[half, row] = grad_inner.astype(BF16)

    each_rows(work)

    @last_step
    def _():
        for owner, outs in ((core, (same0, same1)), (1 - core, (other0, other1))):
            for group, out in enumerate(outs):
                for at in CHUNKS:
                    channel = owner * (2 * GROUP) + group * GROUP + at
                    value = dot_nn(perm[...], get_chunk(out_st, (0, 1), channel)).astype(BF16)
                    give_chunk(out, 0, at, BOTH, value)
                    if out is other0 or out is other1:
                        give_chunk(to_core, group, at, BOTH, value)


def mixture_chunk(left_st, right_st, factors, gate_in, spot, row, half, lanes):
    size = left_st.shape[2]
    grads = (left_st[half, row], right_st[half, row])
    blocks = [
        (grads[n % 2] * factors[spot, n * size : (n + 1) * size, lanes].astype(F32)).astype(BF16)
        for n in range(4)
    ]
    return jnp.concatenate(blocks + [gate_in[spot, :, lanes]], axis=0)


def inward_kernel(
    part, info, middle, gate1, cot, inner_in, gate_in, factors, slopes, own, ypart, xpart, ycpart, xcpart, near,
    norm2, proj2_w, gain1, final1_w,
    grad_out, gate_out, mixture_out, product_out, o_own, o_near, o_y, o_yc, o_x, o_xc,
    left_st, right_st, out_st, perm,
):
    core = info[2]

    @first_step
    def _():
        perm[...] = reorder()
        fill_split(info, perm[...], left_st, own, near, ypart, ycpart, xpart, xcpart)
        beyond = slice(LANES, 3 * LANES)
        for owner, mine, yp, xp in ((core, own, ypart, xpart), (1 - core, near, ycpart, xcpart)):
            for at in CHUNKS:
                channel = owner * (2 * GROUP) + at
                fill_sum(perm[...], right_st, channel, (mine, 0, at, beyond), (yp, 0, at, beyond))
                fill_sum(
                    perm[...], right_st, channel + GROUP, (mine, 1, at, beyond), (xp, 0, at, beyond)
                )

    def work(here, rows):
        mixtures, products = [], []
        for spot, row, half, lanes, among in places_of(here, rows):
            mixture = mixture_chunk(left_st, right_st, factors, gate_in, spot, row, half, lanes)
            mixture_out[spot, :, lanes] = mixture
            mixtures.append(mixture)
        grad_normed = dot_nn(proj2_w[...], side_by_side(mixtures))
        for spot, row, half, lanes, among in places_of(here, rows):
            hat, spread = normalise(middle[spot, :, lanes].astype(F32))
            grad = normalise_back(grad_normed[:, among] * norm2[...], hat, spread)
            grad = grad + turned(cot, spot, lanes)
            grad_out[spot, :, lanes] = grad
            gate_out[spot, :, lanes] = (grad * slopes[spot, :, lanes].astype(F32)).astype(BF16)
            grad_product = (grad * gate1[spot, :, lanes].astype(F32)).astype(BF16)
            product_out[spot, :, lanes] = grad_product
            products.append(grad_product)
        grad_final = dot_nn(final1_w[...], side_by_side(products))
        for spot, row, half, lanes, among in places_of(here, rows):
            hat, spread = normalise(inner_in[spot, :, lanes].astype(F32))
            grad_inner = normalise_back(grad_final[:, among] * gain1[...], hat, spread)
            out_st[half, row] = grad_inner.astype(BF16)

    each_rows(work)

    @last_step
    def _():
        for owner, main, yo, xo in ((core, o_own, o_y, o_x), (1 - core, o_near, o_yc, o_xc)):
            for at in CHUNKS:
                kept = split_out(info, perm[...], out_st, owner, at)
                give_chunk(main, 0, at, LOW, kept[0])
                give_chunk(yo, 0, at, LOW, kept[1])
                give_chunk(main, 1, at, LOW, kept[2])
                give_chunk(xo, 0, at, LOW, kept[3])


def weight_kernel(info, *refs):
    *refs, total = refs
    (mixtures, normeds, *pairs) = paired(refs)
    width, channels = mixtures[0].shape[1], normeds[0].shape[1]

    @pl.when(pl.program_id(0) == 0)
    def _():
        total[...] = jnp.zeros_like(total)

    for part in range(PARTS):
        for first in range(0, mixtures[part].shape[0], PAIRED):
            rows = [first + n for n in range(PAIRED)]
            mixture, normed = stacked(mixtures[part], rows), stacked(normeds[part], rows)
            total[:width, :] += dot_nt(mixture, normed)
            for n, (finals, products) in enumerate((pairs[:2], pairs[2:])):
                where = slice(width + n * channels, width + (n + 1) * channels)
                final, product = stacked(finals[part], rows), stacked(products[part], rows)
                total[where, :] += dot_nt(final, product)


def exit_kernel(
    part, info, pair, grad_in, gate_in, factors, own, ypart, xpart, ycpart, xcpart, near,
    norm1, proj1_w, early, *rest,
):
    out, gproj, *rest, left_st, right_st, perm = rest
    if part:
        before, unused, out, gproj, packed = (out, gproj, *rest)
    core = info[2]

    @first_step
    def _():
        perm[...] = reorder()
        gproj[...] = before[...] if part else jnp.zeros_like(gproj)
        beyond = slice(2 * LANES, 4 * LANES)
        for owner, mine, yp, xp in ((core, own, ypart, xpart), (1 - core, near, ycpart, xcpart)):
            for group, lefts, rights in ((0, yp, xp), (1, xp, yp)):
                for at in CHUNKS:
                    channel = owner * (2 * GROUP) + group * GROUP + at
                    fill_sum(
                        perm[...], left_st, channel, (mine, group, at, BOTH), (lefts, group, at, BOTH)
                    )
                    fill_sum(
                        perm[...],
                        right_st,
                        channel,
                        (mine, group, at, beyond),
                        (rights, group, at, BOTH),
                    )

    def work(here, rows):
        mixtures, normeds = [], []
        for spot, row, half, lanes, among in places_of(here, rows):
            normeds.append(
                (normalise(turned(pair, spot, lanes))[0] * norm1[...]).astype(BF16)
            )
            mixtures.append(
                mixture_chunk(left_st, right_st, factors, gate_in, spot, row, half, lanes)
            )
        mixture = side_by_side(mixtures)
        gproj[...] += dot_nt(mixture, side_by_side(normeds))
        grad_normed = dot_nn(proj1_w[...], mixture)
        for spot, row, half, lanes, among in places_of(here, rows):
            hat, spread = normalise(turned(pair, spot, lanes))
            grad = normalise_back(grad_normed[:, among] * norm1[...], hat, spread)
            out[spot, lanes, :] = (grad_in[spot, :, lanes] + grad).T

    each_rows(work)

    if part:

        @last_step
        def _():
            size = gproj.shape[0]
            packed[:size, :] = gproj[...].astype(BF16)
            packed[size:, :] = early[...].astype(BF16)


CHANNELS = 8
PARTS = 2


def paired(refs):
    return [refs[n : n + PARTS] for n in range(0, len(refs), PARTS)]


def place(one, two, part):
    return pl.multiple_of((one * 2 + two) * (PARTS * BLOCK) + part * BLOCK, BLOCK)


def places(info, group):
    at, core = info[group], info[2]
    return [
        place(at if n < 2 else 1 - at, core if n % 2 == 0 else 1 - core, part)
        for n in range(4)
        for part in range(PARTS)
    ]


def take(ref, group, h):
    return ref[group, h] if len(ref.shape) == 4 else ref[h]


def joined(quads, group, h):
    return jnp.concatenate([take(ref, group, h) for refs in quads for ref in refs], axis=0)


def gather(stage, slot, wheres, quads, group, h):
    for where, ref in zip(wheres, [ref for refs in quads for ref in refs]):
        stage[slot, pl.ds(where, BLOCK), :] = take(ref, group, h)
    return stage[slot]


def give(refs, group, h, lanes, value):
    if len(refs.shape) == 4:
        refs[group, h, :, lanes] = value
    else:
        refs[h, :, lanes] = value


def scatter(quads, group, h, lanes, value):
    for n, ref in enumerate([ref for refs in quads for ref in refs]):
        give(ref, group, h, lanes, value[n * BLOCK : (n + 1) * BLOCK])


def scatter_from(stage, slot, wheres, quads, group, h, lanes):
    for where, ref in zip(wheres, [ref for refs in quads for ref in refs]):
        give(ref, group, h, lanes, stage[slot, pl.ds(where, BLOCK), :])


def outgoing_kernel(info, *refs):
    *refs, stage = refs
    *refs, o_own, o_near, o_y, o_yc, o_x, o_xc = refs
    a_own, b_own, a_y, b_x, a_yc, b_xc, near = paired(refs)
    a_near, b_near = [ref.at[:2] for ref in near], [ref.at[2:] for ref in near]
    along_a, along_b = (a_own, a_near, a_y, a_yc), (b_own, b_near, b_x, b_xc)
    for h in range(CHANNELS):
        for group in range(2):
            lefts, rights = (along_a, along_b) if group == 0 else (along_b, along_a)
            far = (o_y, o_yc) if group == 0 else (o_x, o_xc)
            right = gather(stage, 2 * h + group, places(info, group), rights, group, h)
            inner = dot_nt(joined(lefts, group, h), right).astype(BF16)
            for n, out in enumerate((o_own, o_near) + far):
                rows = PARTS * BLOCK
                give(out, group, h, slice(0, LANES), inner[n * rows : (n + 1) * rows])


def halves(quads, group, h):
    both = joined(quads, group, h)
    return both[:, :LANES], both[:, LANES:]


def incoming_kernel(info, *refs):
    *refs, stage = refs
    own, ypart, xpart, ycpart, xcpart, near, o_own, o_near, o_x, o_xc, o_y, o_yc = paired(refs)
    for h in range(CHANNELS):
        for group in range(2):
            far = (ypart, ycpart) if group == 0 else (xpart, xcpart)
            outs = (o_own, o_near) + ((o_x, o_xc) if group == 0 else (o_y, o_yc))
            slot = 2 * h + group
            left, right = halves((own, near) + far, group, h)
            stage[slot] = dot_tn(left, right).astype(BF16)
            scatter_from(stage, slot, places(info, group), outs, group, h, slice(0, 2 * LANES))


def incoming_back_kernel(info, *refs):
    *refs, stage = refs
    own, ypart, xpart, ycpart, xcpart, near, *more = paired(refs)
    same0, same1, g_y, g_x, g_yc, g_xc, g_near, *more = more
    o_own, o_near, o_y, o_yc, o_x, o_xc = more
    for h in range(CHANNELS):
        for group in range(2):
            far = (ypart, ycpart) if group == 0 else (xpart, xcpart)
            grads = (same0, g_near, g_x, g_xc) if group == 0 else (same1, g_near, g_y, g_yc)
            outs = (o_own, o_near) + ((o_y, o_yc) if group == 0 else (o_x, o_xc))
            grad = gather(stage, 2 * h + group, places(info, group), grads, group, h)
            left, right = halves((own, near) + far, group, h)
            scatter(outs, group, h, slice(0, LANES), dot_nt(right, grad).astype(BF16))
            scatter(outs, group, h, slice(LANES, 3 * LANES), dot_nn(left, grad).astype(BF16))


def outgoing_back_kernel(info, *refs):
    *refs, stage, back = refs
    a_own, b_own, a_y, b_x, a_yc, b_xc, near, *more = paired(refs)
    a_near, b_near = [ref.at[:2] for ref in near], [ref.at[2:] for ref in near]
    g_own, g_y, g_x, g_yc, g_xc, g_near, o_own, o_near, o_y, o_yc, o_x, o_xc = more
    along_a, along_b = (a_own, a_near, a_y, a_yc), (b_own, b_near, b_x, b_xc)
    first, second = slice(0, 2 * LANES), slice(2 * LANES, 4 * LANES)
    for h in range(CHANNELS):
        for group in range(2):
            lefts, rights = (along_a, along_b) if group == 0 else (along_b, along_a)
            far = (g_y, g_yc) if group == 0 else (g_x, g_xc)
            left_far, right_far = ((o_y, o_yc), (o_x, o_xc)) if group == 0 else ((o_x, o_xc), (o_y, o_yc))
            slot = 2 * h + group
            wheres = places(info, group)
            right = gather(stage, slot, wheres, rights, group, h)
            grad = joined((g_own, g_near) + far, group, h)
            grad_left = dot_nn(grad, right).astype(BF16)
            back[slot] = dot_tn(grad, joined(lefts, group, h)).astype(BF16)
            core_rows = 2 * PARTS * BLOCK
            scatter((o_own, o_near), group, h, first, grad_left[:core_rows])
            scatter(left_far, group, h, first, grad_left[core_rows:])
            scatter_from(back, slot, wheres[: 2 * PARTS], (o_own, o_near), group, h, second)
            scatter_from(back, slot, wheres[2 * PARTS :], right_far, group, h, first)


def whole(shape):
    return pl.BlockSpec(shape, lambda step, info: (0,) * len(shape))


def rows_of(part, some=SOME):
    def make(shape):
        first = part * (BLOCK // some)
        return pl.BlockSpec(
            (some,) + shape[1:], lambda step, info: (first + step,) + (0,) * (len(shape) - 1)
        )

    make.kept = True
    return make


def rows_block(part):
    def make(shape):
        return pl.BlockSpec(
            shape[:-2] + (BLOCK, shape[-1]),
            lambda step, info: (0,) * (len(shape) - 2) + (part, 0),
        )

    return make


def anywhere(shape):
    return pl.BlockSpec(memory_space=pl.ANY)


def channel_rows(shape):
    if len(shape) == 4:
        return pl.BlockSpec((shape[0], CHANNELS) + shape[2:], lambda step, info: (0, step, 0, 0))
    return pl.BlockSpec((CHANNELS,) + shape[1:], lambda step, info: (step, 0, 0))


def in_place(array):
    return pltpu.with_memory_space_constraint(array, pltpu.HBM)


def call(kernel, info, steps, ins, outs, scratch, aliases={}, vmem=CELL_VMEM):
    return pl.pallas_call(
        kernel,
        grid_spec=pltpu.PrefetchScalarGridSpec(
            num_scalar_prefetch=1,
            grid=(steps,),
            in_specs=[make(array.shape) for array, make in ins],
            out_specs=[make(shape) for shape, unused, make in outs],
            scratch_shapes=scratch,
        ),
        out_shape=[
            (pltpu.HBM if getattr(make, "kept", False) else jax.ShapeDtypeStruct)(shape, dtype)
            for shape, dtype, make in outs
        ],
        compiler_params=pltpu.CompilerParams(vmem_limit_bytes=vmem),
        input_output_aliases=aliases,
    )(info, *[in_place(array) if getattr(make, "kept", False) else array for array, make in ins])


class Links:
    def __init__(self):
        self.last = {}

    def send(self, array, offset, first=None):
        count = lax.axis_size("axial")
        if first is not None:
            array, unused = lax.optimization_barrier((array, first))
        if offset in self.last and offset in (X, Y):
            array, unused = lax.optimization_barrier((array, self.last[offset]))
        self.last[offset] = lax.ppermute(
            array, "axial", [(n, n ^ offset) for n in range(count)]
        )
        return self.last[offset]

    def __call__(self, *sends, between=None):
        results = [[] for unused in sends]
        for part in range(len(sends[0][0])):
            for result, (arrays, offset) in zip(results, sends):
                result.append(self.send(arrays[part], offset, between if part else None))
        return results


CORE, X, Y = 1, 2, 4


def add_up(share):
    count = lax.axis_size("axial")
    rows, width = share.shape
    shares = share.reshape(count, rows // count, width)
    parts = lax.all_to_all(shares, "axial", split_axis=0, concat_axis=0, tiled=True)
    mine = parts.astype(F32).sum(axis=0).astype(BF16)
    depth = lax.axis_size("dp")
    terms = [mine] + [
        lax.ppermute(mine, "dp", [(n, n ^ offset) for n in range(depth)])
        for offset in range(1, depth)
    ]
    terms = [term.astype(F32) for term in terms]
    while len(terms) > 1:
        terms = [terms[n] + terms[n + 1] for n in range(0, len(terms), 2)]
    copies = jnp.broadcast_to(terms[0].astype(BF16)[None], shares.shape)
    return lax.all_to_all(copies, "axial", split_axis=0, concat_axis=0, tiled=True).reshape(
        rows, width
    )


def gain_grad(weight_grad, weight, gain_row):
    return jnp.sum((weight.astype(F32) * weight_grad).T, axis=0, keepdims=True) / gain_row


def finish_kernel(
    scale, info, sums, proj1, final1, proj2, final2, norm1, gain1, norm2, gain2,
    o_norm1, o_proj1, o_gain1, o_final1, o_norm2, o_proj2, o_gain2, o_final2,
):
    width, channels = proj1.shape[1], final1.shape[1]
    takes = (
        (0, True, proj1, norm1, o_proj1, o_norm1),
        (width, True, proj2, norm2, o_proj2, o_norm2),
        (2 * width, False, final2, gain2, o_final2, o_gain2),
        (2 * width + channels, False, final1, gain1, o_final1, o_gain1),
    )
    for start, flipped, weight, gain, out, gain_out in takes:
        total = sums[start : start + weight.shape[1], :].astype(F32) * scale
        total = total.T if flipped else total
        out[...] = total
        gain_out[...] = gain_grad(total, weight[...].astype(BF16), gain[...])


def fast_body(
    pair,
    cotangent,
    lengths,
    outgo_norm,
    outgo_proj,
    outgo_gain,
    outgo_final,
    incom_norm,
    incom_proj,
    incom_gain,
    incom_final,
):
    rows, tokens, channels = pair.shape[1:]
    hidden = outgo_gain.shape[0]
    index = lax.axis_index("axial")
    info = jnp.stack(
        [(index // 2) % 2, index // 4, index % 2, index * rows, lengths[0]]
    ).astype(jnp.int32)
    hop = Links()
    pair = pair[0]
    cot = cotangent[0]
    parts = range(PARTS)
    turns = GROUP // CHANNELS
    stage = pltpu.VMEM((2, BLOCK, hidden, LANES), F32)
    out_stage = pltpu.VMEM((2, BLOCK, hidden, LANES), BF16)
    perm = pltpu.VMEM((BLOCK * BLOCK, BLOCK * BLOCK), BF16)
    streamed = rows_of(0)
    square = pltpu.VMEM((2 * CHANNELS, 4 * rows, tokens), BF16)

    def two(width, height=BLOCK, make=whole, groups=2):
        return ((groups, GROUP, height, width), BF16, make)

    def one(width, height=BLOCK, make=whole):
        return ((GROUP, height, width), BF16, make)

    turned_block = ((BLOCK, channels, tokens), BF16, streamed)
    factor_block = ((BLOCK, 4 * hidden, tokens), BF16, streamed)
    mixture_block = ((BLOCK, 5 * hidden, tokens), BF16, streamed)

    def cells(kernel, ins, outs, scratch, more=lambda part: []):
        results = []
        for part in parts:
            carried = ins(part, results)
            results.append(
                call(functools.partial(kernel, part), info, STEPS, carried, outs + more(part), scratch)
            )
        shared = results[-1][len(outs) :]
        return [list(each) for each in zip(*results)] + list(shared)

    def wholes(arrays):
        return [(array, whole) for array in arrays]

    def triangle(kernel, operands, outs, scratch, split=PARTS):
        ins = [(array, channel_rows) for arrays in operands for array in arrays]
        each = [out for out in outs for unused in range(split)]
        results = call(kernel, info, turns, ins, each, scratch, vmem=TRIANGLE_VMEM)
        return [list(results[n : n + split]) for n in range(0, len(results), split)]

    raw = (outgo_gain[None], outgo_final, incom_norm[None], incom_proj, incom_gain[None], incom_final)
    gain_wide = ((channels, LANES), F32, whole)
    proj_turned = ((5 * hidden, channels), BF16, whole)
    proj_plain = ((channels, 5 * hidden), BF16, whole)
    final_plain = ((hidden, channels), BF16, whole)
    (
        a_same, a_other, b_same, b_other, to_core, gate_one, factors_one,
        norm1, gain1, norm2, gain2, proj2_t, final1_t, final2_t,
        proj1, final1, proj2, final2,
    ) = cells(
        entry_kernel,
        lambda part, unused: [(pair, rows_of(part)), (outgo_norm[None], whole), (outgo_proj, whole)]
        + (wholes(raw) if part else []),
        [two(tokens)] * 4 + [two(tokens, groups=4), turned_block, factor_block],
        [
            out_stage,
            out_stage,
            pltpu.VMEM((channels, LANES), F32),
            pltpu.VMEM((5 * hidden, channels), BF16),
            perm,
        ],
        lambda part: (
            [gain_wide] * 4
            + [proj_turned]
            + [final_plain] * 2
            + [proj_plain, final_plain] * 2
            if part
            else []
        ),
    )
    held_one = [a_same, b_same] + hop(
        (a_same, Y), (b_same, X), (a_other, Y | CORE), (b_other, X | CORE), (to_core, CORE)
    )
    own, near, to_y, to_yc, to_x, to_xc = triangle(
        outgoing_kernel,
        held_one,
        [two(LANES, rows, channel_rows)] * 2 + [one(LANES, rows, channel_rows)] * 4,
        [square],
        split=1,
    )
    back_one = [
        own,
        *hop(
            (to_y, Y), (to_x, X), (to_yc, Y | CORE), (to_xc, X | CORE), (near, CORE)
        ),
    ]

    (
        middle, inner_one, gate_two, factors_two, normed_two, finals_one, slopes_one,
        own, near, to_y, to_yc, to_x, to_xc,
    ) = cells(
        middle_kernel,
        lambda part, unused: [(pair, rows_of(part))]
        + [(array, rows_block(part)) for array, in back_one]
        + [(gate_one[part], streamed)]
        + wholes((gain1, final1_t, norm2, proj2_t)),
        [turned_block] * 3
        + [factor_block]
        + [turned_block] * 3
        + [two(3 * LANES)] * 2 + [one(3 * LANES)] * 4,
        [stage, out_stage, out_stage, perm],
    )
    held_two = [
        own,
        *hop(
            (to_y, Y), (to_x, X), (to_yc, Y | CORE), (to_xc, X | CORE), (near, CORE)
        ),
    ]
    own, near, to_x, to_xc, to_y, to_yc = triangle(
        incoming_kernel,
        held_two,
        [two(tokens, make=channel_rows)] * 2 + [one(tokens, make=channel_rows)] * 4,
        [square],
    )
    back_two = [
        own,
        *hop(
            (to_y, Y), (to_x, X), (to_yc, Y | CORE), (to_xc, X | CORE), (near, CORE)
        ),
    ]

    gate_grad_two, finals_two, products_two, same0, same1, other0, other1, to_core = cells(
        turn_kernel,
        lambda part, done: [(gate_two[part], streamed), (cot, rows_of(part))]
        + wholes(arrays[part] for arrays in back_two)
        + wholes((gain2, final2_t, final2)),
        [turned_block] * 3 + [one(tokens)] * 4 + [two(tokens)],
        [stage, out_stage, perm],
    )
    grads_two = [
        same0,
        same1,
        *hop(
            (same1, Y), (same0, X), (other1, Y | CORE), (other0, X | CORE), (to_core, CORE)
        ),
    ]
    own, near, to_y, to_yc, to_x, to_xc = triangle(
        incoming_back_kernel,
        held_two + grads_two,
        [two(3 * LANES, make=channel_rows)] * 2 + [one(3 * LANES, make=channel_rows)] * 4,
        [square],
    )
    rows_two = [
        own,
        *hop(
            (to_y, Y), (to_x, X), (to_yc, Y | CORE), (to_xc, X | CORE), (near, CORE)
        ),
    ]

    (
        grad_middle, gate_grad_one, mixtures_two, products_one,
        own, near, to_y, to_yc, to_x, to_xc,
    ) = cells(
        inward_kernel,
        lambda part, done: [
            (middle[part], streamed),
            (gate_one[part], streamed),
            (cot, rows_of(part)),
            (inner_one[part], streamed),
            (gate_grad_two[part], streamed),
            (factors_two[part], streamed),
            (slopes_one[part], streamed),
        ]
        + wholes(arrays[part] for arrays in rows_two)
        + wholes((norm2, proj2, gain1, final1)),
        [((BLOCK, channels, tokens), F32, streamed), turned_block, mixture_block, turned_block]
        + [two(LANES)] * 2
        + [one(LANES)] * 4,
        [stage, stage, out_stage, perm],
    )
    grads_one = [
        own,
        *hop(
            (to_y, Y), (to_x, X), (to_yc, Y | CORE), (to_xc, X | CORE), (near, CORE)
        ),
    ]
    own, near, to_y, to_yc, to_x, to_xc = triangle(
        outgoing_back_kernel,
        held_one + grads_one,
        [two(2 * tokens, make=channel_rows)] * 2 + [two(tokens, make=channel_rows)] * 4,
        [square, square],
    )
    kept = (mixtures_two, normed_two, finals_two, products_two, finals_one, products_one)
    (early,) = call(
        weight_kernel,
        info,
        4,
        [
            (array, rows_of(0, BLOCK // 4))
            for arrays in kept
            for array in arrays
        ],
        [((5 * hidden + 2 * channels, channels), F32, whole)],
        [],
    )
    rows_one = [own] + hop(
        (to_y, Y), (to_x, X), (to_yc, Y | CORE), (to_xc, X | CORE), (near, CORE), between=early
    )
    exit_ins = 10 + 3 + 1 + 1
    result = None
    for part in parts:
        result = call(
            functools.partial(exit_kernel, part),
            info,
            STEPS,
            [
                (pair, rows_of(part)),
                (grad_middle[part], streamed),
                (gate_grad_one[part], streamed),
                (factors_one[part], streamed),
            ]
            + wholes(arrays[part] for arrays in rows_one)
            + wholes((norm1, proj1, early))
            + ([(result[1], whole), (result[0], anywhere)] if part else []),
            [
                ((rows, tokens, channels), F32, rows_of(part)),
                ((5 * hidden, channels), F32, whole),
            ]
            + ([((10 * hidden + 2 * channels, channels), BF16, whole)] if part else []),
            [stage, stage, perm],
            {exit_ins: 0} if part else {},
        )
    grad_begin, unused, packed = result
    sums = add_up(packed)
    scale = 1.0 / math.sqrt(lax.axis_size("dp") * tokens * tokens)
    weights = (outgo_proj, outgo_final, incom_proj, incom_final)
    gains = (outgo_norm, outgo_gain, incom_norm, incom_gain)
    order = (outgo_norm[None], outgo_proj, outgo_gain[None], outgo_final)
    order += (incom_norm[None], incom_proj, incom_gain[None], incom_final)
    totals = call(
        functools.partial(finish_kernel, scale),
        info,
        1,
        wholes((sums,) + weights + tuple(gain[None] for gain in gains)),
        [(array.shape, F32, whole) for array in order],
        [],
    )
    return (grad_begin[None],) + tuple(
        total.reshape(-1) if total.shape[0] == 1 else total for total in totals
    )


def solution(mesh):
    def body(pair, *rest):
        rows, tokens, channels = pair.shape[1:]
        hidden = rest[3].shape[0]
        plane = mesh.shape["axial"] == 8 and rows == 32 and tokens == 2 * LANES
        if plane and channels == LANES and hidden == 4 * GROUP:
            return fast_body(pair, *rest)
        return plain_body(pair, *rest)

    return jax.shard_map(
        body,
        mesh=mesh,
        in_specs=(P("dp", "axial", None, None), P("dp", "axial", None, None), P("dp")) + (P(),) * 8,
        out_specs=(P("dp", "axial", None, None),) + (P(),) * 8,
        check_vma=False,
    )
```

```python
import functools
import math

import jax
import jax.numpy as jnp
from jax import lax
from jax.experimental import pallas as pl
from jax.experimental.pallas import tpu as pltpu
from jax.sharding import PartitionSpec as P

EPSILON = 1e-05


def rounded(inputs):
    return lax.optimization_barrier(inputs.astype(jnp.bfloat16)).astype(jnp.float32)


def layer_norm(inputs, factor):
    average = jnp.mean(inputs, axis=-1, keepdims=True)
    centered = inputs - average
    spread = jnp.mean(centered * centered, axis=-1, keepdims=True)
    return centered * lax.rsqrt(spread + EPSILON) * factor


def gating(mixture, pair_mask, hidden):
    left_part = (
        mixture[:, :hidden] * jax.nn.sigmoid(mixture[:, 2 * hidden : 3 * hidden]) * pair_mask
    )
    right_part = (
        mixture[:, hidden : 2 * hidden]
        * jax.nn.sigmoid(mixture[:, 3 * hidden : 4 * hidden])
        * pair_mask
    )
    gate_part = jax.nn.sigmoid(mixture[:, 4 * hidden :])
    return (left_part, right_part, gate_part)


def entry(flat_pair, norm_gain, projection, pair_mask, hidden):
    normed = layer_norm(flat_pair, norm_gain).astype(jnp.bfloat16)
    mixture = jnp.dot(normed, projection.astype(jnp.bfloat16), preferred_element_type=jnp.float32)
    left_part, right_part, gate_part = gating(mixture, pair_mask, hidden)
    return (normed, mixture, left_part, right_part, gate_part)


def entry_back(
    flat_pair,
    norm_gain,
    projection,
    pair_mask,
    hidden,
    normed,
    mixture,
    grad_left,
    grad_right,
    grad_gate,
):
    unused, pull_gate = jax.vjp(lambda inner_mix: gating(inner_mix, pair_mask, hidden), mixture)
    grad_mixture = pull_gate((grad_left, grad_right, grad_gate))[0].astype(jnp.bfloat16)
    grad_projection = jnp.dot(normed.T, grad_mixture, preferred_element_type=jnp.float32)
    grad_normed = jnp.dot(
        grad_mixture, projection.astype(jnp.bfloat16).T, preferred_element_type=jnp.float32
    )
    unused, pull_norm = jax.vjp(layer_norm, flat_pair, norm_gain)
    grad_flat, grad_gain = pull_norm(grad_normed)
    return (grad_flat, grad_gain, grad_projection)


def leave(inner_sum, gate_part, out_gain, final_weight):
    final_normed = layer_norm(inner_sum, out_gain).astype(jnp.bfloat16)
    product = jnp.dot(
        final_normed, final_weight.astype(jnp.bfloat16), preferred_element_type=jnp.float32
    )
    return (final_normed, product, product * gate_part)


def leave_back(inner_sum, gate_part, out_gain, final_weight, final_normed, product, grad_update):
    grad_product = (grad_update * gate_part).astype(jnp.bfloat16)
    grad_gate = grad_update * product
    grad_final = jnp.dot(final_normed.T, grad_product, preferred_element_type=jnp.float32)
    grad_normed = jnp.dot(
        grad_product, final_weight.astype(jnp.bfloat16).T, preferred_element_type=jnp.float32
    )
    unused, pull_norm = jax.vjp(layer_norm, inner_sum, out_gain)
    grad_inner, grad_gain = pull_norm(grad_normed)
    return (grad_inner, grad_gate, grad_gain, grad_final)


def channel_major(field, row_count, tokens):
    hidden = field.shape[1]
    return jnp.transpose(field.reshape(row_count, tokens, hidden), (2, 0, 1))


def row_major(field):
    hidden = field.shape[0]
    return jnp.transpose(field, (1, 2, 0)).reshape(-1, hidden)


def plain_body(
    pair,
    cotangent,
    lengths,
    outgo_norm,
    outgo_proj,
    outgo_gain,
    outgo_final,
    incom_norm,
    incom_proj,
    incom_gain,
    incom_final,
):
    row_count = pair.shape[1]
    tokens = pair.shape[2]
    channels = pair.shape[3]
    hidden = outgo_gain.shape[0]
    length = lengths[0]
    first_row = lax.axis_index("axial") * row_count
    row_alive = (first_row + jnp.arange(row_count, dtype=jnp.int32) < length).astype(jnp.float32)
    column_alive = (jnp.arange(tokens, dtype=jnp.int32) < length).astype(jnp.float32)
    pair_mask = (row_alive[:, None] * column_alive[None, :]).reshape(-1, 1)
    flat_start = pair[0].reshape(-1, channels).astype(jnp.float32)
    normed_one, mixture_one, left_one, right_one, gate_one = entry(
        flat_start, outgo_norm, outgo_proj, pair_mask, hidden
    )
    left_first = channel_major(left_one.astype(jnp.bfloat16), row_count, tokens)
    right_first = channel_major(right_one.astype(jnp.bfloat16), row_count, tokens)
    left_owned, right_owned = (
        lax.all_to_all(left_first, "axial", split_axis=0, concat_axis=1, tiled=True),
        lax.all_to_all(right_first, "axial", split_axis=0, concat_axis=1, tiled=True),
    )
    inner_cols = jnp.einsum(
        "hik,hjk->hij", left_owned, right_owned, preferred_element_type=jnp.float32
    )
    inner_one = row_major(
        lax.all_to_all(
            inner_cols.astype(jnp.bfloat16), "axial", split_axis=1, concat_axis=0, tiled=True
        ).astype(inner_cols.dtype)
    )
    final_one, product_one, update_one = leave(inner_one, gate_one, outgo_gain, outgo_final)
    flat_middle = rounded(flat_start + update_one)
    normed_two, mixture_two, left_two, right_two, gate_two = entry(
        flat_middle, incom_norm, incom_proj, pair_mask, hidden
    )
    left_second = channel_major(left_two.astype(jnp.bfloat16), row_count, tokens)
    right_second = channel_major(right_two.astype(jnp.bfloat16), row_count, tokens)
    left_held, right_held = (
        lax.all_to_all(left_second, "axial", split_axis=0, concat_axis=1, tiled=True),
        lax.all_to_all(right_second, "axial", split_axis=0, concat_axis=1, tiled=True),
    )
    inner_held = jnp.einsum(
        "hki,hkj->hij", left_held, right_held, preferred_element_type=jnp.float32
    )
    inner_two = row_major(
        lax.all_to_all(
            inner_held.astype(jnp.bfloat16), "axial", split_axis=1, concat_axis=0, tiled=True
        ).astype(inner_held.dtype)
    )
    final_two, product_two, update_two = leave(inner_two, gate_two, incom_gain, incom_final)
    grad_end = cotangent[0].reshape(-1, channels).astype(jnp.float32)
    grad_inner_two, grad_gate_two, grad_gain_two, grad_final_two = leave_back(
        inner_two, gate_two, incom_gain, incom_final, final_two, product_two, grad_end
    )
    grad_cells_two = channel_major(grad_inner_two.astype(jnp.bfloat16), row_count, tokens)
    grad_held_two = lax.all_to_all(grad_cells_two, "axial", split_axis=0, concat_axis=1, tiled=True)
    left_back, right_back = (
        lax.all_to_all(left_second, "axial", split_axis=0, concat_axis=1, tiled=True),
        lax.all_to_all(right_second, "axial", split_axis=0, concat_axis=1, tiled=True),
    )
    grad_left_held = jnp.einsum(
        "hij,hkj->hki", grad_held_two, right_back, preferred_element_type=jnp.float32
    )
    grad_right_held = jnp.einsum(
        "hki,hij->hkj", left_back, grad_held_two, preferred_element_type=jnp.float32
    )
    grad_left_rows, grad_right_rows = (
        lax.all_to_all(
            grad_left_held.astype(jnp.bfloat16), "axial", split_axis=1, concat_axis=0, tiled=True
        ).astype(grad_left_held.dtype),
        lax.all_to_all(
            grad_right_held.astype(jnp.bfloat16), "axial", split_axis=1, concat_axis=0, tiled=True
        ).astype(grad_right_held.dtype),
    )
    grad_left_two = row_major(grad_left_rows)
    grad_right_two = row_major(grad_right_rows)
    grad_flat_two, grad_norm_two, grad_proj_two = entry_back(
        flat_middle,
        incom_norm,
        incom_proj,
        pair_mask,
        hidden,
        normed_two,
        mixture_two,
        grad_left_two,
        grad_right_two,
        grad_gate_two,
    )
    second_sums = lax.psum(
        (grad_norm_two, grad_proj_two, grad_gain_two, grad_final_two), ("dp", "axial")
    )
    grad_middle = grad_end + grad_flat_two
    grad_inner_one, grad_gate_one, grad_gain_one, grad_final_one = leave_back(
        inner_one, gate_one, outgo_gain, outgo_final, final_one, product_one, grad_middle
    )
    grad_cells_one = channel_major(grad_inner_one.astype(jnp.bfloat16), row_count, tokens)
    grad_owned_one = lax.all_to_all(
        grad_cells_one, "axial", split_axis=0, concat_axis=1, tiled=True
    )
    left_again, right_again = (
        lax.all_to_all(left_first, "axial", split_axis=0, concat_axis=1, tiled=True),
        lax.all_to_all(right_first, "axial", split_axis=0, concat_axis=1, tiled=True),
    )
    grad_left_owned = jnp.einsum(
        "hij,hjk->hik", grad_owned_one, right_again, preferred_element_type=jnp.float32
    )
    grad_right_owned = jnp.einsum(
        "hij,hik->hjk", grad_owned_one, left_again, preferred_element_type=jnp.float32
    )
    grad_left_back, grad_right_back = (
        lax.all_to_all(
            grad_left_owned.astype(jnp.bfloat16), "axial", split_axis=1, concat_axis=0, tiled=True
        ).astype(grad_left_owned.dtype),
        lax.all_to_all(
            grad_right_owned.astype(jnp.bfloat16), "axial", split_axis=1, concat_axis=0, tiled=True
        ).astype(grad_right_owned.dtype),
    )
    grad_left_one = row_major(grad_left_back)
    grad_right_one = row_major(grad_right_back)
    grad_flat_one, grad_norm_one, grad_proj_one = entry_back(
        flat_start,
        outgo_norm,
        outgo_proj,
        pair_mask,
        hidden,
        normed_one,
        mixture_one,
        grad_left_one,
        grad_right_one,
        grad_gate_one,
    )
    grad_begin = grad_middle + grad_flat_one
    first_sums = lax.psum(
        (grad_norm_one, grad_proj_one, grad_gain_one, grad_final_one), ("dp", "axial")
    )
    totals = tuple(first_sums) + tuple(second_sums)
    scale = 1.0 / math.sqrt(lax.axis_size("dp") * tokens * tokens)
    return (
        grad_begin.reshape(1, row_count, tokens, channels),
        totals[0] * scale,
        totals[1] * scale,
        totals[2] * scale,
        totals[3] * scale,
        totals[4] * scale,
        totals[5] * scale,
        totals[6] * scale,
        totals[7] * scale,
    )


BF16 = jnp.bfloat16
F32 = jnp.float32
BLOCK = 16
PAIRED = 2
STEPS = 4
SOME = BLOCK // STEPS
LANES = 128
GROUP = 32
MIB = 1024 * 1024
CELL_VMEM = 30 * MIB
TRIANGLE_VMEM = 14 * MIB


def dot_nn(a, b):
    return lax.dot_general(a, b, (((1,), (0,)), ((), ())), preferred_element_type=F32)


def dot_nt(a, b):
    return lax.dot_general(a, b, (((1,), (1,)), ((), ())), preferred_element_type=F32)


def dot_tn(a, b):
    return lax.dot_general(a, b, (((0,), (0,)), ((), ())), preferred_element_type=F32)


def normalise(v):
    centered = v - jnp.mean(v, axis=0, keepdims=True)
    spread = lax.rsqrt(jnp.mean(centered * centered, axis=0, keepdims=True) + EPSILON)
    return centered * spread, spread


def normalise_back(grad, hat, spread):
    first = jnp.mean(grad, axis=0, keepdims=True)
    second = jnp.mean(grad * hat, axis=0, keepdims=True)
    return spread * (grad - first - hat * second)


def reorder():
    size = BLOCK * BLOCK
    one = lax.broadcasted_iota(jnp.int32, (size, size), 0)
    two = lax.broadcasted_iota(jnp.int32, (size, size), 1)
    return jnp.where((one % BLOCK) * BLOCK + one // BLOCK == two, 1.0, 0.0).astype(BF16)


def chunk(ref, group, at, lanes):
    if len(ref.shape) == 4:
        block = ref[group, at : at + BLOCK, :, lanes]
    else:
        block = ref[at : at + BLOCK, :, lanes]
    return block.reshape(BLOCK * BLOCK, block.shape[2])


def put_chunk(stage, half, channel, value):
    channel = pl.multiple_of(channel, BLOCK)
    for row in range(BLOCK):
        stage[half, row, pl.ds(channel, BLOCK), :] = value[row * BLOCK : (row + 1) * BLOCK]


def get_chunk(stage, halves, channel):
    channel = pl.multiple_of(channel, BLOCK)
    return jnp.concatenate(
        [
            jnp.concatenate(
                [stage[half, row, pl.ds(channel, BLOCK), :] for row in range(BLOCK)], axis=0
            )
            for half in halves
        ],
        axis=1,
    )


def give_chunk(ref, group, at, lanes, value):
    block = value.astype(BF16).reshape(BLOCK, BLOCK, value.shape[1])
    if len(ref.shape) == 4:
        ref[group, at : at + BLOCK, :, lanes] = block
    else:
        ref[at : at + BLOCK, :, lanes] = block


LOW, HIGH, BOTH = slice(0, LANES), slice(LANES, 2 * LANES), slice(0, 2 * LANES)
CHUNKS = range(0, GROUP, BLOCK)


def half_swap(first, second):
    low = lax.broadcasted_iota(jnp.int32, first.shape, first.ndim - 1) < LANES // 2
    axis = first.ndim - 1
    return (
        jnp.where(low, first, pltpu.roll(second, LANES // 2, axis)),
        jnp.where(low, pltpu.roll(first, LANES // 2, axis), second),
    )


def pick(flag, zero, one):
    return jnp.where(flag == 0, zero, one)


def mask_chunk(info, part, row, half):
    token = lax.broadcasted_iota(jnp.int32, (1, LANES), 1) + half * LANES
    live = (info[3] + part * BLOCK + row < info[4]).astype(F32)
    return (token < info[4]).astype(F32) * live


def each_rows(work):
    step = pl.program_id(0)

    @pl.loop(0, SOME // PAIRED)
    def _(turn):
        here = [turn * PAIRED + n for n in range(PAIRED)]
        work(here, [step * SOME + row for row in here])


def first_step(work):
    pl.when(pl.program_id(0) == 0)(work)


def last_step(work):
    pl.when(pl.program_id(0) == STEPS - 1)(work)


def places_of(here, rows):
    for n, (spot, row) in enumerate(zip(here, rows)):
        for half in range(2):
            start = (2 * n + half) * LANES
            yield spot, row, half, (LOW, HIGH)[half], slice(start, start + LANES)


def turned(ref, spot, lanes):
    return ref[spot, lanes, :].astype(F32).T


def stacked(ref, rows):
    return jnp.concatenate([ref[row] for row in rows], axis=1)


def side_by_side(chunks):
    return jnp.concatenate(chunks, axis=1)


def put_gated(info, part, mixture, here, rows, left_st, right_st, gate_out, factor_out):
    size = left_st.shape[2]
    for spot, row, half, lanes, among in places_of(here, rows):
        mask = mask_chunk(info, part, row, half)
        for block, stage in enumerate((left_st, right_st)):
            gate = opened(mixture[(2 + block) * size : (3 + block) * size, among])
            opening = gate * mask
            side = mixture[block * size : (block + 1) * size, among] * opening
            stage[half, row] = side.astype(BF16)
            factor_out[spot, block * size : (block + 1) * size, lanes] = opening.astype(BF16)
            slope = (side * (1.0 - gate)).astype(BF16)
            factor_out[spot, (2 + block) * size : (3 + block) * size, lanes] = slope
        gate_out[spot, :, lanes] = opened(mixture[4 * size :, among]).astype(BF16)


def opened(gate):
    return 0.5 * jnp.tanh(gate) + 0.5


def column(row):
    return jnp.broadcast_to(row, (LANES, row.shape[1])).T


def halved_turned(weight):
    values = 2 * weight.shape[0]
    return jnp.concatenate([weight[:, :values].T, weight[:, values:].T * 0.5], axis=0).astype(BF16)


def entry_kernel(part, info, pair, norm_row, proj_w, *rest):
    if part:
        raw, rest = rest[:6], rest[6:]
        gain1, final1, norm2, proj2, gain2, final2 = raw
        prepared, rest = rest[7:18], rest[:7] + rest[18:]
    a_same, a_other, b_same, b_other, to_core, gate_out, factor_out, *rest = rest
    left_st, right_st, norm, proj_t, perm = rest
    hidden = proj_w.shape[1] // 5

    @first_step
    def _():
        norm[...] = column(norm_row[...])
        proj_t[...] = halved_turned(proj_w[...])
        perm[...] = reorder()
        if part:
            for row, out in zip((norm_row, gain1, norm2, gain2), prepared[:4]):
                out[...] = column(row[...])
            prepared[4][...] = halved_turned(proj2[...])
            for weight, out in zip((final1, final2), prepared[5:7]):
                out[...] = weight[...].T.astype(BF16)
            for weight, out in zip((proj_w, final1, proj2, final2), prepared[7:]):
                out[...] = weight[...].astype(BF16)

    def work(here, rows):
        normed = side_by_side(
            [
                (normalise(turned(pair, spot, lanes))[0] * norm[...]).astype(BF16)
                for spot, row, half, lanes, among in places_of(here, rows)
            ]
        )
        mixture = dot_nn(proj_t[...], normed)
        put_gated(info, part, mixture, here, rows, left_st, right_st, gate_out, factor_out)

    each_rows(work)

    @last_step
    def _():
        core = info[2]
        for owner, a_out, b_out in ((core, a_same, b_same), (1 - core, a_other, b_other)):
            for group in range(2):
                for at in CHUNKS:
                    channel = owner * (2 * GROUP) + group * GROUP + at
                    left = dot_nn(perm[...], get_chunk(left_st, (0, 1), channel)).astype(BF16)
                    right = dot_nn(perm[...], get_chunk(right_st, (0, 1), channel)).astype(BF16)
                    first, second = (left, right) if group == 0 else (right, left)
                    give_chunk(a_out, group, at, BOTH, first)
                    give_chunk(b_out, group, at, BOTH, second)
                    if a_out is a_other:
                        give_chunk(to_core, group, at, BOTH, first)
                        give_chunk(to_core, 2 + group, at, BOTH, second)


def fill_split(info, perm, stage, own, near, ypart, ycpart, xpart, xcpart):
    x, y, core = info[0], info[1], info[2]
    for owner, mine, yp, xp in ((core, own, ypart, xpart), (1 - core, near, ycpart, xcpart)):
        for at in CHUNKS:
            channel = owner * (2 * GROUP) + at
            both = jnp.concatenate([chunk(mine, 0, at, LOW), chunk(yp, 0, at, LOW)], axis=1)
            both = dot_nn(perm, both)
            put_chunk(stage, y, channel, both[:, LOW])
            put_chunk(stage, 1 - y, channel, both[:, HIGH])
            both = jnp.concatenate([chunk(mine, 1, at, LOW), chunk(xp, 0, at, LOW)], axis=1)
            both = dot_nn(perm, both)
            here, there = both[:, LOW], both[:, HIGH]
            first, second = half_swap(pick(x, here, there), pick(x, there, here))
            put_chunk(stage, 0, channel + GROUP, first)
            put_chunk(stage, 1, channel + GROUP, second)


def fill_sum(perm, stage, channel, first, second):
    both = (chunk(*first).astype(F32) + chunk(*second).astype(F32)).astype(BF16)
    total = dot_nn(perm, both)
    put_chunk(stage, 0, channel, total[:, LOW])
    put_chunk(stage, 1, channel, total[:, HIGH])


def split_out(info, perm, stage, owner, at):
    x, y = info[0], info[1]
    channel = owner * (2 * GROUP) + at
    both = dot_nn(perm, get_chunk(stage, (y, 1 - y), channel))
    swapped = dot_nn(perm, get_chunk(stage, (0, 1), channel + GROUP))
    first, second = half_swap(swapped[:, LOW], swapped[:, HIGH])
    return both[:, LOW], both[:, HIGH], pick(x, first, second), pick(x, second, first)


def middle_kernel(
    part, info, pair, own, ypart, xpart, ycpart, xcpart, near,
    gate1, gain1, final1_t, norm2, proj2_t,
    middle_out, inner_out, gate_out, factor_out, slope_out, o_own, o_near, o_y, o_yc, o_x, o_xc,
    stage, left_st, right_st, perm,
):
    @first_step
    def _():
        perm[...] = reorder()
        fill_split(info, perm[...], stage, own, near, ypart, ycpart, xpart, xcpart)

    def work(here, rows):
        finals, normeds = [], []
        for spot, row, half, lanes, among in places_of(here, rows):
            inner = stage[half, row]
            final = (normalise(inner)[0] * gain1[...]).astype(BF16)
            inner_out[spot, :, lanes] = inner.astype(BF16)
            finals.append(final)
        product = dot_nn(final1_t[...], side_by_side(finals))
        for spot, row, half, lanes, among in places_of(here, rows):
            gate = gate1[spot, :, lanes].astype(F32)
            update = product[:, among] * gate
            slope_out[spot, :, lanes] = (update * (1.0 - gate)).astype(BF16)
            middle = (turned(pair, spot, lanes) + update).astype(BF16)
            middle_out[spot, :, lanes] = middle
            normed = (normalise(middle.astype(F32))[0] * norm2[...]).astype(BF16)
            normeds.append(normed)
        mixture = dot_nn(proj2_t[...], side_by_side(normeds))
        put_gated(info, part, mixture, here, rows, left_st, right_st, gate_out, factor_out)

    each_rows(work)

    @last_step
    def _():
        core = info[2]
        beyond = slice(LANES, 3 * LANES)
        for owner, main, yo, xo in ((core, o_own, o_y, o_x), (1 - core, o_near, o_yc, o_xc)):
            for at in CHUNKS:
                kept = split_out(info, perm[...], left_st, owner, at)
                give_chunk(main, 0, at, LOW, kept[0])
                give_chunk(yo, 0, at, LOW, kept[1])
                give_chunk(main, 1, at, LOW, kept[2])
                give_chunk(xo, 0, at, LOW, kept[3])
                for group, out in ((0, yo), (1, xo)):
                    channel = owner * (2 * GROUP) + group * GROUP + at
                    right = dot_nn(perm[...], get_chunk(right_st, (0, 1), channel)).astype(BF16)
                    give_chunk(main, group, at, beyond, right)
                    give_chunk(out, 0, at, beyond, right)


def turn_kernel(
    part, info, gate2, cot, own, ypart, xpart, ycpart, xcpart, near,
    gain2, final2_t, final2_w,
    gate_out, final_out, product_out, same0, same1, other0, other1, to_core, stage, out_st, perm,
):
    core = info[2]

    @first_step
    def _():
        perm[...] = reorder()
        for owner, mine, xp, yp in ((core, own, xpart, ypart), (1 - core, near, xcpart, ycpart)):
            for at in CHUNKS:
                channel = owner * (2 * GROUP) + at
                fill_sum(perm[...], stage, channel, (mine, 0, at, BOTH), (xp, 0, at, BOTH))
                fill_sum(perm[...], stage, channel + GROUP, (mine, 1, at, BOTH), (yp, 0, at, BOTH))

    def work(here, rows):
        finals, products = [], []
        for spot, row, half, lanes, among in places_of(here, rows):
            final = (normalise(stage[half, row])[0] * gain2[...]).astype(BF16)
            final_out[spot, :, lanes] = final
            finals.append(final)
            grad_product = turned(cot, spot, lanes) * gate2[spot, :, lanes].astype(F32)
            grad_product = grad_product.astype(BF16)
            product_out[spot, :, lanes] = grad_product
            products.append(grad_product)
        product = dot_nn(final2_t[...], side_by_side(finals))
        grad_final = dot_nn(final2_w[...], side_by_side(products))
        for spot, row, half, lanes, among in places_of(here, rows):
            gate = gate2[spot, :, lanes].astype(F32)
            grad_gate = turned(cot, spot, lanes) * product[:, among] * gate * (1.0 - gate)
            gate_out[spot, :, lanes] = grad_gate.astype(BF16)
            hat, spread = normalise(stage[half, row])
            grad_inner = normalise_back(grad_final[:, among] * gain2[...], hat, spread)
            out_st[half, row] = grad_inner.astype(BF16)

    each_rows(work)

    @last_step
    def _():
        for owner, outs in ((core, (same0, same1)), (1 - core, (other0, other1))):
            for group, out in enumerate(outs):
                for at in CHUNKS:
                    channel = owner * (2 * GROUP) + group * GROUP + at
                    value = dot_nn(perm[...], get_chunk(out_st, (0, 1), channel)).astype(BF16)
                    give_chunk(out, 0, at, BOTH, value)
                    if out is other0 or out is other1:
                        give_chunk(to_core, group, at, BOTH, value)


def mixture_chunk(left_st, right_st, factors, gate_in, spot, row, half, lanes):
    size = left_st.shape[2]
    grads = (left_st[half, row], right_st[half, row])
    blocks = [
        (grads[n % 2] * factors[spot, n * size : (n + 1) * size, lanes].astype(F32)).astype(BF16)
        for n in range(4)
    ]
    return jnp.concatenate(blocks + [gate_in[spot, :, lanes]], axis=0)


def inward_kernel(
    part, info, middle, gate1, cot, inner_in, gate_in, factors, slopes, own, ypart, xpart, ycpart, xcpart, near,
    norm2, proj2_w, gain1, final1_w,
    grad_out, gate_out, mixture_out, product_out, o_own, o_near, o_y, o_yc, o_x, o_xc,
    left_st, right_st, out_st, perm,
):
    core = info[2]

    @first_step
    def _():
        perm[...] = reorder()
        fill_split(info, perm[...], left_st, own, near, ypart, ycpart, xpart, xcpart)
        beyond = slice(LANES, 3 * LANES)
        for owner, mine, yp, xp in ((core, own, ypart, xpart), (1 - core, near, ycpart, xcpart)):
            for at in CHUNKS:
                channel = owner * (2 * GROUP) + at
                fill_sum(perm[...], right_st, channel, (mine, 0, at, beyond), (yp, 0, at, beyond))
                fill_sum(
                    perm[...], right_st, channel + GROUP, (mine, 1, at, beyond), (xp, 0, at, beyond)
                )

    def work(here, rows):
        mixtures, products = [], []
        for spot, row, half, lanes, among in places_of(here, rows):
            mixture = mixture_chunk(left_st, right_st, factors, gate_in, spot, row, half, lanes)
            mixture_out[spot, :, lanes] = mixture
            mixtures.append(mixture)
        grad_normed = dot_nn(proj2_w[...], side_by_side(mixtures))
        for spot, row, half, lanes, among in places_of(here, rows):
            hat, spread = normalise(middle[spot, :, lanes].astype(F32))
            grad = normalise_back(grad_normed[:, among] * norm2[...], hat, spread)
            grad = grad + turned(cot, spot, lanes)
            grad_out[spot, :, lanes] = grad
            gate_out[spot, :, lanes] = (grad * slopes[spot, :, lanes].astype(F32)).astype(BF16)
            grad_product = (grad * gate1[spot, :, lanes].astype(F32)).astype(BF16)
            product_out[spot, :, lanes] = grad_product
            products.append(grad_product)
        grad_final = dot_nn(final1_w[...], side_by_side(products))
        for spot, row, half, lanes, among in places_of(here, rows):
            hat, spread = normalise(inner_in[spot, :, lanes].astype(F32))
            grad_inner = normalise_back(grad_final[:, among] * gain1[...], hat, spread)
            out_st[half, row] = grad_inner.astype(BF16)

    each_rows(work)

    @last_step
    def _():
        for owner, main, yo, xo in ((core, o_own, o_y, o_x), (1 - core, o_near, o_yc, o_xc)):
            for at in CHUNKS:
                kept = split_out(info, perm[...], out_st, owner, at)
                give_chunk(main, 0, at, LOW, kept[0])
                give_chunk(yo, 0, at, LOW, kept[1])
                give_chunk(main, 1, at, LOW, kept[2])
                give_chunk(xo, 0, at, LOW, kept[3])


def weight_kernel(info, *refs):
    *refs, norm2, gain1, total = refs
    mixtures, middles, finals_two, products_two, inners_one, products_one = paired(refs)
    width, channels = mixtures[0].shape[1], norm2.shape[0]

    @pl.when(pl.program_id(0) == 0)
    def _():
        total[...] = jnp.zeros_like(total)

    def normed(ref, rows, gain):
        return side_by_side(
            [
                (normalise(ref[row, :, lanes].astype(F32))[0] * gain[...]).astype(BF16)
                for row in rows
                for lanes in (LOW, HIGH)
            ]
        )

    for part in range(PARTS):
        for first in range(0, mixtures[part].shape[0], PAIRED):
            rows = [first + n for n in range(PAIRED)]
            total[:width, :] += dot_nt(
                stacked(mixtures[part], rows), normed(middles[part], rows, norm2)
            )
            total[width : width + channels, :] += dot_nt(
                stacked(finals_two[part], rows), stacked(products_two[part], rows)
            )
            total[width + channels :, :] += dot_nt(
                normed(inners_one[part], rows, gain1), stacked(products_one[part], rows)
            )


def exit_kernel(
    part, info, pair, grad_in, gate_in, factors, own, ypart, xpart, ycpart, xcpart, near,
    norm1, proj1_w, early, *rest,
):
    out, gproj, *rest, left_st, right_st, perm = rest
    if part:
        before, unused, out, gproj, packed = (out, gproj, *rest)
    core = info[2]

    @first_step
    def _():
        perm[...] = reorder()
        gproj[...] = before[...] if part else jnp.zeros_like(gproj)
        beyond = slice(2 * LANES, 4 * LANES)
        for owner, mine, yp, xp in ((core, own, ypart, xpart), (1 - core, near, ycpart, xcpart)):
            for group, lefts, rights in ((0, yp, xp), (1, xp, yp)):
                for at in CHUNKS:
                    channel = owner * (2 * GROUP) + group * GROUP + at
                    fill_sum(
                        perm[...], left_st, channel, (mine, group, at, BOTH), (lefts, group, at, BOTH)
                    )
                    fill_sum(
                        perm[...],
                        right_st,
                        channel,
                        (mine, group, at, beyond),
                        (rights, group, at, BOTH),
                    )

    def work(here, rows):
        mixtures, normeds = [], []
        for spot, row, half, lanes, among in places_of(here, rows):
            normeds.append(
                (normalise(turned(pair, spot, lanes))[0] * norm1[...]).astype(BF16)
            )
            mixtures.append(
                mixture_chunk(left_st, right_st, factors, gate_in, spot, row, half, lanes)
            )
        mixture = side_by_side(mixtures)
        gproj[...] += dot_nt(mixture, side_by_side(normeds))
        grad_normed = dot_nn(proj1_w[...], mixture)
        for spot, row, half, lanes, among in places_of(here, rows):
            hat, spread = normalise(turned(pair, spot, lanes))
            grad = normalise_back(grad_normed[:, among] * norm1[...], hat, spread)
            out[spot, lanes, :] = (grad_in[spot, :, lanes] + grad).T

    each_rows(work)

    if part:

        @last_step
        def _():
            size = gproj.shape[0]
            packed[:size, :] = gproj[...].astype(BF16)
            packed[size:, :] = early[...].astype(BF16)


CHANNELS = 8
PARTS = 2


def paired(refs):
    return [refs[n : n + PARTS] for n in range(0, len(refs), PARTS)]


def place(one, two, part):
    return pl.multiple_of((one * 2 + two) * (PARTS * BLOCK) + part * BLOCK, BLOCK)


def places(info, group):
    at, core = info[group], info[2]
    return [
        place(at if n < 2 else 1 - at, core if n % 2 == 0 else 1 - core, part)
        for n in range(4)
        for part in range(PARTS)
    ]


def take(ref, group, h):
    return ref[group, h] if len(ref.shape) == 4 else ref[h]


def joined(quads, group, h):
    return jnp.concatenate([take(ref, group, h) for refs in quads for ref in refs], axis=0)


def gather(stage, slot, wheres, quads, group, h):
    for where, ref in zip(wheres, [ref for refs in quads for ref in refs]):
        stage[slot, pl.ds(where, BLOCK), :] = take(ref, group, h)
    return stage[slot]


def give(refs, group, h, lanes, value):
    if len(refs.shape) == 4:
        refs[group, h, :, lanes] = value
    else:
        refs[h, :, lanes] = value


def scatter(quads, group, h, lanes, value):
    for n, ref in enumerate([ref for refs in quads for ref in refs]):
        give(ref, group, h, lanes, value[n * BLOCK : (n + 1) * BLOCK])


def scatter_from(stage, slot, wheres, quads, group, h, lanes):
    for where, ref in zip(wheres, [ref for refs in quads for ref in refs]):
        give(ref, group, h, lanes, stage[slot, pl.ds(where, BLOCK), :])


def outgoing_kernel(info, *refs):
    *refs, stage = refs
    *refs, o_own, o_near, o_y, o_yc, o_x, o_xc = refs
    a_own, b_own, a_y, b_x, a_yc, b_xc, near = paired(refs)
    a_near, b_near = [ref.at[:2] for ref in near], [ref.at[2:] for ref in near]
    along_a, along_b = (a_own, a_near, a_y, a_yc), (b_own, b_near, b_x, b_xc)
    for h in range(CHANNELS):
        for group in range(2):
            lefts, rights = (along_a, along_b) if group == 0 else (along_b, along_a)
            far = (o_y, o_yc) if group == 0 else (o_x, o_xc)
            right = gather(stage, 2 * h + group, places(info, group), rights, group, h)
            inner = dot_nt(joined(lefts, group, h), right).astype(BF16)
            for n, out in enumerate((o_own, o_near) + far):
                rows = PARTS * BLOCK
                give(out, group, h, slice(0, LANES), inner[n * rows : (n + 1) * rows])


def halves(quads, group, h):
    both = joined(quads, group, h)
    return both[:, :LANES], both[:, LANES:]


def incoming_kernel(info, *refs):
    *refs, stage = refs
    own, ypart, xpart, ycpart, xcpart, near, o_own, o_near, o_x, o_xc, o_y, o_yc = paired(refs)
    for h in range(CHANNELS):
        for group in range(2):
            far = (ypart, ycpart) if group == 0 else (xpart, xcpart)
            outs = (o_own, o_near) + ((o_x, o_xc) if group == 0 else (o_y, o_yc))
            slot = 2 * h + group
            left, right = halves((own, near) + far, group, h)
            stage[slot] = dot_tn(left, right).astype(BF16)
            scatter_from(stage, slot, places(info, group), outs, group, h, slice(0, 2 * LANES))


def incoming_back_kernel(info, *refs):
    *refs, stage = refs
    own, ypart, xpart, ycpart, xcpart, near, *more = paired(refs)
    same0, same1, g_y, g_x, g_yc, g_xc, g_near, *more = more
    o_own, o_near, o_y, o_yc, o_x, o_xc = more
    for h in range(CHANNELS):
        for group in range(2):
            far = (ypart, ycpart) if group == 0 else (xpart, xcpart)
            grads = (same0, g_near, g_x, g_xc) if group == 0 else (same1, g_near, g_y, g_yc)
            outs = (o_own, o_near) + ((o_y, o_yc) if group == 0 else (o_x, o_xc))
            grad = gather(stage, 2 * h + group, places(info, group), grads, group, h)
            left, right = halves((own, near) + far, group, h)
            scatter(outs, group, h, slice(0, LANES), dot_nt(right, grad).astype(BF16))
            scatter(outs, group, h, slice(LANES, 3 * LANES), dot_nn(left, grad).astype(BF16))


def outgoing_back_kernel(info, *refs):
    *refs, stage, back = refs
    a_own, b_own, a_y, b_x, a_yc, b_xc, near, *more = paired(refs)
    a_near, b_near = [ref.at[:2] for ref in near], [ref.at[2:] for ref in near]
    g_own, g_y, g_x, g_yc, g_xc, g_near, o_own, o_near, o_y, o_yc, o_x, o_xc = more
    along_a, along_b = (a_own, a_near, a_y, a_yc), (b_own, b_near, b_x, b_xc)
    first, second = slice(0, 2 * LANES), slice(2 * LANES, 4 * LANES)
    for h in range(CHANNELS):
        for group in range(2):
            lefts, rights = (along_a, along_b) if group == 0 else (along_b, along_a)
            far = (g_y, g_yc) if group == 0 else (g_x, g_xc)
            left_far, right_far = ((o_y, o_yc), (o_x, o_xc)) if group == 0 else ((o_x, o_xc), (o_y, o_yc))
            slot = 2 * h + group
            wheres = places(info, group)
            right = gather(stage, slot, wheres, rights, group, h)
            grad = joined((g_own, g_near) + far, group, h)
            grad_left = dot_nn(grad, right).astype(BF16)
            back[slot] = dot_tn(grad, joined(lefts, group, h)).astype(BF16)
            core_rows = 2 * PARTS * BLOCK
            scatter((o_own, o_near), group, h, first, grad_left[:core_rows])
            scatter(left_far, group, h, first, grad_left[core_rows:])
            scatter_from(back, slot, wheres[: 2 * PARTS], (o_own, o_near), group, h, second)
            scatter_from(back, slot, wheres[2 * PARTS :], right_far, group, h, first)


def whole(shape):
    return pl.BlockSpec(shape, lambda step, info: (0,) * len(shape))


def rows_of(part, some=SOME):
    def make(shape):
        first = part * (BLOCK // some)
        return pl.BlockSpec(
            (some,) + shape[1:], lambda step, info: (first + step,) + (0,) * (len(shape) - 1)
        )

    make.kept = True
    return make


def rows_block(part):
    def make(shape):
        return pl.BlockSpec(
            shape[:-2] + (BLOCK, shape[-1]),
            lambda step, info: (0,) * (len(shape) - 2) + (part, 0),
        )

    return make


def anywhere(shape):
    return pl.BlockSpec(memory_space=pl.ANY)


def channel_rows(shape):
    if len(shape) == 4:
        return pl.BlockSpec((shape[0], CHANNELS) + shape[2:], lambda step, info: (0, step, 0, 0))
    return pl.BlockSpec((CHANNELS,) + shape[1:], lambda step, info: (step, 0, 0))


def in_place(array):
    return pltpu.with_memory_space_constraint(array, pltpu.HBM)


def call(kernel, info, steps, ins, outs, scratch, aliases={}, vmem=CELL_VMEM):
    return pl.pallas_call(
        kernel,
        grid_spec=pltpu.PrefetchScalarGridSpec(
            num_scalar_prefetch=1,
            grid=(steps,),
            in_specs=[make(array.shape) for array, make in ins],
            out_specs=[make(shape) for shape, unused, make in outs],
            scratch_shapes=scratch,
        ),
        out_shape=[
            (pltpu.HBM if getattr(make, "kept", False) else jax.ShapeDtypeStruct)(shape, dtype)
            for shape, dtype, make in outs
        ],
        compiler_params=pltpu.CompilerParams(vmem_limit_bytes=vmem),
        input_output_aliases=aliases,
    )(info, *[in_place(array) if getattr(make, "kept", False) else array for array, make in ins])


class Links:
    def __init__(self):
        self.last = {}

    def send(self, array, offset, first=None, core_first=False):
        count = lax.axis_size("axial")
        if first is not None:
            array, unused = lax.optimization_barrier((array, first))
        keys = (offset, CORE) if core_first else (offset,)
        after = [self.last[key] for key in keys if key in self.last]
        if after and offset in (X, Y):
            array, *unused = lax.optimization_barrier((array, *after))
        self.last[offset] = lax.ppermute(
            array, "axial", [(n, n ^ offset) for n in range(count)]
        )
        return self.last[offset]

    def __call__(self, *sends, between=None, core_first=False):
        results = [[] for unused in sends]
        for part in range(len(sends[0][0])):
            for result, (arrays, offset) in zip(results, sends):
                first = between if part else None
                result.append(self.send(arrays[part], offset, first, core_first))
        return results


CORE, X, Y = 1, 2, 4


def add_up(share):
    count = lax.axis_size("axial")
    rows, width = share.shape
    shares = share.reshape(count, rows // count, width)
    parts = lax.all_to_all(shares, "axial", split_axis=0, concat_axis=0, tiled=True)
    mine = parts.astype(F32).sum(axis=0).astype(BF16)
    depth = lax.axis_size("dp")
    terms = [mine] + [
        lax.ppermute(mine, "dp", [(n, n ^ offset) for n in range(depth)])
        for offset in range(1, depth)
    ]
    terms = [term.astype(F32) for term in terms]
    while len(terms) > 1:
        terms = [terms[n] + terms[n + 1] for n in range(0, len(terms), 2)]
    copies = jnp.broadcast_to(terms[0].astype(BF16)[None], shares.shape)
    return lax.all_to_all(copies, "axial", split_axis=0, concat_axis=0, tiled=True).reshape(
        rows, width
    )


def gain_grad(weight_grad, weight, gain_row):
    return jnp.sum((weight.astype(F32) * weight_grad).T, axis=0, keepdims=True) / gain_row


def finish_kernel(
    scale, info, sums, proj1, final1, proj2, final2, norm1, gain1, norm2, gain2,
    o_norm1, o_proj1, o_gain1, o_final1, o_norm2, o_proj2, o_gain2, o_final2,
):
    width, channels = proj1.shape[1], final1.shape[1]
    takes = (
        (0, True, proj1, norm1, o_proj1, o_norm1),
        (width, True, proj2, norm2, o_proj2, o_norm2),
        (2 * width, False, final2, gain2, o_final2, o_gain2),
        (2 * width + channels, False, final1, gain1, o_final1, o_gain1),
    )
    for start, flipped, weight, gain, out, gain_out in takes:
        total = sums[start : start + weight.shape[1], :].astype(F32) * scale
        total = total.T if flipped else total
        out[...] = total
        gain_out[...] = gain_grad(total, weight[...].astype(BF16), gain[...])


def fast_body(
    pair,
    cotangent,
    lengths,
    outgo_norm,
    outgo_proj,
    outgo_gain,
    outgo_final,
    incom_norm,
    incom_proj,
    incom_gain,
    incom_final,
):
    rows, tokens, channels = pair.shape[1:]
    hidden = outgo_gain.shape[0]
    index = lax.axis_index("axial")
    info = jnp.stack(
        [(index // 2) % 2, index // 4, index % 2, index * rows, lengths[0]]
    ).astype(jnp.int32)
    hop = Links()
    pair = pair[0]
    cot = cotangent[0]
    parts = range(PARTS)
    turns = GROUP // CHANNELS
    stage = pltpu.VMEM((2, BLOCK, hidden, LANES), F32)
    out_stage = pltpu.VMEM((2, BLOCK, hidden, LANES), BF16)
    perm = pltpu.VMEM((BLOCK * BLOCK, BLOCK * BLOCK), BF16)
    streamed = rows_of(0)
    square = pltpu.VMEM((2 * CHANNELS, 4 * rows, tokens), BF16)

    def two(width, height=BLOCK, make=whole, groups=2):
        return ((groups, GROUP, height, width), BF16, make)

    def one(width, height=BLOCK, make=whole):
        return ((GROUP, height, width), BF16, make)

    turned_block = ((BLOCK, channels, tokens), BF16, streamed)
    factor_block = ((BLOCK, 4 * hidden, tokens), BF16, streamed)
    mixture_block = ((BLOCK, 5 * hidden, tokens), BF16, streamed)

    def cells(kernel, ins, outs, scratch, more=lambda part: []):
        results = []
        for part in parts:
            carried = ins(part, results)
            results.append(
                call(functools.partial(kernel, part), info, STEPS, carried, outs + more(part), scratch)
            )
        shared = results[-1][len(outs) :]
        return [list(each) for each in zip(*results)] + list(shared)

    def wholes(arrays):
        return [(array, whole) for array in arrays]

    def triangle(kernel, operands, outs, scratch, split=PARTS):
        ins = [(array, channel_rows) for arrays in operands for array in arrays]
        each = [out for out in outs for unused in range(split)]
        results = call(kernel, info, turns, ins, each, scratch, vmem=TRIANGLE_VMEM)
        return [list(results[n : n + split]) for n in range(0, len(results), split)]

    raw = (outgo_gain[None], outgo_final, incom_norm[None], incom_proj, incom_gain[None], incom_final)
    gain_wide = ((channels, LANES), F32, whole)
    proj_turned = ((5 * hidden, channels), BF16, whole)
    proj_plain = ((channels, 5 * hidden), BF16, whole)
    final_plain = ((hidden, channels), BF16, whole)
    (
        a_same, a_other, b_same, b_other, to_core, gate_one, factors_one,
        norm1, gain1, norm2, gain2, proj2_t, final1_t, final2_t,
        proj1, final1, proj2, final2,
    ) = cells(
        entry_kernel,
        lambda part, unused: [(pair, rows_of(part)), (outgo_norm[None], whole), (outgo_proj, whole)]
        + (wholes(raw) if part else []),
        [two(tokens)] * 4 + [two(tokens, groups=4), turned_block, factor_block],
        [
            out_stage,
            out_stage,
            pltpu.VMEM((channels, LANES), F32),
            pltpu.VMEM((5 * hidden, channels), BF16),
            perm,
        ],
        lambda part: (
            [gain_wide] * 4
            + [proj_turned]
            + [final_plain] * 2
            + [proj_plain, final_plain] * 2
            if part
            else []
        ),
    )
    held_one = [a_same, b_same] + hop(
        (a_same, Y),
        (b_same, X),
        (a_other, Y | CORE),
        (b_other, X | CORE),
        (to_core, CORE),
    )
    own, near, to_y, to_yc, to_x, to_xc = triangle(
        outgoing_kernel,
        held_one,
        [two(LANES, rows, channel_rows)] * 2 + [one(LANES, rows, channel_rows)] * 4,
        [square],
        split=1,
    )
    back_one = [
        own,
        *hop(
            (to_y, Y), (to_x, X), (to_yc, Y | CORE), (to_xc, X | CORE), (near, CORE)
        ),
    ]

    (
        middle, inner_one, gate_two, factors_two, slopes_one,
        own, near, to_y, to_yc, to_x, to_xc,
    ) = cells(
        middle_kernel,
        lambda part, unused: [(pair, rows_of(part))]
        + [(array, rows_block(part)) for array, in back_one]
        + [(gate_one[part], streamed)]
        + wholes((gain1, final1_t, norm2, proj2_t)),
        [turned_block] * 3
        + [factor_block, turned_block]
        + [two(3 * LANES)] * 2 + [one(3 * LANES)] * 4,
        [stage, out_stage, out_stage, perm],
    )
    held_two = [own] + hop(
        (to_y, Y), (to_x, X), (to_yc, Y | CORE), (to_xc, X | CORE), (near, CORE), core_first=True
    )
    own, near, to_x, to_xc, to_y, to_yc = triangle(
        incoming_kernel,
        held_two,
        [two(tokens, make=channel_rows)] * 2 + [one(tokens, make=channel_rows)] * 4,
        [square],
    )
    back_two = [
        own,
        *hop(
            (to_y, Y), (to_x, X), (to_yc, Y | CORE), (to_xc, X | CORE), (near, CORE)
        ),
    ]

    gate_grad_two, finals_two, products_two, same0, same1, other0, other1, to_core = cells(
        turn_kernel,
        lambda part, done: [(gate_two[part], streamed), (cot, rows_of(part))]
        + wholes(arrays[part] for arrays in back_two)
        + wholes((gain2, final2_t, final2)),
        [turned_block] * 3 + [one(tokens)] * 4 + [two(tokens)],
        [stage, out_stage, perm],
    )
    grads_two = [
        same0,
        same1,
        *hop(
            (same1, Y), (same0, X), (other1, Y | CORE), (other0, X | CORE), (to_core, CORE)
        ),
    ]
    own, near, to_y, to_yc, to_x, to_xc = triangle(
        incoming_back_kernel,
        held_two + grads_two,
        [two(3 * LANES, make=channel_rows)] * 2 + [one(3 * LANES, make=channel_rows)] * 4,
        [square],
    )
    rows_two = [
        own,
        *hop(
            (to_y, Y), (to_x, X), (to_yc, Y | CORE), (to_xc, X | CORE), (near, CORE)
        ),
    ]

    (
        grad_middle, gate_grad_one, mixtures_two, products_one,
        own, near, to_y, to_yc, to_x, to_xc,
    ) = cells(
        inward_kernel,
        lambda part, done: [
            (middle[part], streamed),
            (gate_one[part], streamed),
            (cot, rows_of(part)),
            (inner_one[part], streamed),
            (gate_grad_two[part], streamed),
            (factors_two[part], streamed),
            (slopes_one[part], streamed),
        ]
        + wholes(arrays[part] for arrays in rows_two)
        + wholes((norm2, proj2, gain1, final1)),
        [((BLOCK, channels, tokens), F32, streamed), turned_block, mixture_block, turned_block]
        + [two(LANES)] * 2
        + [one(LANES)] * 4,
        [stage, stage, out_stage, perm],
    )
    grads_one = [
        own,
        *hop(
            (to_y, Y), (to_x, X), (to_yc, Y | CORE), (to_xc, X | CORE), (near, CORE)
        ),
    ]
    own, near, to_y, to_yc, to_x, to_xc = triangle(
        outgoing_back_kernel,
        held_one + grads_one,
        [two(2 * tokens, make=channel_rows)] * 2 + [two(tokens, make=channel_rows)] * 4,
        [square, square],
    )
    kept = (mixtures_two, middle, finals_two, products_two, inner_one, products_one)
    (early,) = call(
        weight_kernel,
        info,
        4,
        [
            (array, rows_of(0, BLOCK // 4))
            for arrays in kept
            for array in arrays
        ]
        + wholes((norm2, gain1)),
        [((5 * hidden + 2 * channels, channels), F32, whole)],
        [],
    )
    rows_one = [own] + hop(
        (to_y, Y), (to_x, X), (to_yc, Y | CORE), (to_xc, X | CORE), (near, CORE), between=early
    )
    exit_ins = 10 + 3 + 1 + 1
    result = None
    for part in parts:
        result = call(
            functools.partial(exit_kernel, part),
            info,
            STEPS,
            [
                (pair, rows_of(part)),
                (grad_middle[part], streamed),
                (gate_grad_one[part], streamed),
                (factors_one[part], streamed),
            ]
            + wholes(arrays[part] for arrays in rows_one)
            + wholes((norm1, proj1, early))
            + ([(result[1], whole), (result[0], anywhere)] if part else []),
            [
                ((rows, tokens, channels), F32, rows_of(part)),
                ((5 * hidden, channels), F32, whole),
            ]
            + ([((10 * hidden + 2 * channels, channels), BF16, whole)] if part else []),
            [stage, stage, perm],
            {exit_ins: 0} if part else {},
        )
    grad_begin, unused, packed = result
    sums = add_up(packed)
    scale = 1.0 / math.sqrt(lax.axis_size("dp") * tokens * tokens)
    weights = (outgo_proj, outgo_final, incom_proj, incom_final)
    gains = (outgo_norm, outgo_gain, incom_norm, incom_gain)
    order = (outgo_norm[None], outgo_proj, outgo_gain[None], outgo_final)
    order += (incom_norm[None], incom_proj, incom_gain[None], incom_final)
    totals = call(
        functools.partial(finish_kernel, scale),
        info,
        1,
        wholes((sums,) + weights + tuple(gain[None] for gain in gains)),
        [(array.shape, F32, whole) for array in order],
        [],
    )
    return (grad_begin[None],) + tuple(
        total.reshape(-1) if total.shape[0] == 1 else total for total in totals
    )


def solution(mesh):
    def body(pair, *rest):
        rows, tokens, channels = pair.shape[1:]
        hidden = rest[3].shape[0]
        plane = mesh.shape["axial"] == 8 and rows == 32 and tokens == 2 * LANES
        if plane and channels == LANES and hidden == 4 * GROUP:
            return fast_body(pair, *rest)
        return plain_body(pair, *rest)

    return jax.shard_map(
        body,
        mesh=mesh,
        in_specs=(P("dp", "axial", None, None), P("dp", "axial", None, None), P("dp")) + (P(),) * 8,
        out_specs=(P("dp", "axial", None, None),) + (P(),) * 8,
        check_vma=False,
    )
```

```python
import functools
import math

import jax
import jax.numpy as jnp
from jax import lax
from jax.experimental import pallas as pl
from jax.experimental.pallas import tpu as pltpu
from jax.sharding import PartitionSpec as P

EPSILON = 1e-05


def rounded(inputs):
    return lax.optimization_barrier(inputs.astype(jnp.bfloat16)).astype(jnp.float32)


def layer_norm(inputs, factor):
    average = jnp.mean(inputs, axis=-1, keepdims=True)
    centered = inputs - average
    spread = jnp.mean(centered * centered, axis=-1, keepdims=True)
    return centered * lax.rsqrt(spread + EPSILON) * factor


def gating(mixture, pair_mask, hidden):
    left_part = (
        mixture[:, :hidden] * jax.nn.sigmoid(mixture[:, 2 * hidden : 3 * hidden]) * pair_mask
    )
    right_part = (
        mixture[:, hidden : 2 * hidden]
        * jax.nn.sigmoid(mixture[:, 3 * hidden : 4 * hidden])
        * pair_mask
    )
    gate_part = jax.nn.sigmoid(mixture[:, 4 * hidden :])
    return (left_part, right_part, gate_part)


def entry(flat_pair, norm_gain, projection, pair_mask, hidden):
    normed = layer_norm(flat_pair, norm_gain).astype(jnp.bfloat16)
    mixture = jnp.dot(normed, projection.astype(jnp.bfloat16), preferred_element_type=jnp.float32)
    left_part, right_part, gate_part = gating(mixture, pair_mask, hidden)
    return (normed, mixture, left_part, right_part, gate_part)


def entry_back(
    flat_pair,
    norm_gain,
    projection,
    pair_mask,
    hidden,
    normed,
    mixture,
    grad_left,
    grad_right,
    grad_gate,
):
    unused, pull_gate = jax.vjp(lambda inner_mix: gating(inner_mix, pair_mask, hidden), mixture)
    grad_mixture = pull_gate((grad_left, grad_right, grad_gate))[0].astype(jnp.bfloat16)
    grad_projection = jnp.dot(normed.T, grad_mixture, preferred_element_type=jnp.float32)
    grad_normed = jnp.dot(
        grad_mixture, projection.astype(jnp.bfloat16).T, preferred_element_type=jnp.float32
    )
    unused, pull_norm = jax.vjp(layer_norm, flat_pair, norm_gain)
    grad_flat, grad_gain = pull_norm(grad_normed)
    return (grad_flat, grad_gain, grad_projection)


def leave(inner_sum, gate_part, out_gain, final_weight):
    final_normed = layer_norm(inner_sum, out_gain).astype(jnp.bfloat16)
    product = jnp.dot(
        final_normed, final_weight.astype(jnp.bfloat16), preferred_element_type=jnp.float32
    )
    return (final_normed, product, product * gate_part)


def leave_back(inner_sum, gate_part, out_gain, final_weight, final_normed, product, grad_update):
    grad_product = (grad_update * gate_part).astype(jnp.bfloat16)
    grad_gate = grad_update * product
    grad_final = jnp.dot(final_normed.T, grad_product, preferred_element_type=jnp.float32)
    grad_normed = jnp.dot(
        grad_product, final_weight.astype(jnp.bfloat16).T, preferred_element_type=jnp.float32
    )
    unused, pull_norm = jax.vjp(layer_norm, inner_sum, out_gain)
    grad_inner, grad_gain = pull_norm(grad_normed)
    return (grad_inner, grad_gate, grad_gain, grad_final)


def channel_major(field, row_count, tokens):
    hidden = field.shape[1]
    return jnp.transpose(field.reshape(row_count, tokens, hidden), (2, 0, 1))


def row_major(field):
    hidden = field.shape[0]
    return jnp.transpose(field, (1, 2, 0)).reshape(-1, hidden)


def plain_body(
    pair,
    cotangent,
    lengths,
    outgo_norm,
    outgo_proj,
    outgo_gain,
    outgo_final,
    incom_norm,
    incom_proj,
    incom_gain,
    incom_final,
):
    row_count = pair.shape[1]
    tokens = pair.shape[2]
    channels = pair.shape[3]
    hidden = outgo_gain.shape[0]
    length = lengths[0]
    first_row = lax.axis_index("axial") * row_count
    row_alive = (first_row + jnp.arange(row_count, dtype=jnp.int32) < length).astype(jnp.float32)
    column_alive = (jnp.arange(tokens, dtype=jnp.int32) < length).astype(jnp.float32)
    pair_mask = (row_alive[:, None] * column_alive[None, :]).reshape(-1, 1)
    flat_start = pair[0].reshape(-1, channels).astype(jnp.float32)
    normed_one, mixture_one, left_one, right_one, gate_one = entry(
        flat_start, outgo_norm, outgo_proj, pair_mask, hidden
    )
    left_first = channel_major(left_one.astype(jnp.bfloat16), row_count, tokens)
    right_first = channel_major(right_one.astype(jnp.bfloat16), row_count, tokens)
    left_owned, right_owned = (
        lax.all_to_all(left_first, "axial", split_axis=0, concat_axis=1, tiled=True),
        lax.all_to_all(right_first, "axial", split_axis=0, concat_axis=1, tiled=True),
    )
    inner_cols = jnp.einsum(
        "hik,hjk->hij", left_owned, right_owned, preferred_element_type=jnp.float32
    )
    inner_one = row_major(
        lax.all_to_all(
            inner_cols.astype(jnp.bfloat16), "axial", split_axis=1, concat_axis=0, tiled=True
        ).astype(inner_cols.dtype)
    )
    final_one, product_one, update_one = leave(inner_one, gate_one, outgo_gain, outgo_final)
    flat_middle = rounded(flat_start + update_one)
    normed_two, mixture_two, left_two, right_two, gate_two = entry(
        flat_middle, incom_norm, incom_proj, pair_mask, hidden
    )
    left_second = channel_major(left_two.astype(jnp.bfloat16), row_count, tokens)
    right_second = channel_major(right_two.astype(jnp.bfloat16), row_count, tokens)
    left_held, right_held = (
        lax.all_to_all(left_second, "axial", split_axis=0, concat_axis=1, tiled=True),
        lax.all_to_all(right_second, "axial", split_axis=0, concat_axis=1, tiled=True),
    )
    inner_held = jnp.einsum(
        "hki,hkj->hij", left_held, right_held, preferred_element_type=jnp.float32
    )
    inner_two = row_major(
        lax.all_to_all(
            inner_held.astype(jnp.bfloat16), "axial", split_axis=1, concat_axis=0, tiled=True
        ).astype(inner_held.dtype)
    )
    final_two, product_two, update_two = leave(inner_two, gate_two, incom_gain, incom_final)
    grad_end = cotangent[0].reshape(-1, channels).astype(jnp.float32)
    grad_inner_two, grad_gate_two, grad_gain_two, grad_final_two = leave_back(
        inner_two, gate_two, incom_gain, incom_final, final_two, product_two, grad_end
    )
    grad_cells_two = channel_major(grad_inner_two.astype(jnp.bfloat16), row_count, tokens)
    grad_held_two = lax.all_to_all(grad_cells_two, "axial", split_axis=0, concat_axis=1, tiled=True)
    left_back, right_back = (
        lax.all_to_all(left_second, "axial", split_axis=0, concat_axis=1, tiled=True),
        lax.all_to_all(right_second, "axial", split_axis=0, concat_axis=1, tiled=True),
    )
    grad_left_held = jnp.einsum(
        "hij,hkj->hki", grad_held_two, right_back, preferred_element_type=jnp.float32
    )
    grad_right_held = jnp.einsum(
        "hki,hij->hkj", left_back, grad_held_two, preferred_element_type=jnp.float32
    )
    grad_left_rows, grad_right_rows = (
        lax.all_to_all(
            grad_left_held.astype(jnp.bfloat16), "axial", split_axis=1, concat_axis=0, tiled=True
        ).astype(grad_left_held.dtype),
        lax.all_to_all(
            grad_right_held.astype(jnp.bfloat16), "axial", split_axis=1, concat_axis=0, tiled=True
        ).astype(grad_right_held.dtype),
    )
    grad_left_two = row_major(grad_left_rows)
    grad_right_two = row_major(grad_right_rows)
    grad_flat_two, grad_norm_two, grad_proj_two = entry_back(
        flat_middle,
        incom_norm,
        incom_proj,
        pair_mask,
        hidden,
        normed_two,
        mixture_two,
        grad_left_two,
        grad_right_two,
        grad_gate_two,
    )
    second_sums = lax.psum(
        (grad_norm_two, grad_proj_two, grad_gain_two, grad_final_two), ("dp", "axial")
    )
    grad_middle = grad_end + grad_flat_two
    grad_inner_one, grad_gate_one, grad_gain_one, grad_final_one = leave_back(
        inner_one, gate_one, outgo_gain, outgo_final, final_one, product_one, grad_middle
    )
    grad_cells_one = channel_major(grad_inner_one.astype(jnp.bfloat16), row_count, tokens)
    grad_owned_one = lax.all_to_all(
        grad_cells_one, "axial", split_axis=0, concat_axis=1, tiled=True
    )
    left_again, right_again = (
        lax.all_to_all(left_first, "axial", split_axis=0, concat_axis=1, tiled=True),
        lax.all_to_all(right_first, "axial", split_axis=0, concat_axis=1, tiled=True),
    )
    grad_left_owned = jnp.einsum(
        "hij,hjk->hik", grad_owned_one, right_again, preferred_element_type=jnp.float32
    )
    grad_right_owned = jnp.einsum(
        "hij,hik->hjk", grad_owned_one, left_again, preferred_element_type=jnp.float32
    )
    grad_left_back, grad_right_back = (
        lax.all_to_all(
            grad_left_owned.astype(jnp.bfloat16), "axial", split_axis=1, concat_axis=0, tiled=True
        ).astype(grad_left_owned.dtype),
        lax.all_to_all(
            grad_right_owned.astype(jnp.bfloat16), "axial", split_axis=1, concat_axis=0, tiled=True
        ).astype(grad_right_owned.dtype),
    )
    grad_left_one = row_major(grad_left_back)
    grad_right_one = row_major(grad_right_back)
    grad_flat_one, grad_norm_one, grad_proj_one = entry_back(
        flat_start,
        outgo_norm,
        outgo_proj,
        pair_mask,
        hidden,
        normed_one,
        mixture_one,
        grad_left_one,
        grad_right_one,
        grad_gate_one,
    )
    grad_begin = grad_middle + grad_flat_one
    first_sums = lax.psum(
        (grad_norm_one, grad_proj_one, grad_gain_one, grad_final_one), ("dp", "axial")
    )
    totals = tuple(first_sums) + tuple(second_sums)
    scale = 1.0 / math.sqrt(lax.axis_size("dp") * tokens * tokens)
    return (
        grad_begin.reshape(1, row_count, tokens, channels),
        totals[0] * scale,
        totals[1] * scale,
        totals[2] * scale,
        totals[3] * scale,
        totals[4] * scale,
        totals[5] * scale,
        totals[6] * scale,
        totals[7] * scale,
    )


BF16 = jnp.bfloat16
F32 = jnp.float32
BLOCK = 16
PAIRED = 2
STEPS = 4
SOME = BLOCK // STEPS
LANES = 128
GROUP = 32
MIB = 1024 * 1024
CELL_VMEM = 30 * MIB
TRIANGLE_VMEM = 14 * MIB


def dot_nn(a, b):
    return lax.dot_general(a, b, (((1,), (0,)), ((), ())), preferred_element_type=F32)


def dot_nt(a, b):
    return lax.dot_general(a, b, (((1,), (1,)), ((), ())), preferred_element_type=F32)


def dot_tn(a, b):
    return lax.dot_general(a, b, (((0,), (0,)), ((), ())), preferred_element_type=F32)


def normalise(v):
    centered = v - jnp.mean(v, axis=0, keepdims=True)
    spread = lax.rsqrt(jnp.mean(centered * centered, axis=0, keepdims=True) + EPSILON)
    return centered * spread, spread


def normalise_back(grad, hat, spread):
    first = jnp.mean(grad, axis=0, keepdims=True)
    second = jnp.mean(grad * hat, axis=0, keepdims=True)
    return spread * (grad - first - hat * second)


def reorder():
    size = BLOCK * BLOCK
    one = lax.broadcasted_iota(jnp.int32, (size, size), 0)
    two = lax.broadcasted_iota(jnp.int32, (size, size), 1)
    return jnp.where((one % BLOCK) * BLOCK + one // BLOCK == two, 1.0, 0.0).astype(BF16)


def chunk(ref, group, at, lanes):
    if len(ref.shape) == 4:
        block = ref[group, at : at + BLOCK, :, lanes]
    else:
        block = ref[at : at + BLOCK, :, lanes]
    return block.reshape(BLOCK * BLOCK, block.shape[2])


def put_chunk(stage, half, channel, value):
    channel = pl.multiple_of(channel, BLOCK)
    for row in range(BLOCK):
        stage[half, row, pl.ds(channel, BLOCK), :] = value[row * BLOCK : (row + 1) * BLOCK]


def get_chunk(stage, halves, channel):
    channel = pl.multiple_of(channel, BLOCK)
    return jnp.concatenate(
        [
            jnp.concatenate(
                [stage[half, row, pl.ds(channel, BLOCK), :] for row in range(BLOCK)], axis=0
            )
            for half in halves
        ],
        axis=1,
    )


def give_chunk(ref, group, at, lanes, value):
    block = value.astype(BF16).reshape(BLOCK, BLOCK, value.shape[1])
    if len(ref.shape) == 4:
        ref[group, at : at + BLOCK, :, lanes] = block
    else:
        ref[at : at + BLOCK, :, lanes] = block


LOW, HIGH, BOTH = slice(0, LANES), slice(LANES, 2 * LANES), slice(0, 2 * LANES)
CHUNKS = range(0, GROUP, BLOCK)


def half_swap(first, second):
    low = lax.broadcasted_iota(jnp.int32, first.shape, first.ndim - 1) < LANES // 2
    axis = first.ndim - 1
    return (
        jnp.where(low, first, pltpu.roll(second, LANES // 2, axis)),
        jnp.where(low, pltpu.roll(first, LANES // 2, axis), second),
    )


def pick(flag, zero, one):
    return jnp.where(flag == 0, zero, one)


def mask_chunk(info, part, row, half):
    token = lax.broadcasted_iota(jnp.int32, (1, LANES), 1) + half * LANES
    live = (info[3] + part * BLOCK + row < info[4]).astype(F32)
    return (token < info[4]).astype(F32) * live


def each_rows(work):
    step = pl.program_id(0)

    @pl.loop(0, SOME // PAIRED)
    def _(turn):
        here = [turn * PAIRED + n for n in range(PAIRED)]
        work(here, [step * SOME + row for row in here])


def first_step(work):
    pl.when(pl.program_id(0) == 0)(work)


def last_step(work):
    pl.when(pl.program_id(0) == STEPS - 1)(work)


def places_of(here, rows):
    for n, (spot, row) in enumerate(zip(here, rows)):
        for half in range(2):
            start = (2 * n + half) * LANES
            yield spot, row, half, (LOW, HIGH)[half], slice(start, start + LANES)


def turned(ref, spot, lanes):
    return ref[spot, lanes, :].astype(F32).T


def stacked(ref, rows):
    return jnp.concatenate([ref[row] for row in rows], axis=1)


def side_by_side(chunks):
    return jnp.concatenate(chunks, axis=1)


def put_gated(info, part, mixture, here, rows, left_st, right_st, gate_out, factor_out):
    size = left_st.shape[2]
    for spot, row, half, lanes, among in places_of(here, rows):
        mask = mask_chunk(info, part, row, half)
        for block, stage in enumerate((left_st, right_st)):
            gate = opened(mixture[(2 + block) * size : (3 + block) * size, among])
            opening = gate * mask
            side = mixture[block * size : (block + 1) * size, among] * opening
            stage[half, row] = side.astype(BF16)
            factor_out[spot, block * size : (block + 1) * size, lanes] = opening.astype(BF16)
            slope = (side * (1.0 - gate)).astype(BF16)
            factor_out[spot, (2 + block) * size : (3 + block) * size, lanes] = slope
        gate_out[spot, :, lanes] = opened(mixture[4 * size :, among]).astype(BF16)


def opened(gate):
    return 0.5 * jnp.tanh(gate) + 0.5


def column(row):
    return jnp.broadcast_to(row, (LANES, row.shape[1])).T


def halved_turned(weight):
    values = 2 * weight.shape[0]
    return jnp.concatenate([weight[:, :values].T, weight[:, values:].T * 0.5], axis=0).astype(BF16)


def entry_kernel(part, info, pair, norm_row, proj_w, *rest):
    if part:
        raw, rest = rest[:6], rest[6:]
        gain1, final1, norm2, proj2, gain2, final2 = raw
        prepared, rest = rest[7:18], rest[:7] + rest[18:]
    a_same, a_other, b_same, b_other, to_core, gate_out, factor_out, *rest = rest
    left_st, right_st, norm, proj_t, perm = rest
    hidden = proj_w.shape[1] // 5

    @first_step
    def _():
        norm[...] = column(norm_row[...])
        proj_t[...] = halved_turned(proj_w[...])
        perm[...] = reorder()
        if part:
            for row, out in zip((norm_row, gain1, norm2, gain2), prepared[:4]):
                out[...] = column(row[...])
            prepared[4][...] = halved_turned(proj2[...])
            for weight, out in zip((final1, final2), prepared[5:7]):
                out[...] = weight[...].T.astype(BF16)
            for weight, out in zip((proj_w, final1, proj2, final2), prepared[7:]):
                out[...] = weight[...].astype(BF16)

    def work(here, rows):
        normed = side_by_side(
            [
                (normalise(turned(pair, spot, lanes))[0] * norm[...]).astype(BF16)
                for spot, row, half, lanes, among in places_of(here, rows)
            ]
        )
        mixture = dot_nn(proj_t[...], normed)
        put_gated(info, part, mixture, here, rows, left_st, right_st, gate_out, factor_out)

    each_rows(work)

    @last_step
    def _():
        core = info[2]
        for owner, a_out, b_out in ((core, a_same, b_same), (1 - core, a_other, b_other)):
            for group in range(2):
                for at in CHUNKS:
                    channel = owner * (2 * GROUP) + group * GROUP + at
                    left = dot_nn(perm[...], get_chunk(left_st, (0, 1), channel)).astype(BF16)
                    right = dot_nn(perm[...], get_chunk(right_st, (0, 1), channel)).astype(BF16)
                    first, second = (left, right) if group == 0 else (right, left)
                    give_chunk(a_out, group, at, BOTH, first)
                    give_chunk(b_out, group, at, BOTH, second)
                    if a_out is a_other:
                        give_chunk(to_core, group, at, BOTH, first)
                        give_chunk(to_core, 2 + group, at, BOTH, second)


def fill_split(info, perm, stage, own, near, ypart, ycpart, xpart, xcpart):
    x, y, core = info[0], info[1], info[2]
    for owner, mine, yp, xp in ((core, own, ypart, xpart), (1 - core, near, ycpart, xcpart)):
        for at in CHUNKS:
            channel = owner * (2 * GROUP) + at
            both = jnp.concatenate([chunk(mine, 0, at, LOW), chunk(yp, 0, at, LOW)], axis=1)
            both = dot_nn(perm, both)
            put_chunk(stage, y, channel, both[:, LOW])
            put_chunk(stage, 1 - y, channel, both[:, HIGH])
            both = jnp.concatenate([chunk(mine, 1, at, LOW), chunk(xp, 0, at, LOW)], axis=1)
            both = dot_nn(perm, both)
            here, there = both[:, LOW], both[:, HIGH]
            first, second = half_swap(pick(x, here, there), pick(x, there, here))
            put_chunk(stage, 0, channel + GROUP, first)
            put_chunk(stage, 1, channel + GROUP, second)


def fill_sum(perm, stage, channel, first, second):
    both = (chunk(*first).astype(F32) + chunk(*second).astype(F32)).astype(BF16)
    total = dot_nn(perm, both)
    put_chunk(stage, 0, channel, total[:, LOW])
    put_chunk(stage, 1, channel, total[:, HIGH])


def split_out(info, perm, stage, owner, at):
    x, y = info[0], info[1]
    channel = owner * (2 * GROUP) + at
    both = dot_nn(perm, get_chunk(stage, (y, 1 - y), channel))
    swapped = dot_nn(perm, get_chunk(stage, (0, 1), channel + GROUP))
    first, second = half_swap(swapped[:, LOW], swapped[:, HIGH])
    return both[:, LOW], both[:, HIGH], pick(x, first, second), pick(x, second, first)


def middle_kernel(
    part, info, pair, own, ypart, xpart, ycpart, xcpart, near,
    gate1, gain1, final1_t, norm2, proj2_t,
    middle_out, inner_out, gate_out, factor_out, normed_out, final_out, slope_out, o_own, o_near, o_y, o_yc, o_x, o_xc,
    stage, left_st, right_st, perm,
):
    @first_step
    def _():
        perm[...] = reorder()
        fill_split(info, perm[...], stage, own, near, ypart, ycpart, xpart, xcpart)

    def work(here, rows):
        finals, normeds = [], []
        for spot, row, half, lanes, among in places_of(here, rows):
            inner = stage[half, row]
            final = (normalise(inner)[0] * gain1[...]).astype(BF16)
            inner_out[spot, :, lanes] = inner.astype(BF16)
            final_out[spot, :, lanes] = final
            finals.append(final)
        product = dot_nn(final1_t[...], side_by_side(finals))
        for spot, row, half, lanes, among in places_of(here, rows):
            gate = gate1[spot, :, lanes].astype(F32)
            update = product[:, among] * gate
            slope_out[spot, :, lanes] = (update * (1.0 - gate)).astype(BF16)
            middle = (turned(pair, spot, lanes) + update).astype(BF16)
            middle_out[spot, :, lanes] = middle
            normed = (normalise(middle.astype(F32))[0] * norm2[...]).astype(BF16)
            normed_out[spot, :, lanes] = normed
            normeds.append(normed)
        mixture = dot_nn(proj2_t[...], side_by_side(normeds))
        put_gated(info, part, mixture, here, rows, left_st, right_st, gate_out, factor_out)

    each_rows(work)

    @last_step
    def _():
        core = info[2]
        beyond = slice(LANES, 3 * LANES)
        for owner, main, yo, xo in ((core, o_own, o_y, o_x), (1 - core, o_near, o_yc, o_xc)):
            for at in CHUNKS:
                kept = split_out(info, perm[...], left_st, owner, at)
                give_chunk(main, 0, at, LOW, kept[0])
                give_chunk(yo, 0, at, LOW, kept[1])
                give_chunk(main, 1, at, LOW, kept[2])
                give_chunk(xo, 0, at, LOW, kept[3])
                for group, out in ((0, yo), (1, xo)):
                    channel = owner * (2 * GROUP) + group * GROUP + at
                    right = dot_nn(perm[...], get_chunk(right_st, (0, 1), channel)).astype(BF16)
                    give_chunk(main, group, at, beyond, right)
                    give_chunk(out, 0, at, beyond, right)


def turn_kernel(
    part, info, gate2, cot, own, ypart, xpart, ycpart, xcpart, near,
    gain2, final2_t, final2_w,
    gate_out, final_out, product_out, same0, same1, other0, other1, to_core, stage, out_st, perm,
):
    core = info[2]

    @first_step
    def _():
        perm[...] = reorder()
        for owner, mine, xp, yp in ((core, own, xpart, ypart), (1 - core, near, xcpart, ycpart)):
            for at in CHUNKS:
                channel = owner * (2 * GROUP) + at
                fill_sum(perm[...], stage, channel, (mine, 0, at, BOTH), (xp, 0, at, BOTH))
                fill_sum(perm[...], stage, channel + GROUP, (mine, 1, at, BOTH), (yp, 0, at, BOTH))

    def work(here, rows):
        finals, products = [], []
        for spot, row, half, lanes, among in places_of(here, rows):
            final = (normalise(stage[half, row])[0] * gain2[...]).astype(BF16)
            final_out[spot, :, lanes] = final
            finals.append(final)
            grad_product = turned(cot, spot, lanes) * gate2[spot, :, lanes].astype(F32)
            grad_product = grad_product.astype(BF16)
            product_out[spot, :, lanes] = grad_product
            products.append(grad_product)
        product = dot_nn(final2_t[...], side_by_side(finals))
        grad_final = dot_nn(final2_w[...], side_by_side(products))
        for spot, row, half, lanes, among in places_of(here, rows):
            gate = gate2[spot, :, lanes].astype(F32)
            grad_gate = turned(cot, spot, lanes) * product[:, among] * gate * (1.0 - gate)
            gate_out[spot, :, lanes] = grad_gate.astype(BF16)
            hat, spread = normalise(stage[half, row])
            grad_inner = normalise_back(grad_final[:, among] * gain2[...], hat, spread)
            out_st[half, row] = grad_inner.astype(BF16)

    each_rows(work)

    @last_step
    def _():
        for owner, outs in ((core, (same0, same1)), (1 - core, (other0, other1))):
            for group, out in enumerate(outs):
                for at in CHUNKS:
                    channel = owner * (2 * GROUP) + group * GROUP + at
                    value = dot_nn(perm[...], get_chunk(out_st, (0, 1), channel)).astype(BF16)
                    give_chunk(out, 0, at, BOTH, value)
                    if out is other0 or out is other1:
                        give_chunk(to_core, group, at, BOTH, value)


def mixture_chunk(left_st, right_st, factors, gate_in, spot, row, half, lanes):
    size = left_st.shape[2]
    grads = (left_st[half, row], right_st[half, row])
    blocks = [
        (grads[n % 2] * factors[spot, n * size : (n + 1) * size, lanes].astype(F32)).astype(BF16)
        for n in range(4)
    ]
    return jnp.concatenate(blocks + [gate_in[spot, :, lanes]], axis=0)


def inward_kernel(
    part, info, middle, gate1, cot, inner_in, gate_in, factors, slopes, own, ypart, xpart, ycpart, xcpart, near,
    norm2, proj2_w, gain1, final1_w,
    grad_out, gate_out, mixture_out, product_out, o_own, o_near, o_y, o_yc, o_x, o_xc,
    left_st, right_st, out_st, perm,
):
    core = info[2]

    @first_step
    def _():
        perm[...] = reorder()
        fill_split(info, perm[...], left_st, own, near, ypart, ycpart, xpart, xcpart)
        beyond = slice(LANES, 3 * LANES)
        for owner, mine, yp, xp in ((core, own, ypart, xpart), (1 - core, near, ycpart, xcpart)):
            for at in CHUNKS:
                channel = owner * (2 * GROUP) + at
                fill_sum(perm[...], right_st, channel, (mine, 0, at, beyond), (yp, 0, at, beyond))
                fill_sum(
                    perm[...], right_st, channel + GROUP, (mine, 1, at, beyond), (xp, 0, at, beyond)
                )

    def work(here, rows):
        mixtures, products = [], []
        for spot, row, half, lanes, among in places_of(here, rows):
            mixture = mixture_chunk(left_st, right_st, factors, gate_in, spot, row, half, lanes)
            mixture_out[spot, :, lanes] = mixture
            mixtures.append(mixture)
        grad_normed = dot_nn(proj2_w[...], side_by_side(mixtures))
        for spot, row, half, lanes, among in places_of(here, rows):
            hat, spread = normalise(middle[spot, :, lanes].astype(F32))
            grad = normalise_back(grad_normed[:, among] * norm2[...], hat, spread)
            grad = grad + turned(cot, spot, lanes)
            grad_out[spot, :, lanes] = grad.astype(BF16)
            gate_out[spot, :, lanes] = (grad * slopes[spot, :, lanes].astype(F32)).astype(BF16)
            grad_product = (grad * gate1[spot, :, lanes].astype(F32)).astype(BF16)
            product_out[spot, :, lanes] = grad_product
            products.append(grad_product)
        grad_final = dot_nn(final1_w[...], side_by_side(products))
        for spot, row, half, lanes, among in places_of(here, rows):
            hat, spread = normalise(inner_in[spot, :, lanes].astype(F32))
            grad_inner = normalise_back(grad_final[:, among] * gain1[...], hat, spread)
            out_st[half, row] = grad_inner.astype(BF16)

    each_rows(work)

    @last_step
    def _():
        for owner, main, yo, xo in ((core, o_own, o_y, o_x), (1 - core, o_near, o_yc, o_xc)):
            for at in CHUNKS:
                kept = split_out(info, perm[...], out_st, owner, at)
                give_chunk(main, 0, at, LOW, kept[0])
                give_chunk(yo, 0, at, LOW, kept[1])
                give_chunk(main, 1, at, LOW, kept[2])
                give_chunk(xo, 0, at, LOW, kept[3])


def weight_kernel(info, *refs):
    *refs, total = refs
    (mixtures, normeds, *pairs) = paired(refs)
    width, channels = mixtures[0].shape[1], normeds[0].shape[1]

    @pl.when(pl.program_id(0) == 0)
    def _():
        total[...] = jnp.zeros_like(total)

    for part in range(PARTS):
        for first in range(0, mixtures[part].shape[0], PAIRED):
            rows = [first + n for n in range(PAIRED)]
            mixture, normed = stacked(mixtures[part], rows), stacked(normeds[part], rows)
            total[:width, :] += dot_nt(mixture, normed)
            for n, (finals, products) in enumerate((pairs[:2], pairs[2:])):
                where = slice(width + n * channels, width + (n + 1) * channels)
                final, product = stacked(finals[part], rows), stacked(products[part], rows)
                total[where, :] += dot_nt(final, product)


def exit_kernel(
    part, info, pair, grad_in, gate_in, factors, own, ypart, xpart, ycpart, xcpart, near,
    norm1, proj1_w, early, *rest,
):
    out, gproj, *rest, left_st, right_st, perm = rest
    if part:
        before, unused, out, gproj, packed = (out, gproj, *rest)
    core = info[2]

    @first_step
    def _():
        perm[...] = reorder()
        gproj[...] = before[...] if part else jnp.zeros_like(gproj)
        beyond = slice(2 * LANES, 4 * LANES)
        for owner, mine, yp, xp in ((core, own, ypart, xpart), (1 - core, near, ycpart, xcpart)):
            for group, lefts, rights in ((0, yp, xp), (1, xp, yp)):
                for at in CHUNKS:
                    channel = owner * (2 * GROUP) + group * GROUP + at
                    fill_sum(
                        perm[...], left_st, channel, (mine, group, at, BOTH), (lefts, group, at, BOTH)
                    )
                    fill_sum(
                        perm[...],
                        right_st,
                        channel,
                        (mine, group, at, beyond),
                        (rights, group, at, BOTH),
                    )

    def work(here, rows):
        mixtures, normeds = [], []
        for spot, row, half, lanes, among in places_of(here, rows):
            normeds.append(
                (normalise(turned(pair, spot, lanes))[0] * norm1[...]).astype(BF16)
            )
            mixtures.append(
                mixture_chunk(left_st, right_st, factors, gate_in, spot, row, half, lanes)
            )
        mixture = side_by_side(mixtures)
        gproj[...] += dot_nt(mixture, side_by_side(normeds))
        grad_normed = dot_nn(proj1_w[...], mixture)
        for spot, row, half, lanes, among in places_of(here, rows):
            hat, spread = normalise(turned(pair, spot, lanes))
            grad = normalise_back(grad_normed[:, among] * norm1[...], hat, spread)
            out[spot, lanes, :] = (grad_in[spot, :, lanes].astype(F32) + grad).T

    each_rows(work)

    if part:

        @last_step
        def _():
            size = gproj.shape[0]
            packed[:size, :] = gproj[...].astype(BF16)
            packed[size:, :] = early[...].astype(BF16)


CHANNELS = 8
PARTS = 2


def paired(refs):
    return [refs[n : n + PARTS] for n in range(0, len(refs), PARTS)]


def place(one, two, part):
    return pl.multiple_of((one * 2 + two) * (PARTS * BLOCK) + part * BLOCK, BLOCK)


def places(info, group):
    at, core = info[group], info[2]
    return [
        place(at if n < 2 else 1 - at, core if n % 2 == 0 else 1 - core, part)
        for n in range(4)
        for part in range(PARTS)
    ]


def take(ref, group, h):
    return ref[group, h] if len(ref.shape) == 4 else ref[h]


def joined(quads, group, h):
    return jnp.concatenate([take(ref, group, h) for refs in quads for ref in refs], axis=0)


def gather(stage, slot, wheres, quads, group, h):
    for where, ref in zip(wheres, [ref for refs in quads for ref in refs]):
        stage[slot, pl.ds(where, BLOCK), :] = take(ref, group, h)
    return stage[slot]


def give(refs, group, h, lanes, value):
    if len(refs.shape) == 4:
        refs[group, h, :, lanes] = value
    else:
        refs[h, :, lanes] = value


def scatter(quads, group, h, lanes, value):
    for n, ref in enumerate([ref for refs in quads for ref in refs]):
        give(ref, group, h, lanes, value[n * BLOCK : (n + 1) * BLOCK])


def scatter_from(stage, slot, wheres, quads, group, h, lanes):
    for where, ref in zip(wheres, [ref for refs in quads for ref in refs]):
        give(ref, group, h, lanes, stage[slot, pl.ds(where, BLOCK), :])


def outgoing_kernel(info, *refs):
    *refs, stage = refs
    *refs, o_own, o_near, o_y, o_yc, o_x, o_xc = refs
    a_own, b_own, a_y, b_x, a_yc, b_xc, near = paired(refs)
    a_near, b_near = [ref.at[:2] for ref in near], [ref.at[2:] for ref in near]
    along_a, along_b = (a_own, a_near, a_y, a_yc), (b_own, b_near, b_x, b_xc)
    for h in range(CHANNELS):
        for group in range(2):
            lefts, rights = (along_a, along_b) if group == 0 else (along_b, along_a)
            far = (o_y, o_yc) if group == 0 else (o_x, o_xc)
            right = gather(stage, 2 * h + group, places(info, group), rights, group, h)
            inner = dot_nt(joined(lefts, group, h), right).astype(BF16)
            for n, out in enumerate((o_own, o_near) + far):
                rows = PARTS * BLOCK
                give(out, group, h, slice(0, LANES), inner[n * rows : (n + 1) * rows])


def halves(quads, group, h):
    both = joined(quads, group, h)
    return both[:, :LANES], both[:, LANES:]


def incoming_kernel(info, *refs):
    *refs, stage = refs
    own, ypart, xpart, ycpart, xcpart, near, o_own, o_near, o_x, o_xc, o_y, o_yc = paired(refs)
    for h in range(CHANNELS):
        for group in range(2):
            far = (ypart, ycpart) if group == 0 else (xpart, xcpart)
            outs = (o_own, o_near) + ((o_x, o_xc) if group == 0 else (o_y, o_yc))
            slot = 2 * h + group
            left, right = halves((own, near) + far, group, h)
            stage[slot] = dot_tn(left, right).astype(BF16)
            scatter_from(stage, slot, places(info, group), outs, group, h, slice(0, 2 * LANES))


def incoming_back_kernel(info, *refs):
    *refs, stage = refs
    own, ypart, xpart, ycpart, xcpart, near, *more = paired(refs)
    same0, same1, g_y, g_x, g_yc, g_xc, g_near, *more = more
    o_own, o_near, o_y, o_yc, o_x, o_xc = more
    for h in range(CHANNELS):
        for group in range(2):
            far = (ypart, ycpart) if group == 0 else (xpart, xcpart)
            grads = (same0, g_near, g_x, g_xc) if group == 0 else (same1, g_near, g_y, g_yc)
            outs = (o_own, o_near) + ((o_y, o_yc) if group == 0 else (o_x, o_xc))
            grad = gather(stage, 2 * h + group, places(info, group), grads, group, h)
            left, right = halves((own, near) + far, group, h)
            scatter(outs, group, h, slice(0, LANES), dot_nt(right, grad).astype(BF16))
            scatter(outs, group, h, slice(LANES, 3 * LANES), dot_nn(left, grad).astype(BF16))


def outgoing_back_kernel(info, *refs):
    *refs, stage, back = refs
    a_own, b_own, a_y, b_x, a_yc, b_xc, near, *more = paired(refs)
    a_near, b_near = [ref.at[:2] for ref in near], [ref.at[2:] for ref in near]
    g_own, g_y, g_x, g_yc, g_xc, g_near, o_own, o_near, o_y, o_yc, o_x, o_xc = more
    along_a, along_b = (a_own, a_near, a_y, a_yc), (b_own, b_near, b_x, b_xc)
    first, second = slice(0, 2 * LANES), slice(2 * LANES, 4 * LANES)
    for h in range(CHANNELS):
        for group in range(2):
            lefts, rights = (along_a, along_b) if group == 0 else (along_b, along_a)
            far = (g_y, g_yc) if group == 0 else (g_x, g_xc)
            left_far, right_far = ((o_y, o_yc), (o_x, o_xc)) if group == 0 else ((o_x, o_xc), (o_y, o_yc))
            slot = 2 * h + group
            wheres = places(info, group)
            right = gather(stage, slot, wheres, rights, group, h)
            grad = joined((g_own, g_near) + far, group, h)
            grad_left = dot_nn(grad, right).astype(BF16)
            back[slot] = dot_tn(grad, joined(lefts, group, h)).astype(BF16)
            core_rows = 2 * PARTS * BLOCK
            scatter((o_own, o_near), group, h, first, grad_left[:core_rows])
            scatter(left_far, group, h, first, grad_left[core_rows:])
            scatter_from(back, slot, wheres[: 2 * PARTS], (o_own, o_near), group, h, second)
            scatter_from(back, slot, wheres[2 * PARTS :], right_far, group, h, first)


def whole(shape):
    return pl.BlockSpec(shape, lambda step, info: (0,) * len(shape))


def fixed(shape):
    return whole(shape)


fixed.kept = True


def rows_of(part, some=SOME):
    def make(shape):
        first = part * (BLOCK // some)
        return pl.BlockSpec(
            (some,) + shape[1:], lambda step, info: (first + step,) + (0,) * (len(shape) - 1)
        )

    make.kept = True
    return make


def rows_block(part):
    def make(shape):
        return pl.BlockSpec(
            shape[:-2] + (BLOCK, shape[-1]),
            lambda step, info: (0,) * (len(shape) - 2) + (part, 0),
        )

    return make


def anywhere(shape):
    return pl.BlockSpec(memory_space=pl.ANY)


def channel_rows(shape):
    if len(shape) == 4:
        return pl.BlockSpec((shape[0], CHANNELS) + shape[2:], lambda step, info: (0, step, 0, 0))
    return pl.BlockSpec((CHANNELS,) + shape[1:], lambda step, info: (step, 0, 0))


def in_place(array):
    return pltpu.with_memory_space_constraint(array, pltpu.HBM)


def call(kernel, info, steps, ins, outs, scratch, aliases={}, vmem=CELL_VMEM):
    return pl.pallas_call(
        kernel,
        grid_spec=pltpu.PrefetchScalarGridSpec(
            num_scalar_prefetch=1,
            grid=(steps,),
            in_specs=[make(array.shape) for array, make in ins],
            out_specs=[make(shape) for shape, unused, make in outs],
            scratch_shapes=scratch,
        ),
        out_shape=[
            (pltpu.HBM if getattr(make, "kept", False) else jax.ShapeDtypeStruct)(shape, dtype)
            for shape, dtype, make in outs
        ],
        compiler_params=pltpu.CompilerParams(vmem_limit_bytes=vmem),
        input_output_aliases=aliases,
    )(info, *[in_place(array) if getattr(make, "kept", False) else array for array, make in ins])


class Links:
    def __init__(self):
        self.last = {}

    def send(self, array, offset, first=None, core_first=False):
        count = lax.axis_size("axial")
        if first is not None:
            array, unused = lax.optimization_barrier((array, first))
        keys = (offset, CORE) if core_first else (offset,)
        after = [self.last[key] for key in keys if key in self.last]
        if after and offset in (X, Y):
            array, *unused = lax.optimization_barrier((array, *after))
        self.last[offset] = lax.ppermute(
            array, "axial", [(n, n ^ offset) for n in range(count)]
        )
        return self.last[offset]

    def __call__(self, *sends, between=None, core_first=False):
        results = [[] for unused in sends]
        for part in range(len(sends[0][0])):
            for result, (arrays, offset) in zip(results, sends):
                first = between if part else None
                result.append(self.send(arrays[part], offset, first, core_first))
        return results


CORE, X, Y = 1, 2, 4


def add_up(share):
    count = lax.axis_size("axial")
    rows, width = share.shape
    shares = share.reshape(count, rows // count, width)
    parts = lax.all_to_all(shares, "axial", split_axis=0, concat_axis=0, tiled=True)
    mine = parts.astype(F32).sum(axis=0).astype(BF16)
    depth = lax.axis_size("dp")
    terms = [mine] + [
        lax.ppermute(mine, "dp", [(n, n ^ offset) for n in range(depth)])
        for offset in range(1, depth)
    ]
    terms = [term.astype(F32) for term in terms]
    while len(terms) > 1:
        terms = [terms[n] + terms[n + 1] for n in range(0, len(terms), 2)]
    copies = jnp.broadcast_to(terms[0].astype(BF16)[None], shares.shape)
    return lax.all_to_all(copies, "axial", split_axis=0, concat_axis=0, tiled=True).reshape(
        rows, width
    )


def gain_grad(weight_grad, weight, gain_row):
    return jnp.sum((weight.astype(F32) * weight_grad).T, axis=0, keepdims=True) / gain_row


def finish_kernel(
    scale, info, sums, proj1, final1, proj2, final2, norm1, gain1, norm2, gain2,
    o_norm1, o_proj1, o_gain1, o_final1, o_norm2, o_proj2, o_gain2, o_final2,
):
    width, channels = proj1.shape[1], final1.shape[1]
    takes = (
        (0, True, proj1, norm1, o_proj1, o_norm1),
        (width, True, proj2, norm2, o_proj2, o_norm2),
        (2 * width, False, final2, gain2, o_final2, o_gain2),
        (2 * width + channels, False, final1, gain1, o_final1, o_gain1),
    )
    for start, flipped, weight, gain, out, gain_out in takes:
        total = sums[start : start + weight.shape[1], :].astype(F32) * scale
        total = total.T if flipped else total
        out[...] = total
        gain_out[...] = gain_grad(total, weight[...].astype(BF16), gain[...])


def fast_body(
    pair,
    cotangent,
    lengths,
    outgo_norm,
    outgo_proj,
    outgo_gain,
    outgo_final,
    incom_norm,
    incom_proj,
    incom_gain,
    incom_final,
):
    rows, tokens, channels = pair.shape[1:]
    hidden = outgo_gain.shape[0]
    index = lax.axis_index("axial")
    info = jnp.stack(
        [(index // 2) % 2, index // 4, index % 2, index * rows, lengths[0]]
    ).astype(jnp.int32)
    hop = Links()
    pair = pair[0]
    cot = cotangent[0]
    parts = range(PARTS)
    turns = GROUP // CHANNELS
    stage = pltpu.VMEM((2, BLOCK, hidden, LANES), F32)
    out_stage = pltpu.VMEM((2, BLOCK, hidden, LANES), BF16)
    perm = pltpu.VMEM((BLOCK * BLOCK, BLOCK * BLOCK), BF16)
    streamed = rows_of(0)
    square = pltpu.VMEM((2 * CHANNELS, 4 * rows, tokens), BF16)

    def two(width, height=BLOCK, make=whole, groups=2):
        return ((groups, GROUP, height, width), BF16, make)

    def one(width, height=BLOCK, make=whole):
        return ((GROUP, height, width), BF16, make)

    turned_block = ((BLOCK, channels, tokens), BF16, streamed)
    factor_block = ((BLOCK, 4 * hidden, tokens), BF16, streamed)
    mixture_block = ((BLOCK, 5 * hidden, tokens), BF16, streamed)

    def cells(kernel, ins, outs, scratch, more=lambda part: []):
        results = []
        for part in parts:
            carried = ins(part, results)
            results.append(
                call(functools.partial(kernel, part), info, STEPS, carried, outs + more(part), scratch)
            )
        shared = results[-1][len(outs) :]
        return [list(each) for each in zip(*results)] + list(shared)

    def wholes(arrays):
        return [(array, whole) for array in arrays]

    def triangle(kernel, operands, outs, scratch, split=PARTS):
        ins = [(array, channel_rows) for arrays in operands for array in arrays]
        each = [out for out in outs for unused in range(split)]
        results = call(kernel, info, turns, ins, each, scratch, vmem=TRIANGLE_VMEM)
        return [list(results[n : n + split]) for n in range(0, len(results), split)]

    raw = (outgo_gain[None], outgo_final, incom_norm[None], incom_proj, incom_gain[None], incom_final)
    gain_wide = ((channels, LANES), F32, whole)
    proj_turned = ((5 * hidden, channels), BF16, whole)
    proj_plain = ((channels, 5 * hidden), BF16, whole)
    final_plain = ((hidden, channels), BF16, whole)
    (
        a_same, a_other, b_same, b_other, to_core, gate_one, factors_one,
        norm1, gain1, norm2, gain2, proj2_t, final1_t, final2_t,
        proj1, final1, proj2, final2,
    ) = cells(
        entry_kernel,
        lambda part, unused: [(pair, rows_of(part)), (outgo_norm[None], fixed), (outgo_proj, fixed)]
        + ([(weight, fixed) for weight in raw] if part else []),
        [two(tokens)] * 4 + [two(tokens, groups=4), turned_block, factor_block],
        [
            out_stage,
            out_stage,
            pltpu.VMEM((channels, LANES), F32),
            pltpu.VMEM((5 * hidden, channels), BF16),
            perm,
        ],
        lambda part: (
            [gain_wide] * 4
            + [proj_turned]
            + [final_plain] * 2
            + [proj_plain, final_plain] * 2
            if part
            else []
        ),
    )
    held_one = [a_same, b_same] + hop(
        (a_same, Y), (b_same, X), (a_other, Y | CORE), (b_other, X | CORE), (to_core, CORE)
    )
    own, near, to_y, to_yc, to_x, to_xc = triangle(
        outgoing_kernel,
        held_one,
        [two(LANES, rows, channel_rows)] * 2 + [one(LANES, rows, channel_rows)] * 4,
        [square],
        split=1,
    )
    back_one = [
        own,
        *hop(
            (to_y, Y), (to_x, X), (to_yc, Y | CORE), (to_xc, X | CORE), (near, CORE)
        ),
    ]

    (
        middle, inner_one, gate_two, factors_two, normed_two, finals_one, slopes_one,
        own, near, to_y, to_yc, to_x, to_xc,
    ) = cells(
        middle_kernel,
        lambda part, unused: [(pair, rows_of(part))]
        + [(array, rows_block(part)) for array, in back_one]
        + [(gate_one[part], streamed)]
        + wholes((gain1, final1_t, norm2, proj2_t)),
        [turned_block] * 3
        + [factor_block]
        + [turned_block] * 3
        + [two(3 * LANES)] * 2 + [one(3 * LANES)] * 4,
        [stage, out_stage, out_stage, perm],
    )
    held_two = [own] + hop(
        (to_y, Y), (to_x, X), (to_yc, Y | CORE), (to_xc, X | CORE), (near, CORE), core_first=True
    )
    own, near, to_x, to_xc, to_y, to_yc = triangle(
        incoming_kernel,
        held_two,
        [two(tokens, make=channel_rows)] * 2 + [one(tokens, make=channel_rows)] * 4,
        [square],
    )
    back_two = [
        own,
        *hop(
            (to_y, Y), (to_x, X), (to_yc, Y | CORE), (to_xc, X | CORE), (near, CORE)
        ),
    ]

    gate_grad_two, finals_two, products_two, same0, same1, other0, other1, to_core = cells(
        turn_kernel,
        lambda part, done: [(gate_two[part], streamed), (cot, rows_of(part))]
        + wholes(arrays[part] for arrays in back_two)
        + wholes((gain2, final2_t, final2)),
        [turned_block] * 3 + [one(tokens)] * 4 + [two(tokens)],
        [stage, out_stage, perm],
    )
    grads_two = [
        same0,
        same1,
        *hop(
            (same1, Y), (same0, X), (other1, Y | CORE), (other0, X | CORE), (to_core, CORE)
        ),
    ]
    own, near, to_y, to_yc, to_x, to_xc = triangle(
        incoming_back_kernel,
        held_two + grads_two,
        [two(3 * LANES, make=channel_rows)] * 2 + [one(3 * LANES, make=channel_rows)] * 4,
        [square],
    )
    rows_two = [
        own,
        *hop(
            (to_y, Y), (to_x, X), (to_yc, Y | CORE), (to_xc, X | CORE), (near, CORE)
        ),
    ]

    (
        grad_middle, gate_grad_one, mixtures_two, products_one,
        own, near, to_y, to_yc, to_x, to_xc,
    ) = cells(
        inward_kernel,
        lambda part, done: [
            (middle[part], streamed),
            (gate_one[part], streamed),
            (cot, rows_of(part)),
            (inner_one[part], streamed),
            (gate_grad_two[part], streamed),
            (factors_two[part], streamed),
            (slopes_one[part], streamed),
        ]
        + wholes(arrays[part] for arrays in rows_two)
        + wholes((norm2, proj2, gain1, final1)),
        [turned_block, turned_block, mixture_block, turned_block]
        + [two(LANES)] * 2
        + [one(LANES)] * 4,
        [stage, stage, out_stage, perm],
    )
    grads_one = [
        own,
        *hop(
            (to_y, Y), (to_x, X), (to_yc, Y | CORE), (to_xc, X | CORE), (near, CORE)
        ),
    ]
    own, near, to_y, to_yc, to_x, to_xc = triangle(
        outgoing_back_kernel,
        held_one + grads_one,
        [two(2 * tokens, make=channel_rows)] * 2 + [two(tokens, make=channel_rows)] * 4,
        [square, square],
    )
    kept = (mixtures_two, normed_two, finals_two, products_two, finals_one, products_one)
    (early,) = call(
        weight_kernel,
        info,
        4,
        [
            (array, rows_of(0, BLOCK // 4))
            for arrays in kept
            for array in arrays
        ],
        [((5 * hidden + 2 * channels, channels), F32, whole)],
        [],
    )
    rows_one = [own] + hop(
        (to_y, Y), (to_x, X), (to_yc, Y | CORE), (to_xc, X | CORE), (near, CORE), between=early
    )
    exit_ins = 10 + 3 + 1 + 1
    result = None
    for part in parts:
        result = call(
            functools.partial(exit_kernel, part),
            info,
            STEPS,
            [
                (pair, rows_of(part)),
                (grad_middle[part], streamed),
                (gate_grad_one[part], streamed),
                (factors_one[part], streamed),
            ]
            + wholes(arrays[part] for arrays in rows_one)
            + wholes((norm1, proj1, early))
            + ([(result[1], whole), (result[0], anywhere)] if part else []),
            [
                ((rows, tokens, channels), F32, rows_of(part)),
                ((5 * hidden, channels), F32, whole),
            ]
            + ([((10 * hidden + 2 * channels, channels), BF16, whole)] if part else []),
            [stage, stage, perm],
            {exit_ins: 0} if part else {},
        )
    grad_begin, unused, packed = result
    sums = add_up(packed)
    scale = 1.0 / math.sqrt(lax.axis_size("dp") * tokens * tokens)
    weights = (outgo_proj, outgo_final, incom_proj, incom_final)
    gains = (outgo_norm, outgo_gain, incom_norm, incom_gain)
    order = (outgo_norm[None], outgo_proj, outgo_gain[None], outgo_final)
    order += (incom_norm[None], incom_proj, incom_gain[None], incom_final)
    totals = call(
        functools.partial(finish_kernel, scale),
        info,
        1,
        wholes((sums,) + weights + tuple(gain[None] for gain in gains)),
        [(array.shape, F32, whole) for array in order],
        [],
    )
    return (grad_begin[None],) + tuple(
        total.reshape(-1) if total.shape[0] == 1 else total for total in totals
    )


def solution(mesh):
    def body(pair, *rest):
        rows, tokens, channels = pair.shape[1:]
        hidden = rest[3].shape[0]
        plane = mesh.shape["axial"] == 8 and rows == 32 and tokens == 2 * LANES
        if plane and channels == LANES and hidden == 4 * GROUP:
            return fast_body(pair, *rest)
        return plain_body(pair, *rest)

    return jax.shard_map(
        body,
        mesh=mesh,
        in_specs=(P("dp", "axial", None, None), P("dp", "axial", None, None), P("dp")) + (P(),) * 8,
        out_specs=(P("dp", "axial", None, None),) + (P(),) * 8,
        check_vma=False,
    )
```

```python
import functools
import math

import jax
import jax.numpy as jnp
from jax import lax
from jax.experimental import pallas as pl
from jax.experimental.pallas import tpu as pltpu
from jax.sharding import PartitionSpec as P

EPSILON = 1e-05


def rounded(inputs):
    return lax.optimization_barrier(inputs.astype(jnp.bfloat16)).astype(jnp.float32)


def layer_norm(inputs, factor):
    average = jnp.mean(inputs, axis=-1, keepdims=True)
    centered = inputs - average
    spread = jnp.mean(centered * centered, axis=-1, keepdims=True)
    return centered * lax.rsqrt(spread + EPSILON) * factor


def gating(mixture, pair_mask, hidden):
    left_part = (
        mixture[:, :hidden] * jax.nn.sigmoid(mixture[:, 2 * hidden : 3 * hidden]) * pair_mask
    )
    right_part = (
        mixture[:, hidden : 2 * hidden]
        * jax.nn.sigmoid(mixture[:, 3 * hidden : 4 * hidden])
        * pair_mask
    )
    gate_part = jax.nn.sigmoid(mixture[:, 4 * hidden :])
    return (left_part, right_part, gate_part)


def entry(flat_pair, norm_gain, projection, pair_mask, hidden):
    normed = layer_norm(flat_pair, norm_gain).astype(jnp.bfloat16)
    mixture = jnp.dot(normed, projection.astype(jnp.bfloat16), preferred_element_type=jnp.float32)
    left_part, right_part, gate_part = gating(mixture, pair_mask, hidden)
    return (normed, mixture, left_part, right_part, gate_part)


def entry_back(
    flat_pair,
    norm_gain,
    projection,
    pair_mask,
    hidden,
    normed,
    mixture,
    grad_left,
    grad_right,
    grad_gate,
):
    unused, pull_gate = jax.vjp(lambda inner_mix: gating(inner_mix, pair_mask, hidden), mixture)
    grad_mixture = pull_gate((grad_left, grad_right, grad_gate))[0].astype(jnp.bfloat16)
    grad_projection = jnp.dot(normed.T, grad_mixture, preferred_element_type=jnp.float32)
    grad_normed = jnp.dot(
        grad_mixture, projection.astype(jnp.bfloat16).T, preferred_element_type=jnp.float32
    )
    unused, pull_norm = jax.vjp(layer_norm, flat_pair, norm_gain)
    grad_flat, grad_gain = pull_norm(grad_normed)
    return (grad_flat, grad_gain, grad_projection)


def leave(inner_sum, gate_part, out_gain, final_weight):
    final_normed = layer_norm(inner_sum, out_gain).astype(jnp.bfloat16)
    product = jnp.dot(
        final_normed, final_weight.astype(jnp.bfloat16), preferred_element_type=jnp.float32
    )
    return (final_normed, product, product * gate_part)


def leave_back(inner_sum, gate_part, out_gain, final_weight, final_normed, product, grad_update):
    grad_product = (grad_update * gate_part).astype(jnp.bfloat16)
    grad_gate = grad_update * product
    grad_final = jnp.dot(final_normed.T, grad_product, preferred_element_type=jnp.float32)
    grad_normed = jnp.dot(
        grad_product, final_weight.astype(jnp.bfloat16).T, preferred_element_type=jnp.float32
    )
    unused, pull_norm = jax.vjp(layer_norm, inner_sum, out_gain)
    grad_inner, grad_gain = pull_norm(grad_normed)
    return (grad_inner, grad_gate, grad_gain, grad_final)


def channel_major(field, row_count, tokens):
    hidden = field.shape[1]
    return jnp.transpose(field.reshape(row_count, tokens, hidden), (2, 0, 1))


def row_major(field):
    hidden = field.shape[0]
    return jnp.transpose(field, (1, 2, 0)).reshape(-1, hidden)


def plain_body(
    pair,
    cotangent,
    lengths,
    outgo_norm,
    outgo_proj,
    outgo_gain,
    outgo_final,
    incom_norm,
    incom_proj,
    incom_gain,
    incom_final,
):
    row_count = pair.shape[1]
    tokens = pair.shape[2]
    channels = pair.shape[3]
    hidden = outgo_gain.shape[0]
    length = lengths[0]
    first_row = lax.axis_index("axial") * row_count
    row_alive = (first_row + jnp.arange(row_count, dtype=jnp.int32) < length).astype(jnp.float32)
    column_alive = (jnp.arange(tokens, dtype=jnp.int32) < length).astype(jnp.float32)
    pair_mask = (row_alive[:, None] * column_alive[None, :]).reshape(-1, 1)
    flat_start = pair[0].reshape(-1, channels).astype(jnp.float32)
    normed_one, mixture_one, left_one, right_one, gate_one = entry(
        flat_start, outgo_norm, outgo_proj, pair_mask, hidden
    )
    left_first = channel_major(left_one.astype(jnp.bfloat16), row_count, tokens)
    right_first = channel_major(right_one.astype(jnp.bfloat16), row_count, tokens)
    left_owned, right_owned = (
        lax.all_to_all(left_first, "axial", split_axis=0, concat_axis=1, tiled=True),
        lax.all_to_all(right_first, "axial", split_axis=0, concat_axis=1, tiled=True),
    )
    inner_cols = jnp.einsum(
        "hik,hjk->hij", left_owned, right_owned, preferred_element_type=jnp.float32
    )
    inner_one = row_major(
        lax.all_to_all(
            inner_cols.astype(jnp.bfloat16), "axial", split_axis=1, concat_axis=0, tiled=True
        ).astype(inner_cols.dtype)
    )
    final_one, product_one, update_one = leave(inner_one, gate_one, outgo_gain, outgo_final)
    flat_middle = rounded(flat_start + update_one)
    normed_two, mixture_two, left_two, right_two, gate_two = entry(
        flat_middle, incom_norm, incom_proj, pair_mask, hidden
    )
    left_second = channel_major(left_two.astype(jnp.bfloat16), row_count, tokens)
    right_second = channel_major(right_two.astype(jnp.bfloat16), row_count, tokens)
    left_held, right_held = (
        lax.all_to_all(left_second, "axial", split_axis=0, concat_axis=1, tiled=True),
        lax.all_to_all(right_second, "axial", split_axis=0, concat_axis=1, tiled=True),
    )
    inner_held = jnp.einsum(
        "hki,hkj->hij", left_held, right_held, preferred_element_type=jnp.float32
    )
    inner_two = row_major(
        lax.all_to_all(
            inner_held.astype(jnp.bfloat16), "axial", split_axis=1, concat_axis=0, tiled=True
        ).astype(inner_held.dtype)
    )
    final_two, product_two, update_two = leave(inner_two, gate_two, incom_gain, incom_final)
    grad_end = cotangent[0].reshape(-1, channels).astype(jnp.float32)
    grad_inner_two, grad_gate_two, grad_gain_two, grad_final_two = leave_back(
        inner_two, gate_two, incom_gain, incom_final, final_two, product_two, grad_end
    )
    grad_cells_two = channel_major(grad_inner_two.astype(jnp.bfloat16), row_count, tokens)
    grad_held_two = lax.all_to_all(grad_cells_two, "axial", split_axis=0, concat_axis=1, tiled=True)
    left_back, right_back = (
        lax.all_to_all(left_second, "axial", split_axis=0, concat_axis=1, tiled=True),
        lax.all_to_all(right_second, "axial", split_axis=0, concat_axis=1, tiled=True),
    )
    grad_left_held = jnp.einsum(
        "hij,hkj->hki", grad_held_two, right_back, preferred_element_type=jnp.float32
    )
    grad_right_held = jnp.einsum(
        "hki,hij->hkj", left_back, grad_held_two, preferred_element_type=jnp.float32
    )
    grad_left_rows, grad_right_rows = (
        lax.all_to_all(
            grad_left_held.astype(jnp.bfloat16), "axial", split_axis=1, concat_axis=0, tiled=True
        ).astype(grad_left_held.dtype),
        lax.all_to_all(
            grad_right_held.astype(jnp.bfloat16), "axial", split_axis=1, concat_axis=0, tiled=True
        ).astype(grad_right_held.dtype),
    )
    grad_left_two = row_major(grad_left_rows)
    grad_right_two = row_major(grad_right_rows)
    grad_flat_two, grad_norm_two, grad_proj_two = entry_back(
        flat_middle,
        incom_norm,
        incom_proj,
        pair_mask,
        hidden,
        normed_two,
        mixture_two,
        grad_left_two,
        grad_right_two,
        grad_gate_two,
    )
    second_sums = lax.psum(
        (grad_norm_two, grad_proj_two, grad_gain_two, grad_final_two), ("dp", "axial")
    )
    grad_middle = grad_end + grad_flat_two
    grad_inner_one, grad_gate_one, grad_gain_one, grad_final_one = leave_back(
        inner_one, gate_one, outgo_gain, outgo_final, final_one, product_one, grad_middle
    )
    grad_cells_one = channel_major(grad_inner_one.astype(jnp.bfloat16), row_count, tokens)
    grad_owned_one = lax.all_to_all(
        grad_cells_one, "axial", split_axis=0, concat_axis=1, tiled=True
    )
    left_again, right_again = (
        lax.all_to_all(left_first, "axial", split_axis=0, concat_axis=1, tiled=True),
        lax.all_to_all(right_first, "axial", split_axis=0, concat_axis=1, tiled=True),
    )
    grad_left_owned = jnp.einsum(
        "hij,hjk->hik", grad_owned_one, right_again, preferred_element_type=jnp.float32
    )
    grad_right_owned = jnp.einsum(
        "hij,hik->hjk", grad_owned_one, left_again, preferred_element_type=jnp.float32
    )
    grad_left_back, grad_right_back = (
        lax.all_to_all(
            grad_left_owned.astype(jnp.bfloat16), "axial", split_axis=1, concat_axis=0, tiled=True
        ).astype(grad_left_owned.dtype),
        lax.all_to_all(
            grad_right_owned.astype(jnp.bfloat16), "axial", split_axis=1, concat_axis=0, tiled=True
        ).astype(grad_right_owned.dtype),
    )
    grad_left_one = row_major(grad_left_back)
    grad_right_one = row_major(grad_right_back)
    grad_flat_one, grad_norm_one, grad_proj_one = entry_back(
        flat_start,
        outgo_norm,
        outgo_proj,
        pair_mask,
        hidden,
        normed_one,
        mixture_one,
        grad_left_one,
        grad_right_one,
        grad_gate_one,
    )
    grad_begin = grad_middle + grad_flat_one
    first_sums = lax.psum(
        (grad_norm_one, grad_proj_one, grad_gain_one, grad_final_one), ("dp", "axial")
    )
    totals = tuple(first_sums) + tuple(second_sums)
    scale = 1.0 / math.sqrt(lax.axis_size("dp") * tokens * tokens)
    return (
        grad_begin.reshape(1, row_count, tokens, channels),
        totals[0] * scale,
        totals[1] * scale,
        totals[2] * scale,
        totals[3] * scale,
        totals[4] * scale,
        totals[5] * scale,
        totals[6] * scale,
        totals[7] * scale,
    )


BF16 = jnp.bfloat16
F32 = jnp.float32
BLOCK = 16
PAIRED = 4
STEPS = 4
SOME = BLOCK // STEPS
LANES = 128
GROUP = 32
MIB = 1024 * 1024
CELL_VMEM = 30 * MIB
TRIANGLE_VMEM = 14 * MIB


def dot_nn(a, b):
    return lax.dot_general(a, b, (((1,), (0,)), ((), ())), preferred_element_type=F32)


def dot_nt(a, b):
    return lax.dot_general(a, b, (((1,), (1,)), ((), ())), preferred_element_type=F32)


def dot_tn(a, b):
    return lax.dot_general(a, b, (((0,), (0,)), ((), ())), preferred_element_type=F32)


def normalise(v):
    centered = v - jnp.mean(v, axis=0, keepdims=True)
    spread = lax.rsqrt(jnp.mean(centered * centered, axis=0, keepdims=True) + EPSILON)
    return centered * spread, spread


def normalise_back(grad, hat, spread):
    first = jnp.mean(grad, axis=0, keepdims=True)
    second = jnp.mean(grad * hat, axis=0, keepdims=True)
    return spread * (grad - first - hat * second)


def reorder():
    size = BLOCK * BLOCK
    one = lax.broadcasted_iota(jnp.int32, (size, size), 0)
    two = lax.broadcasted_iota(jnp.int32, (size, size), 1)
    return jnp.where((one % BLOCK) * BLOCK + one // BLOCK == two, 1.0, 0.0).astype(BF16)


def chunk(ref, group, at, lanes):
    if len(ref.shape) == 4:
        block = ref[group, at : at + BLOCK, :, lanes]
    else:
        block = ref[at : at + BLOCK, :, lanes]
    return block.reshape(BLOCK * BLOCK, block.shape[2])


def put_chunk(stage, half, channel, value):
    channel = pl.multiple_of(channel, BLOCK)
    for row in range(BLOCK):
        stage[half, row, pl.ds(channel, BLOCK), :] = value[row * BLOCK : (row + 1) * BLOCK]


def get_chunk(stage, halves, channel):
    channel = pl.multiple_of(channel, BLOCK)
    return jnp.concatenate(
        [
            jnp.concatenate(
                [stage[half, row, pl.ds(channel, BLOCK), :] for row in range(BLOCK)], axis=0
            )
            for half in halves
        ],
        axis=1,
    )


def give_chunk(ref, group, at, lanes, value):
    block = value.astype(BF16).reshape(BLOCK, BLOCK, value.shape[1])
    if len(ref.shape) == 4:
        ref[group, at : at + BLOCK, :, lanes] = block
    else:
        ref[at : at + BLOCK, :, lanes] = block


LOW, HIGH, BOTH = slice(0, LANES), slice(LANES, 2 * LANES), slice(0, 2 * LANES)
CHUNKS = range(0, GROUP, BLOCK)


def half_swap(first, second):
    low = lax.broadcasted_iota(jnp.int32, first.shape, first.ndim - 1) < LANES // 2
    axis = first.ndim - 1
    return (
        jnp.where(low, first, pltpu.roll(second, LANES // 2, axis)),
        jnp.where(low, pltpu.roll(first, LANES // 2, axis), second),
    )


def pick(flag, zero, one):
    return jnp.where(flag == 0, zero, one)


def mask_chunk(info, part, row, half):
    token = lax.broadcasted_iota(jnp.int32, (1, LANES), 1) + half * LANES
    live = (info[3] + part * BLOCK + row < info[4]).astype(F32)
    return (token < info[4]).astype(F32) * live


def each_rows(work):
    step = pl.program_id(0)

    @pl.loop(0, SOME // PAIRED)
    def _(turn):
        here = [turn * PAIRED + n for n in range(PAIRED)]
        work(here, [step * SOME + row for row in here])


def first_step(work):
    pl.when(pl.program_id(0) == 0)(work)


def last_step(work):
    pl.when(pl.program_id(0) == STEPS - 1)(work)


def places_of(here, rows):
    for n, (spot, row) in enumerate(zip(here, rows)):
        for half in range(2):
            start = (2 * n + half) * LANES
            yield spot, row, half, (LOW, HIGH)[half], slice(start, start + LANES)


def turned(ref, spot, lanes):
    return ref[spot, lanes, :].astype(F32).T


def stacked(ref, rows):
    return jnp.concatenate([ref[row] for row in rows], axis=1)


def side_by_side(chunks):
    return jnp.concatenate(chunks, axis=1)


def put_gated(info, part, mixture, here, rows, left_st, right_st, gate_out, factor_out):
    size = left_st.shape[2]
    for spot, row, half, lanes, among in places_of(here, rows):
        mask = mask_chunk(info, part, row, half)
        for block, stage in enumerate((left_st, right_st)):
            gate = opened(mixture[(2 + block) * size : (3 + block) * size, among])
            opening = gate * mask
            side = mixture[block * size : (block + 1) * size, among] * opening
            stage[half, row] = side.astype(BF16)
            factor_out[spot, block * size : (block + 1) * size, lanes] = opening.astype(BF16)
            slope = (side * (1.0 - gate)).astype(BF16)
            factor_out[spot, (2 + block) * size : (3 + block) * size, lanes] = slope
        gate_out[spot, :, lanes] = opened(mixture[4 * size :, among]).astype(BF16)


def opened(gate):
    return 0.5 * jnp.tanh(gate) + 0.5


def column(row):
    return jnp.broadcast_to(row, (LANES, row.shape[1])).T


def halved_turned(weight):
    values = 2 * weight.shape[0]
    return jnp.concatenate([weight[:, :values].T, weight[:, values:].T * 0.5], axis=0).astype(BF16)


def entry_kernel(part, info, pair, norm_row, proj_w, *rest):
    if part:
        raw, rest = rest[:6], rest[6:]
        gain1, final1, norm2, proj2, gain2, final2 = raw
        prepared, rest = rest[7:18], rest[:7] + rest[18:]
    a_same, a_other, b_same, b_other, to_core, gate_out, factor_out, *rest = rest
    left_st, right_st, norm, proj_t, perm = rest
    hidden = proj_w.shape[1] // 5

    @first_step
    def _():
        norm[...] = column(norm_row[...])
        proj_t[...] = halved_turned(proj_w[...])
        perm[...] = reorder()
        if part:
            for row, out in zip((norm_row, gain1, norm2, gain2), prepared[:4]):
                out[...] = column(row[...])
            prepared[4][...] = halved_turned(proj2[...])
            for weight, out in zip((final1, final2), prepared[5:7]):
                out[...] = weight[...].T.astype(BF16)
            for weight, out in zip((proj_w, final1, proj2, final2), prepared[7:]):
                out[...] = weight[...].astype(BF16)

    def work(here, rows):
        normed = side_by_side(
            [
                (normalise(turned(pair, spot, lanes))[0] * norm[...]).astype(BF16)
                for spot, row, half, lanes, among in places_of(here, rows)
            ]
        )
        mixture = dot_nn(proj_t[...], normed)
        put_gated(info, part, mixture, here, rows, left_st, right_st, gate_out, factor_out)

    each_rows(work)

    @last_step
    def _():
        core = info[2]
        for owner, a_out, b_out in ((core, a_same, b_same), (1 - core, a_other, b_other)):
            for group in range(2):
                for at in CHUNKS:
                    channel = owner * (2 * GROUP) + group * GROUP + at
                    left = dot_nn(perm[...], get_chunk(left_st, (0, 1), channel)).astype(BF16)
                    right = dot_nn(perm[...], get_chunk(right_st, (0, 1), channel)).astype(BF16)
                    first, second = (left, right) if group == 0 else (right, left)
                    give_chunk(a_out, group, at, BOTH, first)
                    give_chunk(b_out, group, at, BOTH, second)
                    if a_out is a_other:
                        give_chunk(to_core, group, at, BOTH, first)
                        give_chunk(to_core, 2 + group, at, BOTH, second)


def fill_split(info, perm, stage, own, near, ypart, ycpart, xpart, xcpart):
    x, y, core = info[0], info[1], info[2]
    for owner, mine, yp, xp in ((core, own, ypart, xpart), (1 - core, near, ycpart, xcpart)):
        for at in CHUNKS:
            channel = owner * (2 * GROUP) + at
            both = jnp.concatenate([chunk(mine, 0, at, LOW), chunk(yp, 0, at, LOW)], axis=1)
            both = dot_nn(perm, both)
            put_chunk(stage, y, channel, both[:, LOW])
            put_chunk(stage, 1 - y, channel, both[:, HIGH])
            both = jnp.concatenate([chunk(mine, 1, at, LOW), chunk(xp, 0, at, LOW)], axis=1)
            both = dot_nn(perm, both)
            here, there = both[:, LOW], both[:, HIGH]
            first, second = half_swap(pick(x, here, there), pick(x, there, here))
            put_chunk(stage, 0, channel + GROUP, first)
            put_chunk(stage, 1, channel + GROUP, second)


def fill_sum(perm, stage, channel, first, second):
    both = (chunk(*first).astype(F32) + chunk(*second).astype(F32)).astype(BF16)
    total = dot_nn(perm, both)
    put_chunk(stage, 0, channel, total[:, LOW])
    put_chunk(stage, 1, channel, total[:, HIGH])


def split_out(info, perm, stage, owner, at):
    x, y = info[0], info[1]
    channel = owner * (2 * GROUP) + at
    both = dot_nn(perm, get_chunk(stage, (y, 1 - y), channel))
    swapped = dot_nn(perm, get_chunk(stage, (0, 1), channel + GROUP))
    first, second = half_swap(swapped[:, LOW], swapped[:, HIGH])
    return both[:, LOW], both[:, HIGH], pick(x, first, second), pick(x, second, first)


def middle_kernel(
    part, info, pair, own, ypart, xpart, ycpart, xcpart, near,
    gate1, gain1, final1_t, norm2, proj2_t,
    middle_out, inner_out, gate_out, factor_out, normed_out, final_out, slope_out, o_own, o_near, o_y, o_yc, o_x, o_xc,
    stage, left_st, right_st, perm,
):
    @first_step
    def _():
        perm[...] = reorder()
        fill_split(info, perm[...], stage, own, near, ypart, ycpart, xpart, xcpart)

    def work(here, rows):
        finals, normeds = [], []
        for spot, row, half, lanes, among in places_of(here, rows):
            inner = stage[half, row]
            final = (normalise(inner)[0] * gain1[...]).astype(BF16)
            inner_out[spot, :, lanes] = inner.astype(BF16)
            final_out[spot, :, lanes] = final
            finals.append(final)
        product = dot_nn(final1_t[...], side_by_side(finals))
        for spot, row, half, lanes, among in places_of(here, rows):
            gate = gate1[spot, :, lanes].astype(F32)
            update = product[:, among] * gate
            slope_out[spot, :, lanes] = (update * (1.0 - gate)).astype(BF16)
            middle = (turned(pair, spot, lanes) + update).astype(BF16)
            middle_out[spot, :, lanes] = middle
            normed = (normalise(middle.astype(F32))[0] * norm2[...]).astype(BF16)
            normed_out[spot, :, lanes] = normed
            normeds.append(normed)
        mixture = dot_nn(proj2_t[...], side_by_side(normeds))
        put_gated(info, part, mixture, here, rows, left_st, right_st, gate_out, factor_out)

    each_rows(work)

    @last_step
    def _():
        core = info[2]
        beyond = slice(LANES, 3 * LANES)
        for owner, main, yo, xo in ((core, o_own, o_y, o_x), (1 - core, o_near, o_yc, o_xc)):
            for at in CHUNKS:
                kept = split_out(info, perm[...], left_st, owner, at)
                give_chunk(main, 0, at, LOW, kept[0])
                give_chunk(yo, 0, at, LOW, kept[1])
                give_chunk(main, 1, at, LOW, kept[2])
                give_chunk(xo, 0, at, LOW, kept[3])
                for group, out in ((0, yo), (1, xo)):
                    channel = owner * (2 * GROUP) + group * GROUP + at
                    right = dot_nn(perm[...], get_chunk(right_st, (0, 1), channel)).astype(BF16)
                    give_chunk(main, group, at, beyond, right)
                    give_chunk(out, 0, at, beyond, right)


def turn_kernel(
    part, info, gate2, cot, own, ypart, xpart, ycpart, xcpart, near,
    gain2, final2_t, final2_w,
    gate_out, final_out, product_out, same0, same1, other0, other1, to_core, stage, out_st, perm,
):
    core = info[2]

    @first_step
    def _():
        perm[...] = reorder()
        for owner, mine, xp, yp in ((core, own, xpart, ypart), (1 - core, near, xcpart, ycpart)):
            for at in CHUNKS:
                channel = owner * (2 * GROUP) + at
                fill_sum(perm[...], stage, channel, (mine, 0, at, BOTH), (xp, 0, at, BOTH))
                fill_sum(perm[...], stage, channel + GROUP, (mine, 1, at, BOTH), (yp, 0, at, BOTH))

    def work(here, rows):
        finals, products = [], []
        for spot, row, half, lanes, among in places_of(here, rows):
            final = (normalise(stage[half, row])[0] * gain2[...]).astype(BF16)
            final_out[spot, :, lanes] = final
            finals.append(final)
            grad_product = turned(cot, spot, lanes) * gate2[spot, :, lanes].astype(F32)
            grad_product = grad_product.astype(BF16)
            product_out[spot, :, lanes] = grad_product
            products.append(grad_product)
        product = dot_nn(final2_t[...], side_by_side(finals))
        grad_final = dot_nn(final2_w[...], side_by_side(products))
        for spot, row, half, lanes, among in places_of(here, rows):
            gate = gate2[spot, :, lanes].astype(F32)
            grad_gate = turned(cot, spot, lanes) * product[:, among] * gate * (1.0 - gate)
            gate_out[spot, :, lanes] = grad_gate.astype(BF16)
            hat, spread = normalise(stage[half, row])
            grad_inner = normalise_back(grad_final[:, among] * gain2[...], hat, spread)
            out_st[half, row] = grad_inner.astype(BF16)

    each_rows(work)

    @last_step
    def _():
        for owner, outs in ((core, (same0, same1)), (1 - core, (other0, other1))):
            for group, out in enumerate(outs):
                for at in CHUNKS:
                    channel = owner * (2 * GROUP) + group * GROUP + at
                    value = dot_nn(perm[...], get_chunk(out_st, (0, 1), channel)).astype(BF16)
                    give_chunk(out, 0, at, BOTH, value)
                    if out is other0 or out is other1:
                        give_chunk(to_core, group, at, BOTH, value)


def mixture_chunk(left_st, right_st, factors, gate_in, spot, row, half, lanes):
    size = left_st.shape[2]
    grads = (left_st[half, row], right_st[half, row])
    blocks = [
        (grads[n % 2] * factors[spot, n * size : (n + 1) * size, lanes].astype(F32)).astype(BF16)
        for n in range(4)
    ]
    return jnp.concatenate(blocks + [gate_in[spot, :, lanes]], axis=0)


def inward_kernel(
    part, info, middle, gate1, cot, inner_in, gate_in, factors, slopes, own, ypart, xpart, ycpart, xcpart, near,
    norm2, proj2_w, gain1, final1_w,
    grad_out, gate_out, mixture_out, product_out, o_own, o_near, o_y, o_yc, o_x, o_xc,
    left_st, right_st, out_st, perm,
):
    core = info[2]

    @first_step
    def _():
        perm[...] = reorder()
        fill_split(info, perm[...], left_st, own, near, ypart, ycpart, xpart, xcpart)
        beyond = slice(LANES, 3 * LANES)
        for owner, mine, yp, xp in ((core, own, ypart, xpart), (1 - core, near, ycpart, xcpart)):
            for at in CHUNKS:
                channel = owner * (2 * GROUP) + at
                fill_sum(perm[...], right_st, channel, (mine, 0, at, beyond), (yp, 0, at, beyond))
                fill_sum(
                    perm[...], right_st, channel + GROUP, (mine, 1, at, beyond), (xp, 0, at, beyond)
                )

    def work(here, rows):
        mixtures, products = [], []
        for spot, row, half, lanes, among in places_of(here, rows):
            mixture = mixture_chunk(left_st, right_st, factors, gate_in, spot, row, half, lanes)
            mixture_out[spot, :, lanes] = mixture
            mixtures.append(mixture)
        grad_normed = dot_nn(proj2_w[...], side_by_side(mixtures))
        for spot, row, half, lanes, among in places_of(here, rows):
            hat, spread = normalise(middle[spot, :, lanes].astype(F32))
            grad = normalise_back(grad_normed[:, among] * norm2[...], hat, spread)
            grad = grad + turned(cot, spot, lanes)
            grad_out[spot, :, lanes] = grad.astype(BF16)
            gate_out[spot, :, lanes] = (grad * slopes[spot, :, lanes].astype(F32)).astype(BF16)
            grad_product = (grad * gate1[spot, :, lanes].astype(F32)).astype(BF16)
            product_out[spot, :, lanes] = grad_product
            products.append(grad_product)
        grad_final = dot_nn(final1_w[...], side_by_side(products))
        for spot, row, half, lanes, among in places_of(here, rows):
            hat, spread = normalise(inner_in[spot, :, lanes].astype(F32))
            grad_inner = normalise_back(grad_final[:, among] * gain1[...], hat, spread)
            out_st[half, row] = grad_inner.astype(BF16)

    each_rows(work)

    @last_step
    def _():
        for owner, main, yo, xo in ((core, o_own, o_y, o_x), (1 - core, o_near, o_yc, o_xc)):
            for at in CHUNKS:
                kept = split_out(info, perm[...], out_st, owner, at)
                give_chunk(main, 0, at, LOW, kept[0])
                give_chunk(yo, 0, at, LOW, kept[1])
                give_chunk(main, 1, at, LOW, kept[2])
                give_chunk(xo, 0, at, LOW, kept[3])


def weight_kernel(info, *refs):
    *refs, total = refs
    (mixtures, normeds, *pairs) = paired(refs)
    width, channels = mixtures[0].shape[1], normeds[0].shape[1]

    @pl.when(pl.program_id(0) == 0)
    def _():
        total[...] = jnp.zeros_like(total)

    for part in range(PARTS):
        for first in range(0, mixtures[part].shape[0], PAIRED):
            rows = [first + n for n in range(PAIRED)]
            mixture, normed = stacked(mixtures[part], rows), stacked(normeds[part], rows)
            total[:width, :] += dot_nt(mixture, normed)
            for n, (finals, products) in enumerate((pairs[:2], pairs[2:])):
                where = slice(width + n * channels, width + (n + 1) * channels)
                final, product = stacked(finals[part], rows), stacked(products[part], rows)
                total[where, :] += dot_nt(final, product)


def exit_kernel(
    part, info, pair, grad_in, gate_in, factors, own, ypart, xpart, ycpart, xcpart, near,
    norm1, proj1_w, early, *rest,
):
    out, gproj, *rest, left_st, right_st, perm = rest
    if part:
        before, unused, out, gproj, packed = (out, gproj, *rest)
    core = info[2]

    @first_step
    def _():
        perm[...] = reorder()
        gproj[...] = before[...] if part else jnp.zeros_like(gproj)
        beyond = slice(2 * LANES, 4 * LANES)
        for owner, mine, yp, xp in ((core, own, ypart, xpart), (1 - core, near, ycpart, xcpart)):
            for group, lefts, rights in ((0, yp, xp), (1, xp, yp)):
                for at in CHUNKS:
                    channel = owner * (2 * GROUP) + group * GROUP + at
                    fill_sum(
                        perm[...], left_st, channel, (mine, group, at, BOTH), (lefts, group, at, BOTH)
                    )
                    fill_sum(
                        perm[...],
                        right_st,
                        channel,
                        (mine, group, at, beyond),
                        (rights, group, at, BOTH),
                    )

    def work(here, rows):
        mixtures, normeds = [], []
        for spot, row, half, lanes, among in places_of(here, rows):
            normeds.append(
                (normalise(turned(pair, spot, lanes))[0] * norm1[...]).astype(BF16)
            )
            mixtures.append(
                mixture_chunk(left_st, right_st, factors, gate_in, spot, row, half, lanes)
            )
        mixture = side_by_side(mixtures)
        gproj[...] += dot_nt(mixture, side_by_side(normeds))
        grad_normed = dot_nn(proj1_w[...], mixture)
        for spot, row, half, lanes, among in places_of(here, rows):
            hat, spread = normalise(turned(pair, spot, lanes))
            grad = normalise_back(grad_normed[:, among] * norm1[...], hat, spread)
            out[spot, lanes, :] = (grad_in[spot, :, lanes].astype(F32) + grad).T

    each_rows(work)

    if part:

        @last_step
        def _():
            size = gproj.shape[0]
            packed[:size, :] = gproj[...].astype(BF16)
            packed[size:, :] = early[...].astype(BF16)


CHANNELS = 8
PARTS = 2


def paired(refs):
    return [refs[n : n + PARTS] for n in range(0, len(refs), PARTS)]


def place(one, two, part):
    return pl.multiple_of((one * 2 + two) * (PARTS * BLOCK) + part * BLOCK, BLOCK)


def places(info, group):
    at, core = info[group], info[2]
    return [
        place(at if n < 2 else 1 - at, core if n % 2 == 0 else 1 - core, part)
        for n in range(4)
        for part in range(PARTS)
    ]


def take(ref, group, h):
    return ref[group, h] if len(ref.shape) == 4 else ref[h]


def joined(quads, group, h):
    return jnp.concatenate([take(ref, group, h) for refs in quads for ref in refs], axis=0)


def gather(stage, slot, wheres, quads, group, h):
    for where, ref in zip(wheres, [ref for refs in quads for ref in refs]):
        stage[slot, pl.ds(where, BLOCK), :] = take(ref, group, h)
    return stage[slot]


def give(refs, group, h, lanes, value):
    if len(refs.shape) == 4:
        refs[group, h, :, lanes] = value
    else:
        refs[h, :, lanes] = value


def scatter(quads, group, h, lanes, value):
    for n, ref in enumerate([ref for refs in quads for ref in refs]):
        give(ref, group, h, lanes, value[n * BLOCK : (n + 1) * BLOCK])


def scatter_from(stage, slot, wheres, quads, group, h, lanes):
    for where, ref in zip(wheres, [ref for refs in quads for ref in refs]):
        give(ref, group, h, lanes, stage[slot, pl.ds(where, BLOCK), :])


def outgoing_kernel(info, *refs):
    *refs, stage = refs
    *refs, o_own, o_near, o_y, o_yc, o_x, o_xc = refs
    a_own, b_own, a_y, b_x, a_yc, b_xc, near = paired(refs)
    a_near, b_near = [ref.at[:2] for ref in near], [ref.at[2:] for ref in near]
    along_a, along_b = (a_own, a_near, a_y, a_yc), (b_own, b_near, b_x, b_xc)
    for h in range(CHANNELS):
        for group in range(2):
            lefts, rights = (along_a, along_b) if group == 0 else (along_b, along_a)
            far = (o_y, o_yc) if group == 0 else (o_x, o_xc)
            right = gather(stage, 2 * h + group, places(info, group), rights, group, h)
            inner = dot_nt(joined(lefts, group, h), right).astype(BF16)
            for n, out in enumerate((o_own, o_near) + far):
                rows = PARTS * BLOCK
                give(out, group, h, slice(0, LANES), inner[n * rows : (n + 1) * rows])


def halves(quads, group, h):
    both = joined(quads, group, h)
    return both[:, :LANES], both[:, LANES:]


def incoming_kernel(info, *refs):
    *refs, stage = refs
    own, ypart, xpart, ycpart, xcpart, near, o_own, o_near, o_x, o_xc, o_y, o_yc = paired(refs)
    for h in range(CHANNELS):
        for group in range(2):
            far = (ypart, ycpart) if group == 0 else (xpart, xcpart)
            outs = (o_own, o_near) + ((o_x, o_xc) if group == 0 else (o_y, o_yc))
            slot = 2 * h + group
            left, right = halves((own, near) + far, group, h)
            stage[slot] = dot_tn(left, right).astype(BF16)
            scatter_from(stage, slot, places(info, group), outs, group, h, slice(0, 2 * LANES))


def incoming_back_kernel(info, *refs):
    *refs, stage = refs
    own, ypart, xpart, ycpart, xcpart, near, *more = paired(refs)
    same0, same1, g_y, g_x, g_yc, g_xc, g_near, *more = more
    o_own, o_near, o_y, o_yc, o_x, o_xc = more
    for h in range(CHANNELS):
        for group in range(2):
            far = (ypart, ycpart) if group == 0 else (xpart, xcpart)
            grads = (same0, g_near, g_x, g_xc) if group == 0 else (same1, g_near, g_y, g_yc)
            outs = (o_own, o_near) + ((o_y, o_yc) if group == 0 else (o_x, o_xc))
            grad = gather(stage, 2 * h + group, places(info, group), grads, group, h)
            left, right = halves((own, near) + far, group, h)
            scatter(outs, group, h, slice(0, LANES), dot_nt(right, grad).astype(BF16))
            scatter(outs, group, h, slice(LANES, 3 * LANES), dot_nn(left, grad).astype(BF16))


def outgoing_back_kernel(info, *refs):
    *refs, stage, back = refs
    a_own, b_own, a_y, b_x, a_yc, b_xc, near, *more = paired(refs)
    a_near, b_near = [ref.at[:2] for ref in near], [ref.at[2:] for ref in near]
    g_own, g_y, g_x, g_yc, g_xc, g_near, o_own, o_near, o_y, o_yc, o_x, o_xc = more
    along_a, along_b = (a_own, a_near, a_y, a_yc), (b_own, b_near, b_x, b_xc)
    first, second = slice(0, 2 * LANES), slice(2 * LANES, 4 * LANES)
    for h in range(CHANNELS):
        for group in range(2):
            lefts, rights = (along_a, along_b) if group == 0 else (along_b, along_a)
            far = (g_y, g_yc) if group == 0 else (g_x, g_xc)
            left_far, right_far = ((o_y, o_yc), (o_x, o_xc)) if group == 0 else ((o_x, o_xc), (o_y, o_yc))
            slot = 2 * h + group
            wheres = places(info, group)
            right = gather(stage, slot, wheres, rights, group, h)
            grad = joined((g_own, g_near) + far, group, h)
            grad_left = dot_nn(grad, right).astype(BF16)
            back[slot] = dot_tn(grad, joined(lefts, group, h)).astype(BF16)
            core_rows = 2 * PARTS * BLOCK
            scatter((o_own, o_near), group, h, first, grad_left[:core_rows])
            scatter(left_far, group, h, first, grad_left[core_rows:])
            scatter_from(back, slot, wheres[: 2 * PARTS], (o_own, o_near), group, h, second)
            scatter_from(back, slot, wheres[2 * PARTS :], right_far, group, h, first)


def whole(shape):
    return pl.BlockSpec(shape, lambda step, info: (0,) * len(shape))


def fixed(shape):
    return whole(shape)


fixed.kept = True


def rows_of(part, some=SOME):
    def make(shape):
        first = part * (BLOCK // some)
        return pl.BlockSpec(
            (some,) + shape[1:], lambda step, info: (first + step,) + (0,) * (len(shape) - 1)
        )

    make.kept = True
    return make


def rows_block(part):
    def make(shape):
        return pl.BlockSpec(
            shape[:-2] + (BLOCK, shape[-1]),
            lambda step, info: (0,) * (len(shape) - 2) + (part, 0),
        )

    return make


def anywhere(shape):
    return pl.BlockSpec(memory_space=pl.ANY)


def channel_rows(shape):
    if len(shape) == 4:
        return pl.BlockSpec((shape[0], CHANNELS) + shape[2:], lambda step, info: (0, step, 0, 0))
    return pl.BlockSpec((CHANNELS,) + shape[1:], lambda step, info: (step, 0, 0))


def in_place(array):
    return pltpu.with_memory_space_constraint(array, pltpu.HBM)


def call(kernel, info, steps, ins, outs, scratch, aliases={}, vmem=CELL_VMEM):
    return pl.pallas_call(
        kernel,
        grid_spec=pltpu.PrefetchScalarGridSpec(
            num_scalar_prefetch=1,
            grid=(steps,),
            in_specs=[make(array.shape) for array, make in ins],
            out_specs=[make(shape) for shape, unused, make in outs],
            scratch_shapes=scratch,
        ),
        out_shape=[
            (pltpu.HBM if getattr(make, "kept", False) else jax.ShapeDtypeStruct)(shape, dtype)
            for shape, dtype, make in outs
        ],
        compiler_params=pltpu.CompilerParams(vmem_limit_bytes=vmem),
        input_output_aliases=aliases,
    )(info, *[in_place(array) if getattr(make, "kept", False) else array for array, make in ins])


class Links:
    def __init__(self):
        self.last = {}

    def send(self, array, offset, first=None, core_first=False):
        count = lax.axis_size("axial")
        if first is not None:
            array, unused = lax.optimization_barrier((array, first))
        keys = (offset, CORE) if core_first else (offset,)
        after = [self.last[key] for key in keys if key in self.last]
        if after and offset in (X, Y):
            array, *unused = lax.optimization_barrier((array, *after))
        self.last[offset] = lax.ppermute(
            array, "axial", [(n, n ^ offset) for n in range(count)]
        )
        return self.last[offset]

    def __call__(self, *sends, between=None, core_first=False):
        results = [[] for unused in sends]
        for part in range(len(sends[0][0])):
            for result, (arrays, offset) in zip(results, sends):
                first = between if part else None
                result.append(self.send(arrays[part], offset, first, core_first))
        return results


CORE, X, Y = 1, 2, 4


def add_up(share):
    count = lax.axis_size("axial")
    rows, width = share.shape
    shares = share.reshape(count, rows // count, width)
    parts = lax.all_to_all(shares, "axial", split_axis=0, concat_axis=0, tiled=True)
    mine = parts.astype(F32).sum(axis=0).astype(BF16)
    depth = lax.axis_size("dp")
    terms = [mine] + [
        lax.ppermute(mine, "dp", [(n, n ^ offset) for n in range(depth)])
        for offset in range(1, depth)
    ]
    terms = [term.astype(F32) for term in terms]
    while len(terms) > 1:
        terms = [terms[n] + terms[n + 1] for n in range(0, len(terms), 2)]
    copies = jnp.broadcast_to(terms[0].astype(BF16)[None], shares.shape)
    return lax.all_to_all(copies, "axial", split_axis=0, concat_axis=0, tiled=True).reshape(
        rows, width
    )


def gain_grad(weight_grad, weight, gain_row):
    return jnp.sum((weight.astype(F32) * weight_grad).T, axis=0, keepdims=True) / gain_row


def finish_kernel(
    scale, info, sums, proj1, final1, proj2, final2, norm1, gain1, norm2, gain2,
    o_norm1, o_proj1, o_gain1, o_final1, o_norm2, o_proj2, o_gain2, o_final2,
):
    width, channels = proj1.shape[1], final1.shape[1]
    takes = (
        (0, True, proj1, norm1, o_proj1, o_norm1),
        (width, True, proj2, norm2, o_proj2, o_norm2),
        (2 * width, False, final2, gain2, o_final2, o_gain2),
        (2 * width + channels, False, final1, gain1, o_final1, o_gain1),
    )
    for start, flipped, weight, gain, out, gain_out in takes:
        total = sums[start : start + weight.shape[1], :].astype(F32) * scale
        total = total.T if flipped else total
        out[...] = total
        gain_out[...] = gain_grad(total, weight[...].astype(BF16), gain[...])


def fast_body(
    pair,
    cotangent,
    lengths,
    outgo_norm,
    outgo_proj,
    outgo_gain,
    outgo_final,
    incom_norm,
    incom_proj,
    incom_gain,
    incom_final,
):
    rows, tokens, channels = pair.shape[1:]
    hidden = outgo_gain.shape[0]
    index = lax.axis_index("axial")
    info = jnp.stack(
        [(index // 2) % 2, index // 4, index % 2, index * rows, lengths[0]]
    ).astype(jnp.int32)
    hop = Links()
    pair = pair[0]
    cot = cotangent[0]
    parts = range(PARTS)
    turns = GROUP // CHANNELS
    stage = pltpu.VMEM((2, BLOCK, hidden, LANES), F32)
    out_stage = pltpu.VMEM((2, BLOCK, hidden, LANES), BF16)
    perm = pltpu.VMEM((BLOCK * BLOCK, BLOCK * BLOCK), BF16)
    streamed = rows_of(0)
    square = pltpu.VMEM((2 * CHANNELS, 4 * rows, tokens), BF16)

    def two(width, height=BLOCK, make=whole, groups=2):
        return ((groups, GROUP, height, width), BF16, make)

    def one(width, height=BLOCK, make=whole):
        return ((GROUP, height, width), BF16, make)

    turned_block = ((BLOCK, channels, tokens), BF16, streamed)
    factor_block = ((BLOCK, 4 * hidden, tokens), BF16, streamed)
    mixture_block = ((BLOCK, 5 * hidden, tokens), BF16, streamed)

    def cells(kernel, ins, outs, scratch, more=lambda part: []):
        results = []
        for part in parts:
            carried = ins(part, results)
            results.append(
                call(functools.partial(kernel, part), info, STEPS, carried, outs + more(part), scratch)
            )
        shared = results[-1][len(outs) :]
        return [list(each) for each in zip(*results)] + list(shared)

    def wholes(arrays):
        return [(array, whole) for array in arrays]

    def triangle(kernel, operands, outs, scratch, split=PARTS):
        ins = [(array, channel_rows) for arrays in operands for array in arrays]
        each = [out for out in outs for unused in range(split)]
        results = call(kernel, info, turns, ins, each, scratch, vmem=TRIANGLE_VMEM)
        return [list(results[n : n + split]) for n in range(0, len(results), split)]

    raw = (outgo_gain[None], outgo_final, incom_norm[None], incom_proj, incom_gain[None], incom_final)
    gain_wide = ((channels, LANES), F32, whole)
    proj_turned = ((5 * hidden, channels), BF16, whole)
    proj_plain = ((channels, 5 * hidden), BF16, whole)
    final_plain = ((hidden, channels), BF16, whole)
    (
        a_same, a_other, b_same, b_other, to_core, gate_one, factors_one,
        norm1, gain1, norm2, gain2, proj2_t, final1_t, final2_t,
        proj1, final1, proj2, final2,
    ) = cells(
        entry_kernel,
        lambda part, unused: [(pair, rows_of(part)), (outgo_norm[None], fixed), (outgo_proj, fixed)]
        + ([(weight, fixed) for weight in raw] if part else []),
        [two(tokens)] * 4 + [two(tokens, groups=4), turned_block, factor_block],
        [
            out_stage,
            out_stage,
            pltpu.VMEM((channels, LANES), F32),
            pltpu.VMEM((5 * hidden, channels), BF16),
            perm,
        ],
        lambda part: (
            [gain_wide] * 4
            + [proj_turned]
            + [final_plain] * 2
            + [proj_plain, final_plain] * 2
            if part
            else []
        ),
    )
    held_one = [a_same, b_same] + hop(
        (a_same, Y), (b_same, X), (a_other, Y | CORE), (b_other, X | CORE), (to_core, CORE)
    )
    own, near, to_y, to_yc, to_x, to_xc = triangle(
        outgoing_kernel,
        held_one,
        [two(LANES, rows, channel_rows)] * 2 + [one(LANES, rows, channel_rows)] * 4,
        [square],
        split=1,
    )
    back_one = [
        own,
        *hop(
            (to_y, Y), (to_x, X), (to_yc, Y | CORE), (to_xc, X | CORE), (near, CORE)
        ),
    ]

    (
        middle, inner_one, gate_two, factors_two, normed_two, finals_one, slopes_one,
        own, near, to_y, to_yc, to_x, to_xc,
    ) = cells(
        middle_kernel,
        lambda part, unused: [(pair, rows_of(part))]
        + [(array, rows_block(part)) for array, in back_one]
        + [(gate_one[part], streamed)]
        + wholes((gain1, final1_t, norm2, proj2_t)),
        [turned_block] * 3
        + [factor_block]
        + [turned_block] * 3
        + [two(3 * LANES)] * 2 + [one(3 * LANES)] * 4,
        [stage, out_stage, out_stage, perm],
    )
    held_two = [own] + hop(
        (to_y, Y), (to_x, X), (to_yc, Y | CORE), (to_xc, X | CORE), (near, CORE), core_first=True
    )
    own, near, to_x, to_xc, to_y, to_yc = triangle(
        incoming_kernel,
        held_two,
        [two(tokens, make=channel_rows)] * 2 + [one(tokens, make=channel_rows)] * 4,
        [square],
    )
    back_two = [
        own,
        *hop(
            (to_y, Y), (to_x, X), (to_yc, Y | CORE), (to_xc, X | CORE), (near, CORE)
        ),
    ]

    gate_grad_two, finals_two, products_two, same0, same1, other0, other1, to_core = cells(
        turn_kernel,
        lambda part, done: [(gate_two[part], streamed), (cot, rows_of(part))]
        + wholes(arrays[part] for arrays in back_two)
        + wholes((gain2, final2_t, final2)),
        [turned_block] * 3 + [one(tokens)] * 4 + [two(tokens)],
        [stage, out_stage, perm],
    )
    grads_two = [
        same0,
        same1,
        *hop(
            (same1, Y), (same0, X), (other1, Y | CORE), (other0, X | CORE), (to_core, CORE)
        ),
    ]
    own, near, to_y, to_yc, to_x, to_xc = triangle(
        incoming_back_kernel,
        held_two + grads_two,
        [two(3 * LANES, make=channel_rows)] * 2 + [one(3 * LANES, make=channel_rows)] * 4,
        [square],
    )
    rows_two = [
        own,
        *hop(
            (to_y, Y), (to_x, X), (to_yc, Y | CORE), (to_xc, X | CORE), (near, CORE)
        ),
    ]

    (
        grad_middle, gate_grad_one, mixtures_two, products_one,
        own, near, to_y, to_yc, to_x, to_xc,
    ) = cells(
        inward_kernel,
        lambda part, done: [
            (middle[part], streamed),
            (gate_one[part], streamed),
            (cot, rows_of(part)),
            (inner_one[part], streamed),
            (gate_grad_two[part], streamed),
            (factors_two[part], streamed),
            (slopes_one[part], streamed),
        ]
        + wholes(arrays[part] for arrays in rows_two)
        + wholes((norm2, proj2, gain1, final1)),
        [turned_block, turned_block, mixture_block, turned_block]
        + [two(LANES)] * 2
        + [one(LANES)] * 4,
        [stage, stage, out_stage, perm],
    )
    grads_one = [
        own,
        *hop(
            (to_y, Y), (to_x, X), (to_yc, Y | CORE), (to_xc, X | CORE), (near, CORE)
        ),
    ]
    own, near, to_y, to_yc, to_x, to_xc = triangle(
        outgoing_back_kernel,
        held_one + grads_one,
        [two(2 * tokens, make=channel_rows)] * 2 + [two(tokens, make=channel_rows)] * 4,
        [square, square],
    )
    kept = (mixtures_two, normed_two, finals_two, products_two, finals_one, products_one)
    (early,) = call(
        weight_kernel,
        info,
        4,
        [
            (array, rows_of(0, BLOCK // 4))
            for arrays in kept
            for array in arrays
        ],
        [((5 * hidden + 2 * channels, channels), F32, whole)],
        [],
    )
    rows_one = [own] + hop(
        (to_y, Y), (to_x, X), (to_yc, Y | CORE), (to_xc, X | CORE), (near, CORE), between=early
    )
    exit_ins = 10 + 3 + 1 + 1
    result = None
    for part in parts:
        result = call(
            functools.partial(exit_kernel, part),
            info,
            STEPS,
            [
                (pair, rows_of(part)),
                (grad_middle[part], streamed),
                (gate_grad_one[part], streamed),
                (factors_one[part], streamed),
            ]
            + wholes(arrays[part] for arrays in rows_one)
            + wholes((norm1, proj1, early))
            + ([(result[1], whole), (result[0], anywhere)] if part else []),
            [
                ((rows, tokens, channels), F32, rows_of(part)),
                ((5 * hidden, channels), F32, whole),
            ]
            + ([((10 * hidden + 2 * channels, channels), BF16, whole)] if part else []),
            [stage, stage, perm],
            {exit_ins: 0} if part else {},
        )
    grad_begin, unused, packed = result
    sums = add_up(packed)
    scale = 1.0 / math.sqrt(lax.axis_size("dp") * tokens * tokens)
    weights = (outgo_proj, outgo_final, incom_proj, incom_final)
    gains = (outgo_norm, outgo_gain, incom_norm, incom_gain)
    order = (outgo_norm[None], outgo_proj, outgo_gain[None], outgo_final)
    order += (incom_norm[None], incom_proj, incom_gain[None], incom_final)
    totals = call(
        functools.partial(finish_kernel, scale),
        info,
        1,
        wholes((sums,) + weights + tuple(gain[None] for gain in gains)),
        [(array.shape, F32, whole) for array in order],
        [],
    )
    return (grad_begin[None],) + tuple(
        total.reshape(-1) if total.shape[0] == 1 else total for total in totals
    )


def solution(mesh):
    def body(pair, *rest):
        rows, tokens, channels = pair.shape[1:]
        hidden = rest[3].shape[0]
        plane = mesh.shape["axial"] == 8 and rows == 32 and tokens == 2 * LANES
        if plane and channels == LANES and hidden == 4 * GROUP:
            return fast_body(pair, *rest)
        return plain_body(pair, *rest)

    return jax.shard_map(
        body,
        mesh=mesh,
        in_specs=(P("dp", "axial", None, None), P("dp", "axial", None, None), P("dp")) + (P(),) * 8,
        out_specs=(P("dp", "axial", None, None),) + (P(),) * 8,
        check_vma=False,
    )
```
